32 devices in a mesh: group: 2 (over y), row: 4 (over z), col: 2 (over x), rep: 2 (over core).
Axes of the slice: x: 2, y: 2, z: 4, core: 2. Of those that a mesh axis runs over, the one named last changes fastest.
Arguments:
- matrix: float32 [192, 7, 64, 64], P(('group', 'row', 'col'), None, 'rep'), parts along dimension 0, as said below
- pattern: int32 [192, 7], P('group'), parts along dimension 0, may hold values from 0 to 1, as said below
Outputs:
- square: float32 [192, 7, 64, 64], P(('group', 'row', 'col'), None, 'rep'), parts along dimension 0
- sign_next: float32 [192, 7, 64, 64], P(('group', 'row', 'col'), None, 'rep'), parts along dimension 0
The draws below stay inside these ranges and needn't reach their ends.
There are 2 independent parts, one for each index of `group`. The reference program is written for one: setup_inputs(seed, part) draws one part's arguments, and reference() takes and returns one part's arrays. A program takes and returns all parts, laid end to end along the dimension named above; each array names one. Nothing has to cross between parts.
Inputs may be any that keep to these rules, and one draw needn't show every extreme that they name: symmetric: pattern[a, k] equals pattern[(a + k - 3) mod 96, 6 - k]; ones at k = 3; from distances between block positions. Symmetric as a whole matrix; zero in the blocks whose pattern flag is 0.
All inputs are finite; a program needn't handle non-finite values.
Results may differ from the reference program's by a relative error of at most 0.0001.
Values sent between devices are 32-bit elements; how exact they have to be, the bound alone decides.
No kernel may reach another device: no remote copies, remote signals or barrier semaphores. Data moves between devices by JAX's collectives and lax.ppermute only.
A program may use at most 64 MiB of HBM per device.

```python
import math
import jax
import jax.numpy as jnp
from jax import lax

BS = 64
REACH = 3
SPAN = 7
NB = 96


def shared_pattern(key):
    shifts = jax.random.randint(jax.random.fold_in(key, 11), (NB,), 0, 3)
    height = jax.random.randint(jax.random.fold_in(key, 12), (NB,), 0, 4)
    depth = jax.random.randint(jax.random.fold_in(key, 13), (NB,), 0, 4)
    offsets = jnp.arange(SPAN, dtype=jnp.int32) - REACH
    partner = (jnp.arange(NB, dtype=jnp.int32)[:, None] + offsets[None, :]) % NB
    along = 3 * offsets[None, :] + shifts[partner] - shifts[:, None]
    across_y = height[partner] - height[:, None]
    across_z = depth[partner] - depth[:, None]
    reach_sq = along * along + 9 * (across_y * across_y + across_z * across_z)
    return (reach_sq <= 9 * REACH * REACH + 36).astype(jnp.int32)


def draw_pattern(key, part):
    return shared_pattern(key)


def draw_matrix(key, part):
    pattern = shared_pattern(key)
    key = jax.random.fold_in(key, 5)
    noise_key, diag_key = jax.random.split(key, 2)
    offsets = jnp.arange(SPAN, dtype=jnp.int32) - REACH
    partner = (jnp.arange(NB, dtype=jnp.int32)[:, None] + offsets[None, :]) % NB
    mirror = (SPAN - 1 - jnp.arange(SPAN, dtype=jnp.int32))[None, :]
    noise = jax.random.truncated_normal(noise_key, -4.0, 4.0, (NB, SPAN, BS, BS), jnp.float32)
    facing = jnp.swapaxes(noise[partner, mirror], 2, 3)
    coupled = (noise + facing) * (0.4 / math.sqrt(BS * SPAN))
    diag_vals = jax.random.uniform(diag_key, (NB, BS), jnp.float32, -0.8, 0.8)
    centre = (jnp.arange(SPAN) == REACH).astype(jnp.float32)[None, :, None, None]
    eye_block = jnp.eye(BS, dtype=jnp.float32)[None, None]
    flags = pattern.astype(jnp.float32)[:, :, None, None]
    return flags * coupled + centre * eye_block * diag_vals[:, None, :, None]


def setup_inputs(seed: int = 0, part: int = 0) -> dict:
    seeds = jax.random.split(jax.random.key(seed), 3)
    part_keys = jax.random.split(jax.random.fold_in(seeds[2], part), 3)
    matrix = draw_matrix(jax.random.fold_in(jax.random.fold_in(seeds[2], part), 71), part)
    pattern = draw_pattern(jax.random.fold_in(jax.random.fold_in(seeds[2], part), 71), part)
    return dict(matrix=matrix, pattern=pattern)


def band_product(factor, others, reach):
    count = factor.shape[0]
    span = factor.shape[1]
    columns = []
    for target in range(span):
        total = None
        for offset in range(span):
            source_col = target - offset + reach
            if source_col >= 0 and source_col < span:
                piece = jnp.einsum("rij,rjl->ril", factor[:, offset], others[offset:offset + count, source_col], precision=lax.Precision.HIGHEST, preferred_element_type=jnp.float32)
                total = piece if total is None else total + piece
        columns.append(total)
    return jnp.stack(columns, axis=1)


def extend(blocks, reach):
    return jnp.concatenate([blocks[-reach:], blocks, blocks[:reach]], axis=0)


def reference(matrix, pattern):
    flags = pattern.astype(jnp.float32)[:, :, None, None]
    square = flags * band_product(matrix, extend(matrix, REACH), REACH)
    second = flags * band_product(matrix, extend(square, REACH), REACH)
    sign_next = 1.5 * matrix - 0.5 * second
    return square, sign_next
```

```python
import functools

import jax
import jax.numpy as jnp
from jax import lax
from jax.experimental import pallas as pl
from jax.experimental.pallas import tpu as pltpu
from jax.sharding import PartitionSpec as P

REACH = 3
SPAN = 7
BS = 64
HALF = 32
GROUP = 4
WIDE = GROUP * BS
BF = jnp.bfloat16
F32 = jnp.float32
LIMIT = 40 * 1024 * 1024


def split(x):
    hi = x.astype(BF)
    return hi, (x - hi.astype(F32)).astype(BF)


def dot3(a, b, transposed):
    dims = (((1,), (1 if transposed else 0,)), ((), ()))
    one = functools.partial(lax.dot_general, dimension_numbers=dims, preferred_element_type=F32)
    return one(a[0], b[0]) + (one(a[0], b[1]) + one(a[1], b[0]))


def flag_row(pat, row, places):
    lane = lax.broadcasted_iota(jnp.int32, (1, WIDE), 1)
    line = jnp.zeros((1, WIDE), F32)
    for place, k in places:
        value = pat[k, row].astype(F32)
        line = jnp.where((lane >= place * BS) & (lane < (place + 1) * BS), value, line)
    return line


def edge_kernel(top, bottom, to_left, to_right):
    for s in range(REACH):
        rows = slice(s * HALF, (s + 1) * HALF)
        for t in range(2):
            lanes = slice(t * 2 * BS, (t + 1) * 2 * BS)
            to_left[rows, lanes] = jnp.concatenate(
                [top[s, REACH + 2 * t], top[s, REACH + 2 * t + 1]], axis=1
            )
            to_right[rows, lanes] = jnp.concatenate([bottom[s, 2 * t], bottom[s, 2 * t + 1]], axis=1)


def interior_kernel(
    own, other, pat, square, sign, low_a, low_b, low_m, low_p, high_a, high_b, high_m, high_p,
    full, mine, tile, keep, *, axes, half_axis
):
    count = own.shape[0]
    total = pat.shape[1]
    groups = count // GROUP
    first = lax.axis_index(axes) * count
    half = lax.axis_index(half_axis)
    own_at = half * HALF
    other_at = HALF - own_at

    for a in range(count):
        g, s = divmod(a, GROUP)
        for src, at in ((own, own_at), (other, other_at)):
            rows = pl.ds(pl.multiple_of(s * BS + at, HALF), HALF)
            for t in range(3 * GROUP // 2):
                ks = [2 * t + e - s - 1 for e in range(2)]
                lanes = slice(t * 2 * BS, (t + 1) * 2 * BS)
                if all(k < 0 or k >= SPAN for k in ks):
                    parts = (jnp.zeros((HALF, 2 * BS), BF),) * 2
                else:
                    parts = split(
                        jnp.concatenate(
                            [
                                src[a, k] if 0 <= k < SPAN else jnp.zeros((HALF, BS), F32)
                                for k in ks
                            ],
                            axis=1,
                        )
                    )
                for p in range(2):
                    full[p, g, rows, lanes] = parts[p]
                    if src is own:
                        mine[p, g, s * HALF : (s + 1) * HALF, lanes] = parts[p]

    def panel(ref, g, lo, hi, r0=0, r1=None):
        return [ref[p, g, r0:r1, lo * WIDE : hi * WIDE] for p in range(2)]

    def flags(g, s, delta):
        a = g * GROUP + s
        places = [
            (t, t + GROUP * delta - s + REACH)
            for t in range(GROUP)
            if 0 <= t + GROUP * delta - s + REACH < SPAN
        ]
        row = lax.rem(first + a + total, total)
        return flag_row(pat, row, places)

    def masked(g, delta, value):
        return jnp.concatenate(
            [value[s * BS : (s + 1) * BS] * flags(g, s, delta) for s in range(GROUP)], axis=0
        )

    def emit_square(g, delta, value):
        tile[...] = value
        for s in range(GROUP):
            part = tile[pl.ds(pl.multiple_of(s * BS + own_at, HALF), HALF), :]
            for t in range(GROUP):
                k = t + GROUP * delta - s + REACH
                if 0 <= k < SPAN:
                    square[g * GROUP + s, k] = part[:, t * BS : (t + 1) * BS]

    def emit_sign(g, delta, value):
        for s in range(GROUP):
            part = value[s * HALF : (s + 1) * HALF] * (flags(g, s, delta) * 0.5)
            for t in range(GROUP):
                k = t + GROUP * delta - s + REACH
                if 0 <= k < SPAN:
                    a = g * GROUP + s
                    sign[a, k] = 1.5 * own[a, k] - part[:, t * BS : (t + 1) * BS]

    diag = []
    upper = []
    for g in range(groups):
        r = panel(full, g, 0, 3)
        value = masked(g, 0, dot3(r, r, True))
        emit_square(g, 0, value)
        for p, part in enumerate(split(value)):
            keep[p, 2 * g] = part
        if g + 1 < groups:
            value = masked(g, 1, dot3(panel(full, g, 1, 3), panel(full, g + 1, 0, 2), True))
            emit_square(g, 1, value)
            emit_square(g + 1, -1, value.T)
            for p, part in enumerate(split(value)):
                keep[p, 2 * g + 1] = part

    def kept(i):
        return [keep[p, i] for p in range(2)]

    for g in range(groups):
        low = panel(mine, g, 0, 1)
        mid = panel(mine, g, 1, 2)
        high = panel(mine, g, 2, 3)
        centre = dot3(mid, kept(2 * g), True)
        if g > 0:
            centre = centre + dot3(low, kept(2 * g - 1), False)
            emit_sign(g, -1, dot3(low, kept(2 * g - 2), True) + dot3(mid, kept(2 * g - 1), True))
        if g + 1 < groups:
            centre = centre + dot3(high, kept(2 * g + 1), True)
            emit_sign(g, 1, dot3(mid, kept(2 * g + 1), False) + dot3(high, kept(2 * g + 2), True))
        emit_sign(g, 0, centre)
    for s in range(REACH):
        for t in range(REACH - s):
            sign[s, t] = 1.5 * own[s, t]
            sign[count - 1 - s, SPAN - 1 - t] = 1.5 * own[count - 1 - s, SPAN - 1 - t]

    last = groups - 1
    for a_ref, b_ref, m_ref, p_ref, g, part, r0 in (
        (low_a, low_b, low_m, low_p, 0, 0, 0),
        (high_a, high_b, high_m, high_p, last, 2, BS),
    ):
        rows = slice(r0, r0 + REACH * BS)
        out = panel(full, g, part, part + 1)
        turned = [x.astype(F32).T.astype(BF) for x in out]
        a_ref[...] = dot3(turned, turned, True)
        b_ref[...] = dot3(panel(full, g, 1, 2), turned, True)[rows]
        for p in range(2):
            m_ref[p] = out[p][rows]
            p_ref[p, 0] = mine[p, g, r0 // 2 : r0 // 2 + REACH * HALF, part * WIDE : (part + 1) * WIDE]
            p_ref[p, 1] = mine[p, g, r0 // 2 : r0 // 2 + REACH * HALF, WIDE : 2 * WIDE]


def border_kernel(
    low_own, low_other, high_own, high_other, pat, low_a, low_b, low_m, low_p, high_a, high_b,
    high_m, high_p, square_in, sign_in, square_out, sign_out, near, halo, tile, keep, blocks, sems,
    *, axes, half_axis
):
    count = square_in.shape[0]
    total = pat.shape[1]
    first = lax.axis_index(axes) * count
    own_at = lax.axis_index(half_axis) * HALF
    other_at = HALF - own_at
    ends = (0, count - REACH)
    loads = [
        pltpu.make_async_copy(ref.at[pl.ds(ends[side], REACH)], blocks.at[i, side], sems.at[i, side])
        for i, ref in enumerate((square_in, sign_in))
        for side in range(2)
    ]
    for load in loads:
        load.start()

    def put(p, rows, lanes, value):
        for q, part in enumerate(split(value)):
            halo[q, rows, lanes] = part

    def sides(side):
        return (
            (low_own, low_other, low_a, low_b, low_m, low_p)
            if side == 0
            else (high_own, high_other, high_a, high_b, high_m, high_p)
        )

    squares = []
    for side in range(2):
        mine, theirs, a_ref, b_ref, m_ref, p_ref = sides(side)
        for p in range(REACH):
            for src, at in ((mine, own_at), (theirs, other_at)):
                near[side, pl.ds(pl.multiple_of(p * BS + at, HALF), HALF), :] = src[
                    p * HALF : (p + 1) * HALF, :
                ]
        def block(p, c):
            k = c - p + (REACH if side == 0 else 0)
            if 0 <= k <= REACH:
                return near[side, p * BS : (p + 1) * BS, k * BS : (k + 1) * BS]
            k = p - c + (REACH if side == 0 else 0)
            if 0 <= c < REACH and 0 <= k <= REACH:
                return near[side, c * BS : (c + 1) * BS, k * BS : (k + 1) * BS].T
            return jnp.zeros((BS, BS), F32)

        base = -5 if side == 0 else 0
        for p in range(REACH):
            for t in range(4):
                cs = [base + 2 * t, base + 2 * t + 1]
                value = jnp.concatenate([block(p, c) for c in cs], axis=1)
                for q, part in enumerate(split(value)):
                    halo[side, q, p * BS : (p + 1) * BS, t * 2 * BS : (t + 1) * 2 * BS] = part
    for load in loads:
        load.wait()

    lane = lax.broadcasted_iota(jnp.int32, (1, WIDE), 1)
    for side in range(2):
        mine, theirs, a_ref, b_ref, m_ref, p_ref = sides(side)
        shift = 1 if side == 0 else 0
        row0 = shift * BS
        whole = [halo[side, q] for q in range(2)]
        inner = [halo[side, q, :, (WIDE if side == 0 else 0) : (2 * WIDE if side == 0 else WIDE)] for q in range(2)]
        outer_first = first - REACH if side == 0 else first + count
        edge_first = first + ends[side]

        rows = []
        value = dot3(whole, whole, True) + a_ref[row0 : row0 + REACH * BS, row0 : row0 + REACH * BS]
        lane3 = lax.broadcasted_iota(jnp.int32, (1, REACH * BS), 1)
        for p in range(REACH):
            row = lax.rem(outer_first + p + total, total)
            line = jnp.zeros((1, REACH * BS), F32)
            for t in range(REACH):
                f = pat[t - p + REACH, row].astype(F32)
                line = jnp.where((lane3 >= t * BS) & (lane3 < (t + 1) * BS), f, line)
            rows.append(value[p * BS : (p + 1) * BS] * line)
        corner = split(jnp.concatenate(rows, axis=0))

        m = [m_ref[q] for q in range(2)]
        m3 = [x[:, row0 : row0 + REACH * BS] for x in m]
        inner3 = [x[:, row0 : row0 + REACH * BS] for x in inner]
        value = dot3(m3, inner3, True) + b_ref[:, row0 : row0 + REACH * BS]
        rows = []
        lines = []
        for s in range(REACH):
            row = lax.rem(edge_first + s, total)
            line = jnp.zeros((1, REACH * BS), F32)
            for t in range(REACH):
                k = t - s + (0 if side == 0 else 2 * REACH)
                if 0 <= k < SPAN:
                    f = pat[k, row].astype(F32)
                    line = jnp.where((lane3 >= t * BS) & (lane3 < (t + 1) * BS), f, line)
            lines.append(line)
            rows.append(value[s * BS : (s + 1) * BS] * line)
        value = jnp.concatenate(rows, axis=0)
        tile[side] = value
        across = split(value)

        reach_out = [p_ref[q, 0][:, row0 : row0 + REACH * BS] for q in range(2)]
        col0 = 0 if side == 0 else BS
        inside = [p_ref[q, 1][:, col0 : col0 + REACH * BS] for q in range(2)]
        out = dot3(reach_out, corner, True) + dot3(inside, across, False)
        back = dot3(reach_out, across, True)
        for s in range(REACH):
            row = lax.rem(edge_first + s, total)
            part = tile[side, pl.ds(pl.multiple_of(s * BS + own_at, HALF), HALF), :]
            far = out[s * HALF : (s + 1) * HALF] * (lines[s] * 0.5)
            near_line = jnp.zeros((1, REACH * BS), F32)
            for t in range(REACH):
                f = pat[t - s + REACH, row].astype(F32)
                near_line = jnp.where((lane3 >= t * BS) & (lane3 < (t + 1) * BS), f, near_line)
            close = back[s * HALF : (s + 1) * HALF] * (near_line * 0.5)
            for t in range(REACH):
                k = t - s + (0 if side == 0 else 2 * REACH)
                lanes = slice(t * BS, (t + 1) * BS)
                if 0 <= k < SPAN:
                    blocks[0, side, s, k] = part[:, lanes]
                    blocks[1, side, s, k] = blocks[1, side, s, k] - far[:, lanes]
                k = t - s + REACH
                blocks[1, side, s, k] = blocks[1, side, s, k] - close[:, lanes]

    stores = [
        pltpu.make_async_copy(blocks.at[i, side], ref.at[pl.ds(ends[side], REACH)], sems.at[i, side])
        for i, ref in enumerate((square_out, sign_out))
        for side in range(2)
    ]
    for store in stores:
        store.start()
    for store in stores:
        store.wait()


def shards(matrix, pattern, *, axes, half_axis):
    count = matrix.shape[0]
    groups = count // GROUP
    flags = pattern.T
    vmem = pl.BlockSpec(memory_space=pltpu.VMEM)
    smem = pl.BlockSpec(memory_space=pltpu.SMEM)
    anywhere = pl.BlockSpec(memory_space=pl.ANY)
    params = pltpu.CompilerParams(vmem_limit_bytes=LIMIT)

    edge = jax.ShapeDtypeStruct((REACH * HALF, (REACH + 1) * BS), F32)
    ends = count // REACH - 1
    to_left, to_right = pl.pallas_call(
        edge_kernel,
        grid=(1,),
        out_shape=(edge, edge),
        in_specs=[
            pl.BlockSpec((REACH, SPAN, HALF, BS), lambda i: (0, 0, 0, 0)),
            pl.BlockSpec((REACH, SPAN, HALF, BS), lambda i: (ends, 0, 0, 0)),
        ],
        out_specs=[pl.BlockSpec(edge.shape, lambda i: (0, 0))] * 2,
        compiler_params=params,
    )(matrix, matrix)

    size = 1
    for axis in axes:
        size *= lax.axis_size(axis)
    swap = [(0, 1), (1, 0)]
    other = lax.ppermute(matrix, half_axis, swap)
    ring = axes + (half_axis,)

    def around(step, cross):
        return [
            (2 * i + r, 2 * ((i + step) % size) + (1 - r if cross else r))
            for i in range(size)
            for r in range(2)
        ]

    low_own = lax.ppermute(to_right, ring, around(1, False))
    high_own = lax.ppermute(to_left, ring, around(-1, False))
    low_other = lax.ppermute(to_right, ring, around(1, True))
    high_other = lax.ppermute(to_left, ring, around(-1, True))

    names = dict(axes=axes, half_axis=half_axis)
    ends_out = [
        jax.ShapeDtypeStruct((WIDE, WIDE), F32),
        jax.ShapeDtypeStruct((REACH * BS, WIDE), F32),
        jax.ShapeDtypeStruct((2, REACH * BS, WIDE), BF),
        jax.ShapeDtypeStruct((2, 2, REACH * HALF, WIDE), BF),
    ] * 2
    band = jax.ShapeDtypeStruct(matrix.shape, F32)
    square, sign, *inside = pl.pallas_call(
        functools.partial(interior_kernel, **names),
        out_shape=[band, band] + ends_out,
        in_specs=[vmem, vmem, smem],
        out_specs=[vmem] * 10,
        scratch_shapes=[
            pltpu.VMEM((2, groups, WIDE, 3 * WIDE), BF),
            pltpu.VMEM((2, groups, GROUP * HALF, 3 * WIDE), BF),
            pltpu.VMEM((WIDE, WIDE), F32),
            pltpu.VMEM((2, 2 * groups - 1, WIDE, WIDE), BF),
        ],
        compiler_params=params,
        cost_estimate=pl.CostEstimate(
            flops=3 * 2 * 16 * WIDE**3, bytes_accessed=6 * 2**20, transcendentals=0
        ),
    )(matrix, other, flags)

    return tuple(
        pl.pallas_call(
            functools.partial(border_kernel, **names),
            out_shape=(band, band),
            in_specs=[vmem] * 4 + [smem] + [vmem] * 8 + [anywhere] * 2,
            out_specs=[anywhere] * 2,
            scratch_shapes=[
                pltpu.VMEM((2, REACH * BS, WIDE), F32),
                pltpu.VMEM((2, 2, REACH * BS, 2 * WIDE), BF),
                pltpu.VMEM((2, REACH * BS, REACH * BS), F32),
                pltpu.VMEM((8, 128), F32),
                pltpu.VMEM((2, 2, REACH, SPAN, HALF, BS), F32),
                pltpu.SemaphoreType.DMA((2, 2)),
            ],
            input_output_aliases={13: 0, 14: 1},
            compiler_params=params,
            cost_estimate=pl.CostEstimate(
                flops=3 * 2 * 4 * WIDE**3, bytes_accessed=2 * 2**20, transcendentals=0
            ),
        )(low_own, low_other, high_own, high_other, flags, *inside, square, sign)
    )


def solution(mesh):
    band = P(("group", "row", "col"), None, "rep", None)
    return jax.shard_map(
        functools.partial(shards, axes=("row", "col"), half_axis="rep"),
        mesh=mesh,
        in_specs=(band, P("group", None)),
        out_specs=(band, band),
        check_vma=False,
    )
```

```python
import functools

import jax
import jax.numpy as jnp
from jax import lax
from jax.experimental import pallas as pl
from jax.experimental.pallas import tpu as pltpu
from jax.sharding import PartitionSpec as P

REACH = 3
SPAN = 7
BS = 64
HALF = 32
GROUP = 4
WIDE = GROUP * BS
BF = jnp.bfloat16
F32 = jnp.float32
LIMIT = 40 * 1024 * 1024


def split(x):
    hi = x.astype(BF)
    return hi, (x - hi.astype(F32)).astype(BF)


def dot3(a, b, transposed):
    dims = (((1,), (1 if transposed else 0,)), ((), ()))
    one = functools.partial(lax.dot_general, dimension_numbers=dims, preferred_element_type=F32)
    return one(a[0], b[0]) + (one(a[0], b[1]) + one(a[1], b[0]))


def flag_row(pat, row, places):
    lane = lax.broadcasted_iota(jnp.int32, (1, WIDE), 1)
    line = jnp.zeros((1, WIDE), F32)
    for place, k in places:
        value = pat[k, row].astype(F32)
        line = jnp.where((lane >= place * BS) & (lane < (place + 1) * BS), value, line)
    return line


def edge_kernel(matrix, to_left, to_right, blocks, sems):
    count = matrix.shape[0]
    loads = [
        pltpu.make_async_copy(source, blocks.at[i], sems.at[i])
        for i, source in enumerate(
            (
                matrix.at[pl.ds(0, REACH), pl.ds(REACH, REACH + 1)],
                matrix.at[pl.ds(count - REACH, REACH), pl.ds(0, REACH + 1)],
            )
        )
    ]
    for load in loads:
        load.start()
    for i, target in enumerate((to_left, to_right)):
        loads[i].wait()
        for s in range(REACH):
            for t in range(2):
                target[s * HALF : (s + 1) * HALF, t * 2 * BS : (t + 1) * 2 * BS] = jnp.concatenate(
                    [blocks[i, s, 2 * t], blocks[i, s, 2 * t + 1]], axis=1
                )


def span_of(a, count, is_square):
    if a < REACH:
        return (REACH - a if is_square else 2 * REACH - a), SPAN
    s = a - (count - REACH)
    if s >= 0:
        return 0, (2 * REACH - s if is_square else REACH - s)
    return 0, SPAN


def interior_kernel(
    own, other, pat, square_out, sign_out, seed, low_a, low_b, low_m, low_p, high_a, high_b,
    high_m, high_p, square, sign, full, mine, tile, keep, sems, *, axes, half_axis
):
    count = own.shape[0]
    total = pat.shape[1]
    groups = count // GROUP
    first = lax.axis_index(axes) * count
    half = lax.axis_index(half_axis)
    own_at = half * HALF
    other_at = HALF - own_at

    for a in range(count):
        g, s = divmod(a, GROUP)
        for src, at in ((own, own_at), (other, other_at)):
            rows = pl.ds(pl.multiple_of(s * BS + at, HALF), HALF)
            for t in range(3 * GROUP // 2):
                ks = [2 * t + e - s - 1 for e in range(2)]
                lanes = slice(t * 2 * BS, (t + 1) * 2 * BS)
                if all(k < 0 or k >= SPAN for k in ks):
                    parts = (jnp.zeros((HALF, 2 * BS), BF),) * 2
                else:
                    parts = split(
                        jnp.concatenate(
                            [
                                src[a, k] if 0 <= k < SPAN else jnp.zeros((HALF, BS), F32)
                                for k in ks
                            ],
                            axis=1,
                        )
                    )
                for p in range(2):
                    full[p, g, rows, lanes] = parts[p]
                    if src is own:
                        mine[p, g, s * HALF : (s + 1) * HALF, lanes] = parts[p]

    def panel(ref, g, lo, hi, r0=0, r1=None):
        return [ref[p, g, r0:r1, lo * WIDE : hi * WIDE] for p in range(2)]

    def flags(g, s, delta):
        a = g * GROUP + s
        places = [
            (t, t + GROUP * delta - s + REACH)
            for t in range(GROUP)
            if 0 <= t + GROUP * delta - s + REACH < SPAN
        ]
        row = lax.rem(first + a + total, total)
        return flag_row(pat, row, places)

    def masked(g, delta, value):
        return jnp.concatenate(
            [value[s * BS : (s + 1) * BS] * flags(g, s, delta) for s in range(GROUP)], axis=0
        )

    def emit_square(g, delta, value):
        tile[...] = value
        for s in range(GROUP):
            part = tile[pl.ds(pl.multiple_of(s * BS + own_at, HALF), HALF), :]
            for t in range(GROUP):
                k = t + GROUP * delta - s + REACH
                if 0 <= k < SPAN:
                    square[g * GROUP + s, k] = part[:, t * BS : (t + 1) * BS]

    def emit_sign(g, delta, value):
        for s in range(GROUP):
            part = value[s * HALF : (s + 1) * HALF] * (flags(g, s, delta) * 0.5)
            for t in range(GROUP):
                k = t + GROUP * delta - s + REACH
                if 0 <= k < SPAN:
                    a = g * GROUP + s
                    k0, k1 = span_of(a, count, False)
                    value_k = 1.5 * own[a, k] - part[:, t * BS : (t + 1) * BS]
                    if k0 <= k < k1:
                        sign[a, k] = value_k
                    else:
                        side = 0 if a < REACH else 1
                        seed[side, a - side * (count - REACH), k] = value_k

    stores = []

    def send_rows(g, i, source, target):
        for a in range(g * GROUP, (g + 1) * GROUP):
            k0, k1 = span_of(a, count, i == 0)
            store = pltpu.make_async_copy(
                source.at[a, pl.ds(k0, k1 - k0)], target.at[a, pl.ds(k0, k1 - k0)], sems.at[i, a]
            )
            store.start()
            stores.append(store)

    for g in range(groups):
        r = panel(full, g, 0, 3)
        value = masked(g, 0, dot3(r, r, True))
        emit_square(g, 0, value)
        for p, part in enumerate(split(value)):
            keep[p, 2 * g] = part
        if g + 1 < groups:
            value = masked(g, 1, dot3(panel(full, g, 1, 3), panel(full, g + 1, 0, 2), True))
            emit_square(g, 1, value)
            emit_square(g + 1, -1, value.T)
            for p, part in enumerate(split(value)):
                keep[p, 2 * g + 1] = part
        send_rows(g, 0, square, square_out)

    def kept(i):
        return [keep[p, i] for p in range(2)]

    for g in range(groups):
        low = panel(mine, g, 0, 1)
        mid = panel(mine, g, 1, 2)
        high = panel(mine, g, 2, 3)
        centre = dot3(mid, kept(2 * g), True)
        if g > 0:
            centre = centre + dot3(low, kept(2 * g - 1), False)
            emit_sign(g, -1, dot3(low, kept(2 * g - 2), True) + dot3(mid, kept(2 * g - 1), True))
        if g + 1 < groups:
            centre = centre + dot3(high, kept(2 * g + 1), True)
            emit_sign(g, 1, dot3(mid, kept(2 * g + 1), False) + dot3(high, kept(2 * g + 2), True))
        emit_sign(g, 0, centre)
        send_rows(g, 1, sign, sign_out)
    for s in range(REACH):
        for t in range(REACH - s):
            seed[0, s, t] = 1.5 * own[s, t]
            k = SPAN - 1 - t
            seed[1, REACH - 1 - s, k] = 1.5 * own[count - 1 - s, k]

    last = groups - 1
    for a_ref, b_ref, m_ref, p_ref, g, part, r0 in (
        (low_a, low_b, low_m, low_p, 0, 0, 0),
        (high_a, high_b, high_m, high_p, last, 2, BS),
    ):
        rows = slice(r0, r0 + REACH * BS)
        out = panel(full, g, part, part + 1)
        turned = [x.astype(F32).T.astype(BF) for x in out]
        a_ref[...] = dot3(turned, turned, True)
        b_ref[...] = dot3(panel(full, g, 1, 2, r0, r0 + REACH * BS), turned, True)
        for p in range(2):
            m_ref[p] = out[p][rows]
            p_ref[p, 0] = mine[p, g, r0 // 2 : r0 // 2 + REACH * HALF, part * WIDE : (part + 1) * WIDE]
            p_ref[p, 1] = mine[p, g, r0 // 2 : r0 // 2 + REACH * HALF, WIDE : 2 * WIDE]
    for store in stores:
        store.wait()


def border_kernel(
    low_own, low_other, high_own, high_other, pat, seed, low_a, low_b, low_m, low_p, high_a, high_b,
    high_m, high_p, square_in, sign_in, square_out, sign_out, near, halo, tile, blocks, sems,
    *, axes, half_axis
):
    count = square_in.shape[0]
    total = pat.shape[1]
    first = lax.axis_index(axes) * count
    own_at = lax.axis_index(half_axis) * HALF
    other_at = HALF - own_at
    ends = (0, count - REACH)
    def sides(side):
        return (
            (low_own, low_other, low_a, low_b, low_m, low_p)
            if side == 0
            else (high_own, high_other, high_a, high_b, high_m, high_p)
        )

    for side in range(2):
        mine, theirs, a_ref, b_ref, m_ref, p_ref = sides(side)
        for p in range(REACH):
            for src, at in ((mine, own_at), (theirs, other_at)):
                near[side, pl.ds(pl.multiple_of(p * BS + at, HALF), HALF), :] = src[
                    p * HALF : (p + 1) * HALF, :
                ]
        def block(p, c):
            k = c - p + (REACH if side == 0 else 0)
            if 0 <= k <= REACH:
                return near[side, p * BS : (p + 1) * BS, k * BS : (k + 1) * BS]
            k = p - c + (REACH if side == 0 else 0)
            if 0 <= c < REACH and 0 <= k <= REACH:
                return near[side, c * BS : (c + 1) * BS, k * BS : (k + 1) * BS].T
            return jnp.zeros((BS, BS), F32)

        base = -5 if side == 0 else 0
        for p in range(REACH):
            for t in range(4):
                cs = [base + 2 * t, base + 2 * t + 1]
                value = jnp.concatenate([block(p, c) for c in cs], axis=1)
                for q, part in enumerate(split(value)):
                    halo[side, q, p * BS : (p + 1) * BS, t * 2 * BS : (t + 1) * 2 * BS] = part
    stores = []
    for side in range(2):
        mine, theirs, a_ref, b_ref, m_ref, p_ref = sides(side)
        shift = 1 if side == 0 else 0
        row0 = shift * BS
        whole = [halo[side, q] for q in range(2)]
        inner = [halo[side, q, :, (WIDE if side == 0 else 0) : (2 * WIDE if side == 0 else WIDE)] for q in range(2)]
        outer_first = first - REACH if side == 0 else first + count
        edge_first = first + ends[side]

        rows = []
        value = dot3(whole, whole, True) + a_ref[row0 : row0 + REACH * BS, row0 : row0 + REACH * BS]
        lane3 = lax.broadcasted_iota(jnp.int32, (1, REACH * BS), 1)
        for p in range(REACH):
            row = lax.rem(outer_first + p + total, total)
            line = jnp.zeros((1, REACH * BS), F32)
            for t in range(REACH):
                f = pat[t - p + REACH, row].astype(F32)
                line = jnp.where((lane3 >= t * BS) & (lane3 < (t + 1) * BS), f, line)
            rows.append(value[p * BS : (p + 1) * BS] * line)
        corner = split(jnp.concatenate(rows, axis=0))

        m = [m_ref[q] for q in range(2)]
        m3 = [x[:, row0 : row0 + REACH * BS] for x in m]
        inner3 = [x[:, row0 : row0 + REACH * BS] for x in inner]
        value = dot3(m3, inner3, True) + b_ref[:, row0 : row0 + REACH * BS]
        rows = []
        lines = []
        for s in range(REACH):
            row = lax.rem(edge_first + s, total)
            line = jnp.zeros((1, REACH * BS), F32)
            for t in range(REACH):
                k = t - s + (0 if side == 0 else 2 * REACH)
                if 0 <= k < SPAN:
                    f = pat[k, row].astype(F32)
                    line = jnp.where((lane3 >= t * BS) & (lane3 < (t + 1) * BS), f, line)
            lines.append(line)
            rows.append(value[s * BS : (s + 1) * BS] * line)
        value = jnp.concatenate(rows, axis=0)
        tile[side] = value
        across = split(value)

        reach_out = [p_ref[q, 0][:, row0 : row0 + REACH * BS] for q in range(2)]
        col0 = 0 if side == 0 else BS
        inside = [p_ref[q, 1][:, col0 : col0 + REACH * BS] for q in range(2)]
        out = dot3(reach_out, corner, True) + dot3(inside, across, False)
        back = dot3(reach_out, across, True)
        for s in range(REACH):
            row = lax.rem(edge_first + s, total)
            part = tile[side, pl.ds(pl.multiple_of(s * BS + own_at, HALF), HALF), :]
            far = out[s * HALF : (s + 1) * HALF] * (lines[s] * 0.5)
            near_line = jnp.zeros((1, REACH * BS), F32)
            for t in range(REACH):
                f = pat[t - s + REACH, row].astype(F32)
                near_line = jnp.where((lane3 >= t * BS) & (lane3 < (t + 1) * BS), f, near_line)
            close = back[s * HALF : (s + 1) * HALF] * (near_line * 0.5)
            for t in range(REACH):
                k = t - s + (0 if side == 0 else 2 * REACH)
                lanes = slice(t * BS, (t + 1) * BS)
                if 0 <= k < SPAN:
                    blocks[0, side, s, k] = part[:, lanes]
                    blocks[1, side, s, k] = seed[side, s, k] - far[:, lanes]
                k = t - s + REACH
                blocks[1, side, s, k] = seed[side, s, k] - close[:, lanes]
            a = ends[side] + s
            for i, ref in enumerate((square_out, sign_out)):
                k0, k1 = span_of(a, count, i == 0)
                k0, k1 = (0, k0) if side == 0 else (k1, SPAN)
                store = pltpu.make_async_copy(
                    blocks.at[i, side, s, pl.ds(k0, k1 - k0)],
                    ref.at[a, pl.ds(k0, k1 - k0)],
                    sems.at[i, side, s],
                )
                store.start()
                stores.append(store)
    for store in stores:
        store.wait()


def shards(matrix, pattern, *, axes, half_axis):
    count = matrix.shape[0]
    groups = count // GROUP
    flags = pattern.T
    vmem = pl.BlockSpec(memory_space=pltpu.VMEM)
    smem = pl.BlockSpec(memory_space=pltpu.SMEM)
    hbm = pl.BlockSpec(memory_space=pltpu.HBM)
    params = pltpu.CompilerParams(vmem_limit_bytes=LIMIT)

    edge = jax.ShapeDtypeStruct((REACH * HALF, (REACH + 1) * BS), F32)
    to_left, to_right = pl.pallas_call(
        edge_kernel,
        out_shape=(edge, edge),
        in_specs=[hbm],
        out_specs=[vmem] * 2,
        scratch_shapes=[
            pltpu.VMEM((2, REACH, REACH + 1, HALF, BS), F32),
            pltpu.SemaphoreType.DMA((2,)),
        ],
        compiler_params=params,
    )(matrix)

    size = 1
    for axis in axes:
        size *= lax.axis_size(axis)
    swap = [(0, 1), (1, 0)]
    other = lax.ppermute(matrix, half_axis, swap)
    forward = [(i, (i + 1) % size) for i in range(size)]
    backward = [(target, source) for source, target in forward]
    low_own = lax.ppermute(to_right, axes, forward)
    high_own = lax.ppermute(to_left, axes, backward)
    low_other = lax.ppermute(low_own, half_axis, swap)
    high_other = lax.ppermute(high_own, half_axis, swap)

    names = dict(axes=axes, half_axis=half_axis)
    ends_out = [
        jax.ShapeDtypeStruct((WIDE, WIDE), F32),
        jax.ShapeDtypeStruct((REACH * BS, WIDE), F32),
        jax.ShapeDtypeStruct((2, REACH * BS, WIDE), BF),
        jax.ShapeDtypeStruct((2, 2, REACH * HALF, WIDE), BF),
    ] * 2
    band = jax.ShapeDtypeStruct(matrix.shape, F32)
    seed = jax.ShapeDtypeStruct((2, REACH, SPAN, HALF, BS), F32)
    square, sign, *inside = pl.pallas_call(
        functools.partial(interior_kernel, **names),
        out_shape=[band, band, seed] + ends_out,
        in_specs=[vmem, vmem, smem],
        out_specs=[hbm] * 2 + [vmem] * 9,
        scratch_shapes=[
            pltpu.VMEM(matrix.shape, F32),
            pltpu.VMEM(matrix.shape, F32),
            pltpu.VMEM((2, groups, WIDE, 3 * WIDE), BF),
            pltpu.VMEM((2, groups, GROUP * HALF, 3 * WIDE), BF),
            pltpu.VMEM((WIDE, WIDE), F32),
            pltpu.VMEM((2, 2 * groups - 1, WIDE, WIDE), BF),
            pltpu.SemaphoreType.DMA((2, count)),
        ],
        compiler_params=params,
        cost_estimate=pl.CostEstimate(
            flops=3 * 2 * 16 * WIDE**3, bytes_accessed=6 * 2**20, transcendentals=0
        ),
    )(matrix, other, flags)

    return tuple(
        pl.pallas_call(
            functools.partial(border_kernel, **names),
            out_shape=(band, band),
            in_specs=[vmem] * 4 + [smem] + [vmem] * 9 + [hbm] * 2,
            out_specs=[hbm] * 2,
            scratch_shapes=[
                pltpu.VMEM((2, REACH * BS, WIDE), F32),
                pltpu.VMEM((2, 2, REACH * BS, 2 * WIDE), BF),
                pltpu.VMEM((2, REACH * BS, REACH * BS), F32),
                pltpu.VMEM((2, 2, REACH, SPAN, HALF, BS), F32),
                pltpu.SemaphoreType.DMA((2, 2, REACH)),
            ],
            input_output_aliases={14: 0, 15: 1},
            compiler_params=params,
            cost_estimate=pl.CostEstimate(
                flops=3 * 2 * 4 * WIDE**3, bytes_accessed=2 * 2**20, transcendentals=0
            ),
        )(low_own, low_other, high_own, high_other, flags, *inside, square, sign)
    )


def solution(mesh):
    band = P(("group", "row", "col"), None, "rep", None)
    return jax.shard_map(
        functools.partial(shards, axes=("row", "col"), half_axis="rep"),
        mesh=mesh,
        in_specs=(band, P("group", None)),
        out_specs=(band, band),
        check_vma=False,
    )
```

```python
import functools

import jax
import jax.numpy as jnp
from jax import lax
from jax.experimental import pallas as pl
from jax.experimental.pallas import tpu as pltpu
from jax.sharding import PartitionSpec as P

REACH = 3
SPAN = 7
BS = 64
HALF = 32
GROUP = 4
WIDE = GROUP * BS
BF = jnp.bfloat16
F32 = jnp.float32
LIMIT = 32 * 1024 * 1024
EDGE_LIMIT = 58 * 1024 * 1024


def split(x):
    hi = x.astype(BF)
    return hi, (x - hi.astype(F32)).astype(BF)


def product(pairs, transposed=False):
    side = 1 if transposed else 0
    left = [x for a, _ in pairs for x in (a[0], a[0], a[1])]
    right = [x for _, b in pairs for x in (b[0], b[1], b[0])]
    return lax.dot_general(
        jnp.concatenate(left, axis=1),
        jnp.concatenate(right, axis=side),
        (((1,), (side,)), ((), ())),
        preferred_element_type=F32,
    )


def turn(x):
    return split((x[0].astype(F32) + x[1].astype(F32)).T)


def flag_line(pat, row, places):
    lane = lax.broadcasted_iota(jnp.int32, (1, WIDE), 1)
    line = jnp.zeros((1, WIDE), F32)
    for place, k in places:
        if 0 <= k < SPAN:
            value = pat[k, row].astype(F32)
            line = jnp.where((lane >= place * BS) & (lane < (place + 1) * BS), value, line)
    return line


def span_of(a, count, is_square):
    if a < REACH:
        return (REACH - a if is_square else 2 * REACH - a), SPAN
    s = a - (count - REACH)
    if s >= 0:
        return 0, (2 * REACH - s if is_square else REACH - s)
    return 0, SPAN


def edge_kernel(matrix, to_left, to_right, blocks, sems):
    count = matrix.shape[0]
    loads = [
        pltpu.make_async_copy(source, blocks.at[i], sems.at[i])
        for i, source in enumerate(
            (
                matrix.at[pl.ds(0, REACH), pl.ds(REACH, REACH + 1)],
                matrix.at[pl.ds(count - REACH, REACH), pl.ds(0, REACH + 1)],
            )
        )
    ]
    for load in loads:
        load.start()
    for i, target in enumerate((to_left, to_right)):
        loads[i].wait()
        for s in range(REACH):
            for t in range(2):
                target[s * HALF : (s + 1) * HALF, t * 2 * BS : (t + 1) * 2 * BS] = jnp.concatenate(
                    [blocks[i, s, 2 * t], blocks[i, s, 2 * t + 1]], axis=1
                )


class Interior:
    def __init__(self, own, pat, full, mine, keep, axes):
        self.own = own
        self.pat = pat
        self.full = full
        self.mine = mine
        self.keep = keep
        self.count = own.shape[0]
        self.groups = self.count // GROUP
        self.first = lax.axis_index(axes) * self.count
        self.lines = {}
        self.stores = []

    def flags(self, g, s, delta):
        if (g, s, delta) not in self.lines:
            row = lax.rem(self.first + g * GROUP + s, self.pat.shape[1])
            places = [(t, t + GROUP * delta - s + REACH) for t in range(GROUP)]
            self.lines[g, s, delta] = flag_line(self.pat, row, places)
        return self.lines[g, s, delta]

    def part(self, g, h, rows=slice(None)):
        at = (h - g + 1) * WIDE
        return [self.full[p, g, rows, at : at + WIDE] for p in range(2)]

    def my_part(self, g, h):
        at = (h - g + 1) * WIDE
        return [self.mine[p, g, :, at : at + WIDE] for p in range(2)]

    def tile(self, g, h):
        return 3 * g + h - g + 1

    def kept(self, g, h):
        return [self.keep[p, self.tile(g, h)] for p in range(2)]

    def second(self, g, sign, seed):
        near = [e for e in (g - 1, g, g + 1) if 0 <= e < self.groups]
        for h in near:
            value = product([(self.my_part(g, e), self.kept(e, h)) for e in near if abs(e - h) <= 1])
            for s in range(GROUP):
                a = g * GROUP + s
                k0, k1 = span_of(a, self.count, False)
                part = value[s * HALF : (s + 1) * HALF] * (self.flags(g, s, h - g) * 0.5)
                for t in range(GROUP):
                    k = t + GROUP * (h - g) - s + REACH
                    if 0 <= k < SPAN:
                        block = 1.5 * self.own[a, k] - part[:, t * BS : (t + 1) * BS]
                        if k0 <= k < k1:
                            sign[a - sign_first(sign, self.count, g), k] = block
                        else:
                            seed[a if a < REACH else a - (self.count - REACH), k] = block

    def far_seed(self, g, seed):
        for s in range(REACH):
            a = s if g == 0 else self.count - REACH + s
            for k in range(0, REACH - s) if g == 0 else range(2 * REACH - s, SPAN):
                seed[s, k] = 1.5 * self.own[a, k]

    def send(self, g, i, source, target, sems):
        for a in range(g * GROUP, (g + 1) * GROUP):
            k0, k1 = span_of(a, self.count, i == 0)
            store = pltpu.make_async_copy(
                source.at[a - sign_first(source, self.count, g), pl.ds(k0, k1 - k0)],
                target.at[a, pl.ds(k0, k1 - k0)],
                sems.at[i, a],
            )
            store.start()
            self.stores.append(store)

    def finish(self):
        for store in self.stores:
            store.wait()


def sign_first(ref, count, g):
    return 0 if ref.shape[0] == count else g * GROUP


def first_kernel(
    own, other, pat, square_out, sign_out, seed, full, mine, keep, square, sign, sems, *, axes,
    half_axis
):
    it = Interior(own, pat, full, mine, keep, axes)
    groups = it.groups
    upper_half = lax.axis_index(half_axis) == 1

    def build(g):
        for s in range(GROUP):
            a = g * GROUP + s
            for t in range(3 * GROUP // 2):
                ks = [2 * t + e - s - 1 for e in range(2)]
                lanes = slice(t * 2 * BS, (t + 1) * 2 * BS)
                rows = slice(s * BS, (s + 1) * BS)
                mine_rows = slice(s * HALF, (s + 1) * HALF)
                if all(k < 0 or k >= SPAN for k in ks):
                    for p in range(2):
                        full[p, g, rows, lanes] = jnp.zeros((BS, 2 * BS), BF)
                        mine[p, g, mine_rows, lanes] = jnp.zeros((HALF, 2 * BS), BF)
                    continue
                two = [
                    jnp.concatenate(
                        [src[a, k] if 0 <= k < SPAN else jnp.zeros((HALF, BS), F32) for k in ks],
                        axis=1,
                    )
                    for src in (own, other)
                ]
                parts = [split(x) for x in two]
                for p in range(2):
                    mine[p, g, mine_rows, lanes] = parts[0][p]
                whole = jnp.concatenate(
                    [
                        jnp.where(upper_half, two[1], two[0]),
                        jnp.where(upper_half, two[0], two[1]),
                    ],
                    axis=0,
                )
                for p, x in enumerate(split(whole)):
                    full[p, g, rows, lanes] = x

    def emit(g, h, value):
        for s in range(GROUP):
            rows = value[s * BS : (s + 1) * BS]
            part = jnp.where(upper_half, rows[HALF:], rows[:HALF])
            for t in range(GROUP):
                k = t + GROUP * (h - g) - s + REACH
                if 0 <= k < SPAN:
                    square[g * GROUP + s, k] = part[:, t * BS : (t + 1) * BS]
        for p, x in enumerate(split(value)):
            keep[p, it.tile(g, h)] = x

    def squares(g, h):
        pairs = []
        for e in (g - 1, g, g + 1):
            if abs(e - h) <= 1:
                inside = 0 <= e < groups
                pairs.append((it.part(g, e), it.part(e, h) if inside else turn(it.part(h, e))))
        value = product(pairs)
        value = jnp.concatenate(
            [value[s * BS : (s + 1) * BS] * it.flags(g, s, h - g) for s in range(GROUP)], axis=0
        )
        emit(g, h, value)
        if h > g:
            emit(h, g, value.T)

    build(0)
    for g in range(groups):
        if g + 1 < groups:
            build(g + 1)
        squares(g, g)
        if g + 1 < groups:
            squares(g, g + 1)
        it.send(g, 0, square, square_out, sems)
        if g > 0:
            it.second(g - 1, sign, seed)
            it.send(g - 1, 1, sign, sign_out, sems)
    it.far_seed(0, seed)
    it.finish()


def last_kernel(
    own, pat, full, mine, keep, sign_in, sign_out, seed, low_a, low_b, low_m, low_p, high_a,
    high_b, high_m, high_p, sign, sems, *, axes
):
    it = Interior(own, pat, full, mine, keep, axes)
    last = it.groups - 1
    it.second(last, sign, seed)
    it.send(last, 1, sign, sign_out, sems)
    it.far_seed(last, seed)
    for a_ref, b_ref, m_ref, p_ref, g, e, r0 in (
        (low_a, low_b, low_m, low_p, 0, -1, 0),
        (high_a, high_b, high_m, high_p, last, last + 1, BS),
    ):
        rows = slice(r0, r0 + REACH * BS)
        mine_rows = slice(r0 // 2, r0 // 2 + REACH * HALF)
        out = it.part(g, e)
        turned = turn(out)
        outer = slice(BS - r0, BS - r0 + REACH * BS)
        a_ref[...] = product([([x[outer] for x in turned], out)])
        b_ref[...] = product([(it.part(g, g, rows), out)])
        for p in range(2):
            m_ref[p] = out[p][rows]
            p_ref[p, 0] = it.my_part(g, e)[p][mine_rows]
            p_ref[p, 1] = it.my_part(g, g)[p][mine_rows]
    it.finish()


def border_kernel(
    low_own, low_other, high_own, high_other, pat, low_seed, low_a, low_b, low_m, low_p, high_seed,
    high_a, high_b, high_m, high_p, square_in, sign_in, square_out, sign_out, halo, blocks, sems,
    *, axes, half_axis
):
    count = square_in.shape[0]
    total = pat.shape[1]
    first = lax.axis_index(axes) * count
    upper_half = lax.axis_index(half_axis) == 1
    ends = (0, count - REACH)
    given = (
        (low_own, low_other, low_seed, low_a, low_b, low_m, low_p),
        (high_own, high_other, high_seed, high_a, high_b, high_m, high_p),
    )
    shift = (1, 0)
    zero = jnp.zeros((BS, WIDE), F32)

    for side in range(2):
        mine, theirs = given[side][:2]
        below = REACH if side == 0 else 0
        lines = []
        for p in range(REACH):
            rows = slice(p * HALF, (p + 1) * HALF)
            lines.append(
                jnp.concatenate(
                    [
                        jnp.where(upper_half, theirs[rows, :], mine[rows, :]),
                        jnp.where(upper_half, mine[rows, :], theirs[rows, :]),
                    ],
                    axis=0,
                )
            )

        def block(p, c):
            k = c - p + below
            if 0 <= k <= REACH:
                return lines[p][:, k * BS : (k + 1) * BS]
            k = p - c + below
            if 0 <= c < REACH and 0 <= k <= REACH:
                return lines[c][:, k * BS : (k + 1) * BS].T
            return jnp.zeros((BS, BS), F32)

        base = -5 if side == 0 else 0
        for p in range(REACH):
            rows = slice((p + shift[side]) * BS, (p + shift[side] + 1) * BS)
            for t in range(4):
                value = jnp.concatenate([block(p, base + 2 * t), block(p, base + 2 * t + 1)], axis=1)
                for q, x in enumerate(split(value)):
                    halo[side, q, rows, t * 2 * BS : (t + 1) * 2 * BS] = x
        rows = slice(0, BS) if side == 0 else slice(REACH * BS, WIDE)
        for q in range(2):
            halo[side, q, rows, :] = jnp.zeros((BS, 2 * WIDE), BF)

    corners = []
    across = []
    far_lines = []
    for side in range(2):
        _, _, _, a_ref, b_ref, m_ref, _ = given[side]
        at = shift[side]
        whole = [halo[side, q] for q in range(2)]
        outer_rows = slice(at * BS, (at + REACH) * BS)
        inner = slice(WIDE, 2 * WIDE) if side == 0 else slice(0, WIDE)
        outer_first = first - REACH if side == 0 else first + count
        edge_first = first + ends[side]

        value = product([([x[outer_rows] for x in whole], whole)], True) + a_ref[...]
        rows = []
        for p in range(REACH):
            row = lax.rem(outer_first + p + total, total)
            line = flag_line(pat, row, [(t + at, t - p + REACH) for t in range(REACH)])
            rows.append(value[p * BS : (p + 1) * BS] * line)
        rows = [zero] + rows if side == 0 else rows + [zero]
        corners.append(split(jnp.concatenate(rows, axis=0)))

        value = product([([m_ref[q] for q in range(2)], [x[:, inner] for x in whole])], True)
        value = value + b_ref[...]
        rows = []
        lines = []
        for s in range(REACH):
            row = lax.rem(edge_first + s, total)
            offset = 0 if side == 0 else 2 * REACH
            line = flag_line(pat, row, [(t + at, t - s + offset) for t in range(REACH)])
            lines.append(line)
            rows.append(value[s * BS : (s + 1) * BS] * line)
            part = jnp.where(upper_half, rows[s][HALF:], rows[s][:HALF])
            for t in range(REACH):
                k = t - s + offset
                if 0 <= k < SPAN:
                    blocks[0, side, s, k] = part[:, (t + at) * BS : (t + at + 1) * BS]
        far_lines.append(lines)
        rows = rows + [zero] if side == 0 else [zero] + rows
        across.append(split(jnp.concatenate(rows, axis=0)))

    stores = []
    for side in range(2):
        seed, p_ref = given[side][2], given[side][6]
        at = shift[side]
        reach_out = [p_ref[q, 0] for q in range(2)]
        inside = [p_ref[q, 1] for q in range(2)]
        out = product([(reach_out, corners[side]), (inside, across[side])])
        back = product([(reach_out, across[side])], True)
        offset = 0 if side == 0 else 2 * REACH
        for s in range(REACH):
            a = ends[side] + s
            row = lax.rem(first + a, total)
            line = flag_line(pat, row, [(t + 1 - at, t - s + REACH) for t in range(REACH)])
            far = out[s * HALF : (s + 1) * HALF] * (far_lines[side][s] * 0.5)
            close = back[s * HALF : (s + 1) * HALF] * (line * 0.5)
            for t in range(REACH):
                k = t - s + offset
                if 0 <= k < SPAN:
                    lanes = slice((t + at) * BS, (t + at + 1) * BS)
                    blocks[1, side, s, k] = seed[s, k] - far[:, lanes]
                k = t - s + REACH
                lanes = slice((t + 1 - at) * BS, (t + 2 - at) * BS)
                blocks[1, side, s, k] = seed[s, k] - close[:, lanes]
            for i, ref in enumerate((square_out, sign_out)):
                k0, k1 = span_of(a, count, i == 0)
                k0, k1 = (0, k0) if side == 0 else (k1, SPAN)
                store = pltpu.make_async_copy(
                    blocks.at[i, side, s, pl.ds(k0, k1 - k0)],
                    ref.at[a, pl.ds(k0, k1 - k0)],
                    sems.at[i, side, s],
                )
                store.start()
                stores.append(store)
    for store in stores:
        store.wait()


def shards(matrix, pattern, *, axes, half_axis):
    count = matrix.shape[0]
    groups = count // GROUP
    flags = pattern.T
    vmem = pl.BlockSpec(memory_space=pltpu.VMEM)
    smem = pl.BlockSpec(memory_space=pltpu.SMEM)
    hbm = pl.BlockSpec(memory_space=pl.ANY)
    params = pltpu.CompilerParams(vmem_limit_bytes=LIMIT)

    edge = jax.ShapeDtypeStruct((REACH * HALF, (REACH + 1) * BS), F32)
    to_left, to_right = pl.pallas_call(
        edge_kernel,
        out_shape=(edge, edge),
        in_specs=[hbm],
        out_specs=[vmem] * 2,
        scratch_shapes=[
            pltpu.VMEM((2, REACH, REACH + 1, HALF, BS), F32),
            pltpu.SemaphoreType.DMA((2,)),
        ],
        compiler_params=pltpu.CompilerParams(vmem_limit_bytes=EDGE_LIMIT),
    )(matrix)

    size = 1
    for axis in axes:
        size *= lax.axis_size(axis)
    swap = [(0, 1), (1, 0)]
    other = lax.ppermute(matrix, half_axis, swap)
    forward = [(i, (i + 1) % size) for i in range(size)]
    backward = [(target, source) for source, target in forward]
    low_own = lax.ppermute(to_right, axes, forward)
    high_own = lax.ppermute(to_left, axes, backward)

    band = jax.ShapeDtypeStruct(matrix.shape, F32)
    seed = jax.ShapeDtypeStruct((REACH, SPAN, HALF, BS), F32)
    full = jax.ShapeDtypeStruct((2, groups, WIDE, 3 * WIDE), BF)
    mine = jax.ShapeDtypeStruct((2, groups, GROUP * HALF, 3 * WIDE), BF)
    keep = jax.ShapeDtypeStruct((2, 3 * groups, WIDE, WIDE), BF)
    square, sign, low_seed, full, mine, keep = pl.pallas_call(
        functools.partial(first_kernel, axes=axes, half_axis=half_axis),
        out_shape=[band, band, seed, full, mine, keep],
        in_specs=[vmem, vmem, smem],
        out_specs=[hbm] * 2 + [vmem] * 4,
        scratch_shapes=[
            pltpu.VMEM(matrix.shape, F32),
            pltpu.VMEM(matrix.shape, F32),
            pltpu.SemaphoreType.DMA((2, count)),
        ],
        compiler_params=params,
        cost_estimate=pl.CostEstimate(
            flops=3 * 2 * 16 * WIDE**3, bytes_accessed=16 * 2**20, transcendentals=0
        ),
    )(matrix, other, flags)

    low_own, high_own, low_seed = lax.optimization_barrier((low_own, high_own, low_seed))
    low_other = lax.ppermute(low_own, half_axis, swap)
    high_other = lax.ppermute(high_own, half_axis, swap)

    ends_out = [
        jax.ShapeDtypeStruct((REACH * BS, WIDE), F32),
        jax.ShapeDtypeStruct((REACH * BS, WIDE), F32),
        jax.ShapeDtypeStruct((2, REACH * BS, WIDE), BF),
        jax.ShapeDtypeStruct((2, 2, REACH * HALF, WIDE), BF),
    ]
    sign, high_seed, *ends = pl.pallas_call(
        functools.partial(last_kernel, axes=axes),
        out_shape=[band, seed] + ends_out * 2,
        in_specs=[vmem, smem] + [vmem] * 3 + [hbm],
        out_specs=[hbm] + [vmem] * 9,
        scratch_shapes=[
            pltpu.VMEM((GROUP, SPAN, HALF, BS), F32),
            pltpu.SemaphoreType.DMA((2, count)),
        ],
        input_output_aliases={5: 0},
        compiler_params=params,
        cost_estimate=pl.CostEstimate(
            flops=3 * 2 * 4 * WIDE**3, bytes_accessed=4 * 2**20, transcendentals=0
        ),
    )(matrix, flags, full, mine, keep, sign)

    return tuple(
        pl.pallas_call(
            functools.partial(border_kernel, axes=axes, half_axis=half_axis),
            out_shape=(band, band),
            in_specs=[vmem] * 4 + [smem] + [vmem] * 10 + [hbm] * 2,
            out_specs=[hbm] * 2,
            scratch_shapes=[
                pltpu.VMEM((2, 2, WIDE, 2 * WIDE), BF),
                pltpu.VMEM((2, 2, REACH, SPAN, HALF, BS), F32),
                pltpu.SemaphoreType.DMA((2, 2, REACH)),
            ],
            input_output_aliases={15: 0, 16: 1},
            compiler_params=params,
            cost_estimate=pl.CostEstimate(
                flops=3 * 2 * 4 * WIDE**3, bytes_accessed=2 * 2**20, transcendentals=0
            ),
        )(
            low_own, low_other, high_own, high_other, flags, low_seed, *ends[:4], high_seed,
            *ends[4:], square, sign,
        )
    )


def solution(mesh):
    band = P(("group", "row", "col"), None, "rep", None)
    return jax.shard_map(
        functools.partial(shards, axes=("row", "col"), half_axis="rep"),
        mesh=mesh,
        in_specs=(band, P("group", None)),
        out_specs=(band, band),
        check_vma=False,
    )
```

```python
import functools

import jax
import jax.numpy as jnp
from jax import lax
from jax.experimental import pallas as pl
from jax.experimental.pallas import tpu as pltpu
from jax.sharding import PartitionSpec as P

REACH = 3
SPAN = 7
BS = 64
HALF = 32
GROUP = 4
WIDE = GROUP * BS
BF = jnp.bfloat16
F32 = jnp.float32
LIMIT = 32 * 1024 * 1024


def split(x):
    hi = x.astype(BF)
    return hi, (x - hi.astype(F32)).astype(BF)


def product(pairs, transposed=False):
    side = 1 if transposed else 0
    left = [x for a, _ in pairs for x in (a[0], a[0], a[1])]
    right = [x for _, b in pairs for x in (b[0], b[1], b[0])]
    return lax.dot_general(
        jnp.concatenate(left, axis=1),
        jnp.concatenate(right, axis=side),
        (((1,), (side,)), ((), ())),
        preferred_element_type=F32,
    )


def turn(x):
    return split((x[0].astype(F32) + x[1].astype(F32)).T)


def write_lines(pat, lines, first, groups):
    total = pat.shape[1]
    lane = lax.broadcasted_iota(jnp.int32, (1, 2 * BS), 1)
    for g in range(-1, groups + 1):
        for s in range(GROUP):
            row = lax.rem(first + g * GROUP + s + total, total)
            for t in range(3 * GROUP // 2):
                ks = [2 * t + e - s - 1 for e in range(2)]
                f = [pat[k, row].astype(F32) if 0 <= k < SPAN else F32(0) for k in ks]
                at = (g + 1) * GROUP + s
                lines[at : at + 1, t * 2 * BS : (t + 1) * 2 * BS] = jnp.where(lane < BS, f[0], f[1])


def line_of(lines, g, s, h):
    at = (g + 1) * GROUP + s
    lo = (h - g + 1) * WIDE
    return lines[at : at + 1, lo : lo + WIDE]


def span_of(a, count, is_square):
    if a < REACH:
        return (REACH - a if is_square else 2 * REACH - a), SPAN
    s = a - (count - REACH)
    if s >= 0:
        return 0, (2 * REACH - s if is_square else REACH - s)
    return 0, SPAN


def edge_kernel(top, bottom, to_left, to_right):
    for source, target in ((top, to_left), (bottom, to_right)):
        for s in range(REACH):
            for t in range(2):
                target[s * HALF : (s + 1) * HALF, t * 2 * BS : (t + 1) * 2 * BS] = jnp.concatenate(
                    [source[s, 2 * t], source[s, 2 * t + 1]], axis=1
                )


class Interior:
    def __init__(self, own, lines, full, mine, keep):
        self.own = own
        self.lines = lines
        self.full = full
        self.mine = mine
        self.keep = keep
        self.count = own.shape[0]
        self.groups = self.count // GROUP
        self.stores = []

    def part(self, g, h, rows=slice(None)):
        at = (h - g + 1) * WIDE
        return [self.full[p, g, rows, at : at + WIDE] for p in range(2)]

    def my_part(self, g, h):
        at = (h - g + 1) * WIDE
        return [self.mine[p, g, :, at : at + WIDE] for p in range(2)]

    def tile(self, g, h):
        return 3 * g + h - g + 1

    def kept(self, g, h):
        return [self.keep[p, self.tile(g, h)] for p in range(2)]

    def second(self, g, sign, seed):
        near = [e for e in (g - 1, g, g + 1) if 0 <= e < self.groups]
        for h in near:
            value = product([(self.my_part(g, e), self.kept(e, h)) for e in near if abs(e - h) <= 1])
            for s in range(GROUP):
                a = g * GROUP + s
                k0, k1 = span_of(a, self.count, False)
                part = value[s * HALF : (s + 1) * HALF] * (line_of(self.lines, g, s, h) * 0.5)
                for t in range(GROUP):
                    k = t + GROUP * (h - g) - s + REACH
                    if 0 <= k < SPAN:
                        block = 1.5 * self.own[a, k] - part[:, t * BS : (t + 1) * BS]
                        if k0 <= k < k1:
                            sign[s, k] = block
                        else:
                            seed[a if a < REACH else a - (self.count - REACH), k] = block

    def far_seed(self, g, seed):
        for s in range(REACH):
            a = s if g == 0 else self.count - REACH + s
            for k in range(0, REACH - s) if g == 0 else range(2 * REACH - s, SPAN):
                seed[s, k] = 1.5 * self.own[a, k]

    def send(self, g, i, source, target, sems):
        for s in range(GROUP):
            a = g * GROUP + s
            k0, k1 = span_of(a, self.count, i == 0)
            store = pltpu.make_async_copy(
                source.at[s, pl.ds(k0, k1 - k0)], target.at[a, pl.ds(k0, k1 - k0)], sems.at[i, a]
            )
            store.start()
            self.stores.append(store)

    def finish(self):
        for store in self.stores:
            store.wait()


def first_kernel(
    own, other, pattern, square_out, sign_out, seed, full, mine, keep, lines, square_left, sign_left,
    pat, square, sign, sems, pat_sem, *, axes, half_axis
):
    load = pltpu.make_async_copy(pattern, pat, pat_sem)
    load.start()
    it = Interior(own, lines, full, mine, keep)
    groups = it.groups
    upper_half = lax.axis_index(half_axis) == 1

    def build(g):
        for s in range(GROUP):
            a = g * GROUP + s
            for t in range(3 * GROUP // 2):
                ks = [2 * t + e - s - 1 for e in range(2)]
                lanes = slice(t * 2 * BS, (t + 1) * 2 * BS)
                rows = slice(s * BS, (s + 1) * BS)
                mine_rows = slice(s * HALF, (s + 1) * HALF)
                if all(k < 0 or k >= SPAN for k in ks):
                    for p in range(2):
                        full[p, g, rows, lanes] = jnp.zeros((BS, 2 * BS), BF)
                        mine[p, g, mine_rows, lanes] = jnp.zeros((HALF, 2 * BS), BF)
                    continue
                two = [
                    jnp.concatenate(
                        [src[a, k] if 0 <= k < SPAN else jnp.zeros((HALF, BS), F32) for k in ks],
                        axis=1,
                    )
                    for src in (own, other)
                ]
                for p, (x, y) in enumerate(zip(*[split(x) for x in two])):
                    mine[p, g, mine_rows, lanes] = x
                    full[p, g, rows, lanes] = jnp.concatenate(
                        [jnp.where(upper_half, y, x), jnp.where(upper_half, x, y)], axis=0
                    )

    def emit(g, h, value):
        for s in range(GROUP):
            rows = value[s * BS : (s + 1) * BS]
            part = jnp.where(upper_half, rows[HALF:], rows[:HALF])
            for t in range(GROUP):
                k = t + GROUP * (h - g) - s + REACH
                if 0 <= k < SPAN:
                    staged[g][s, k] = part[:, t * BS : (t + 1) * BS]
        for p, x in enumerate(split(value)):
            keep[p, it.tile(g, h)] = x

    def squares(g, h):
        pairs = []
        for e in (g - 1, g, g + 1):
            if abs(e - h) <= 1:
                inside = 0 <= e < groups
                pairs.append((it.part(g, e), it.part(e, h) if inside else turn(it.part(h, e))))
        value = product(pairs)
        value = jnp.concatenate(
            [value[s * BS : (s + 1) * BS] * line_of(lines, g, s, h) for s in range(GROUP)], axis=0
        )
        emit(g, h, value)
        if h > g:
            emit(h, g, value.T)

    staged = [square.at[g] for g in range(groups - 1)] + [square_left]
    build(0)
    for g in range(groups):
        if g + 1 < groups:
            build(g + 1)
        if g == 0:
            load.wait()
            write_lines(pat, lines, lax.axis_index(axes) * it.count, groups)
        squares(g, g)
        if g + 1 < groups:
            squares(g, g + 1)
            it.send(g, 0, staged[g], square_out, sems)
        if 0 < g < groups - 1:
            it.second(g - 1, sign.at[g - 1], seed)
            it.send(g - 1, 1, sign.at[g - 1], sign_out, sems)
    it.far_seed(0, seed)
    it.second(groups - 2, sign_left, seed)
    it.finish()


def last_kernel(
    own, lines, full, mine, keep, square_left, sign_left, square_in, sign_in, square_out, sign_out,
    seed, low_a, low_b, low_m, low_p, high_a, high_b, high_m, high_p, sign, sems
):
    it = Interior(own, lines, full, mine, keep)
    last = it.groups - 1
    it.send(last, 0, square_left, square_out, sems)
    it.send(last - 1, 1, sign_left, sign_out, sems)
    it.second(last, sign, seed)
    it.send(last, 1, sign, sign_out, sems)
    it.far_seed(last, seed)
    for a_ref, b_ref, m_ref, p_ref, g, e, r0 in (
        (low_a, low_b, low_m, low_p, 0, -1, 0),
        (high_a, high_b, high_m, high_p, last, last + 1, BS),
    ):
        rows = slice(r0, r0 + REACH * BS)
        mine_rows = slice(r0 // 2, r0 // 2 + REACH * HALF)
        out = it.part(g, e)
        turned = turn(out)
        outer = slice(BS - r0, BS - r0 + REACH * BS)
        a_ref[...] = product([([x[outer] for x in turned], out)])
        b_ref[...] = product([(it.part(g, g, rows), out)])
        for p in range(2):
            m_ref[p] = out[p][rows]
            p_ref[p, 0] = it.my_part(g, e)[p][mine_rows]
            p_ref[p, 1] = it.my_part(g, g)[p][mine_rows]
    it.finish()


def border_kernel(
    low_own, low_other, high_own, high_other, lines, low_seed, low_a, low_b, low_m, low_p, high_seed,
    high_a, high_b, high_m, high_p, square_in, sign_in, square_out, sign_out, halo, blocks, sems,
    *, half_axis
):
    count = square_in.shape[0]
    groups = count // GROUP
    upper_half = lax.axis_index(half_axis) == 1
    ends = (0, count - REACH)
    given = (
        (low_own, low_other, low_seed, low_a, low_b, low_m, low_p),
        (high_own, high_other, high_seed, high_a, high_b, high_m, high_p),
    )
    shift = (1, 0)
    zero = jnp.zeros((BS, WIDE), F32)

    for side in range(2):
        mine, theirs = given[side][:2]
        below = REACH if side == 0 else 0
        whole_rows = []
        for p in range(REACH):
            rows = slice(p * HALF, (p + 1) * HALF)
            whole_rows.append(
                jnp.concatenate(
                    [
                        jnp.where(upper_half, theirs[rows, :], mine[rows, :]),
                        jnp.where(upper_half, mine[rows, :], theirs[rows, :]),
                    ],
                    axis=0,
                )
            )

        def block(p, c):
            k = c - p + below
            if 0 <= k <= REACH:
                return whole_rows[p][:, k * BS : (k + 1) * BS]
            k = p - c + below
            if 0 <= c < REACH and 0 <= k <= REACH:
                return whole_rows[c][:, k * BS : (k + 1) * BS].T
            return jnp.zeros((BS, BS), F32)

        base = -5 if side == 0 else 0
        for p in range(REACH):
            rows = slice((p + shift[side]) * BS, (p + shift[side] + 1) * BS)
            for t in range(4):
                value = jnp.concatenate([block(p, base + 2 * t), block(p, base + 2 * t + 1)], axis=1)
                for q, x in enumerate(split(value)):
                    halo[side, q, rows, t * 2 * BS : (t + 1) * 2 * BS] = x
        rows = slice(0, BS) if side == 0 else slice(REACH * BS, WIDE)
        for q in range(2):
            halo[side, q, rows, :] = jnp.zeros((BS, 2 * WIDE), BF)

    corners = []
    across = []
    for side in range(2):
        _, _, _, a_ref, b_ref, m_ref, _ = given[side]
        at = shift[side]
        whole = [halo[side, q] for q in range(2)]
        outer_rows = slice(at * BS, (at + REACH) * BS)
        inner = slice(WIDE, 2 * WIDE) if side == 0 else slice(0, WIDE)
        edge_group, outer_group = ((0, -1), (groups - 1, groups))[side]
        low_row = 1 - at

        value = product([([x[outer_rows] for x in whole], whole)], True) + a_ref[...]
        rows = []
        for p in range(REACH):
            line = line_of(lines, outer_group, p + at, outer_group)
            rows.append(value[p * BS : (p + 1) * BS] * line)
        rows = [zero] + rows if side == 0 else rows + [zero]
        corners.append(split(jnp.concatenate(rows, axis=0)))

        value = product([([m_ref[q] for q in range(2)], [x[:, inner] for x in whole])], True)
        value = value + b_ref[...]
        rows = []
        offset = 0 if side == 0 else 2 * REACH
        for s in range(REACH):
            line = line_of(lines, edge_group, s + low_row, outer_group)
            rows.append(value[s * BS : (s + 1) * BS] * line)
            part = jnp.where(upper_half, rows[s][HALF:], rows[s][:HALF])
            for t in range(REACH):
                k = t - s + offset
                if 0 <= k < SPAN:
                    blocks[0, side, s, k] = part[:, (t + at) * BS : (t + at + 1) * BS]
        rows = rows + [zero] if side == 0 else [zero] + rows
        across.append(split(jnp.concatenate(rows, axis=0)))

    stores = []
    for side in range(2):
        seed, p_ref = given[side][2], given[side][6]
        at = shift[side]
        reach_out = [p_ref[q, 0] for q in range(2)]
        inside = [p_ref[q, 1] for q in range(2)]
        out = product([(reach_out, corners[side]), (inside, across[side])])
        back = product([(reach_out, across[side])], True)
        offset = 0 if side == 0 else 2 * REACH
        edge_group, outer_group = ((0, -1), (groups - 1, groups))[side]
        for s in range(REACH):
            a = ends[side] + s
            far_line = line_of(lines, edge_group, s + 1 - at, outer_group)
            line = line_of(lines, edge_group, s + 1 - at, edge_group)
            far = out[s * HALF : (s + 1) * HALF] * (far_line * 0.5)
            close = back[s * HALF : (s + 1) * HALF] * (line * 0.5)
            for t in range(REACH):
                k = t - s + offset
                if 0 <= k < SPAN:
                    lanes = slice((t + at) * BS, (t + at + 1) * BS)
                    blocks[1, side, s, k] = seed[s, k] - far[:, lanes]
                k = t - s + REACH
                lanes = slice((t + 1 - at) * BS, (t + 2 - at) * BS)
                blocks[1, side, s, k] = seed[s, k] - close[:, lanes]
            for i, ref in enumerate((square_out, sign_out)):
                k0, k1 = span_of(a, count, i == 0)
                k0, k1 = (0, k0) if side == 0 else (k1, SPAN)
                store = pltpu.make_async_copy(
                    blocks.at[i, side, s, pl.ds(k0, k1 - k0)],
                    ref.at[a, pl.ds(k0, k1 - k0)],
                    sems.at[i, side, s],
                )
                store.start()
                stores.append(store)
    for store in stores:
        store.wait()


def shards(matrix, pattern, *, axes, half_axis):
    count = matrix.shape[0]
    groups = count // GROUP
    flags = pattern.T
    vmem = pl.BlockSpec(memory_space=pltpu.VMEM)
    hbm = pl.BlockSpec(memory_space=pl.ANY)
    params = pltpu.CompilerParams(vmem_limit_bytes=LIMIT)

    top, bottom = matrix[:REACH, REACH:], matrix[count - REACH :, : REACH + 1]
    matrix, top, bottom = lax.optimization_barrier((matrix, top, bottom))
    edge = jax.ShapeDtypeStruct((REACH * HALF, (REACH + 1) * BS), F32)
    to_left, to_right = pl.pallas_call(
        edge_kernel,
        out_shape=(edge, edge),
        in_specs=[vmem] * 2,
        out_specs=[vmem] * 2,
        compiler_params=params,
        cost_estimate=pl.CostEstimate(
            flops=1 * 10**9, bytes_accessed=2**20, transcendentals=0
        ),
    )(top, bottom)
    size = 1
    for axis in axes:
        size *= lax.axis_size(axis)
    swap = [(0, 1), (1, 0)]
    other = lax.ppermute(matrix, half_axis, swap)
    forward = [(i, (i + 1) % size) for i in range(size)]
    backward = [(target, source) for source, target in forward]
    high_own = lax.ppermute(to_left, axes, backward)
    low_own = lax.ppermute(to_right, axes, forward)

    band = jax.ShapeDtypeStruct(matrix.shape, F32)
    seed = jax.ShapeDtypeStruct((REACH, SPAN, HALF, BS), F32)
    full = jax.ShapeDtypeStruct((2, groups, WIDE, 3 * WIDE), BF)
    mine = jax.ShapeDtypeStruct((2, groups, GROUP * HALF, 3 * WIDE), BF)
    keep = jax.ShapeDtypeStruct((2, 3 * groups, WIDE, WIDE), BF)
    lines = jax.ShapeDtypeStruct(((groups + 2) * GROUP, 3 * WIDE), F32)
    rows = jax.ShapeDtypeStruct((GROUP,) + matrix.shape[1:], F32)
    square, sign, low_seed, full, mine, keep, lines, square_left, sign_left = pl.pallas_call(
        functools.partial(first_kernel, axes=axes, half_axis=half_axis),
        out_shape=[band, band, seed, full, mine, keep, lines, rows, rows],
        in_specs=[vmem, vmem, hbm],
        out_specs=[hbm] * 2 + [vmem] * 7,
        scratch_shapes=[
            pltpu.SMEM(flags.shape, jnp.int32),
            pltpu.VMEM((groups - 1,) + rows.shape, F32),
            pltpu.VMEM((groups - 2,) + rows.shape, F32),
            pltpu.SemaphoreType.DMA((2, count)),
            pltpu.SemaphoreType.DMA,
        ],
        compiler_params=params,
        cost_estimate=pl.CostEstimate(
            flops=3 * 2 * 16 * WIDE**3, bytes_accessed=16 * 2**20, transcendentals=0
        ),
    )(matrix, other, flags)

    low_own, high_own, low_seed = lax.optimization_barrier((low_own, high_own, low_seed))
    low_other = lax.ppermute(low_own, half_axis, swap)
    high_other = lax.ppermute(high_own, half_axis, swap)

    ends_out = [
        jax.ShapeDtypeStruct((REACH * BS, WIDE), F32),
        jax.ShapeDtypeStruct((REACH * BS, WIDE), F32),
        jax.ShapeDtypeStruct((2, REACH * BS, WIDE), BF),
        jax.ShapeDtypeStruct((2, 2, REACH * HALF, WIDE), BF),
    ]
    square, sign, high_seed, *ends = pl.pallas_call(
        last_kernel,
        out_shape=[band, band, seed] + ends_out * 2,
        in_specs=[vmem] * 7 + [hbm] * 2,
        out_specs=[hbm] * 2 + [vmem] * 9,
        scratch_shapes=[
            pltpu.VMEM(rows.shape, F32),
            pltpu.SemaphoreType.DMA((2, count)),
        ],
        input_output_aliases={7: 0, 8: 1},
        compiler_params=params,
        cost_estimate=pl.CostEstimate(
            flops=3 * 2 * 4 * WIDE**3, bytes_accessed=4 * 2**20, transcendentals=0
        ),
    )(matrix, lines, full, mine, keep, square_left, sign_left, square, sign)

    return tuple(
        pl.pallas_call(
            functools.partial(border_kernel, half_axis=half_axis),
            out_shape=(band, band),
            in_specs=[vmem] * 15 + [hbm] * 2,
            out_specs=[hbm] * 2,
            scratch_shapes=[
                pltpu.VMEM((2, 2, WIDE, 2 * WIDE), BF),
                pltpu.VMEM((2, 2, REACH, SPAN, HALF, BS), F32),
                pltpu.SemaphoreType.DMA((2, 2, REACH)),
            ],
            input_output_aliases={15: 0, 16: 1},
            compiler_params=params,
            cost_estimate=pl.CostEstimate(
                flops=3 * 2 * 4 * WIDE**3, bytes_accessed=2 * 2**20, transcendentals=0
            ),
        )(
            low_own, low_other, high_own, high_other, lines, low_seed, *ends[:4], high_seed,
            *ends[4:], square, sign,
        )
    )


def solution(mesh):
    band = P(("group", "row", "col"), None, "rep", None)
    return jax.shard_map(
        functools.partial(shards, axes=("row", "col"), half_axis="rep"),
        mesh=mesh,
        in_specs=(band, P("group", None)),
        out_specs=(band, band),
        check_vma=False,
    )
```

```python
import functools

import jax
import jax.numpy as jnp
from jax import lax
from jax.experimental import pallas as pl
from jax.experimental.pallas import tpu as pltpu
from jax.sharding import PartitionSpec as P

REACH = 3
SPAN = 7
BS = 64
HALF = 32
GROUP = 4
WIDE = GROUP * BS
BF = jnp.bfloat16
F32 = jnp.float32
LIMIT = 32 * 1024 * 1024


def split(x):
    hi = x.astype(BF)
    return hi, (x - hi.astype(F32)).astype(BF)


def product(pairs, transposed=False):
    side = 1 if transposed else 0
    left = [x for a, _ in pairs for x in (a[0], a[0], a[1])]
    right = [x for _, b in pairs for x in (b[0], b[1], b[0])]
    return lax.dot_general(
        jnp.concatenate(left, axis=1),
        jnp.concatenate(right, axis=side),
        (((1,), (side,)), ((), ())),
        preferred_element_type=F32,
    )


def turn(x):
    return split((x[0].astype(F32) + x[1].astype(F32)).T)


def write_lines(pat, lines, first, groups):
    total = pat.shape[1]
    lane = lax.broadcasted_iota(jnp.int32, (1, 2 * BS), 1)
    for g in range(-1, groups + 1):
        for s in range(GROUP):
            row = lax.rem(first + g * GROUP + s + total, total)
            for t in range(3 * GROUP // 2):
                ks = [2 * t + e - s - 1 for e in range(2)]
                f = [pat[k, row].astype(F32) if 0 <= k < SPAN else F32(0) for k in ks]
                at = (g + 1) * GROUP + s
                lines[at : at + 1, t * 2 * BS : (t + 1) * 2 * BS] = jnp.where(lane < BS, f[0], f[1])


def line_of(lines, g, s, h):
    at = (g + 1) * GROUP + s
    lo = (h - g + 1) * WIDE
    return lines[at : at + 1, lo : lo + WIDE]


def span_of(a, count, is_square):
    if a < REACH:
        return (REACH - a if is_square else 2 * REACH - a), SPAN
    s = a - (count - REACH)
    if s >= 0:
        return 0, (2 * REACH - s if is_square else REACH - s)
    return 0, SPAN


def edge_kernel(top, bottom, to_left, to_right):
    for source, target in ((top, to_left), (bottom, to_right)):
        for s in range(REACH):
            for t in range(2):
                target[s * HALF : (s + 1) * HALF, t * 2 * BS : (t + 1) * 2 * BS] = jnp.concatenate(
                    [source[s, 2 * t], source[s, 2 * t + 1]], axis=1
                )


class Interior:
    def __init__(self, own, lines, full, mine, keep):
        self.own = own
        self.lines = lines
        self.full = full
        self.mine = mine
        self.keep = keep
        self.count = own.shape[0]
        self.groups = self.count // GROUP
        self.stores = []

    def part(self, g, h, rows=slice(None)):
        at = (h - g + 1) * WIDE
        return [self.full[p, g, rows, at : at + WIDE] for p in range(2)]

    def my_part(self, g, h):
        at = (h - g + 1) * WIDE
        return [self.mine[p, g, :, at : at + WIDE] for p in range(2)]

    def tile(self, g, h):
        return 3 * g + h - g + 1

    def kept(self, g, h):
        return [self.keep[p, self.tile(g, h)] for p in range(2)]

    def near(self, g):
        return [e for e in (g - 1, g, g + 1) if 0 <= e < self.groups]

    def second(self, g, h, sign, seed, result):
        span = range(1 if h > g else 0, GROUP - 1 if h < g else GROUP)
        rows = slice(span[0] * HALF, (span[-1] + 1) * HALF)

        def dot():
            result[rows] = product(
                [
                    ([x[rows] for x in self.my_part(g, e)], self.kept(e, h))
                    for e in self.near(g)
                    if abs(e - h) <= 1
                ]
            )

        def post():
            for s in span:
                a = g * GROUP + s
                k0, k1 = span_of(a, self.count, False)
                part = result[s * HALF : (s + 1) * HALF] * (line_of(self.lines, g, s, h) * 0.5)
                for t in range(GROUP):
                    k = t + GROUP * (h - g) - s + REACH
                    if 0 <= k < SPAN:
                        block = 1.5 * self.own[a, k] - part[:, t * BS : (t + 1) * BS]
                        if k0 <= k < k1:
                            sign[s, k] = block
                        else:
                            seed[a if a < REACH else a - (self.count - REACH), k] = block

        return dot, post

    def far_seed(self, g, seed):
        for s in range(REACH):
            a = s if g == 0 else self.count - REACH + s
            for k in range(0, REACH - s) if g == 0 else range(2 * REACH - s, SPAN):
                seed[s, k] = 1.5 * self.own[a, k]

    def send(self, g, i, source, target, sems):
        for s in range(GROUP):
            a = g * GROUP + s
            k0, k1 = span_of(a, self.count, i == 0)
            store = pltpu.make_async_copy(
                source.at[s, pl.ds(k0, k1 - k0)], target.at[a, pl.ds(k0, k1 - k0)], sems.at[i, a]
            )
            store.start()
            self.stores.append(store)

    def finish(self):
        for store in self.stores:
            store.wait()


def count_dots(steps):
    return sum(isinstance(step, tuple) for step in steps)


def staggered(steps):
    pending = []
    for step in steps:
        if not isinstance(step, tuple):
            pending.append(step)
            continue
        dot, post = step
        dot()
        for work in pending:
            work()
        pending = [post]
    for work in pending:
        work()


def first_kernel(
    own, other, pattern, square_out, sign_out, seed, full, mine, keep, lines, square_left, sign_left,
    pat, square, sign, results, sems, pat_sem, *, axes, half_axis
):
    load = pltpu.make_async_copy(pattern, pat, pat_sem)
    load.start()
    it = Interior(own, lines, full, mine, keep)
    groups = it.groups
    upper_half = lax.axis_index(half_axis) == 1

    def build(g):
        for s in range(GROUP):
            a = g * GROUP + s
            for t in range(3 * GROUP // 2):
                ks = [2 * t + e - s - 1 for e in range(2)]
                lanes = slice(t * 2 * BS, (t + 1) * 2 * BS)
                rows = slice(s * BS, (s + 1) * BS)
                mine_rows = slice(s * HALF, (s + 1) * HALF)
                if all(k < 0 or k >= SPAN for k in ks):
                    for p in range(2):
                        full[p, g, rows, lanes] = jnp.zeros((BS, 2 * BS), BF)
                        mine[p, g, mine_rows, lanes] = jnp.zeros((HALF, 2 * BS), BF)
                    continue
                two = [
                    jnp.concatenate(
                        [src[a, k] if 0 <= k < SPAN else jnp.zeros((HALF, BS), F32) for k in ks],
                        axis=1,
                    )
                    for src in (own, other)
                ]
                for p, (x, y) in enumerate(zip(*[split(x) for x in two])):
                    mine[p, g, mine_rows, lanes] = x
                    full[p, g, rows, lanes] = jnp.concatenate(
                        [jnp.where(upper_half, y, x), jnp.where(upper_half, x, y)], axis=0
                    )

    def squares(g, h, result):
        pairs = []
        for e in (g - 1, g, g + 1):
            if abs(e - h) <= 1:
                inside = 0 <= e < groups
                pairs.append((e, (lambda e=e: it.part(e, h)) if inside else (lambda e=e: turn(it.part(h, e)))))
        span = range(1 if h > g else 0, GROUP)
        rows = slice(span[0] * BS, WIDE)

        def dot():
            result[rows] = product([([x[rows] for x in it.part(g, e)], f()) for e, f in pairs])

        def post():
            masked = [jnp.zeros((BS, WIDE), F32)] * GROUP
            for s in span:
                masked[s] = result[s * BS : (s + 1) * BS] * line_of(lines, g, s, h)
            for s in range(GROUP):
                for p, x in enumerate(split(masked[s])):
                    keep[p, it.tile(g, h), s * BS : (s + 1) * BS] = x
            for s in span:
                part = jnp.where(upper_half, masked[s][HALF:], masked[s][:HALF])
                for t in range(GROUP):
                    k = t + GROUP * (h - g) - s + REACH
                    if 0 <= k < SPAN:
                        staged[g][s, k] = part[:, t * BS : (t + 1) * BS]
            if h == g:
                return
            for c in range(0, GROUP, 2):
                turned = jnp.concatenate(masked[c : c + 2], axis=0).T
                lanes = slice(c * BS, (c + 2) * BS)
                for p, x in enumerate(split(turned)):
                    keep[p, it.tile(h, g), :, lanes] = x
                for t in range(GROUP):
                    rows = turned[t * BS : (t + 1) * BS]
                    part = jnp.where(upper_half, rows[HALF:], rows[:HALF])
                    for s in range(c, c + 2):
                        k = s + GROUP * (g - h) - t + REACH
                        if 0 <= k < SPAN:
                            staged[h][t, k] = part[:, (s - c) * BS : (s - c + 1) * BS]

        return dot, post

    staged = [square.at[g] for g in range(groups - 1)] + [square_left]
    signs = [sign.at[g] for g in range(groups - 2)] + [sign_left]

    def begin():
        load.wait()
        write_lines(pat, lines, lax.axis_index(axes) * it.count, groups)
        it.far_seed(0, seed)

    build(0)
    build(1)
    steps = [begin]
    for g in range(groups):
        if g + 1 < groups:
            steps.append(squares(g, g + 1, results.at[count_dots(steps)]))
            if g + 2 < groups:
                steps.append(functools.partial(build, g + 2))
        steps.append(squares(g, g, results.at[count_dots(steps)]))
        if g + 1 < groups:
            steps.append(functools.partial(it.send, g, 0, staged[g], square_out, sems))
        if g > 0:
            for h in it.near(g - 1):
                steps.append(it.second(g - 1, h, signs[g - 1], seed, results.at[count_dots(steps)]))
            if g < groups - 1:
                steps.append(functools.partial(it.send, g - 1, 1, signs[g - 1], sign_out, sems))
    staggered(steps)
    it.finish()


def last_kernel(
    own, lines, full, mine, keep, square_left, sign_left, square_in, sign_in, square_out, sign_out,
    seed, low_a, low_b, low_m, low_p, high_a, high_b, high_m, high_p, sign, results, sems
):
    it = Interior(own, lines, full, mine, keep)
    last = it.groups - 1
    it.send(last, 0, square_left, square_out, sems)
    it.send(last - 1, 1, sign_left, sign_out, sems)
    steps = [it.second(last, h, sign, seed, results.at[i]) for i, h in enumerate(it.near(last))]
    steps.append(functools.partial(it.send, last, 1, sign, sign_out, sems))
    steps.append(functools.partial(it.far_seed, last, seed))

    def reaching(a_ref, b_ref, m_ref, p_ref, g, e, r0):
        rows = slice(r0, r0 + REACH * BS)
        mine_rows = slice(r0 // 2, r0 // 2 + REACH * HALF)
        outer = slice(BS - r0, BS - r0 + REACH * BS)

        def dot():
            out = it.part(g, e)
            a_ref[...] = product([([x[outer] for x in turn(out)], out)])
            b_ref[...] = product([(it.part(g, g, rows), out)])

        def post():
            for p in range(2):
                m_ref[p] = it.part(g, e)[p][rows]
                p_ref[p, 0] = it.my_part(g, e)[p][mine_rows]
                p_ref[p, 1] = it.my_part(g, g)[p][mine_rows]

        return dot, post

    steps.append(reaching(low_a, low_b, low_m, low_p, 0, -1, 0))
    steps.append(reaching(high_a, high_b, high_m, high_p, last, last + 1, BS))
    staggered(steps)
    it.finish()


def border_kernel(
    low_own, low_other, high_own, high_other, lines, low_seed, low_a, low_b, low_m, low_p, high_seed,
    high_a, high_b, high_m, high_p, square_in, sign_in, square_out, sign_out, halo, first, last, blocks, sems,
    *, half_axis
):
    count = square_in.shape[0]
    groups = count // GROUP
    upper_half = lax.axis_index(half_axis) == 1
    ends = (0, count - REACH)
    given = (
        (low_own, low_other, low_seed, low_a, low_b, low_m, low_p),
        (high_own, high_other, high_seed, high_a, high_b, high_m, high_p),
    )
    shift = (1, 0)
    zero = jnp.zeros((BS, WIDE), F32)

    def build(side):
        mine, theirs = given[side][:2]
        below = REACH if side == 0 else 0
        whole_rows = []
        for p in range(REACH):
            rows = slice(p * HALF, (p + 1) * HALF)
            whole_rows.append(
                jnp.concatenate(
                    [
                        jnp.where(upper_half, theirs[rows, :], mine[rows, :]),
                        jnp.where(upper_half, mine[rows, :], theirs[rows, :]),
                    ],
                    axis=0,
                )
            )

        def block(p, c):
            k = c - p + below
            if 0 <= k <= REACH:
                return whole_rows[p][:, k * BS : (k + 1) * BS]
            k = p - c + below
            if 0 <= c < REACH and 0 <= k <= REACH:
                return whole_rows[c][:, k * BS : (k + 1) * BS].T
            return jnp.zeros((BS, BS), F32)

        base = -5 if side == 0 else 0
        for p in range(REACH):
            rows = slice((p + shift[side]) * BS, (p + shift[side] + 1) * BS)
            for t in range(4):
                value = jnp.concatenate([block(p, base + 2 * t), block(p, base + 2 * t + 1)], axis=1)
                for q, x in enumerate(split(value)):
                    halo[side, q, rows, t * 2 * BS : (t + 1) * 2 * BS] = x
        rows = slice(0, BS) if side == 0 else slice(REACH * BS, WIDE)
        for q in range(2):
            halo[side, q, rows, :] = jnp.zeros((BS, 2 * WIDE), BF)

    edge_groups, outer_groups = (0, groups - 1), (-1, groups)
    offsets = (0, 2 * REACH)
    corners = [None, None]
    across = [None, None]
    stores = []

    def dots(side):
        _, _, _, a_ref, b_ref, m_ref, _ = given[side]
        whole = [halo[side, q] for q in range(2)]
        outer_rows = slice(shift[side] * BS, (shift[side] + REACH) * BS)
        inner = slice(WIDE, 2 * WIDE) if side == 0 else slice(0, WIDE)
        first[side, 0] = product([([x[outer_rows] for x in whole], whole)], True) + a_ref[...]
        first[side, 1] = (
            product([([m_ref[q] for q in range(2)], [x[:, inner] for x in whole])], True) + b_ref[...]
        )

    def masks(side):
        at = shift[side]
        edge_group, outer_group = edge_groups[side], outer_groups[side]
        pad = (lambda rows: [zero] + rows, lambda rows: rows + [zero])
        rows = [
            first[side, 0, p * BS : (p + 1) * BS] * line_of(lines, outer_group, p + at, outer_group)
            for p in range(REACH)
        ]
        corners[side] = split(jnp.concatenate(pad[side](rows), axis=0))
        rows = [
            first[side, 1, s * BS : (s + 1) * BS]
            * line_of(lines, edge_group, s + 1 - at, outer_group)
            for s in range(REACH)
        ]
        across[side] = split(jnp.concatenate(pad[1 - side](rows), axis=0))
        for s in range(REACH):
            part = jnp.where(upper_half, rows[s][HALF:], rows[s][:HALF])
            for t in range(REACH):
                k = t - s + offsets[side]
                if 0 <= k < SPAN:
                    blocks[0, side, s, k] = part[:, (t + at) * BS : (t + at + 1) * BS]
        send(side, 0, square_out)

    def send(side, i, ref):
        for s in range(REACH):
            a = ends[side] + s
            k0, k1 = span_of(a, count, i == 0)
            k0, k1 = (0, k0) if side == 0 else (k1, SPAN)
            store = pltpu.make_async_copy(
                blocks.at[i, side, s, pl.ds(k0, k1 - k0)],
                ref.at[a, pl.ds(k0, k1 - k0)],
                sems.at[i, side, s],
            )
            store.start()
            stores.append(store)

    def second_dots(side):
        p_ref = given[side][6]
        reach_out = [p_ref[q, 0] for q in range(2)]
        inside = [p_ref[q, 1] for q in range(2)]
        last[side, 0] = product([(reach_out, corners[side]), (inside, across[side])])
        last[side, 1] = product([(reach_out, across[side])], True)

    def emit(side):
        seed = given[side][2]
        at = shift[side]
        edge_group, outer_group = edge_groups[side], outer_groups[side]
        for s in range(REACH):
            rows = slice(s * HALF, (s + 1) * HALF)
            far = last[side, 0, rows] * (line_of(lines, edge_group, s + 1 - at, outer_group) * 0.5)
            close = last[side, 1, rows] * (line_of(lines, edge_group, s + 1 - at, edge_group) * 0.5)
            for t in range(REACH):
                k = t - s + offsets[side]
                if 0 <= k < SPAN:
                    lanes = slice((t + at) * BS, (t + at + 1) * BS)
                    blocks[1, side, s, k] = seed[s, k] - far[:, lanes]
                k = t - s + REACH
                lanes = slice((t + 1 - at) * BS, (t + 2 - at) * BS)
                blocks[1, side, s, k] = seed[s, k] - close[:, lanes]
        send(side, 1, sign_out)

    build(0)
    dots(0)
    build(1)
    dots(1)
    masks(0)
    second_dots(0)
    masks(1)
    second_dots(1)
    emit(0)
    emit(1)
    for store in stores:
        store.wait()


def shards(matrix, pattern, *, axes, half_axis):
    count = matrix.shape[0]
    groups = count // GROUP
    flags = pattern.T
    vmem = pl.BlockSpec(memory_space=pltpu.VMEM)
    hbm = pl.BlockSpec(memory_space=pl.ANY)
    params = pltpu.CompilerParams(vmem_limit_bytes=LIMIT)

    top, bottom = matrix[:REACH, REACH:], matrix[count - REACH :, : REACH + 1]
    matrix, top, bottom = lax.optimization_barrier((matrix, top, bottom))
    edge = jax.ShapeDtypeStruct((REACH * HALF, (REACH + 1) * BS), F32)
    to_left, to_right = pl.pallas_call(
        edge_kernel,
        out_shape=(edge, edge),
        in_specs=[vmem] * 2,
        out_specs=[vmem] * 2,
        compiler_params=params,
        cost_estimate=pl.CostEstimate(
            flops=1 * 10**9, bytes_accessed=2**20, transcendentals=0
        ),
    )(top, bottom)
    size = 1
    for axis in axes:
        size *= lax.axis_size(axis)
    swap = [(0, 1), (1, 0)]
    other = lax.ppermute(matrix, half_axis, swap)
    forward = [(i, (i + 1) % size) for i in range(size)]
    backward = [(target, source) for source, target in forward]
    high_own = lax.ppermute(to_left, axes, backward)
    low_own = lax.ppermute(to_right, axes, forward)

    band = jax.ShapeDtypeStruct(matrix.shape, F32)
    seed = jax.ShapeDtypeStruct((REACH, SPAN, HALF, BS), F32)
    full = jax.ShapeDtypeStruct((2, groups, WIDE, 3 * WIDE), BF)
    mine = jax.ShapeDtypeStruct((2, groups, GROUP * HALF, 3 * WIDE), BF)
    keep = jax.ShapeDtypeStruct((2, 3 * groups, WIDE, WIDE), BF)
    lines = jax.ShapeDtypeStruct(((groups + 2) * GROUP, 3 * WIDE), F32)
    rows = jax.ShapeDtypeStruct((GROUP,) + matrix.shape[1:], F32)
    square, sign, low_seed, full, mine, keep, lines, square_left, sign_left = pl.pallas_call(
        functools.partial(first_kernel, axes=axes, half_axis=half_axis),
        out_shape=[band, band, seed, full, mine, keep, lines, rows, rows],
        in_specs=[vmem, vmem, hbm],
        out_specs=[hbm] * 2 + [vmem] * 7,
        scratch_shapes=[
            pltpu.SMEM(flags.shape, jnp.int32),
            pltpu.VMEM((groups - 1,) + rows.shape, F32),
            pltpu.VMEM((groups - 2,) + rows.shape, F32),
            pltpu.VMEM((2 * groups - 1 + 3 * groups - 4, WIDE, WIDE), F32),
            pltpu.SemaphoreType.DMA((2, count)),
            pltpu.SemaphoreType.DMA,
        ],
        compiler_params=params,
        cost_estimate=pl.CostEstimate(
            flops=3 * 2 * 16 * WIDE**3, bytes_accessed=16 * 2**20, transcendentals=0
        ),
    )(matrix, other, flags)

    low_own, high_own, low_seed = lax.optimization_barrier((low_own, high_own, low_seed))
    low_other = lax.ppermute(low_own, half_axis, swap)
    high_other = lax.ppermute(high_own, half_axis, swap)

    ends_out = [
        jax.ShapeDtypeStruct((REACH * BS, WIDE), F32),
        jax.ShapeDtypeStruct((REACH * BS, WIDE), F32),
        jax.ShapeDtypeStruct((2, REACH * BS, WIDE), BF),
        jax.ShapeDtypeStruct((2, 2, REACH * HALF, WIDE), BF),
    ]
    square, sign, high_seed, *ends = pl.pallas_call(
        last_kernel,
        out_shape=[band, band, seed] + ends_out * 2,
        in_specs=[vmem] * 7 + [hbm] * 2,
        out_specs=[hbm] * 2 + [vmem] * 9,
        scratch_shapes=[
            pltpu.VMEM(rows.shape, F32),
            pltpu.VMEM((2, GROUP * HALF, WIDE), F32),
            pltpu.SemaphoreType.DMA((2, count)),
        ],
        input_output_aliases={7: 0, 8: 1},
        compiler_params=params,
        cost_estimate=pl.CostEstimate(
            flops=3 * 2 * 4 * WIDE**3, bytes_accessed=4 * 2**20, transcendentals=0
        ),
    )(matrix, lines, full, mine, keep, square_left, sign_left, square, sign)

    return tuple(
        pl.pallas_call(
            functools.partial(border_kernel, half_axis=half_axis),
            out_shape=(band, band),
            in_specs=[vmem] * 15 + [hbm] * 2,
            out_specs=[hbm] * 2,
            scratch_shapes=[
                pltpu.VMEM((2, 2, WIDE, 2 * WIDE), BF),
                pltpu.VMEM((2, 2, REACH * BS, WIDE), F32),
                pltpu.VMEM((2, 2, REACH * HALF, WIDE), F32),
                pltpu.VMEM((2, 2, REACH, SPAN, HALF, BS), F32),
                pltpu.SemaphoreType.DMA((2, 2, REACH)),
            ],
            input_output_aliases={15: 0, 16: 1},
            compiler_params=params,
            cost_estimate=pl.CostEstimate(
                flops=3 * 2 * 4 * WIDE**3, bytes_accessed=2 * 2**20, transcendentals=0
            ),
        )(
            low_own, low_other, high_own, high_other, lines, low_seed, *ends[:4], high_seed,
            *ends[4:], square, sign,
        )
    )


def solution(mesh):
    band = P(("group", "row", "col"), None, "rep", None)
    return jax.shard_map(
        functools.partial(shards, axes=("row", "col"), half_axis="rep"),
        mesh=mesh,
        in_specs=(band, P("group", None)),
        out_specs=(band, band),
        check_vma=False,
    )
```

```python
import functools

import jax
import jax.numpy as jnp
from jax import lax
from jax.experimental import pallas as pl
from jax.experimental.pallas import tpu as pltpu
from jax.sharding import PartitionSpec as P

REACH = 3
SPAN = 7
BS = 64
HALF = 32
GROUP = 4
WIDE = GROUP * BS
BF = jnp.bfloat16
F32 = jnp.float32
LIMIT = 32 * 1024 * 1024


def split(x):
    hi = x.astype(BF)
    return hi, (x - hi.astype(F32)).astype(BF)


def product(pairs, transposed=False):
    side = 1 if transposed else 0
    left = [x for a, _ in pairs for x in (a[0], a[0], a[1])]
    right = [x for _, b in pairs for x in (b[0], b[1], b[0])]
    return lax.dot_general(
        jnp.concatenate(left, axis=1),
        jnp.concatenate(right, axis=side),
        (((1,), (side,)), ((), ())),
        preferred_element_type=F32,
    )


def turn(x):
    return split((x[0].astype(F32) + x[1].astype(F32)).T)


def write_lines(pat, lines, first, groups):
    total = pat.shape[1]
    lane = lax.broadcasted_iota(jnp.int32, (1, 2 * BS), 1)
    for g in range(-1, groups + 1):
        for s in range(GROUP):
            row = lax.rem(first + g * GROUP + s + total, total)
            for t in range(3 * GROUP // 2):
                ks = [2 * t + e - s - 1 for e in range(2)]
                f = [pat[k, row].astype(F32) if 0 <= k < SPAN else F32(0) for k in ks]
                at = (g + 1) * GROUP + s
                lines[at : at + 1, t * 2 * BS : (t + 1) * 2 * BS] = jnp.where(lane < BS, f[0], f[1])


def line_of(lines, g, s, h):
    at = (g + 1) * GROUP + s
    lo = (h - g + 1) * WIDE
    return lines[at : at + 1, lo : lo + WIDE]


def span_of(a, count, is_square):
    if a < REACH:
        return (REACH - a if is_square else 2 * REACH - a), SPAN
    s = a - (count - REACH)
    if s >= 0:
        return 0, (2 * REACH - s if is_square else REACH - s)
    return 0, SPAN


def edge_kernel(top, bottom, to_left, to_right):
    for source, target in ((top, to_left), (bottom, to_right)):
        for s in range(REACH):
            for t in range(2):
                target[s * HALF : (s + 1) * HALF, t * 2 * BS : (t + 1) * 2 * BS] = jnp.concatenate(
                    [source[s, 2 * t], source[s, 2 * t + 1]], axis=1
                )


class Interior:
    def __init__(self, own, lines, full, mine, keep):
        self.own = own
        self.lines = lines
        self.full = full
        self.mine = mine
        self.keep = keep
        self.count = own.shape[0]
        self.groups = self.count // GROUP
        self.stores = []

    def part(self, g, h, rows=slice(None)):
        at = (h - g + 1) * WIDE
        return [self.full[p, g, rows, at : at + WIDE] for p in range(2)]

    def my_part(self, g, h):
        at = (h - g + 1) * WIDE
        return [self.mine[p, g, :, at : at + WIDE] for p in range(2)]

    def tile(self, g, h):
        return 3 * g + h - g + 1

    def kept(self, g, h):
        return [self.keep[p, self.tile(g, h)] for p in range(2)]

    def near(self, g):
        return [e for e in (g - 1, g, g + 1) if 0 <= e < self.groups]

    def second(self, g, h, sign, seed, result):
        span = range(1 if h > g else 0, GROUP - 1 if h < g else GROUP)
        rows = slice(span[0] * HALF, (span[-1] + 1) * HALF)

        def dot():
            return product(
                [
                    ([x[rows] for x in self.my_part(g, e)], self.kept(e, h))
                    for e in self.near(g)
                    if abs(e - h) <= 1
                ]
            )

        def store(value):
            result[rows] = value

        def post():
            for s in span:
                a = g * GROUP + s
                k0, k1 = span_of(a, self.count, False)
                part = result[s * HALF : (s + 1) * HALF] * (line_of(self.lines, g, s, h) * 0.5)
                for t in range(GROUP):
                    k = t + GROUP * (h - g) - s + REACH
                    if 0 <= k < SPAN:
                        block = 1.5 * self.own[a, k] - part[:, t * BS : (t + 1) * BS]
                        if k0 <= k < k1:
                            sign[s, k] = block
                        else:
                            seed[a if a < REACH else a - (self.count - REACH), k] = block

        return dot, store, post

    def far_seed(self, g, seed):
        for s in range(REACH):
            a = s if g == 0 else self.count - REACH + s
            for k in range(0, REACH - s) if g == 0 else range(2 * REACH - s, SPAN):
                seed[s, k] = 1.5 * self.own[a, k]

    def send(self, g, i, source, target, sems):
        for s in range(GROUP):
            a = g * GROUP + s
            k0, k1 = span_of(a, self.count, i == 0)
            store = pltpu.make_async_copy(
                source.at[s, pl.ds(k0, k1 - k0)], target.at[a, pl.ds(k0, k1 - k0)], sems.at[i, a]
            )
            store.start()
            self.stores.append(store)

    def finish(self):
        for store in self.stores:
            store.wait()


def count_dots(steps):
    return sum(isinstance(step, tuple) for step in steps)


def staggered(steps):
    pending = []
    for step in steps:
        if not isinstance(step, tuple):
            pending.append(step)
            continue
        dot, store, post = step
        value = dot()
        for work in pending:
            work()
        store(value)
        pending = [post]
    for work in pending:
        work()


def first_kernel(
    own, other, pattern, square_out, sign_out, seed, full, mine, keep, lines, square_left, sign_left,
    pat, square, sign, results, sems, pat_sem, *, axes, half_axis
):
    load = pltpu.make_async_copy(pattern, pat, pat_sem)
    load.start()
    it = Interior(own, lines, full, mine, keep)
    groups = it.groups
    upper_half = lax.axis_index(half_axis) == 1

    def build(g):
        for s in range(GROUP):
            a = g * GROUP + s
            for t in range(3 * GROUP // 2):
                ks = [2 * t + e - s - 1 for e in range(2)]
                lanes = slice(t * 2 * BS, (t + 1) * 2 * BS)
                rows = slice(s * BS, (s + 1) * BS)
                mine_rows = slice(s * HALF, (s + 1) * HALF)
                if all(k < 0 or k >= SPAN for k in ks):
                    for p in range(2):
                        full[p, g, rows, lanes] = jnp.zeros((BS, 2 * BS), BF)
                        mine[p, g, mine_rows, lanes] = jnp.zeros((HALF, 2 * BS), BF)
                    continue
                two = [
                    jnp.concatenate(
                        [src[a, k] if 0 <= k < SPAN else jnp.zeros((HALF, BS), F32) for k in ks],
                        axis=1,
                    )
                    for src in (own, other)
                ]
                for p, (x, y) in enumerate(zip(*[split(x) for x in two])):
                    mine[p, g, mine_rows, lanes] = x
                    full[p, g, rows, lanes] = jnp.concatenate(
                        [jnp.where(upper_half, y, x), jnp.where(upper_half, x, y)], axis=0
                    )

    def squares(g, h, result):
        pairs = []
        for e in (g - 1, g, g + 1):
            if abs(e - h) <= 1:
                inside = 0 <= e < groups
                pairs.append((e, (lambda e=e: it.part(e, h)) if inside else (lambda e=e: turn(it.part(h, e)))))
        span = range(1 if h > g else 0, GROUP)
        rows = slice(span[0] * BS, WIDE)

        def dot():
            return product([([x[rows] for x in it.part(g, e)], f()) for e, f in pairs])

        def store(value):
            result[rows] = value

        def post():
            masked = [jnp.zeros((BS, WIDE), F32)] * GROUP
            for s in span:
                masked[s] = result[s * BS : (s + 1) * BS] * line_of(lines, g, s, h)
            for s in range(GROUP):
                for p, x in enumerate(split(masked[s])):
                    keep[p, it.tile(g, h), s * BS : (s + 1) * BS] = x
            for s in span:
                part = jnp.where(upper_half, masked[s][HALF:], masked[s][:HALF])
                for t in range(GROUP):
                    k = t + GROUP * (h - g) - s + REACH
                    if 0 <= k < SPAN:
                        staged[g][s, k] = part[:, t * BS : (t + 1) * BS]
            if h == g:
                return
            for c in range(0, GROUP, 2):
                turned = jnp.concatenate(masked[c : c + 2], axis=0).T
                lanes = slice(c * BS, (c + 2) * BS)
                for p, x in enumerate(split(turned)):
                    keep[p, it.tile(h, g), :, lanes] = x
                for t in range(GROUP):
                    rows = turned[t * BS : (t + 1) * BS]
                    part = jnp.where(upper_half, rows[HALF:], rows[:HALF])
                    for s in range(c, c + 2):
                        k = s + GROUP * (g - h) - t + REACH
                        if 0 <= k < SPAN:
                            staged[h][t, k] = part[:, (s - c) * BS : (s - c + 1) * BS]

        return dot, store, post

    staged = [square.at[g] for g in range(groups - 1)] + [square_left]
    signs = [sign.at[g] for g in range(groups - 2)] + [sign_left]

    def begin():
        load.wait()
        write_lines(pat, lines, lax.axis_index(axes) * it.count, groups)
        it.far_seed(0, seed)

    build(0)
    build(1)
    steps = [begin]
    for g in range(groups):
        if g + 1 < groups:
            steps.append(squares(g, g + 1, results.at[count_dots(steps)]))
            if g + 2 < groups:
                steps.append(functools.partial(build, g + 2))
        steps.append(squares(g, g, results.at[count_dots(steps)]))
        if g + 1 < groups:
            steps.append(functools.partial(it.send, g, 0, staged[g], square_out, sems))
        if g > 0:
            for h in it.near(g - 1):
                steps.append(it.second(g - 1, h, signs[g - 1], seed, results.at[count_dots(steps)]))
            if g < groups - 1:
                steps.append(functools.partial(it.send, g - 1, 1, signs[g - 1], sign_out, sems))
    staggered(steps)
    it.finish()


def last_kernel(
    own, lines, full, mine, keep, square_left, sign_left, square_in, sign_in, square_out, sign_out,
    seed, low_a, low_b, low_m, low_p, high_a, high_b, high_m, high_p, sign, results, sems
):
    it = Interior(own, lines, full, mine, keep)
    last = it.groups - 1
    it.send(last, 0, square_left, square_out, sems)
    it.send(last - 1, 1, sign_left, sign_out, sems)
    steps = [it.second(last, h, sign, seed, results.at[i]) for i, h in enumerate(it.near(last))]
    steps.append(functools.partial(it.send, last, 1, sign, sign_out, sems))
    steps.append(functools.partial(it.far_seed, last, seed))

    def reaching(a_ref, b_ref, m_ref, p_ref, g, e, r0):
        rows = slice(r0, r0 + REACH * BS)
        mine_rows = slice(r0 // 2, r0 // 2 + REACH * HALF)
        outer = slice(BS - r0, BS - r0 + REACH * BS)

        def dot():
            out = it.part(g, e)
            return (
                product([([x[outer] for x in turn(out)], out)]),
                product([(it.part(g, g, rows), out)]),
            )

        def store(value):
            a_ref[...], b_ref[...] = value

        def post():
            for p in range(2):
                m_ref[p] = it.part(g, e)[p][rows]
                p_ref[p, 0] = it.my_part(g, e)[p][mine_rows]
                p_ref[p, 1] = it.my_part(g, g)[p][mine_rows]

        return dot, store, post

    steps.append(reaching(low_a, low_b, low_m, low_p, 0, -1, 0))
    steps.append(reaching(high_a, high_b, high_m, high_p, last, last + 1, BS))
    staggered(steps)
    it.finish()


def border_kernel(
    low_own, low_other, high_own, high_other, lines, low_seed, low_a, low_b, low_m, low_p, high_seed,
    high_a, high_b, high_m, high_p, square_in, sign_in, square_out, sign_out, halo, first, last, blocks, sems,
    *, half_axis
):
    count = square_in.shape[0]
    groups = count // GROUP
    upper_half = lax.axis_index(half_axis) == 1
    ends = (0, count - REACH)
    given = (
        (low_own, low_other, low_seed, low_a, low_b, low_m, low_p),
        (high_own, high_other, high_seed, high_a, high_b, high_m, high_p),
    )
    shift = (1, 0)
    zero = jnp.zeros((BS, WIDE), F32)

    def build(side):
        mine, theirs = given[side][:2]
        below = REACH if side == 0 else 0
        whole_rows = []
        for p in range(REACH):
            rows = slice(p * HALF, (p + 1) * HALF)
            whole_rows.append(
                jnp.concatenate(
                    [
                        jnp.where(upper_half, theirs[rows, :], mine[rows, :]),
                        jnp.where(upper_half, mine[rows, :], theirs[rows, :]),
                    ],
                    axis=0,
                )
            )

        def block(p, c):
            k = c - p + below
            if 0 <= k <= REACH:
                return whole_rows[p][:, k * BS : (k + 1) * BS]
            k = p - c + below
            if 0 <= c < REACH and 0 <= k <= REACH:
                return whole_rows[c][:, k * BS : (k + 1) * BS].T
            return jnp.zeros((BS, BS), F32)

        base = -5 if side == 0 else 0
        for p in range(REACH):
            rows = slice((p + shift[side]) * BS, (p + shift[side] + 1) * BS)
            for t in range(4):
                value = jnp.concatenate([block(p, base + 2 * t), block(p, base + 2 * t + 1)], axis=1)
                for q, x in enumerate(split(value)):
                    halo[side, q, rows, t * 2 * BS : (t + 1) * 2 * BS] = x
        rows = slice(0, BS) if side == 0 else slice(REACH * BS, WIDE)
        for q in range(2):
            halo[side, q, rows, :] = jnp.zeros((BS, 2 * WIDE), BF)

    edge_groups, outer_groups = (0, groups - 1), (-1, groups)
    offsets = (0, 2 * REACH)
    corners = [None, None]
    across = [None, None]
    stores = []

    def dots(side):
        m_ref = given[side][5]
        whole = [halo[side, q] for q in range(2)]
        outer_rows = slice(shift[side] * BS, (shift[side] + REACH) * BS)
        inner = slice(WIDE, 2 * WIDE) if side == 0 else slice(0, WIDE)
        return (
            product([([x[outer_rows] for x in whole], whole)], True),
            product([([m_ref[q] for q in range(2)], [x[:, inner] for x in whole])], True),
        )

    def keep_first(side, value):
        _, _, _, a_ref, b_ref, _, _ = given[side]
        first[side, 0] = value[0] + a_ref[...]
        first[side, 1] = value[1] + b_ref[...]

    def masks(side):
        at = shift[side]
        edge_group, outer_group = edge_groups[side], outer_groups[side]
        pad = (lambda rows: [zero] + rows, lambda rows: rows + [zero])
        rows = [
            first[side, 0, p * BS : (p + 1) * BS] * line_of(lines, outer_group, p + at, outer_group)
            for p in range(REACH)
        ]
        corners[side] = split(jnp.concatenate(pad[side](rows), axis=0))
        rows = [
            first[side, 1, s * BS : (s + 1) * BS]
            * line_of(lines, edge_group, s + 1 - at, outer_group)
            for s in range(REACH)
        ]
        across[side] = split(jnp.concatenate(pad[1 - side](rows), axis=0))
        for s in range(REACH):
            part = jnp.where(upper_half, rows[s][HALF:], rows[s][:HALF])
            for t in range(REACH):
                k = t - s + offsets[side]
                if 0 <= k < SPAN:
                    blocks[0, side, s, k] = part[:, (t + at) * BS : (t + at + 1) * BS]
        send(side, 0, square_out)

    def send(side, i, ref):
        for s in range(REACH):
            a = ends[side] + s
            k0, k1 = span_of(a, count, i == 0)
            k0, k1 = (0, k0) if side == 0 else (k1, SPAN)
            store = pltpu.make_async_copy(
                blocks.at[i, side, s, pl.ds(k0, k1 - k0)],
                ref.at[a, pl.ds(k0, k1 - k0)],
                sems.at[i, side, s],
            )
            store.start()
            stores.append(store)

    def second_dots(side):
        p_ref = given[side][6]
        reach_out = [p_ref[q, 0] for q in range(2)]
        inside = [p_ref[q, 1] for q in range(2)]
        return (
            product([(reach_out, corners[side]), (inside, across[side])]),
            product([(reach_out, across[side])], True),
        )

    def keep_last(side, value):
        last[side, 0], last[side, 1] = value

    def emit(side):
        seed = given[side][2]
        at = shift[side]
        edge_group, outer_group = edge_groups[side], outer_groups[side]
        for s in range(REACH):
            rows = slice(s * HALF, (s + 1) * HALF)
            far = last[side, 0, rows] * (line_of(lines, edge_group, s + 1 - at, outer_group) * 0.5)
            close = last[side, 1, rows] * (line_of(lines, edge_group, s + 1 - at, edge_group) * 0.5)
            for t in range(REACH):
                k = t - s + offsets[side]
                if 0 <= k < SPAN:
                    lanes = slice((t + at) * BS, (t + at + 1) * BS)
                    blocks[1, side, s, k] = seed[s, k] - far[:, lanes]
                k = t - s + REACH
                lanes = slice((t + 1 - at) * BS, (t + 2 - at) * BS)
                blocks[1, side, s, k] = seed[s, k] - close[:, lanes]
        send(side, 1, sign_out)

    build(0)
    value = dots(0)
    build(1)
    keep_first(0, value)
    value = dots(1)
    masks(0)
    keep_first(1, value)
    value = second_dots(0)
    masks(1)
    keep_last(0, value)
    value = second_dots(1)
    emit(0)
    keep_last(1, value)
    emit(1)
    for store in stores:
        store.wait()


def shards(matrix, pattern, *, axes, half_axis):
    count = matrix.shape[0]
    groups = count // GROUP
    flags = pattern.T
    vmem = pl.BlockSpec(memory_space=pltpu.VMEM)
    hbm = pl.BlockSpec(memory_space=pl.ANY)
    params = pltpu.CompilerParams(vmem_limit_bytes=LIMIT)

    top, bottom = matrix[:REACH, REACH:], matrix[count - REACH :, : REACH + 1]
    matrix, top, bottom = lax.optimization_barrier((matrix, top, bottom))
    edge = jax.ShapeDtypeStruct((REACH * HALF, (REACH + 1) * BS), F32)
    to_left, to_right = pl.pallas_call(
        edge_kernel,
        out_shape=(edge, edge),
        in_specs=[vmem] * 2,
        out_specs=[vmem] * 2,
        compiler_params=params,
        cost_estimate=pl.CostEstimate(
            flops=1 * 10**9, bytes_accessed=2**20, transcendentals=0
        ),
    )(top, bottom)
    size = 1
    for axis in axes:
        size *= lax.axis_size(axis)
    swap = [(0, 1), (1, 0)]
    other = lax.ppermute(matrix, half_axis, swap)
    forward = [(i, (i + 1) % size) for i in range(size)]
    backward = [(target, source) for source, target in forward]
    high_own = lax.ppermute(to_left, axes, backward)
    low_own = lax.ppermute(to_right, axes, forward)

    band = jax.ShapeDtypeStruct(matrix.shape, F32)
    seed = jax.ShapeDtypeStruct((REACH, SPAN, HALF, BS), F32)
    full = jax.ShapeDtypeStruct((2, groups, WIDE, 3 * WIDE), BF)
    mine = jax.ShapeDtypeStruct((2, groups, GROUP * HALF, 3 * WIDE), BF)
    keep = jax.ShapeDtypeStruct((2, 3 * groups, WIDE, WIDE), BF)
    lines = jax.ShapeDtypeStruct(((groups + 2) * GROUP, 3 * WIDE), F32)
    rows = jax.ShapeDtypeStruct((GROUP,) + matrix.shape[1:], F32)
    square, sign, low_seed, full, mine, keep, lines, square_left, sign_left = pl.pallas_call(
        functools.partial(first_kernel, axes=axes, half_axis=half_axis),
        out_shape=[band, band, seed, full, mine, keep, lines, rows, rows],
        in_specs=[vmem, vmem, hbm],
        out_specs=[hbm] * 2 + [vmem] * 7,
        scratch_shapes=[
            pltpu.SMEM(flags.shape, jnp.int32),
            pltpu.VMEM((groups - 1,) + rows.shape, F32),
            pltpu.VMEM((groups - 2,) + rows.shape, F32),
            pltpu.VMEM((2 * groups - 1 + 3 * groups - 4, WIDE, WIDE), F32),
            pltpu.SemaphoreType.DMA((2, count)),
            pltpu.SemaphoreType.DMA,
        ],
        compiler_params=params,
        cost_estimate=pl.CostEstimate(
            flops=3 * 2 * 16 * WIDE**3, bytes_accessed=16 * 2**20, transcendentals=0
        ),
    )(matrix, other, flags)

    low_own, high_own, low_seed = lax.optimization_barrier((low_own, high_own, low_seed))
    low_other = lax.ppermute(low_own, half_axis, swap)
    high_other = lax.ppermute(high_own, half_axis, swap)

    ends_out = [
        jax.ShapeDtypeStruct((REACH * BS, WIDE), F32),
        jax.ShapeDtypeStruct((REACH * BS, WIDE), F32),
        jax.ShapeDtypeStruct((2, REACH * BS, WIDE), BF),
        jax.ShapeDtypeStruct((2, 2, REACH * HALF, WIDE), BF),
    ]
    square, sign, high_seed, *ends = pl.pallas_call(
        last_kernel,
        out_shape=[band, band, seed] + ends_out * 2,
        in_specs=[vmem] * 7 + [hbm] * 2,
        out_specs=[hbm] * 2 + [vmem] * 9,
        scratch_shapes=[
            pltpu.VMEM(rows.shape, F32),
            pltpu.VMEM((2, GROUP * HALF, WIDE), F32),
            pltpu.SemaphoreType.DMA((2, count)),
        ],
        input_output_aliases={7: 0, 8: 1},
        compiler_params=params,
        cost_estimate=pl.CostEstimate(
            flops=3 * 2 * 4 * WIDE**3, bytes_accessed=4 * 2**20, transcendentals=0
        ),
    )(matrix, lines, full, mine, keep, square_left, sign_left, square, sign)

    return tuple(
        pl.pallas_call(
            functools.partial(border_kernel, half_axis=half_axis),
            out_shape=(band, band),
            in_specs=[vmem] * 15 + [hbm] * 2,
            out_specs=[hbm] * 2,
            scratch_shapes=[
                pltpu.VMEM((2, 2, WIDE, 2 * WIDE), BF),
                pltpu.VMEM((2, 2, REACH * BS, WIDE), F32),
                pltpu.VMEM((2, 2, REACH * HALF, WIDE), F32),
                pltpu.VMEM((2, 2, REACH, SPAN, HALF, BS), F32),
                pltpu.SemaphoreType.DMA((2, 2, REACH)),
            ],
            input_output_aliases={15: 0, 16: 1},
            compiler_params=params,
            cost_estimate=pl.CostEstimate(
                flops=3 * 2 * 4 * WIDE**3, bytes_accessed=2 * 2**20, transcendentals=0
            ),
        )(
            low_own, low_other, high_own, high_other, lines, low_seed, *ends[:4], high_seed,
            *ends[4:], square, sign,
        )
    )


def solution(mesh):
    band = P(("group", "row", "col"), None, "rep", None)
    return jax.shard_map(
        functools.partial(shards, axes=("row", "col"), half_axis="rep"),
        mesh=mesh,
        in_specs=(band, P("group", None)),
        out_specs=(band, band),
        check_vma=False,
    )
```

```python
import functools

import jax
import jax.numpy as jnp
from jax import lax
from jax.experimental import pallas as pl
from jax.experimental.pallas import tpu as pltpu
from jax.sharding import PartitionSpec as P

REACH = 3
SPAN = 7
BS = 64
HALF = 32
GROUP = 4
WIDE = GROUP * BS
BF = jnp.bfloat16
F32 = jnp.float32
LIMIT = 32 * 1024 * 1024


def split(x):
    hi = x.astype(BF)
    return hi, (x - hi.astype(F32)).astype(BF)


def product(pairs, transposed=False):
    side = 1 if transposed else 0
    left = [x for a, _ in pairs for x in (a[0], a[0], a[1])]
    right = [x for _, b in pairs for x in (b[0], b[1], b[0])]
    return lax.dot_general(
        jnp.concatenate(left, axis=1),
        jnp.concatenate(right, axis=side),
        (((1,), (side,)), ((), ())),
        preferred_element_type=F32,
    )


def turn(x):
    return split((x[0].astype(F32) + x[1].astype(F32)).T)


def write_lines(pat, lines, first, groups):
    total = pat.shape[1]
    lane = lax.broadcasted_iota(jnp.int32, (1, 2 * BS), 1)
    for g in range(-1, groups + 1):
        for s in range(GROUP):
            row = lax.rem(first + g * GROUP + s + total, total)
            for t in range(3 * GROUP // 2):
                ks = [2 * t + e - s - 1 for e in range(2)]
                f = [pat[k, row].astype(F32) if 0 <= k < SPAN else F32(0) for k in ks]
                at = (g + 1) * GROUP + s
                lines[at : at + 1, t * 2 * BS : (t + 1) * 2 * BS] = jnp.where(lane < BS, f[0], f[1])


def line_of(lines, g, s, h):
    at = (g + 1) * GROUP + s
    lo = (h - g + 1) * WIDE
    return lines[at : at + 1, lo : lo + WIDE]


def span_of(a, count, is_square):
    if a < REACH:
        return (REACH - a if is_square else 2 * REACH - a), SPAN
    s = a - (count - REACH)
    if s >= 0:
        return 0, (2 * REACH - s if is_square else REACH - s)
    return 0, SPAN


def edge_kernel(top, bottom, to_left, to_right):
    for source, target in ((top, to_left), (bottom, to_right)):
        for s in range(REACH):
            for t in range(2):
                target[s * HALF : (s + 1) * HALF, t * 2 * BS : (t + 1) * 2 * BS] = jnp.concatenate(
                    [source[s, 2 * t], source[s, 2 * t + 1]], axis=1
                )


class Interior:
    def __init__(self, own, lines, full, mine, keep):
        self.own = own
        self.lines = lines
        self.full = full
        self.mine = mine
        self.keep = keep
        self.count = own.shape[0]
        self.groups = self.count // GROUP
        self.stores = []

    def part(self, g, h, rows=slice(None)):
        at = (h - g + 1) * WIDE
        return [self.full[p, g, rows, at : at + WIDE] for p in range(2)]

    def my_part(self, g, h):
        at = (h - g + 1) * WIDE
        return [self.mine[p, g, :, at : at + WIDE] for p in range(2)]

    def tile(self, g, h):
        return 3 * g + h - g + 1

    def kept(self, g, h):
        return [self.keep[p, self.tile(g, h)] for p in range(2)]

    def near(self, g):
        return [e for e in (g - 1, g, g + 1) if 0 <= e < self.groups]

    def second(self, g, h, sign, seed, result):
        span = range(1 if h > g else 0, GROUP - 1 if h < g else GROUP)
        rows = slice(span[0] * HALF, (span[-1] + 1) * HALF)

        def dot():
            return product(
                [
                    ([x[rows] for x in self.my_part(g, e)], self.kept(e, h))
                    for e in self.near(g)
                    if abs(e - h) <= 1
                ]
            )

        def store(value):
            result[rows] = value

        def post():
            for s in span:
                a = g * GROUP + s
                k0, k1 = span_of(a, self.count, False)
                part = result[s * HALF : (s + 1) * HALF] * (line_of(self.lines, g, s, h) * 0.5)
                for t in range(GROUP):
                    k = t + GROUP * (h - g) - s + REACH
                    if 0 <= k < SPAN:
                        block = 1.5 * self.own[a, k] - part[:, t * BS : (t + 1) * BS]
                        if k0 <= k < k1:
                            sign[s, k] = block
                        else:
                            seed[a if a < REACH else a - (self.count - REACH), k] = block

        return dot, store, post

    def far_seed(self, g, seed):
        for s in range(REACH):
            a = s if g == 0 else self.count - REACH + s
            for k in range(0, REACH - s) if g == 0 else range(2 * REACH - s, SPAN):
                seed[s, k] = 1.5 * self.own[a, k]

    def send(self, g, i, source, target, sems):
        for s in range(GROUP):
            a = g * GROUP + s
            k0, k1 = span_of(a, self.count, i == 0)
            store = pltpu.make_async_copy(
                source.at[s, pl.ds(k0, k1 - k0)], target.at[a, pl.ds(k0, k1 - k0)], sems.at[i, a]
            )
            store.start()
            self.stores.append(store)

    def finish(self):
        for store in self.stores:
            store.wait()


def count_dots(steps):
    return sum(isinstance(step, tuple) for step in steps)


def staggered(steps):
    pending = []
    for step in steps:
        if not isinstance(step, tuple):
            pending.append(step)
            continue
        dot, store, post = step
        value = dot()
        for work in pending:
            work()
        store(value)
        pending = [post]
    for work in pending:
        work()


def first_kernel(
    own, other, pattern, square_out, sign_out, seed, full, mine, keep, lines, sign_left,
    pat, square, sign, results, sems, pat_sem, *, axes, half_axis
):
    load = pltpu.make_async_copy(pattern, pat, pat_sem)
    load.start()
    it = Interior(own, lines, full, mine, keep)
    groups = it.groups
    upper_half = lax.axis_index(half_axis) == 1

    def build(g):
        for s in range(GROUP):
            a = g * GROUP + s
            for t in range(3 * GROUP // 2):
                ks = [2 * t + e - s - 1 for e in range(2)]
                lanes = slice(t * 2 * BS, (t + 1) * 2 * BS)
                rows = slice(s * BS, (s + 1) * BS)
                mine_rows = slice(s * HALF, (s + 1) * HALF)
                if all(k < 0 or k >= SPAN for k in ks):
                    for p in range(2):
                        full[p, g, rows, lanes] = jnp.zeros((BS, 2 * BS), BF)
                        mine[p, g, mine_rows, lanes] = jnp.zeros((HALF, 2 * BS), BF)
                    continue
                two = [
                    jnp.concatenate(
                        [src[a, k] if 0 <= k < SPAN else jnp.zeros((HALF, BS), F32) for k in ks],
                        axis=1,
                    )
                    for src in (own, other)
                ]
                for p, (x, y) in enumerate(zip(*[split(x) for x in two])):
                    mine[p, g, mine_rows, lanes] = x
                    full[p, g, rows, lanes] = jnp.concatenate(
                        [jnp.where(upper_half, y, x), jnp.where(upper_half, x, y)], axis=0
                    )

    def squares(g, h, result):
        pairs = []
        for e in (g - 1, g, g + 1):
            if abs(e - h) <= 1:
                inside = 0 <= e < groups
                pairs.append((e, (lambda e=e: it.part(e, h)) if inside else (lambda e=e: turn(it.part(h, e)))))
        span = range(1 if h > g else 0, GROUP)
        rows = slice(span[0] * BS, WIDE)

        def dot():
            return product([([x[rows] for x in it.part(g, e)], f()) for e, f in pairs])

        def store(value):
            result[rows] = value

        def post():
            masked = [jnp.zeros((BS, WIDE), F32)] * GROUP
            for s in span:
                masked[s] = result[s * BS : (s + 1) * BS] * line_of(lines, g, s, h)
            for s in range(GROUP):
                for p, x in enumerate(split(masked[s])):
                    keep[p, it.tile(g, h), s * BS : (s + 1) * BS] = x
            for s in span:
                part = jnp.where(upper_half, masked[s][HALF:], masked[s][:HALF])
                for t in range(GROUP):
                    k = t + GROUP * (h - g) - s + REACH
                    if 0 <= k < SPAN:
                        staged[g][s, k] = part[:, t * BS : (t + 1) * BS]
            if h == g:
                return
            for c in range(0, GROUP, 2):
                turned = jnp.concatenate(masked[c : c + 2], axis=0).T
                lanes = slice(c * BS, (c + 2) * BS)
                for p, x in enumerate(split(turned)):
                    keep[p, it.tile(h, g), :, lanes] = x
                for t in range(GROUP):
                    rows = turned[t * BS : (t + 1) * BS]
                    part = jnp.where(upper_half, rows[HALF:], rows[:HALF])
                    for s in range(c, c + 2):
                        k = s + GROUP * (g - h) - t + REACH
                        if 0 <= k < SPAN:
                            staged[h][t, k] = part[:, (s - c) * BS : (s - c + 1) * BS]

        return dot, store, post

    staged = [square.at[g] for g in range(groups)]
    signs = [sign.at[g] for g in range(groups - 2)] + [sign_left]

    def begin():
        load.wait()
        write_lines(pat, lines, lax.axis_index(axes) * it.count, groups)
        it.far_seed(0, seed)

    build(0)
    build(1)
    steps = [begin]
    for g in range(groups):
        if g + 1 < groups:
            steps.append(squares(g, g + 1, results.at[count_dots(steps)]))
            if g + 2 < groups:
                steps.append(functools.partial(build, g + 2))
        steps.append(squares(g, g, results.at[count_dots(steps)]))
        steps.append(functools.partial(it.send, g, 0, staged[g], square_out, sems))
        if g > 0:
            for h in it.near(g - 1):
                steps.append(it.second(g - 1, h, signs[g - 1], seed, results.at[count_dots(steps)]))
            if g < groups - 1:
                steps.append(functools.partial(it.send, g - 1, 1, signs[g - 1], sign_out, sems))
    staggered(steps)
    it.finish()


def last_kernel(
    own, lines, full, mine, keep, sign_left, sign_in, sign_out, sign, seed, low_a, low_b, low_m, low_p, high_a, high_b, high_m, high_p, results, sems
):
    it = Interior(own, lines, full, mine, keep)
    last = it.groups - 1
    it.send(last - 1, 1, sign_left, sign_out, sems)
    steps = [it.second(last, h, sign, seed, results.at[i]) for i, h in enumerate(it.near(last))]
    steps.append(functools.partial(it.far_seed, last, seed))

    def reaching(a_ref, b_ref, m_ref, p_ref, g, e, r0):
        rows = slice(r0, r0 + REACH * BS)
        mine_rows = slice(r0 // 2, r0 // 2 + REACH * HALF)
        outer = slice(BS - r0, BS - r0 + REACH * BS)

        def dot():
            out = it.part(g, e)
            return (
                product([([x[outer] for x in turn(out)], out)]),
                product([(it.part(g, g, rows), out)]),
            )

        def store(value):
            a_ref[...], b_ref[...] = value

        def post():
            for p in range(2):
                m_ref[p] = it.part(g, e)[p][rows]
                p_ref[p, 0] = it.my_part(g, e)[p][mine_rows]
                p_ref[p, 1] = it.my_part(g, g)[p][mine_rows]

        return dot, store, post

    steps.append(reaching(low_a, low_b, low_m, low_p, 0, -1, 0))
    steps.append(reaching(high_a, high_b, high_m, high_p, last, last + 1, BS))
    staggered(steps)
    it.finish()


def border_kernel(
    low_own, low_other, high_own, high_other, lines, sign_last, low_seed, low_a, low_b, low_m, low_p, high_seed,
    high_a, high_b, high_m, high_p, square_in, sign_in, square_out, sign_out, halo, first, last, blocks, sems, last_sems,
    *, half_axis
):
    count = square_in.shape[0]
    groups = count // GROUP
    upper_half = lax.axis_index(half_axis) == 1
    ends = (0, count - REACH)
    given = (
        (low_own, low_other, low_seed, low_a, low_b, low_m, low_p),
        (high_own, high_other, high_seed, high_a, high_b, high_m, high_p),
    )
    shift = (1, 0)
    zero = jnp.zeros((BS, WIDE), F32)

    def build(side):
        mine, theirs = given[side][:2]
        below = REACH if side == 0 else 0
        whole_rows = []
        for p in range(REACH):
            rows = slice(p * HALF, (p + 1) * HALF)
            whole_rows.append(
                jnp.concatenate(
                    [
                        jnp.where(upper_half, theirs[rows, :], mine[rows, :]),
                        jnp.where(upper_half, mine[rows, :], theirs[rows, :]),
                    ],
                    axis=0,
                )
            )

        def block(p, c):
            k = c - p + below
            if 0 <= k <= REACH:
                return whole_rows[p][:, k * BS : (k + 1) * BS]
            k = p - c + below
            if 0 <= c < REACH and 0 <= k <= REACH:
                return whole_rows[c][:, k * BS : (k + 1) * BS].T
            return jnp.zeros((BS, BS), F32)

        base = -5 if side == 0 else 0
        for p in range(REACH):
            rows = slice((p + shift[side]) * BS, (p + shift[side] + 1) * BS)
            for t in range(4):
                value = jnp.concatenate([block(p, base + 2 * t), block(p, base + 2 * t + 1)], axis=1)
                for q, x in enumerate(split(value)):
                    halo[side, q, rows, t * 2 * BS : (t + 1) * 2 * BS] = x
        rows = slice(0, BS) if side == 0 else slice(REACH * BS, WIDE)
        for q in range(2):
            halo[side, q, rows, :] = jnp.zeros((BS, 2 * WIDE), BF)

    edge_groups, outer_groups = (0, groups - 1), (-1, groups)
    offsets = (0, 2 * REACH)
    corners = [None, None]
    across = [None, None]
    stores = []

    def dots(side):
        m_ref = given[side][5]
        whole = [halo[side, q] for q in range(2)]
        outer_rows = slice(shift[side] * BS, (shift[side] + REACH) * BS)
        inner = slice(WIDE, 2 * WIDE) if side == 0 else slice(0, WIDE)
        return (
            product([([x[outer_rows] for x in whole], whole)], True),
            product([([m_ref[q] for q in range(2)], [x[:, inner] for x in whole])], True),
        )

    def keep_first(side, value):
        _, _, _, a_ref, b_ref, _, _ = given[side]
        first[side, 0] = value[0] + a_ref[...]
        first[side, 1] = value[1] + b_ref[...]

    def masks(side):
        at = shift[side]
        edge_group, outer_group = edge_groups[side], outer_groups[side]
        pad = (lambda rows: [zero] + rows, lambda rows: rows + [zero])
        rows = [
            first[side, 0, p * BS : (p + 1) * BS] * line_of(lines, outer_group, p + at, outer_group)
            for p in range(REACH)
        ]
        corners[side] = split(jnp.concatenate(pad[side](rows), axis=0))
        rows = [
            first[side, 1, s * BS : (s + 1) * BS]
            * line_of(lines, edge_group, s + 1 - at, outer_group)
            for s in range(REACH)
        ]
        across[side] = split(jnp.concatenate(pad[1 - side](rows), axis=0))
        for s in range(REACH):
            part = jnp.where(upper_half, rows[s][HALF:], rows[s][:HALF])
            for t in range(REACH):
                k = t - s + offsets[side]
                if 0 <= k < SPAN:
                    blocks[0, side, s, k] = part[:, (t + at) * BS : (t + at + 1) * BS]
        send(side, 0, square_out)

    def send(side, i, ref):
        for s in range(REACH):
            a = ends[side] + s
            k0, k1 = span_of(a, count, i == 0)
            k0, k1 = (0, k0) if side == 0 else (k1, SPAN)
            store = pltpu.make_async_copy(
                blocks.at[i, side, s, pl.ds(k0, k1 - k0)],
                ref.at[a, pl.ds(k0, k1 - k0)],
                sems.at[i, side, s],
            )
            store.start()
            stores.append(store)

    def second_dots(side):
        p_ref = given[side][6]
        reach_out = [p_ref[q, 0] for q in range(2)]
        inside = [p_ref[q, 1] for q in range(2)]
        return (
            product([(reach_out, corners[side]), (inside, across[side])]),
            product([(reach_out, across[side])], True),
        )

    def keep_last(side, value):
        last[side, 0], last[side, 1] = value

    def emit(side):
        seed = given[side][2]
        at = shift[side]
        edge_group, outer_group = edge_groups[side], outer_groups[side]
        for s in range(REACH):
            rows = slice(s * HALF, (s + 1) * HALF)
            far = last[side, 0, rows] * (line_of(lines, edge_group, s + 1 - at, outer_group) * 0.5)
            close = last[side, 1, rows] * (line_of(lines, edge_group, s + 1 - at, edge_group) * 0.5)
            for t in range(REACH):
                k = t - s + offsets[side]
                if 0 <= k < SPAN:
                    lanes = slice((t + at) * BS, (t + at + 1) * BS)
                    blocks[1, side, s, k] = seed[s, k] - far[:, lanes]
                k = t - s + REACH
                lanes = slice((t + 1 - at) * BS, (t + 2 - at) * BS)
                blocks[1, side, s, k] = seed[s, k] - close[:, lanes]
        send(side, 1, sign_out)

    for s in range(GROUP):
        a = count - GROUP + s
        k0, k1 = span_of(a, count, False)
        store = pltpu.make_async_copy(
            sign_last.at[s, pl.ds(k0, k1 - k0)], sign_out.at[a, pl.ds(k0, k1 - k0)], last_sems.at[s]
        )
        store.start()
        stores.append(store)
    build(0)
    value = dots(0)
    build(1)
    keep_first(0, value)
    value = dots(1)
    masks(0)
    keep_first(1, value)
    value = second_dots(0)
    masks(1)
    keep_last(0, value)
    value = second_dots(1)
    emit(0)
    keep_last(1, value)
    emit(1)
    for store in stores:
        store.wait()


def shards(matrix, pattern, *, axes, half_axis):
    count = matrix.shape[0]
    groups = count // GROUP
    flags = pattern.T
    vmem = pl.BlockSpec(memory_space=pltpu.VMEM)
    hbm = pl.BlockSpec(memory_space=pl.ANY)
    params = pltpu.CompilerParams(vmem_limit_bytes=LIMIT)

    top, bottom = matrix[:REACH, REACH:], matrix[count - REACH :, : REACH + 1]
    matrix, top, bottom = lax.optimization_barrier((matrix, top, bottom))
    edge = jax.ShapeDtypeStruct((REACH * HALF, (REACH + 1) * BS), F32)
    to_left, to_right = pl.pallas_call(
        edge_kernel,
        out_shape=(edge, edge),
        in_specs=[vmem] * 2,
        out_specs=[vmem] * 2,
        compiler_params=params,
        cost_estimate=pl.CostEstimate(
            flops=1 * 10**9, bytes_accessed=2**20, transcendentals=0
        ),
    )(top, bottom)
    size = 1
    for axis in axes:
        size *= lax.axis_size(axis)
    swap = [(0, 1), (1, 0)]
    other = lax.ppermute(matrix, half_axis, swap)
    forward = [(i, (i + 1) % size) for i in range(size)]
    backward = [(target, source) for source, target in forward]
    high_own = lax.ppermute(to_left, axes, backward)
    low_own = lax.ppermute(to_right, axes, forward)

    band = jax.ShapeDtypeStruct(matrix.shape, F32)
    seed = jax.ShapeDtypeStruct((REACH, SPAN, HALF, BS), F32)
    full = jax.ShapeDtypeStruct((2, groups, WIDE, 3 * WIDE), BF)
    mine = jax.ShapeDtypeStruct((2, groups, GROUP * HALF, 3 * WIDE), BF)
    keep = jax.ShapeDtypeStruct((2, 3 * groups, WIDE, WIDE), BF)
    lines = jax.ShapeDtypeStruct(((groups + 2) * GROUP, 3 * WIDE), F32)
    rows = jax.ShapeDtypeStruct((GROUP,) + matrix.shape[1:], F32)
    square, sign, low_seed, full, mine, keep, lines, sign_left = pl.pallas_call(
        functools.partial(first_kernel, axes=axes, half_axis=half_axis),
        out_shape=[band, band, seed, full, mine, keep, lines, rows],
        in_specs=[vmem, vmem, hbm],
        out_specs=[hbm] * 2 + [vmem] * 6,
        scratch_shapes=[
            pltpu.SMEM(flags.shape, jnp.int32),
            pltpu.VMEM((groups,) + rows.shape, F32),
            pltpu.VMEM((groups - 2,) + rows.shape, F32),
            pltpu.VMEM((2 * groups - 1 + 3 * groups - 4, WIDE, WIDE), F32),
            pltpu.SemaphoreType.DMA((2, count)),
            pltpu.SemaphoreType.DMA,
        ],
        compiler_params=params,
        cost_estimate=pl.CostEstimate(
            flops=3 * 2 * 16 * WIDE**3, bytes_accessed=16 * 2**20, transcendentals=0
        ),
    )(matrix, other, flags)

    low_own, high_own, low_seed = lax.optimization_barrier((low_own, high_own, low_seed))
    low_other = lax.ppermute(low_own, half_axis, swap)
    high_other = lax.ppermute(high_own, half_axis, swap)

    ends_out = [
        jax.ShapeDtypeStruct((REACH * BS, WIDE), F32),
        jax.ShapeDtypeStruct((REACH * BS, WIDE), F32),
        jax.ShapeDtypeStruct((2, REACH * BS, WIDE), BF),
        jax.ShapeDtypeStruct((2, 2, REACH * HALF, WIDE), BF),
    ]
    sign, sign_last, high_seed, *ends = pl.pallas_call(
        last_kernel,
        out_shape=[band, rows, seed] + ends_out * 2,
        in_specs=[vmem] * 6 + [hbm],
        out_specs=[hbm] + [vmem] * 10,
        scratch_shapes=[
            pltpu.VMEM((2, GROUP * HALF, WIDE), F32),
            pltpu.SemaphoreType.DMA((2, count)),
        ],
        input_output_aliases={6: 0},
        compiler_params=params,
        cost_estimate=pl.CostEstimate(
            flops=3 * 2 * 4 * WIDE**3, bytes_accessed=4 * 2**20, transcendentals=0
        ),
    )(matrix, lines, full, mine, keep, sign_left, sign)

    return tuple(
        pl.pallas_call(
            functools.partial(border_kernel, half_axis=half_axis),
            out_shape=(band, band),
            in_specs=[vmem] * 16 + [hbm] * 2,
            out_specs=[hbm] * 2,
            scratch_shapes=[
                pltpu.VMEM((2, 2, WIDE, 2 * WIDE), BF),
                pltpu.VMEM((2, 2, REACH * BS, WIDE), F32),
                pltpu.VMEM((2, 2, REACH * HALF, WIDE), F32),
                pltpu.VMEM((2, 2, REACH, SPAN, HALF, BS), F32),
                pltpu.SemaphoreType.DMA((2, 2, REACH)),
                pltpu.SemaphoreType.DMA((GROUP,)),
            ],
            input_output_aliases={16: 0, 17: 1},
            compiler_params=params,
            cost_estimate=pl.CostEstimate(
                flops=3 * 2 * 4 * WIDE**3, bytes_accessed=2 * 2**20, transcendentals=0
            ),
        )(
            low_own, low_other, high_own, high_other, lines, sign_last, low_seed, *ends[:4], high_seed,
            *ends[4:], square, sign,
        )
    )


def solution(mesh):
    band = P(("group", "row", "col"), None, "rep", None)
    return jax.shard_map(
        functools.partial(shards, axes=("row", "col"), half_axis="rep"),
        mesh=mesh,
        in_specs=(band, P("group", None)),
        out_specs=(band, band),
        check_vma=False,
    )
```

```python
import functools

import jax
import jax.numpy as jnp
from jax import lax
from jax.experimental import pallas as pl
from jax.experimental.pallas import tpu as pltpu
from jax.sharding import PartitionSpec as P

REACH = 3
SPAN = 7
BS = 64
HALF = 32
GROUP = 4
WIDE = GROUP * BS
BF = jnp.bfloat16
F32 = jnp.float32
LIMIT = 32 * 1024 * 1024


def split(x):
    hi = x.astype(BF)
    return hi, (x - hi.astype(F32)).astype(BF)


def product(pairs, transposed=False):
    side = 1 if transposed else 0
    high, low = [jnp.concatenate([a[p] for a, _ in pairs], axis=1) for p in range(2)]
    right = [jnp.concatenate([b[p] for _, b in pairs], axis=side) for p in range(2)]
    dot = functools.partial(
        lax.dot_general,
        dimension_numbers=(((1,), (side,)), ((), ())),
        preferred_element_type=F32,
    )
    both = dot(jnp.concatenate([high, low], axis=0), right[0])
    count = high.shape[0]
    return both[:count] + (both[count:] + dot(high, right[1]))


def turn(x):
    return split((x[0].astype(F32) + x[1].astype(F32)).T)


def write_lines(pat, lines, first, groups):
    total = pat.shape[1]
    lane = lax.broadcasted_iota(jnp.int32, (1, 2 * BS), 1)
    for g in range(-1, groups + 1):
        for s in range(GROUP):
            row = lax.rem(first + g * GROUP + s + total, total)
            for t in range(3 * GROUP // 2):
                ks = [2 * t + e - s - 1 for e in range(2)]
                f = [pat[k, row].astype(F32) if 0 <= k < SPAN else F32(0) for k in ks]
                at = (g + 1) * GROUP + s
                lines[at : at + 1, t * 2 * BS : (t + 1) * 2 * BS] = jnp.where(lane < BS, f[0], f[1])


def line_of(lines, g, s, h):
    at = (g + 1) * GROUP + s
    lo = (h - g + 1) * WIDE
    return lines[at : at + 1, lo : lo + WIDE]


def span_of(a, count, is_square):
    if a < REACH:
        return (REACH - a if is_square else 2 * REACH - a), SPAN
    s = a - (count - REACH)
    if s >= 0:
        return 0, (2 * REACH - s if is_square else REACH - s)
    return 0, SPAN


def edge_kernel(top, bottom, to_left, to_right):
    for source, target in ((top, to_left), (bottom, to_right)):
        for s in range(REACH):
            for t in range(2):
                target[s * HALF : (s + 1) * HALF, t * 2 * BS : (t + 1) * 2 * BS] = jnp.concatenate(
                    [source[s, 2 * t], source[s, 2 * t + 1]], axis=1
                )


class Interior:
    def __init__(self, own, lines, full, mine, keep):
        self.own = own
        self.lines = lines
        self.full = full
        self.mine = mine
        self.keep = keep
        self.count = own.shape[0]
        self.groups = self.count // GROUP
        self.stores = []

    def part(self, g, h, rows=slice(None)):
        at = (h - g + 1) * WIDE
        return [self.full[p, g, rows, at : at + WIDE] for p in range(2)]

    def my_part(self, g, h):
        at = (h - g + 1) * WIDE
        return [self.mine[p, g, :, at : at + WIDE] for p in range(2)]

    def tile(self, g, h):
        return 3 * g + h - g + 1

    def kept(self, g, h):
        return [self.keep[p, self.tile(g, h)] for p in range(2)]

    def near(self, g):
        return [e for e in (g - 1, g, g + 1) if 0 <= e < self.groups]

    def second(self, g, h, sign, seed, result):
        span = range(1 if h > g else 0, GROUP - 1 if h < g else GROUP)
        rows = slice(span[0] * HALF, (span[-1] + 1) * HALF)

        def dot():
            return product(
                [
                    ([x[rows] for x in self.my_part(g, e)], self.kept(e, h))
                    for e in self.near(g)
                    if abs(e - h) <= 1
                ]
            )

        def store(value):
            result[rows] = value

        def post():
            for s in span:
                a = g * GROUP + s
                k0, k1 = span_of(a, self.count, False)
                part = result[s * HALF : (s + 1) * HALF] * (line_of(self.lines, g, s, h) * 0.5)
                for t in range(GROUP):
                    k = t + GROUP * (h - g) - s + REACH
                    if 0 <= k < SPAN:
                        block = 1.5 * self.own[a, k] - part[:, t * BS : (t + 1) * BS]
                        if k0 <= k < k1:
                            sign[s, k] = block
                        else:
                            seed[a if a < REACH else a - (self.count - REACH), k] = block

        return dot, store, post

    def far_seed(self, g, seed):
        for s in range(REACH):
            a = s if g == 0 else self.count - REACH + s
            for k in range(0, REACH - s) if g == 0 else range(2 * REACH - s, SPAN):
                seed[s, k] = 1.5 * self.own[a, k]

    def send(self, g, i, source, target, sems):
        for s in range(GROUP):
            a = g * GROUP + s
            k0, k1 = span_of(a, self.count, i == 0)
            store = pltpu.make_async_copy(
                source.at[s, pl.ds(k0, k1 - k0)], target.at[a, pl.ds(k0, k1 - k0)], sems.at[i, a]
            )
            store.start()
            self.stores.append(store)

    def finish(self):
        for store in self.stores:
            store.wait()


def count_dots(steps):
    return sum(isinstance(step, tuple) for step in steps)


def staggered(steps):
    pending = []
    for step in steps:
        if not isinstance(step, tuple):
            pending.append(step)
            continue
        dot, store, post = step
        value = dot()
        for work in pending:
            work()
        store(value)
        pending = [post]
    for work in pending:
        work()


def first_kernel(
    own, other, pattern, square_out, sign_out, seed, full, mine, keep, lines, sign_left,
    pat, square, sign, results, sems, pat_sem, *, axes, half_axis
):
    load = pltpu.make_async_copy(pattern, pat, pat_sem)
    load.start()
    it = Interior(own, lines, full, mine, keep)
    groups = it.groups
    upper_half = lax.axis_index(half_axis) == 1

    def build(g):
        for s in range(GROUP):
            a = g * GROUP + s
            for t in range(3 * GROUP // 2):
                ks = [2 * t + e - s - 1 for e in range(2)]
                lanes = slice(t * 2 * BS, (t + 1) * 2 * BS)
                rows = slice(s * BS, (s + 1) * BS)
                mine_rows = slice(s * HALF, (s + 1) * HALF)
                if all(k < 0 or k >= SPAN for k in ks):
                    for p in range(2):
                        full[p, g, rows, lanes] = jnp.zeros((BS, 2 * BS), BF)
                        mine[p, g, mine_rows, lanes] = jnp.zeros((HALF, 2 * BS), BF)
                    continue
                two = [
                    jnp.concatenate(
                        [src[a, k] if 0 <= k < SPAN else jnp.zeros((HALF, BS), F32) for k in ks],
                        axis=1,
                    )
                    for src in (own, other)
                ]
                for p, (x, y) in enumerate(zip(*[split(x) for x in two])):
                    mine[p, g, mine_rows, lanes] = x
                    full[p, g, rows, lanes] = jnp.concatenate(
                        [jnp.where(upper_half, y, x), jnp.where(upper_half, x, y)], axis=0
                    )

    def squares(g, h, result):
        pairs = []
        for e in (g - 1, g, g + 1):
            if abs(e - h) <= 1:
                inside = 0 <= e < groups
                pairs.append((e, (lambda e=e: it.part(e, h)) if inside else (lambda e=e: turn(it.part(h, e)))))
        span = range(1 if h > g else 0, GROUP)
        rows = slice(span[0] * BS, WIDE)

        def dot():
            return product([([x[rows] for x in it.part(g, e)], f()) for e, f in pairs])

        def store(value):
            result[rows] = value

        def post():
            masked = [jnp.zeros((BS, WIDE), F32)] * GROUP
            for s in span:
                masked[s] = result[s * BS : (s + 1) * BS] * line_of(lines, g, s, h)
            for s in range(GROUP):
                for p, x in enumerate(split(masked[s])):
                    keep[p, it.tile(g, h), s * BS : (s + 1) * BS] = x
            for s in span:
                part = jnp.where(upper_half, masked[s][HALF:], masked[s][:HALF])
                for t in range(GROUP):
                    k = t + GROUP * (h - g) - s + REACH
                    if 0 <= k < SPAN:
                        staged[g][s, k] = part[:, t * BS : (t + 1) * BS]
            if h == g:
                return
            for c in range(0, GROUP, 2):
                turned = jnp.concatenate(masked[c : c + 2], axis=0).T
                lanes = slice(c * BS, (c + 2) * BS)
                for p, x in enumerate(split(turned)):
                    keep[p, it.tile(h, g), :, lanes] = x
                for t in range(GROUP):
                    rows = turned[t * BS : (t + 1) * BS]
                    part = jnp.where(upper_half, rows[HALF:], rows[:HALF])
                    for s in range(c, c + 2):
                        k = s + GROUP * (g - h) - t + REACH
                        if 0 <= k < SPAN:
                            staged[h][t, k] = part[:, (s - c) * BS : (s - c + 1) * BS]

        return dot, store, post

    staged = [square.at[g] for g in range(groups)]
    signs = [sign.at[g] for g in range(groups - 2)] + [sign_left]

    def begin():
        load.wait()
        write_lines(pat, lines, lax.axis_index(axes) * it.count, groups)
        it.far_seed(0, seed)

    build(0)
    build(1)
    steps = [begin]
    for g in range(groups):
        if g + 1 < groups:
            steps.append(squares(g, g + 1, results.at[count_dots(steps)]))
            if g + 2 < groups:
                steps.append(functools.partial(build, g + 2))
        steps.append(squares(g, g, results.at[count_dots(steps)]))
        steps.append(functools.partial(it.send, g, 0, staged[g], square_out, sems))
        if g > 0:
            for h in it.near(g - 1):
                steps.append(it.second(g - 1, h, signs[g - 1], seed, results.at[count_dots(steps)]))
            if g < groups - 1:
                steps.append(functools.partial(it.send, g - 1, 1, signs[g - 1], sign_out, sems))
    staggered(steps)
    it.finish()


def last_kernel(
    own, lines, full, mine, keep, sign_left, sign_in, sign_out, sign, seed, low_a, low_b, low_m, low_p, high_a, high_b, high_m, high_p, results, sems
):
    it = Interior(own, lines, full, mine, keep)
    last = it.groups - 1
    it.send(last - 1, 1, sign_left, sign_out, sems)
    steps = [it.second(last, h, sign, seed, results.at[i]) for i, h in enumerate(it.near(last))]
    steps.append(functools.partial(it.far_seed, last, seed))

    def reaching(a_ref, b_ref, m_ref, p_ref, g, e, r0):
        rows = slice(r0, r0 + REACH * BS)
        mine_rows = slice(r0 // 2, r0 // 2 + REACH * HALF)
        outer = slice(BS - r0, BS - r0 + REACH * BS)

        def dot():
            out = it.part(g, e)
            return (
                product([([x[outer] for x in turn(out)], out)]),
                product([(it.part(g, g, rows), out)]),
            )

        def store(value):
            a_ref[...], b_ref[...] = value

        def post():
            for p in range(2):
                m_ref[p] = it.part(g, e)[p][rows]
                p_ref[p, 0] = it.my_part(g, e)[p][mine_rows]
                p_ref[p, 1] = it.my_part(g, g)[p][mine_rows]

        return dot, store, post

    steps.append(reaching(low_a, low_b, low_m, low_p, 0, -1, 0))
    steps.append(reaching(high_a, high_b, high_m, high_p, last, last + 1, BS))
    staggered(steps)
    it.finish()


def border_kernel(
    low_own, low_other, high_own, high_other, lines, sign_last, low_seed, low_a, low_b, low_m, low_p, high_seed,
    high_a, high_b, high_m, high_p, square_in, sign_in, square_out, sign_out, halo, first, last, blocks, sems, last_sems,
    *, half_axis
):
    count = square_in.shape[0]
    groups = count // GROUP
    upper_half = lax.axis_index(half_axis) == 1
    ends = (0, count - REACH)
    given = (
        (low_own, low_other, low_seed, low_a, low_b, low_m, low_p),
        (high_own, high_other, high_seed, high_a, high_b, high_m, high_p),
    )
    shift = (1, 0)
    zero = jnp.zeros((BS, WIDE), F32)

    def build(side):
        mine, theirs = given[side][:2]
        below = REACH if side == 0 else 0
        whole_rows = []
        for p in range(REACH):
            rows = slice(p * HALF, (p + 1) * HALF)
            whole_rows.append(
                jnp.concatenate(
                    [
                        jnp.where(upper_half, theirs[rows, :], mine[rows, :]),
                        jnp.where(upper_half, mine[rows, :], theirs[rows, :]),
                    ],
                    axis=0,
                )
            )

        def block(p, c):
            k = c - p + below
            if 0 <= k <= REACH:
                return whole_rows[p][:, k * BS : (k + 1) * BS]
            k = p - c + below
            if 0 <= c < REACH and 0 <= k <= REACH:
                return whole_rows[c][:, k * BS : (k + 1) * BS].T
            return jnp.zeros((BS, BS), F32)

        base = -5 if side == 0 else 0
        for p in range(REACH):
            rows = slice((p + shift[side]) * BS, (p + shift[side] + 1) * BS)
            for t in range(4):
                value = jnp.concatenate([block(p, base + 2 * t), block(p, base + 2 * t + 1)], axis=1)
                for q, x in enumerate(split(value)):
                    halo[side, q, rows, t * 2 * BS : (t + 1) * 2 * BS] = x
        rows = slice(0, BS) if side == 0 else slice(REACH * BS, WIDE)
        for q in range(2):
            halo[side, q, rows, :] = jnp.zeros((BS, 2 * WIDE), BF)

    edge_groups, outer_groups = (0, groups - 1), (-1, groups)
    offsets = (0, 2 * REACH)
    corners = [None, None]
    across = [None, None]
    stores = []

    def dots(side):
        m_ref = given[side][5]
        whole = [halo[side, q] for q in range(2)]
        outer_rows = slice(shift[side] * BS, (shift[side] + REACH) * BS)
        inner = slice(WIDE, 2 * WIDE) if side == 0 else slice(0, WIDE)
        return (
            product([([x[outer_rows] for x in whole], whole)], True),
            product([([m_ref[q] for q in range(2)], [x[:, inner] for x in whole])], True),
        )

    def keep_first(side, value):
        _, _, _, a_ref, b_ref, _, _ = given[side]
        first[side, 0] = value[0] + a_ref[...]
        first[side, 1] = value[1] + b_ref[...]

    def masks(side):
        at = shift[side]
        edge_group, outer_group = edge_groups[side], outer_groups[side]
        pad = (lambda rows: [zero] + rows, lambda rows: rows + [zero])
        rows = [
            first[side, 0, p * BS : (p + 1) * BS] * line_of(lines, outer_group, p + at, outer_group)
            for p in range(REACH)
        ]
        corners[side] = split(jnp.concatenate(pad[side](rows), axis=0))
        rows = [
            first[side, 1, s * BS : (s + 1) * BS]
            * line_of(lines, edge_group, s + 1 - at, outer_group)
            for s in range(REACH)
        ]
        across[side] = split(jnp.concatenate(pad[1 - side](rows), axis=0))
        for s in range(REACH):
            part = jnp.where(upper_half, rows[s][HALF:], rows[s][:HALF])
            for t in range(REACH):
                k = t - s + offsets[side]
                if 0 <= k < SPAN:
                    blocks[0, side, s, k] = part[:, (t + at) * BS : (t + at + 1) * BS]
        send(side, 0, square_out)

    def send(side, i, ref):
        for s in range(REACH):
            a = ends[side] + s
            k0, k1 = span_of(a, count, i == 0)
            k0, k1 = (0, k0) if side == 0 else (k1, SPAN)
            store = pltpu.make_async_copy(
                blocks.at[i, side, s, pl.ds(k0, k1 - k0)],
                ref.at[a, pl.ds(k0, k1 - k0)],
                sems.at[i, side, s],
            )
            store.start()
            stores.append(store)

    def second_dots(side):
        p_ref = given[side][6]
        reach_out = [p_ref[q, 0] for q in range(2)]
        inside = [p_ref[q, 1] for q in range(2)]
        return (
            product([(reach_out, corners[side]), (inside, across[side])]),
            product([(reach_out, across[side])], True),
        )

    def keep_last(side, value):
        last[side, 0], last[side, 1] = value

    def emit(side):
        seed = given[side][2]
        at = shift[side]
        edge_group, outer_group = edge_groups[side], outer_groups[side]
        for s in range(REACH):
            rows = slice(s * HALF, (s + 1) * HALF)
            far = last[side, 0, rows] * (line_of(lines, edge_group, s + 1 - at, outer_group) * 0.5)
            close = last[side, 1, rows] * (line_of(lines, edge_group, s + 1 - at, edge_group) * 0.5)
            for t in range(REACH):
                k = t - s + offsets[side]
                if 0 <= k < SPAN:
                    lanes = slice((t + at) * BS, (t + at + 1) * BS)
                    blocks[1, side, s, k] = seed[s, k] - far[:, lanes]
                k = t - s + REACH
                lanes = slice((t + 1 - at) * BS, (t + 2 - at) * BS)
                blocks[1, side, s, k] = seed[s, k] - close[:, lanes]
        send(side, 1, sign_out)

    for s in range(GROUP):
        a = count - GROUP + s
        k0, k1 = span_of(a, count, False)
        store = pltpu.make_async_copy(
            sign_last.at[s, pl.ds(k0, k1 - k0)], sign_out.at[a, pl.ds(k0, k1 - k0)], last_sems.at[s]
        )
        store.start()
        stores.append(store)
    build(0)
    value = dots(0)
    build(1)
    keep_first(0, value)
    value = dots(1)
    masks(0)
    keep_first(1, value)
    value = second_dots(0)
    masks(1)
    keep_last(0, value)
    value = second_dots(1)
    emit(0)
    keep_last(1, value)
    emit(1)
    for store in stores:
        store.wait()


def shards(matrix, pattern, *, axes, half_axis):
    count = matrix.shape[0]
    groups = count // GROUP
    flags = pattern.T
    vmem = pl.BlockSpec(memory_space=pltpu.VMEM)
    hbm = pl.BlockSpec(memory_space=pl.ANY)
    params = pltpu.CompilerParams(vmem_limit_bytes=LIMIT)

    top, bottom = matrix[:REACH, REACH:], matrix[count - REACH :, : REACH + 1]
    matrix, top, bottom = lax.optimization_barrier((matrix, top, bottom))
    edge = jax.ShapeDtypeStruct((REACH * HALF, (REACH + 1) * BS), F32)
    to_left, to_right = pl.pallas_call(
        edge_kernel,
        out_shape=(edge, edge),
        in_specs=[vmem] * 2,
        out_specs=[vmem] * 2,
        compiler_params=params,
        cost_estimate=pl.CostEstimate(
            flops=1 * 10**9, bytes_accessed=2**20, transcendentals=0
        ),
    )(top, bottom)
    size = 1
    for axis in axes:
        size *= lax.axis_size(axis)
    swap = [(0, 1), (1, 0)]
    other = lax.ppermute(matrix, half_axis, swap)
    forward = [(i, (i + 1) % size) for i in range(size)]
    backward = [(target, source) for source, target in forward]
    high_own = lax.ppermute(to_left, axes, backward)
    low_own = lax.ppermute(to_right, axes, forward)

    band = jax.ShapeDtypeStruct(matrix.shape, F32)
    seed = jax.ShapeDtypeStruct((REACH, SPAN, HALF, BS), F32)
    full = jax.ShapeDtypeStruct((2, groups, WIDE, 3 * WIDE), BF)
    mine = jax.ShapeDtypeStruct((2, groups, GROUP * HALF, 3 * WIDE), BF)
    keep = jax.ShapeDtypeStruct((2, 3 * groups, WIDE, WIDE), BF)
    lines = jax.ShapeDtypeStruct(((groups + 2) * GROUP, 3 * WIDE), F32)
    rows = jax.ShapeDtypeStruct((GROUP,) + matrix.shape[1:], F32)
    square, sign, low_seed, full, mine, keep, lines, sign_left = pl.pallas_call(
        functools.partial(first_kernel, axes=axes, half_axis=half_axis),
        out_shape=[band, band, seed, full, mine, keep, lines, rows],
        in_specs=[vmem, vmem, hbm],
        out_specs=[hbm] * 2 + [vmem] * 6,
        scratch_shapes=[
            pltpu.SMEM(flags.shape, jnp.int32),
            pltpu.VMEM((groups,) + rows.shape, F32),
            pltpu.VMEM((groups - 2,) + rows.shape, F32),
            pltpu.VMEM((2 * groups - 1 + 3 * groups - 4, WIDE, WIDE), F32),
            pltpu.SemaphoreType.DMA((2, count)),
            pltpu.SemaphoreType.DMA,
        ],
        compiler_params=params,
        cost_estimate=pl.CostEstimate(
            flops=3 * 2 * 16 * WIDE**3, bytes_accessed=16 * 2**20, transcendentals=0
        ),
    )(matrix, other, flags)

    low_own, high_own, low_seed = lax.optimization_barrier((low_own, high_own, low_seed))
    low_other = lax.ppermute(low_own, half_axis, swap)
    high_other = lax.ppermute(high_own, half_axis, swap)

    ends_out = [
        jax.ShapeDtypeStruct((REACH * BS, WIDE), F32),
        jax.ShapeDtypeStruct((REACH * BS, WIDE), F32),
        jax.ShapeDtypeStruct((2, REACH * BS, WIDE), BF),
        jax.ShapeDtypeStruct((2, 2, REACH * HALF, WIDE), BF),
    ]
    sign, sign_last, high_seed, *ends = pl.pallas_call(
        last_kernel,
        out_shape=[band, rows, seed] + ends_out * 2,
        in_specs=[vmem] * 6 + [hbm],
        out_specs=[hbm] + [vmem] * 10,
        scratch_shapes=[
            pltpu.VMEM((2, GROUP * HALF, WIDE), F32),
            pltpu.SemaphoreType.DMA((2, count)),
        ],
        input_output_aliases={6: 0},
        compiler_params=params,
        cost_estimate=pl.CostEstimate(
            flops=3 * 2 * 4 * WIDE**3, bytes_accessed=4 * 2**20, transcendentals=0
        ),
    )(matrix, lines, full, mine, keep, sign_left, sign)

    return tuple(
        pl.pallas_call(
            functools.partial(border_kernel, half_axis=half_axis),
            out_shape=(band, band),
            in_specs=[vmem] * 16 + [hbm] * 2,
            out_specs=[hbm] * 2,
            scratch_shapes=[
                pltpu.VMEM((2, 2, WIDE, 2 * WIDE), BF),
                pltpu.VMEM((2, 2, REACH * BS, WIDE), F32),
                pltpu.VMEM((2, 2, REACH * HALF, WIDE), F32),
                pltpu.VMEM((2, 2, REACH, SPAN, HALF, BS), F32),
                pltpu.SemaphoreType.DMA((2, 2, REACH)),
                pltpu.SemaphoreType.DMA((GROUP,)),
            ],
            input_output_aliases={16: 0, 17: 1},
            compiler_params=params,
            cost_estimate=pl.CostEstimate(
                flops=3 * 2 * 4 * WIDE**3, bytes_accessed=2 * 2**20, transcendentals=0
            ),
        )(
            low_own, low_other, high_own, high_other, lines, sign_last, low_seed, *ends[:4], high_seed,
            *ends[4:], square, sign,
        )
    )


def solution(mesh):
    band = P(("group", "row", "col"), None, "rep", None)
    return jax.shard_map(
        functools.partial(shards, axes=("row", "col"), half_axis="rep"),
        mesh=mesh,
        in_specs=(band, P("group", None)),
        out_specs=(band, band),
        check_vma=False,
    )
```

```python
import functools

import jax
import jax.numpy as jnp
from jax import lax
from jax.experimental import pallas as pl
from jax.experimental.pallas import tpu as pltpu
from jax.sharding import PartitionSpec as P

REACH = 3
SPAN = 7
BS = 64
HALF = 32
GROUP = 4
WIDE = GROUP * BS
BF = jnp.bfloat16
F32 = jnp.float32
LIMIT = 32 * 1024 * 1024


def split(x):
    hi = x.astype(BF)
    return hi, (x - hi.astype(F32)).astype(BF)


def product(pairs, transposed=False):
    side = 1 if transposed else 0
    high, low = [jnp.concatenate([a[p] for a, _ in pairs], axis=1) for p in range(2)]
    right = [jnp.concatenate([b[p] for _, b in pairs], axis=side) for p in range(2)]
    dot = functools.partial(
        lax.dot_general,
        dimension_numbers=(((1,), (side,)), ((), ())),
        preferred_element_type=F32,
    )
    both = dot(jnp.concatenate([high, low], axis=0), right[0])
    count = high.shape[0]
    return both[:count] + (both[count:] + dot(high, right[1]))


def turn(x):
    return split((x[0].astype(F32) + x[1].astype(F32)).T)


def write_lines(pat, lines, first, groups):
    total = pat.shape[1]
    lane = lax.broadcasted_iota(jnp.int32, (1, 2 * BS), 1)
    for g in range(-1, groups + 1):
        for s in range(GROUP):
            row = lax.rem(first + g * GROUP + s + total, total)
            for t in range(3 * GROUP // 2):
                ks = [2 * t + e - s - 1 for e in range(2)]
                f = [pat[k, row].astype(F32) if 0 <= k < SPAN else F32(0) for k in ks]
                at = (g + 1) * GROUP + s
                lines[at : at + 1, t * 2 * BS : (t + 1) * 2 * BS] = jnp.where(lane < BS, f[0], f[1])


def line_of(lines, g, s, h):
    at = (g + 1) * GROUP + s
    lo = (h - g + 1) * WIDE
    return lines[at : at + 1, lo : lo + WIDE]


def span_of(a, count, is_square):
    if a < REACH:
        return (REACH - a if is_square else 2 * REACH - a), SPAN
    s = a - (count - REACH)
    if s >= 0:
        return 0, (2 * REACH - s if is_square else REACH - s)
    return 0, SPAN


def edge_kernel(top, bottom, to_left, to_right):
    for source, target in ((top, to_left), (bottom, to_right)):
        for s in range(REACH):
            for t in range(2):
                target[s * HALF : (s + 1) * HALF, t * 2 * BS : (t + 1) * 2 * BS] = jnp.concatenate(
                    [source[s, 2 * t], source[s, 2 * t + 1]], axis=1
                )


class Interior:
    def __init__(self, own, lines, full, mine, keep):
        self.own = own
        self.lines = lines
        self.full = full
        self.mine = mine
        self.keep = keep
        self.count = own.shape[0]
        self.groups = self.count // GROUP
        self.stores = []

    def part(self, g, h, rows=slice(None)):
        at = (h - g + 1) * WIDE
        return [self.full[p, g, rows, at : at + WIDE] for p in range(2)]

    def my_part(self, g, h):
        at = (h - g + 1) * WIDE
        return [self.mine[p, g, :, at : at + WIDE] for p in range(2)]

    def tile(self, g, h):
        return 3 * g + h - g + 1

    def kept(self, g, h):
        return [self.keep[p, self.tile(g, h)] for p in range(2)]

    def near(self, g):
        return [e for e in (g - 1, g, g + 1) if 0 <= e < self.groups]

    def second(self, g, h, sign, seed, result):
        span = range(1 if h > g else 0, GROUP - 1 if h < g else GROUP)
        rows = slice(span[0] * HALF, (span[-1] + 1) * HALF)

        def dot():
            return product(
                [
                    ([x[rows] for x in self.my_part(g, e)], self.kept(e, h))
                    for e in self.near(g)
                    if abs(e - h) <= 1
                ]
            )

        def store(value):
            result[rows] = value

        def post():
            for s in span:
                a = g * GROUP + s
                k0, k1 = span_of(a, self.count, False)
                part = result[s * HALF : (s + 1) * HALF] * (line_of(self.lines, g, s, h) * 0.5)
                for t in range(GROUP):
                    k = t + GROUP * (h - g) - s + REACH
                    if 0 <= k < SPAN:
                        block = 1.5 * self.own[a, k] - part[:, t * BS : (t + 1) * BS]
                        if k0 <= k < k1:
                            sign[s, k] = block
                        else:
                            seed[a if a < REACH else a - (self.count - REACH), k] = block

        return dot, store, post

    def far_seed(self, g, seed):
        for s in range(REACH):
            a = s if g == 0 else self.count - REACH + s
            for k in range(0, REACH - s) if g == 0 else range(2 * REACH - s, SPAN):
                seed[s, k] = 1.5 * self.own[a, k]

    def send(self, g, i, source, target, sems):
        for s in range(GROUP):
            a = g * GROUP + s
            k0, k1 = span_of(a, self.count, i == 0)
            store = pltpu.make_async_copy(
                source.at[s, pl.ds(k0, k1 - k0)], target.at[a, pl.ds(k0, k1 - k0)], sems.at[i, a]
            )
            store.start()
            self.stores.append(store)

    def finish(self):
        for store in self.stores:
            store.wait()


def count_dots(steps):
    return sum(isinstance(step, tuple) for step in steps)


def staggered(steps):
    pending = []
    for step in steps:
        if not isinstance(step, tuple):
            pending.append(step)
            continue
        dot, store, post = step
        value = dot()
        for work in pending:
            work()
        store(value)
        pending = [post]
    for work in pending:
        work()


def first_kernel(
    own, other, pattern, square_out, sign_out, seed, full, mine, keep, lines, sign_left,
    pat, square, sign, results, sems, pat_sem, *, axes, half_axis
):
    load = pltpu.make_async_copy(pattern, pat, pat_sem)
    load.start()
    it = Interior(own, lines, full, mine, keep)
    groups = it.groups
    upper_half = lax.axis_index(half_axis) == 1

    def build(g):
        for s in range(GROUP):
            a = g * GROUP + s
            for t in range(3 * GROUP // 2):
                ks = [2 * t + e - s - 1 for e in range(2)]
                lanes = slice(t * 2 * BS, (t + 1) * 2 * BS)
                rows = slice(s * BS, (s + 1) * BS)
                mine_rows = slice(s * HALF, (s + 1) * HALF)
                if all(k < 0 or k >= SPAN for k in ks):
                    for p in range(2):
                        full[p, g, rows, lanes] = jnp.zeros((BS, 2 * BS), BF)
                        mine[p, g, mine_rows, lanes] = jnp.zeros((HALF, 2 * BS), BF)
                    continue
                two = [
                    jnp.concatenate(
                        [src[a, k] if 0 <= k < SPAN else jnp.zeros((HALF, BS), F32) for k in ks],
                        axis=1,
                    )
                    for src in (own, other)
                ]
                for p, (x, y) in enumerate(zip(*[split(x) for x in two])):
                    mine[p, g, mine_rows, lanes] = x
                    full[p, g, rows, lanes] = jnp.concatenate(
                        [jnp.where(upper_half, y, x), jnp.where(upper_half, x, y)], axis=0
                    )

    def squares(g, h, result):
        pairs = []
        for e in (g - 1, g, g + 1):
            if abs(e - h) <= 1:
                inside = 0 <= e < groups
                pairs.append((e, (lambda e=e: it.part(e, h)) if inside else (lambda e=e: turn(it.part(h, e)))))
        span = range(1 if h > g else 0, GROUP)
        rows = slice(span[0] * BS, WIDE)

        def dot():
            return product([([x[rows] for x in it.part(g, e)], f()) for e, f in pairs])

        def store(value):
            result[rows] = value

        def post():
            masked = [jnp.zeros((BS, WIDE), F32)] * GROUP
            for s in span:
                masked[s] = result[s * BS : (s + 1) * BS] * line_of(lines, g, s, h)
            for s in range(GROUP):
                for p, x in enumerate(split(masked[s])):
                    keep[p, it.tile(g, h), s * BS : (s + 1) * BS] = x
            for s in span:
                part = jnp.where(upper_half, masked[s][HALF:], masked[s][:HALF])
                for t in range(GROUP):
                    k = t + GROUP * (h - g) - s + REACH
                    if 0 <= k < SPAN:
                        staged[g][s, k] = part[:, t * BS : (t + 1) * BS]
            if h == g:
                return
            for c in range(0, GROUP, 2):
                turned = jnp.concatenate(masked[c : c + 2], axis=0).T
                lanes = slice(c * BS, (c + 2) * BS)
                for p, x in enumerate(split(turned)):
                    keep[p, it.tile(h, g), :, lanes] = x
                for t in range(GROUP):
                    rows = turned[t * BS : (t + 1) * BS]
                    part = jnp.where(upper_half, rows[HALF:], rows[:HALF])
                    for s in range(c, c + 2):
                        k = s + GROUP * (g - h) - t + REACH
                        if 0 <= k < SPAN:
                            staged[h][t, k] = part[:, (s - c) * BS : (s - c + 1) * BS]

        return dot, store, post

    staged = [square.at[g] for g in range(groups)]
    signs = [sign.at[g] for g in range(groups - 2)] + [sign_left]

    def begin():
        load.wait()
        write_lines(pat, lines, lax.axis_index(axes) * it.count, groups)
        it.far_seed(0, seed)

    lax.fori_loop(0, groups, lambda g, _: build(g), None)
    steps = [begin]
    for g in range(groups):
        if g + 1 < groups:
            steps.append(squares(g, g + 1, results.at[count_dots(steps)]))
        steps.append(squares(g, g, results.at[count_dots(steps)]))
        steps.append(functools.partial(it.send, g, 0, staged[g], square_out, sems))
        if g > 0:
            for h in it.near(g - 1):
                steps.append(it.second(g - 1, h, signs[g - 1], seed, results.at[count_dots(steps)]))
            if g < groups - 1:
                steps.append(functools.partial(it.send, g - 1, 1, signs[g - 1], sign_out, sems))
    staggered(steps)
    it.finish()


def last_kernel(
    own, lines, full, mine, keep, sign_left, sign_in, sign_out, sign, seed, low_a, low_b, low_m, low_p, high_a, high_b, high_m, high_p, results, sems
):
    it = Interior(own, lines, full, mine, keep)
    last = it.groups - 1
    it.send(last - 1, 1, sign_left, sign_out, sems)
    steps = [it.second(last, h, sign, seed, results.at[i]) for i, h in enumerate(it.near(last))]
    steps.append(functools.partial(it.far_seed, last, seed))

    def reaching(a_ref, b_ref, m_ref, p_ref, g, e, r0):
        rows = slice(r0, r0 + REACH * BS)
        mine_rows = slice(r0 // 2, r0 // 2 + REACH * HALF)
        outer = slice(BS - r0, BS - r0 + REACH * BS)

        def dot():
            out = it.part(g, e)
            return (
                product([([x[outer] for x in turn(out)], out)]),
                product([(it.part(g, g, rows), out)]),
            )

        def store(value):
            a_ref[...], b_ref[...] = value

        def post():
            for p in range(2):
                m_ref[p] = it.part(g, e)[p][rows]
                p_ref[p, 0] = it.my_part(g, e)[p][mine_rows]
                p_ref[p, 1] = it.my_part(g, g)[p][mine_rows]

        return dot, store, post

    steps.append(reaching(low_a, low_b, low_m, low_p, 0, -1, 0))
    steps.append(reaching(high_a, high_b, high_m, high_p, last, last + 1, BS))
    staggered(steps)
    it.finish()


def border_kernel(
    low_own, low_other, high_own, high_other, lines, sign_last, low_seed, low_a, low_b, low_m, low_p, high_seed,
    high_a, high_b, high_m, high_p, square_in, sign_in, square_out, sign_out, halo, first, last, blocks, sems, last_sems,
    *, half_axis
):
    count = square_in.shape[0]
    groups = count // GROUP
    upper_half = lax.axis_index(half_axis) == 1
    ends = (0, count - REACH)
    given = (
        (low_own, low_other, low_seed, low_a, low_b, low_m, low_p),
        (high_own, high_other, high_seed, high_a, high_b, high_m, high_p),
    )
    shift = (1, 0)
    zero = jnp.zeros((BS, WIDE), F32)

    def build(side):
        mine, theirs = given[side][:2]
        below = REACH if side == 0 else 0
        whole_rows = []
        for p in range(REACH):
            rows = slice(p * HALF, (p + 1) * HALF)
            whole_rows.append(
                jnp.concatenate(
                    [
                        jnp.where(upper_half, theirs[rows, :], mine[rows, :]),
                        jnp.where(upper_half, mine[rows, :], theirs[rows, :]),
                    ],
                    axis=0,
                )
            )

        def block(p, c):
            k = c - p + below
            if 0 <= k <= REACH:
                return whole_rows[p][:, k * BS : (k + 1) * BS]
            k = p - c + below
            if 0 <= c < REACH and 0 <= k <= REACH:
                return whole_rows[c][:, k * BS : (k + 1) * BS].T
            return jnp.zeros((BS, BS), F32)

        base = -5 if side == 0 else 0
        for p in range(REACH):
            rows = slice((p + shift[side]) * BS, (p + shift[side] + 1) * BS)
            for t in range(4):
                value = jnp.concatenate([block(p, base + 2 * t), block(p, base + 2 * t + 1)], axis=1)
                for q, x in enumerate(split(value)):
                    halo[side, q, rows, t * 2 * BS : (t + 1) * 2 * BS] = x
        rows = slice(0, BS) if side == 0 else slice(REACH * BS, WIDE)
        for q in range(2):
            halo[side, q, rows, :] = jnp.zeros((BS, 2 * WIDE), BF)

    edge_groups, outer_groups = (0, groups - 1), (-1, groups)
    offsets = (0, 2 * REACH)
    corners = [None, None]
    across = [None, None]
    stores = []

    def dots(side):
        m_ref = given[side][5]
        whole = [halo[side, q] for q in range(2)]
        outer_rows = slice(shift[side] * BS, (shift[side] + REACH) * BS)
        inner = slice(WIDE, 2 * WIDE) if side == 0 else slice(0, WIDE)
        return (
            product([([x[outer_rows] for x in whole], whole)], True),
            product([([m_ref[q] for q in range(2)], [x[:, inner] for x in whole])], True),
        )

    def keep_first(side, value):
        _, _, _, a_ref, b_ref, _, _ = given[side]
        first[side, 0] = value[0] + a_ref[...]
        first[side, 1] = value[1] + b_ref[...]

    def masks(side):
        at = shift[side]
        edge_group, outer_group = edge_groups[side], outer_groups[side]
        pad = (lambda rows: [zero] + rows, lambda rows: rows + [zero])
        rows = [
            first[side, 0, p * BS : (p + 1) * BS] * line_of(lines, outer_group, p + at, outer_group)
            for p in range(REACH)
        ]
        corners[side] = split(jnp.concatenate(pad[side](rows), axis=0))
        rows = [
            first[side, 1, s * BS : (s + 1) * BS]
            * line_of(lines, edge_group, s + 1 - at, outer_group)
            for s in range(REACH)
        ]
        across[side] = split(jnp.concatenate(pad[1 - side](rows), axis=0))
        for s in range(REACH):
            part = jnp.where(upper_half, rows[s][HALF:], rows[s][:HALF])
            for t in range(REACH):
                k = t - s + offsets[side]
                if 0 <= k < SPAN:
                    blocks[0, side, s, k] = part[:, (t + at) * BS : (t + at + 1) * BS]
        send(side, 0, square_out)

    def send(side, i, ref):
        for s in range(REACH):
            a = ends[side] + s
            k0, k1 = span_of(a, count, i == 0)
            k0, k1 = (0, k0) if side == 0 else (k1, SPAN)
            store = pltpu.make_async_copy(
                blocks.at[i, side, s, pl.ds(k0, k1 - k0)],
                ref.at[a, pl.ds(k0, k1 - k0)],
                sems.at[i, side, s],
            )
            store.start()
            stores.append(store)

    def second_dots(side):
        p_ref = given[side][6]
        reach_out = [p_ref[q, 0] for q in range(2)]
        inside = [p_ref[q, 1] for q in range(2)]
        return (
            product([(reach_out, corners[side]), (inside, across[side])]),
            product([(reach_out, across[side])], True),
        )

    def keep_last(side, value):
        last[side, 0], last[side, 1] = value

    def emit(side):
        seed = given[side][2]
        at = shift[side]
        edge_group, outer_group = edge_groups[side], outer_groups[side]
        for s in range(REACH):
            rows = slice(s * HALF, (s + 1) * HALF)
            far = last[side, 0, rows] * (line_of(lines, edge_group, s + 1 - at, outer_group) * 0.5)
            close = last[side, 1, rows] * (line_of(lines, edge_group, s + 1 - at, edge_group) * 0.5)
            for t in range(REACH):
                k = t - s + offsets[side]
                if 0 <= k < SPAN:
                    lanes = slice((t + at) * BS, (t + at + 1) * BS)
                    blocks[1, side, s, k] = seed[s, k] - far[:, lanes]
                k = t - s + REACH
                lanes = slice((t + 1 - at) * BS, (t + 2 - at) * BS)
                blocks[1, side, s, k] = seed[s, k] - close[:, lanes]
        send(side, 1, sign_out)

    for s in range(GROUP):
        a = count - GROUP + s
        k0, k1 = span_of(a, count, False)
        store = pltpu.make_async_copy(
            sign_last.at[s, pl.ds(k0, k1 - k0)], sign_out.at[a, pl.ds(k0, k1 - k0)], last_sems.at[s]
        )
        store.start()
        stores.append(store)
    build(0)
    value = dots(0)
    build(1)
    keep_first(0, value)
    value = dots(1)
    masks(0)
    keep_first(1, value)
    value = second_dots(0)
    masks(1)
    keep_last(0, value)
    value = second_dots(1)
    emit(0)
    keep_last(1, value)
    emit(1)
    for store in stores:
        store.wait()


def shards(matrix, pattern, *, axes, half_axis):
    count = matrix.shape[0]
    groups = count // GROUP
    flags = pattern.T
    vmem = pl.BlockSpec(memory_space=pltpu.VMEM)
    hbm = pl.BlockSpec(memory_space=pl.ANY)
    params = pltpu.CompilerParams(vmem_limit_bytes=LIMIT)

    top, bottom = matrix[:REACH, REACH:], matrix[count - REACH :, : REACH + 1]
    matrix, top, bottom = lax.optimization_barrier((matrix, top, bottom))
    edge = jax.ShapeDtypeStruct((REACH * HALF, (REACH + 1) * BS), F32)
    to_left, to_right = pl.pallas_call(
        edge_kernel,
        out_shape=(edge, edge),
        in_specs=[vmem] * 2,
        out_specs=[vmem] * 2,
        compiler_params=params,
        cost_estimate=pl.CostEstimate(
            flops=1 * 10**9, bytes_accessed=2**20, transcendentals=0
        ),
    )(top, bottom)
    size = 1
    for axis in axes:
        size *= lax.axis_size(axis)
    swap = [(0, 1), (1, 0)]
    other = lax.ppermute(matrix, half_axis, swap)
    forward = [(i, (i + 1) % size) for i in range(size)]
    backward = [(target, source) for source, target in forward]
    high_own = lax.ppermute(to_left, axes, backward)
    low_own = lax.ppermute(to_right, axes, forward)

    band = jax.ShapeDtypeStruct(matrix.shape, F32)
    seed = jax.ShapeDtypeStruct((REACH, SPAN, HALF, BS), F32)
    full = jax.ShapeDtypeStruct((2, groups, WIDE, 3 * WIDE), BF)
    mine = jax.ShapeDtypeStruct((2, groups, GROUP * HALF, 3 * WIDE), BF)
    keep = jax.ShapeDtypeStruct((2, 3 * groups, WIDE, WIDE), BF)
    lines = jax.ShapeDtypeStruct(((groups + 2) * GROUP, 3 * WIDE), F32)
    rows = jax.ShapeDtypeStruct((GROUP,) + matrix.shape[1:], F32)
    square, sign, low_seed, full, mine, keep, lines, sign_left = pl.pallas_call(
        functools.partial(first_kernel, axes=axes, half_axis=half_axis),
        out_shape=[band, band, seed, full, mine, keep, lines, rows],
        in_specs=[vmem, vmem, hbm],
        out_specs=[hbm] * 2 + [vmem] * 6,
        scratch_shapes=[
            pltpu.SMEM(flags.shape, jnp.int32),
            pltpu.VMEM((groups,) + rows.shape, F32),
            pltpu.VMEM((groups - 2,) + rows.shape, F32),
            pltpu.VMEM((2 * groups - 1 + 3 * groups - 4, WIDE, WIDE), F32),
            pltpu.SemaphoreType.DMA((2, count)),
            pltpu.SemaphoreType.DMA,
        ],
        compiler_params=params,
        cost_estimate=pl.CostEstimate(
            flops=3 * 2 * 16 * WIDE**3, bytes_accessed=16 * 2**20, transcendentals=0
        ),
    )(matrix, other, flags)

    low_own, high_own, low_seed = lax.optimization_barrier((low_own, high_own, low_seed))
    low_other = lax.ppermute(low_own, half_axis, swap)
    high_other = lax.ppermute(high_own, half_axis, swap)

    ends_out = [
        jax.ShapeDtypeStruct((REACH * BS, WIDE), F32),
        jax.ShapeDtypeStruct((REACH * BS, WIDE), F32),
        jax.ShapeDtypeStruct((2, REACH * BS, WIDE), BF),
        jax.ShapeDtypeStruct((2, 2, REACH * HALF, WIDE), BF),
    ]
    sign, sign_last, high_seed, *ends = pl.pallas_call(
        last_kernel,
        out_shape=[band, rows, seed] + ends_out * 2,
        in_specs=[vmem] * 6 + [hbm],
        out_specs=[hbm] + [vmem] * 10,
        scratch_shapes=[
            pltpu.VMEM((2, GROUP * HALF, WIDE), F32),
            pltpu.SemaphoreType.DMA((2, count)),
        ],
        input_output_aliases={6: 0},
        compiler_params=params,
        cost_estimate=pl.CostEstimate(
            flops=3 * 2 * 4 * WIDE**3, bytes_accessed=4 * 2**20, transcendentals=0
        ),
    )(matrix, lines, full, mine, keep, sign_left, sign)

    return tuple(
        pl.pallas_call(
            functools.partial(border_kernel, half_axis=half_axis),
            out_shape=(band, band),
            in_specs=[vmem] * 16 + [hbm] * 2,
            out_specs=[hbm] * 2,
            scratch_shapes=[
                pltpu.VMEM((2, 2, WIDE, 2 * WIDE), BF),
                pltpu.VMEM((2, 2, REACH * BS, WIDE), F32),
                pltpu.VMEM((2, 2, REACH * HALF, WIDE), F32),
                pltpu.VMEM((2, 2, REACH, SPAN, HALF, BS), F32),
                pltpu.SemaphoreType.DMA((2, 2, REACH)),
                pltpu.SemaphoreType.DMA((GROUP,)),
            ],
            input_output_aliases={16: 0, 17: 1},
            compiler_params=params,
            cost_estimate=pl.CostEstimate(
                flops=3 * 2 * 4 * WIDE**3, bytes_accessed=2 * 2**20, transcendentals=0
            ),
        )(
            low_own, low_other, high_own, high_other, lines, sign_last, low_seed, *ends[:4], high_seed,
            *ends[4:], square, sign,
        )
    )


def solution(mesh):
    band = P(("group", "row", "col"), None, "rep", None)
    return jax.shard_map(
        functools.partial(shards, axes=("row", "col"), half_axis="rep"),
        mesh=mesh,
        in_specs=(band, P("group", None)),
        out_specs=(band, band),
        check_vma=False,
    )
```

```python
import functools

import jax
import jax.numpy as jnp
from jax import lax
from jax.experimental import pallas as pl
from jax.experimental.pallas import tpu as pltpu
from jax.sharding import PartitionSpec as P

REACH = 3
SPAN = 7
BS = 64
HALF = 32
GROUP = 4
WIDE = GROUP * BS
BF = jnp.bfloat16
F32 = jnp.float32
LIMIT = 32 * 1024 * 1024


def split(x):
    hi = x.astype(BF)
    return hi, (x - hi.astype(F32)).astype(BF)


def product(pairs, transposed=False):
    side = 1 if transposed else 0
    high, low = [jnp.concatenate([a[p] for a, _ in pairs], axis=1) for p in range(2)]
    right = [jnp.concatenate([b[p] for _, b in pairs], axis=side) for p in range(2)]
    dot = functools.partial(
        lax.dot_general,
        dimension_numbers=(((1,), (side,)), ((), ())),
        preferred_element_type=F32,
    )
    both = dot(jnp.concatenate([high, low], axis=0), right[0])
    count = high.shape[0]
    return both[:count] + (both[count:] + dot(high, right[1]))


def turn(x):
    return split((x[0].astype(F32) + x[1].astype(F32)).T)


def write_lines(pat, lines, first, groups):
    total = pat.shape[1]
    rows = lines.shape[0]
    iota = functools.partial(lax.broadcasted_iota, jnp.int32)
    dot = functools.partial(lax.dot_general, preferred_element_type=F32)
    wanted = lax.rem(first - GROUP + total + iota((rows, total), 0), total)
    chosen = (iota((rows, total), 1) == wanted).astype(BF)
    flags = dot(chosen, pat[...].astype(BF), (((1,), (1,)), ((), ())))
    place = iota((rows, 1), 0) % GROUP
    spread = jnp.concatenate(
        [jnp.where(place == s, flags, 0.0) for s in range(GROUP)], axis=1
    ).astype(BF)
    block = iota((SPAN, 3 * WIDE), 1) // BS - iota((SPAN, 3 * WIDE), 0) - 1
    spots = jnp.concatenate([(block == s).astype(BF) for s in range(GROUP)], axis=0)
    lines[...] = dot(spread, spots, (((1,), (0,)), ((), ())))


def line_of(lines, g, s, h):
    at = (g + 1) * GROUP + s
    lo = (h - g + 1) * WIDE
    return lines[at : at + 1, lo : lo + WIDE]


def span_of(a, count, is_square):
    if a < REACH:
        return (REACH - a if is_square else 2 * REACH - a), SPAN
    s = a - (count - REACH)
    if s >= 0:
        return 0, (2 * REACH - s if is_square else REACH - s)
    return 0, SPAN


def edge_kernel(top, bottom, to_left, to_right):
    for source, target in ((top, to_left), (bottom, to_right)):
        for s in range(REACH):
            for t in range(2):
                target[s * HALF : (s + 1) * HALF, t * 2 * BS : (t + 1) * 2 * BS] = jnp.concatenate(
                    [source[s, 2 * t], source[s, 2 * t + 1]], axis=1
                )


class Interior:
    def __init__(self, own, lines, full, mine, keep):
        self.own = own
        self.lines = lines
        self.full = full
        self.mine = mine
        self.keep = keep
        self.count = own.shape[0]
        self.groups = self.count // GROUP
        self.stores = []

    def part(self, g, h, rows=slice(None)):
        at = (h - g + 1) * WIDE
        return [self.full[p, g, rows, at : at + WIDE] for p in range(2)]

    def my_part(self, g, h):
        at = (h - g + 1) * WIDE
        return [self.mine[p, g, :, at : at + WIDE] for p in range(2)]

    def tile(self, g, h):
        return 3 * g + h - g + 1

    def kept(self, g, h):
        return [self.keep[p, self.tile(g, h)] for p in range(2)]

    def near(self, g):
        return [e for e in (g - 1, g, g + 1) if 0 <= e < self.groups]

    def second(self, g, h, sign, seed, result):
        span = range(1 if h > g else 0, GROUP - 1 if h < g else GROUP)
        rows = slice(span[0] * HALF, (span[-1] + 1) * HALF)

        def dot():
            return product(
                [
                    ([x[rows] for x in self.my_part(g, e)], self.kept(e, h))
                    for e in self.near(g)
                    if abs(e - h) <= 1
                ]
            )

        def store(value):
            result[rows] = value

        def post():
            for s in span:
                a = g * GROUP + s
                k0, k1 = span_of(a, self.count, False)
                part = result[s * HALF : (s + 1) * HALF] * (line_of(self.lines, g, s, h) * 0.5)
                for t in range(GROUP):
                    k = t + GROUP * (h - g) - s + REACH
                    if 0 <= k < SPAN:
                        block = 1.5 * self.own[a, k] - part[:, t * BS : (t + 1) * BS]
                        if k0 <= k < k1:
                            sign[s, k] = block
                        else:
                            seed[a if a < REACH else a - (self.count - REACH), k] = block

        return dot, store, post

    def far_seed(self, g, seed):
        for s in range(REACH):
            a = s if g == 0 else self.count - REACH + s
            for k in range(0, REACH - s) if g == 0 else range(2 * REACH - s, SPAN):
                seed[s, k] = 1.5 * self.own[a, k]

    def send(self, g, i, source, target, sems):
        for s in range(GROUP):
            a = g * GROUP + s
            k0, k1 = span_of(a, self.count, i == 0)
            store = pltpu.make_async_copy(
                source.at[s, pl.ds(k0, k1 - k0)], target.at[a, pl.ds(k0, k1 - k0)], sems.at[i, a]
            )
            store.start()
            self.stores.append(store)

    def finish(self):
        for store in self.stores:
            store.wait()


def count_dots(steps):
    return sum(isinstance(step, tuple) for step in steps)


def staggered(steps):
    pending = []
    for step in steps:
        if not isinstance(step, tuple):
            pending.append(step)
            continue
        dot, store, post = step
        value = dot()
        for work in pending:
            work()
        store(value)
        pending = [post]
    for work in pending:
        work()


def first_kernel(
    own, other, pat, square_out, seed, full, mine, keep, lines, sign,
    square, results, sems, *, axes, half_axis
):
    it = Interior(own, lines, full, mine, keep)
    groups = it.groups
    upper_half = lax.axis_index(half_axis) == 1

    def build(g):
        for s in range(GROUP):
            a = g * GROUP + s
            for t in range(3 * GROUP // 2):
                ks = [2 * t + e - s - 1 for e in range(2)]
                lanes = slice(t * 2 * BS, (t + 1) * 2 * BS)
                rows = slice(s * BS, (s + 1) * BS)
                mine_rows = slice(s * HALF, (s + 1) * HALF)
                if all(k < 0 or k >= SPAN for k in ks):
                    for p in range(2):
                        full[p, g, rows, lanes] = jnp.zeros((BS, 2 * BS), BF)
                        mine[p, g, mine_rows, lanes] = jnp.zeros((HALF, 2 * BS), BF)
                    continue
                two = [
                    jnp.concatenate(
                        [src[a, k] if 0 <= k < SPAN else jnp.zeros((HALF, BS), F32) for k in ks],
                        axis=1,
                    )
                    for src in (own, other)
                ]
                for p, (x, y) in enumerate(zip(*[split(x) for x in two])):
                    mine[p, g, mine_rows, lanes] = x
                    full[p, g, rows, lanes] = jnp.concatenate(
                        [jnp.where(upper_half, y, x), jnp.where(upper_half, x, y)], axis=0
                    )

    def squares(g, h, result):
        pairs = []
        for e in (g - 1, g, g + 1):
            if abs(e - h) <= 1:
                inside = 0 <= e < groups
                pairs.append((e, (lambda e=e: it.part(e, h)) if inside else (lambda e=e: turn(it.part(h, e)))))
        span = range(1 if h > g else 0, GROUP)
        rows = slice(span[0] * BS, WIDE)

        def dot():
            return product([([x[rows] for x in it.part(g, e)], f()) for e, f in pairs])

        def store(value):
            result[rows] = value

        def post():
            masked = [jnp.zeros((BS, WIDE), F32)] * GROUP
            for s in span:
                masked[s] = result[s * BS : (s + 1) * BS] * line_of(lines, g, s, h)
            for s in range(GROUP):
                for p, x in enumerate(split(masked[s])):
                    keep[p, it.tile(g, h), s * BS : (s + 1) * BS] = x
            for s in span:
                part = jnp.where(upper_half, masked[s][HALF:], masked[s][:HALF])
                for t in range(GROUP):
                    k = t + GROUP * (h - g) - s + REACH
                    if 0 <= k < SPAN:
                        staged[g][s, k] = part[:, t * BS : (t + 1) * BS]
            if h == g:
                return
            for c in range(0, GROUP, 2):
                turned = jnp.concatenate(masked[c : c + 2], axis=0).T
                lanes = slice(c * BS, (c + 2) * BS)
                for p, x in enumerate(split(turned)):
                    keep[p, it.tile(h, g), :, lanes] = x
                for t in range(GROUP):
                    rows = turned[t * BS : (t + 1) * BS]
                    part = jnp.where(upper_half, rows[HALF:], rows[:HALF])
                    for s in range(c, c + 2):
                        k = s + GROUP * (g - h) - t + REACH
                        if 0 <= k < SPAN:
                            staged[h][t, k] = part[:, (s - c) * BS : (s - c + 1) * BS]

        return dot, store, post

    staged = [square.at[g] for g in range(groups)]

    def begin():
        write_lines(pat, lines, lax.axis_index(axes) * it.count, groups)
        it.far_seed(0, seed)

    build(0)
    build(1)
    steps = [begin]
    for g in range(groups):
        if g + 1 < groups:
            steps.append(squares(g, g + 1, results.at[count_dots(steps)]))
            if g + 2 < groups:
                steps.append(functools.partial(build, g + 2))
        steps.append(squares(g, g, results.at[count_dots(steps)]))
        steps.append(functools.partial(it.send, g, 0, staged[g], square_out, sems))
    for g in range(groups - 1):
        for h in it.near(g):
            steps.append(it.second(g, h, sign.at[g], seed, results.at[count_dots(steps)]))
    staggered(steps)
    it.finish()


def last_kernel(
    own, lines, full, mine, keep, sign_first, sign_out, sign, seed, low_a, low_b, low_m, low_p, high_a, high_b, high_m, high_p, results, sems
):
    it = Interior(own, lines, full, mine, keep)
    last = it.groups - 1
    for g in range(last):
        it.send(g, 1, sign_first.at[g], sign_out, sems)
    steps = [it.second(last, h, sign, seed, results.at[i]) for i, h in enumerate(it.near(last))]
    steps.append(functools.partial(it.far_seed, last, seed))

    def reaching(a_ref, b_ref, m_ref, p_ref, g, e, r0):
        rows = slice(r0, r0 + REACH * BS)
        mine_rows = slice(r0 // 2, r0 // 2 + REACH * HALF)
        outer = slice(BS - r0, BS - r0 + REACH * BS)

        def dot():
            out = it.part(g, e)
            return (
                product([([x[outer] for x in turn(out)], out)]),
                product([(it.part(g, g, rows), out)]),
            )

        def store(value):
            a_ref[...], b_ref[...] = value

        def post():
            for p in range(2):
                m_ref[p] = it.part(g, e)[p][rows]
                p_ref[p, 0] = it.my_part(g, e)[p][mine_rows]
                p_ref[p, 1] = it.my_part(g, g)[p][mine_rows]

        return dot, store, post

    steps.append(reaching(low_a, low_b, low_m, low_p, 0, -1, 0))
    steps.append(reaching(high_a, high_b, high_m, high_p, last, last + 1, BS))
    staggered(steps)
    it.finish()


def border_kernel(
    low_own, low_other, high_own, high_other, lines, sign_last, low_seed, low_a, low_b, low_m, low_p, high_seed,
    high_a, high_b, high_m, high_p, square_in, sign_in, square_out, sign_out, halo, first, last, blocks, sems, last_sems,
    *, half_axis
):
    count = square_in.shape[0]
    groups = count // GROUP
    upper_half = lax.axis_index(half_axis) == 1
    ends = (0, count - REACH)
    given = (
        (low_own, low_other, low_seed, low_a, low_b, low_m, low_p),
        (high_own, high_other, high_seed, high_a, high_b, high_m, high_p),
    )
    shift = (1, 0)
    zero = jnp.zeros((BS, WIDE), F32)

    def build(side):
        mine, theirs = given[side][:2]
        below = REACH if side == 0 else 0
        whole_rows = []
        for p in range(REACH):
            rows = slice(p * HALF, (p + 1) * HALF)
            whole_rows.append(
                jnp.concatenate(
                    [
                        jnp.where(upper_half, theirs[rows, :], mine[rows, :]),
                        jnp.where(upper_half, mine[rows, :], theirs[rows, :]),
                    ],
                    axis=0,
                )
            )

        def block(p, c):
            k = c - p + below
            if 0 <= k <= REACH:
                return whole_rows[p][:, k * BS : (k + 1) * BS]
            k = p - c + below
            if 0 <= c < REACH and 0 <= k <= REACH:
                return whole_rows[c][:, k * BS : (k + 1) * BS].T
            return jnp.zeros((BS, BS), F32)

        base = -5 if side == 0 else 0
        for p in range(REACH):
            rows = slice((p + shift[side]) * BS, (p + shift[side] + 1) * BS)
            for t in range(4):
                value = jnp.concatenate([block(p, base + 2 * t), block(p, base + 2 * t + 1)], axis=1)
                for q, x in enumerate(split(value)):
                    halo[side, q, rows, t * 2 * BS : (t + 1) * 2 * BS] = x
        rows = slice(0, BS) if side == 0 else slice(REACH * BS, WIDE)
        for q in range(2):
            halo[side, q, rows, :] = jnp.zeros((BS, 2 * WIDE), BF)

    edge_groups, outer_groups = (0, groups - 1), (-1, groups)
    offsets = (0, 2 * REACH)
    corners = [None, None]
    across = [None, None]
    stores = []

    def dots(side):
        m_ref = given[side][5]
        whole = [halo[side, q] for q in range(2)]
        outer_rows = slice(shift[side] * BS, (shift[side] + REACH) * BS)
        inner = slice(WIDE, 2 * WIDE) if side == 0 else slice(0, WIDE)
        return (
            product([([x[outer_rows] for x in whole], whole)], True),
            product([([m_ref[q] for q in range(2)], [x[:, inner] for x in whole])], True),
        )

    def keep_first(side, value):
        _, _, _, a_ref, b_ref, _, _ = given[side]
        first[side, 0] = value[0] + a_ref[...]
        first[side, 1] = value[1] + b_ref[...]

    def masks(side):
        at = shift[side]
        edge_group, outer_group = edge_groups[side], outer_groups[side]
        pad = (lambda rows: [zero] + rows, lambda rows: rows + [zero])
        rows = [
            first[side, 0, p * BS : (p + 1) * BS] * line_of(lines, outer_group, p + at, outer_group)
            for p in range(REACH)
        ]
        corners[side] = split(jnp.concatenate(pad[side](rows), axis=0))
        rows = [
            first[side, 1, s * BS : (s + 1) * BS]
            * line_of(lines, edge_group, s + 1 - at, outer_group)
            for s in range(REACH)
        ]
        across[side] = split(jnp.concatenate(pad[1 - side](rows), axis=0))
        for s in range(REACH):
            part = jnp.where(upper_half, rows[s][HALF:], rows[s][:HALF])
            for t in range(REACH):
                k = t - s + offsets[side]
                if 0 <= k < SPAN:
                    blocks[0, side, s, k] = part[:, (t + at) * BS : (t + at + 1) * BS]
        send(side, 0, square_out)

    def send(side, i, ref):
        for s in range(REACH):
            a = ends[side] + s
            k0, k1 = span_of(a, count, i == 0)
            k0, k1 = (0, k0) if side == 0 else (k1, SPAN)
            store = pltpu.make_async_copy(
                blocks.at[i, side, s, pl.ds(k0, k1 - k0)],
                ref.at[a, pl.ds(k0, k1 - k0)],
                sems.at[i, side, s],
            )
            store.start()
            stores.append(store)

    def second_dots(side):
        p_ref = given[side][6]
        reach_out = [p_ref[q, 0] for q in range(2)]
        inside = [p_ref[q, 1] for q in range(2)]
        return (
            product([(reach_out, corners[side]), (inside, across[side])]),
            product([(reach_out, across[side])], True),
        )

    def keep_last(side, value):
        last[side, 0], last[side, 1] = value

    def emit(side):
        seed = given[side][2]
        at = shift[side]
        edge_group, outer_group = edge_groups[side], outer_groups[side]
        for s in range(REACH):
            rows = slice(s * HALF, (s + 1) * HALF)
            far = last[side, 0, rows] * (line_of(lines, edge_group, s + 1 - at, outer_group) * 0.5)
            close = last[side, 1, rows] * (line_of(lines, edge_group, s + 1 - at, edge_group) * 0.5)
            for t in range(REACH):
                k = t - s + offsets[side]
                if 0 <= k < SPAN:
                    lanes = slice((t + at) * BS, (t + at + 1) * BS)
                    blocks[1, side, s, k] = seed[s, k] - far[:, lanes]
                k = t - s + REACH
                lanes = slice((t + 1 - at) * BS, (t + 2 - at) * BS)
                blocks[1, side, s, k] = seed[s, k] - close[:, lanes]
        send(side, 1, sign_out)

    for s in range(GROUP):
        a = count - GROUP + s
        k0, k1 = span_of(a, count, False)
        store = pltpu.make_async_copy(
            sign_last.at[s, pl.ds(k0, k1 - k0)], sign_out.at[a, pl.ds(k0, k1 - k0)], last_sems.at[s]
        )
        store.start()
        stores.append(store)
    build(0)
    value = dots(0)
    build(1)
    keep_first(0, value)
    value = dots(1)
    masks(0)
    keep_first(1, value)
    value = second_dots(0)
    masks(1)
    keep_last(0, value)
    value = second_dots(1)
    emit(0)
    keep_last(1, value)
    emit(1)
    for store in stores:
        store.wait()


def shards(matrix, pattern, *, axes, half_axis):
    count = matrix.shape[0]
    groups = count // GROUP
    flags = pattern.T
    vmem = pl.BlockSpec(memory_space=pltpu.VMEM)
    hbm = pl.BlockSpec(memory_space=pl.ANY)
    params = pltpu.CompilerParams(vmem_limit_bytes=LIMIT)

    top, bottom = matrix[:REACH, REACH:], matrix[count - REACH :, : REACH + 1]
    matrix, top, bottom = lax.optimization_barrier((matrix, top, bottom))
    edge = jax.ShapeDtypeStruct((REACH * HALF, (REACH + 1) * BS), F32)
    to_left, to_right = pl.pallas_call(
        edge_kernel,
        out_shape=(edge, edge),
        in_specs=[vmem] * 2,
        out_specs=[vmem] * 2,
        compiler_params=params,
        cost_estimate=pl.CostEstimate(
            flops=1 * 10**9, bytes_accessed=2**20, transcendentals=0
        ),
    )(top, bottom)
    size = 1
    for axis in axes:
        size *= lax.axis_size(axis)
    swap = [(0, 1), (1, 0)]
    other = lax.ppermute(matrix, half_axis, swap)
    forward = [(i, (i + 1) % size) for i in range(size)]
    backward = [(target, source) for source, target in forward]
    high_own = lax.ppermute(to_left, axes, backward)
    low_own = lax.ppermute(to_right, axes, forward)

    band = jax.ShapeDtypeStruct(matrix.shape, F32)
    seed = jax.ShapeDtypeStruct((REACH, SPAN, HALF, BS), F32)
    full = jax.ShapeDtypeStruct((2, groups, WIDE, 3 * WIDE), BF)
    mine = jax.ShapeDtypeStruct((2, groups, GROUP * HALF, 3 * WIDE), BF)
    keep = jax.ShapeDtypeStruct((2, 3 * groups, WIDE, WIDE), BF)
    lines = jax.ShapeDtypeStruct(((groups + 2) * GROUP, 3 * WIDE), F32)
    rows = jax.ShapeDtypeStruct((GROUP,) + matrix.shape[1:], F32)
    first_rows = jax.ShapeDtypeStruct((groups - 1,) + rows.shape, F32)
    square, low_seed, full, mine, keep, lines, sign_first = pl.pallas_call(
        functools.partial(first_kernel, axes=axes, half_axis=half_axis),
        out_shape=[band, seed, full, mine, keep, lines, first_rows],
        in_specs=[vmem] * 3,
        out_specs=[hbm] + [vmem] * 6,
        scratch_shapes=[
            pltpu.VMEM((groups,) + rows.shape, F32),
            pltpu.VMEM((2 * groups - 1 + 3 * groups - 4, WIDE, WIDE), F32),
            pltpu.SemaphoreType.DMA((2, count)),
        ],
        compiler_params=params,
        cost_estimate=pl.CostEstimate(
            flops=3 * 2 * 16 * WIDE**3, bytes_accessed=16 * 2**20, transcendentals=0
        ),
    )(matrix, other, flags)

    low_own, high_own, low_seed = lax.optimization_barrier((low_own, high_own, low_seed))
    low_other = lax.ppermute(low_own, half_axis, swap)
    high_other = lax.ppermute(high_own, half_axis, swap)

    ends_out = [
        jax.ShapeDtypeStruct((REACH * BS, WIDE), F32),
        jax.ShapeDtypeStruct((REACH * BS, WIDE), F32),
        jax.ShapeDtypeStruct((2, REACH * BS, WIDE), BF),
        jax.ShapeDtypeStruct((2, 2, REACH * HALF, WIDE), BF),
    ]
    sign, sign_last, high_seed, *ends = pl.pallas_call(
        last_kernel,
        out_shape=[band, rows, seed] + ends_out * 2,
        in_specs=[vmem] * 6,
        out_specs=[hbm] + [vmem] * 10,
        scratch_shapes=[
            pltpu.VMEM((2, GROUP * HALF, WIDE), F32),
            pltpu.SemaphoreType.DMA((2, count)),
        ],
        compiler_params=params,
        cost_estimate=pl.CostEstimate(
            flops=3 * 2 * 4 * WIDE**3, bytes_accessed=4 * 2**20, transcendentals=0
        ),
    )(matrix, lines, full, mine, keep, sign_first)

    return tuple(
        pl.pallas_call(
            functools.partial(border_kernel, half_axis=half_axis),
            out_shape=(band, band),
            in_specs=[vmem] * 16 + [hbm] * 2,
            out_specs=[hbm] * 2,
            scratch_shapes=[
                pltpu.VMEM((2, 2, WIDE, 2 * WIDE), BF),
                pltpu.VMEM((2, 2, REACH * BS, WIDE), F32),
                pltpu.VMEM((2, 2, REACH * HALF, WIDE), F32),
                pltpu.VMEM((2, 2, REACH, SPAN, HALF, BS), F32),
                pltpu.SemaphoreType.DMA((2, 2, REACH)),
                pltpu.SemaphoreType.DMA((GROUP,)),
            ],
            input_output_aliases={16: 0, 17: 1},
            compiler_params=params,
            cost_estimate=pl.CostEstimate(
                flops=3 * 2 * 4 * WIDE**3, bytes_accessed=2 * 2**20, transcendentals=0
            ),
        )(
            low_own, low_other, high_own, high_other, lines, sign_last, low_seed, *ends[:4], high_seed,
            *ends[4:], square, sign,
        )
    )


def solution(mesh):
    band = P(("group", "row", "col"), None, "rep", None)
    return jax.shard_map(
        functools.partial(shards, axes=("row", "col"), half_axis="rep"),
        mesh=mesh,
        in_specs=(band, P("group", None)),
        out_specs=(band, band),
        check_vma=False,
    )
```

```python
import functools

import jax
import jax.numpy as jnp
from jax import lax
from jax.experimental import pallas as pl
from jax.experimental.pallas import tpu as pltpu
from jax.sharding import PartitionSpec as P

REACH = 3
SPAN = 7
BS = 64
HALF = 32
GROUP = 4
WIDE = GROUP * BS
BF = jnp.bfloat16
F32 = jnp.float32
LIMIT = 32 * 1024 * 1024


def split(x):
    hi = x.astype(BF)
    return hi, (x - hi.astype(F32)).astype(BF)


def product(pairs, transposed=False):
    side = 1 if transposed else 0
    high, low = [jnp.concatenate([a[p] for a, _ in pairs], axis=1) for p in range(2)]
    right = [jnp.concatenate([b[p] for _, b in pairs], axis=side) for p in range(2)]
    dot = functools.partial(
        lax.dot_general,
        dimension_numbers=(((1,), (side,)), ((), ())),
        preferred_element_type=F32,
    )
    both = dot(jnp.concatenate([high, low], axis=0), right[0])
    count = high.shape[0]
    return both[:count] + (both[count:] + dot(high, right[1]))


def turn(x):
    return split((x[0].astype(F32) + x[1].astype(F32)).T)


def write_lines(pat, lines, first, groups):
    total = pat.shape[1]
    rows = lines.shape[0]
    iota = functools.partial(lax.broadcasted_iota, jnp.int32)
    dot = functools.partial(lax.dot_general, preferred_element_type=F32)
    wanted = lax.rem(first - GROUP + total + iota((rows, total), 0), total)
    chosen = (iota((rows, total), 1) == wanted).astype(BF)
    flags = dot(chosen, pat[...].astype(BF), (((1,), (1,)), ((), ())))
    place = iota((rows, 1), 0) % GROUP
    spread = jnp.concatenate(
        [jnp.where(place == s, flags, 0.0) for s in range(GROUP)], axis=1
    ).astype(BF)
    block = iota((SPAN, 3 * WIDE), 1) // BS - iota((SPAN, 3 * WIDE), 0) - 1
    spots = jnp.concatenate([(block == s).astype(BF) for s in range(GROUP)], axis=0)
    lines[...] = dot(spread, spots, (((1,), (0,)), ((), ())))


def line_of(lines, g, s, h):
    at = (g + 1) * GROUP + s
    lo = (h - g + 1) * WIDE
    return lines[at : at + 1, lo : lo + WIDE]


def span_of(a, count, is_square):
    if a < REACH:
        return (REACH - a if is_square else 2 * REACH - a), SPAN
    s = a - (count - REACH)
    if s >= 0:
        return 0, (2 * REACH - s if is_square else REACH - s)
    return 0, SPAN


def edge_kernel(top, bottom, to_left, to_right):
    for source, target in ((top, to_left), (bottom, to_right)):
        for s in range(REACH):
            for t in range(2):
                target[s * HALF : (s + 1) * HALF, t * 2 * BS : (t + 1) * 2 * BS] = jnp.concatenate(
                    [source[s, 2 * t], source[s, 2 * t + 1]], axis=1
                )


class Interior:
    def __init__(self, own, lines, full, mine, keep):
        self.own = own
        self.lines = lines
        self.full = full
        self.mine = mine
        self.keep = keep
        self.count = own.shape[0]
        self.groups = self.count // GROUP
        self.stores = []

    def part(self, g, h, rows=slice(None)):
        at = (h - g + 1) * WIDE
        return [self.full[p, g, rows, at : at + WIDE] for p in range(2)]

    def my_part(self, g, h):
        at = (h - g + 1) * WIDE
        return [self.mine[p, g, :, at : at + WIDE] for p in range(2)]

    def tile(self, g, h):
        return 3 * g + h - g + 1

    def kept(self, g, h):
        return [self.keep[p, self.tile(g, h)] for p in range(2)]

    def near(self, g):
        return [e for e in (g - 1, g, g + 1) if 0 <= e < self.groups]

    def second(self, g, h, sign, seed, result):
        span = range(1 if h > g else 0, GROUP - 1 if h < g else GROUP)
        rows = slice(span[0] * HALF, (span[-1] + 1) * HALF)

        def dot():
            return product(
                [
                    ([x[rows] for x in self.my_part(g, e)], self.kept(e, h))
                    for e in self.near(g)
                    if abs(e - h) <= 1
                ]
            )

        def store(value):
            result[rows] = value

        def post():
            for s in span:
                a = g * GROUP + s
                k0, k1 = span_of(a, self.count, False)
                part = result[s * HALF : (s + 1) * HALF] * (line_of(self.lines, g, s, h) * 0.5)
                for t in range(GROUP):
                    k = t + GROUP * (h - g) - s + REACH
                    if 0 <= k < SPAN:
                        block = 1.5 * self.own[a, k] - part[:, t * BS : (t + 1) * BS]
                        if k0 <= k < k1:
                            sign[s, k] = block
                        else:
                            seed[a if a < REACH else a - (self.count - REACH), k] = block

        return dot, store, post

    def far_seed(self, g, seed):
        for s in range(REACH):
            a = s if g == 0 else self.count - REACH + s
            for k in range(0, REACH - s) if g == 0 else range(2 * REACH - s, SPAN):
                seed[s, k] = 1.5 * self.own[a, k]

    def reaching(self, a_ref, b_ref, m_ref, p_ref, g, e, r0):
        rows = slice(r0, r0 + REACH * BS)
        mine_rows = slice(r0 // 2, r0 // 2 + REACH * HALF)
        outer = slice(BS - r0, BS - r0 + REACH * BS)

        def dot():
            out = self.part(g, e)
            return (
                product([([x[outer] for x in turn(out)], out)]),
                product([(self.part(g, g, rows), out)]),
            )

        def store(value):
            a_ref[...], b_ref[...] = value

        def post():
            for p in range(2):
                m_ref[p] = self.part(g, e)[p][rows]
                p_ref[p, 0] = self.my_part(g, e)[p][mine_rows]
                p_ref[p, 1] = self.my_part(g, g)[p][mine_rows]

        return dot, store, post

    def send(self, g, i, source, target, sems):
        for s in range(GROUP):
            a = g * GROUP + s
            k0, k1 = span_of(a, self.count, i == 0)
            store = pltpu.make_async_copy(
                source.at[s, pl.ds(k0, k1 - k0)], target.at[a, pl.ds(k0, k1 - k0)], sems.at[i, a]
            )
            store.start()
            self.stores.append(store)

    def finish(self):
        for store in self.stores:
            store.wait()


def count_dots(steps):
    return sum(isinstance(step, tuple) for step in steps)


def staggered(steps):
    pending = []
    for step in steps:
        if not isinstance(step, tuple):
            pending.append(step)
            continue
        dot, store, post = step
        value = dot()
        for work in pending:
            work()
        store(value)
        pending = [post]
    for work in pending:
        work()


def first_kernel(
    own, other, pat, square_out, sign_out, seed, full, mine, keep, lines, low_a, low_b, low_m, low_p,
    high_a, high_b, high_m, high_p, square, sign, results, sems, *, axes, half_axis
):
    it = Interior(own, lines, full, mine, keep)
    groups = it.groups
    upper_half = lax.axis_index(half_axis) == 1

    def build(g):
        for s in range(GROUP):
            a = g * GROUP + s
            for t in range(3 * GROUP // 2):
                ks = [2 * t + e - s - 1 for e in range(2)]
                lanes = slice(t * 2 * BS, (t + 1) * 2 * BS)
                rows = slice(s * BS, (s + 1) * BS)
                mine_rows = slice(s * HALF, (s + 1) * HALF)
                if all(k < 0 or k >= SPAN for k in ks):
                    for p in range(2):
                        full[p, g, rows, lanes] = jnp.zeros((BS, 2 * BS), BF)
                        mine[p, g, mine_rows, lanes] = jnp.zeros((HALF, 2 * BS), BF)
                    continue
                two = [
                    jnp.concatenate(
                        [src[a, k] if 0 <= k < SPAN else jnp.zeros((HALF, BS), F32) for k in ks],
                        axis=1,
                    )
                    for src in (own, other)
                ]
                for p, (x, y) in enumerate(zip(*[split(x) for x in two])):
                    mine[p, g, mine_rows, lanes] = x
                    full[p, g, rows, lanes] = jnp.concatenate(
                        [jnp.where(upper_half, y, x), jnp.where(upper_half, x, y)], axis=0
                    )

    def squares(g, h, result):
        pairs = []
        for e in (g - 1, g, g + 1):
            if abs(e - h) <= 1:
                inside = 0 <= e < groups
                pairs.append((e, (lambda e=e: it.part(e, h)) if inside else (lambda e=e: turn(it.part(h, e)))))
        span = range(1 if h > g else 0, GROUP)
        rows = slice(span[0] * BS, WIDE)

        def dot():
            return product([([x[rows] for x in it.part(g, e)], f()) for e, f in pairs])

        def store(value):
            result[rows] = value

        def post():
            masked = [jnp.zeros((BS, WIDE), F32)] * GROUP
            for s in span:
                masked[s] = result[s * BS : (s + 1) * BS] * line_of(lines, g, s, h)
            for s in range(GROUP):
                for p, x in enumerate(split(masked[s])):
                    keep[p, it.tile(g, h), s * BS : (s + 1) * BS] = x
            for s in span:
                part = jnp.where(upper_half, masked[s][HALF:], masked[s][:HALF])
                for t in range(GROUP):
                    k = t + GROUP * (h - g) - s + REACH
                    if 0 <= k < SPAN:
                        staged[g][s, k] = part[:, t * BS : (t + 1) * BS]
            if h == g:
                return
            for c in range(0, GROUP, 2):
                turned = jnp.concatenate(masked[c : c + 2], axis=0).T
                lanes = slice(c * BS, (c + 2) * BS)
                for p, x in enumerate(split(turned)):
                    keep[p, it.tile(h, g), :, lanes] = x
                for t in range(GROUP):
                    rows = turned[t * BS : (t + 1) * BS]
                    part = jnp.where(upper_half, rows[HALF:], rows[:HALF])
                    for s in range(c, c + 2):
                        k = s + GROUP * (g - h) - t + REACH
                        if 0 <= k < SPAN:
                            staged[h][t, k] = part[:, (s - c) * BS : (s - c + 1) * BS]

        return dot, store, post

    staged = [square.at[g] for g in range(groups)]

    def begin():
        write_lines(pat, lines, lax.axis_index(axes) * it.count, groups)
        it.far_seed(0, seed)

    build(0)
    build(1)
    steps = [begin]
    for g in range(groups):
        if g + 1 < groups:
            steps.append(squares(g, g + 1, results.at[count_dots(steps)]))
            if g + 2 < groups:
                steps.append(functools.partial(build, g + 2))
        steps.append(squares(g, g, results.at[count_dots(steps)]))
        steps.append(functools.partial(it.send, g, 0, staged[g], square_out, sems))
    for g in range(groups - 1):
        for h in it.near(g):
            steps.append(it.second(g, h, sign.at[g], seed, results.at[count_dots(steps)]))
        steps.append(functools.partial(it.send, g, 1, sign.at[g], sign_out, sems))
    steps.append(it.reaching(low_a, low_b, low_m, low_p, 0, -1, 0))
    steps.append(it.reaching(high_a, high_b, high_m, high_p, groups - 1, groups, BS))
    staggered(steps)
    it.finish()


def last_kernel(own, lines, full, mine, keep, sign, seed, results):
    it = Interior(own, lines, full, mine, keep)
    last = it.groups - 1
    steps = [it.second(last, h, sign, seed, results.at[i]) for i, h in enumerate(it.near(last))]
    steps.append(functools.partial(it.far_seed, last, seed))

    staggered(steps)


def border_kernel(
    low_own, low_other, high_own, high_other, lines, sign_last, low_seed, low_a, low_b, low_m, low_p, high_seed,
    high_a, high_b, high_m, high_p, square_in, sign_in, square_out, sign_out, halo, first, last, blocks, sems, last_sems,
    *, half_axis
):
    count = square_in.shape[0]
    groups = count // GROUP
    upper_half = lax.axis_index(half_axis) == 1
    ends = (0, count - REACH)
    given = (
        (low_own, low_other, low_seed, low_a, low_b, low_m, low_p),
        (high_own, high_other, high_seed, high_a, high_b, high_m, high_p),
    )
    shift = (1, 0)
    zero = jnp.zeros((BS, WIDE), F32)

    def build(side):
        mine, theirs = given[side][:2]
        below = REACH if side == 0 else 0
        whole_rows = []
        for p in range(REACH):
            rows = slice(p * HALF, (p + 1) * HALF)
            whole_rows.append(
                jnp.concatenate(
                    [
                        jnp.where(upper_half, theirs[rows, :], mine[rows, :]),
                        jnp.where(upper_half, mine[rows, :], theirs[rows, :]),
                    ],
                    axis=0,
                )
            )

        def block(p, c):
            k = c - p + below
            if 0 <= k <= REACH:
                return whole_rows[p][:, k * BS : (k + 1) * BS]
            k = p - c + below
            if 0 <= c < REACH and 0 <= k <= REACH:
                return whole_rows[c][:, k * BS : (k + 1) * BS].T
            return jnp.zeros((BS, BS), F32)

        base = -5 if side == 0 else 0
        for p in range(REACH):
            rows = slice((p + shift[side]) * BS, (p + shift[side] + 1) * BS)
            for t in range(4):
                value = jnp.concatenate([block(p, base + 2 * t), block(p, base + 2 * t + 1)], axis=1)
                for q, x in enumerate(split(value)):
                    halo[side, q, rows, t * 2 * BS : (t + 1) * 2 * BS] = x
        rows = slice(0, BS) if side == 0 else slice(REACH * BS, WIDE)
        for q in range(2):
            halo[side, q, rows, :] = jnp.zeros((BS, 2 * WIDE), BF)

    edge_groups, outer_groups = (0, groups - 1), (-1, groups)
    offsets = (0, 2 * REACH)
    corners = [None, None]
    across = [None, None]
    stores = []

    def dots(side):
        m_ref = given[side][5]
        whole = [halo[side, q] for q in range(2)]
        outer_rows = slice(shift[side] * BS, (shift[side] + REACH) * BS)
        inner = slice(WIDE, 2 * WIDE) if side == 0 else slice(0, WIDE)
        return (
            product([([x[outer_rows] for x in whole], whole)], True),
            product([([m_ref[q] for q in range(2)], [x[:, inner] for x in whole])], True),
        )

    def keep_first(side, value):
        _, _, _, a_ref, b_ref, _, _ = given[side]
        first[side, 0] = value[0] + a_ref[...]
        first[side, 1] = value[1] + b_ref[...]

    def masks(side):
        at = shift[side]
        edge_group, outer_group = edge_groups[side], outer_groups[side]
        pad = (lambda rows: [zero] + rows, lambda rows: rows + [zero])
        rows = [
            first[side, 0, p * BS : (p + 1) * BS] * line_of(lines, outer_group, p + at, outer_group)
            for p in range(REACH)
        ]
        corners[side] = split(jnp.concatenate(pad[side](rows), axis=0))
        rows = [
            first[side, 1, s * BS : (s + 1) * BS]
            * line_of(lines, edge_group, s + 1 - at, outer_group)
            for s in range(REACH)
        ]
        across[side] = split(jnp.concatenate(pad[1 - side](rows), axis=0))
        for s in range(REACH):
            part = jnp.where(upper_half, rows[s][HALF:], rows[s][:HALF])
            for t in range(REACH):
                k = t - s + offsets[side]
                if 0 <= k < SPAN:
                    blocks[0, side, s, k] = part[:, (t + at) * BS : (t + at + 1) * BS]
        send(side, 0, square_out)

    def send(side, i, ref):
        for s in range(REACH):
            a = ends[side] + s
            k0, k1 = span_of(a, count, i == 0)
            k0, k1 = (0, k0) if side == 0 else (k1, SPAN)
            store = pltpu.make_async_copy(
                blocks.at[i, side, s, pl.ds(k0, k1 - k0)],
                ref.at[a, pl.ds(k0, k1 - k0)],
                sems.at[i, side, s],
            )
            store.start()
            stores.append(store)

    def second_dots(side):
        p_ref = given[side][6]
        reach_out = [p_ref[q, 0] for q in range(2)]
        inside = [p_ref[q, 1] for q in range(2)]
        return (
            product([(reach_out, corners[side]), (inside, across[side])]),
            product([(reach_out, across[side])], True),
        )

    def keep_last(side, value):
        last[side, 0], last[side, 1] = value

    def emit(side):
        seed = given[side][2]
        at = shift[side]
        edge_group, outer_group = edge_groups[side], outer_groups[side]
        for s in range(REACH):
            rows = slice(s * HALF, (s + 1) * HALF)
            far = last[side, 0, rows] * (line_of(lines, edge_group, s + 1 - at, outer_group) * 0.5)
            close = last[side, 1, rows] * (line_of(lines, edge_group, s + 1 - at, edge_group) * 0.5)
            for t in range(REACH):
                k = t - s + offsets[side]
                if 0 <= k < SPAN:
                    lanes = slice((t + at) * BS, (t + at + 1) * BS)
                    blocks[1, side, s, k] = seed[s, k] - far[:, lanes]
                k = t - s + REACH
                lanes = slice((t + 1 - at) * BS, (t + 2 - at) * BS)
                blocks[1, side, s, k] = seed[s, k] - close[:, lanes]
        send(side, 1, sign_out)

    for s in range(GROUP):
        a = count - GROUP + s
        k0, k1 = span_of(a, count, False)
        store = pltpu.make_async_copy(
            sign_last.at[s, pl.ds(k0, k1 - k0)], sign_out.at[a, pl.ds(k0, k1 - k0)], last_sems.at[s]
        )
        store.start()
        stores.append(store)
    build(0)
    value = dots(0)
    build(1)
    keep_first(0, value)
    value = dots(1)
    masks(0)
    keep_first(1, value)
    value = second_dots(0)
    masks(1)
    keep_last(0, value)
    value = second_dots(1)
    emit(0)
    keep_last(1, value)
    emit(1)
    for store in stores:
        store.wait()


def shards(matrix, pattern, *, axes, half_axis):
    count = matrix.shape[0]
    groups = count // GROUP
    flags = pattern.T
    vmem = pl.BlockSpec(memory_space=pltpu.VMEM)
    hbm = pl.BlockSpec(memory_space=pl.ANY)
    params = pltpu.CompilerParams(vmem_limit_bytes=LIMIT)

    top, bottom = matrix[:REACH, REACH:], matrix[count - REACH :, : REACH + 1]
    matrix, top, bottom = lax.optimization_barrier((matrix, top, bottom))
    edge = jax.ShapeDtypeStruct((REACH * HALF, (REACH + 1) * BS), F32)
    to_left, to_right = pl.pallas_call(
        edge_kernel,
        out_shape=(edge, edge),
        in_specs=[vmem] * 2,
        out_specs=[vmem] * 2,
        compiler_params=params,
        cost_estimate=pl.CostEstimate(
            flops=1 * 10**9, bytes_accessed=2**20, transcendentals=0
        ),
    )(top, bottom)
    size = 1
    for axis in axes:
        size *= lax.axis_size(axis)
    swap = [(0, 1), (1, 0)]
    other = lax.ppermute(matrix, half_axis, swap)
    forward = [(i, (i + 1) % size) for i in range(size)]
    backward = [(target, source) for source, target in forward]
    high_own = lax.ppermute(to_left, axes, backward)
    low_own = lax.ppermute(to_right, axes, forward)

    band = jax.ShapeDtypeStruct(matrix.shape, F32)
    seed = jax.ShapeDtypeStruct((REACH, SPAN, HALF, BS), F32)
    full = jax.ShapeDtypeStruct((2, groups, WIDE, 3 * WIDE), BF)
    mine = jax.ShapeDtypeStruct((2, groups, GROUP * HALF, 3 * WIDE), BF)
    keep = jax.ShapeDtypeStruct((2, 3 * groups, WIDE, WIDE), BF)
    lines = jax.ShapeDtypeStruct(((groups + 2) * GROUP, 3 * WIDE), F32)
    ends_out = [
        jax.ShapeDtypeStruct((REACH * BS, WIDE), F32),
        jax.ShapeDtypeStruct((REACH * BS, WIDE), F32),
        jax.ShapeDtypeStruct((2, REACH * BS, WIDE), BF),
        jax.ShapeDtypeStruct((2, 2, REACH * HALF, WIDE), BF),
    ]
    rows = jax.ShapeDtypeStruct((GROUP,) + matrix.shape[1:], F32)
    square, sign, low_seed, full, mine, keep, lines, *ends = pl.pallas_call(
        functools.partial(first_kernel, axes=axes, half_axis=half_axis),
        out_shape=[band, band, seed, full, mine, keep, lines] + ends_out * 2,
        in_specs=[vmem] * 3,
        out_specs=[hbm] * 2 + [vmem] * 13,
        scratch_shapes=[
            pltpu.VMEM((groups,) + rows.shape, F32),
            pltpu.VMEM((groups - 1,) + rows.shape, F32),
            pltpu.VMEM((2 * groups - 1 + 3 * groups - 4, WIDE, WIDE), F32),
            pltpu.SemaphoreType.DMA((2, count)),
        ],
        compiler_params=params,
        cost_estimate=pl.CostEstimate(
            flops=3 * 2 * 16 * WIDE**3, bytes_accessed=16 * 2**20, transcendentals=0
        ),
    )(matrix, other, flags)

    low_own, high_own, low_seed = lax.optimization_barrier((low_own, high_own, low_seed))
    low_other = lax.ppermute(low_own, half_axis, swap)
    high_other = lax.ppermute(high_own, half_axis, swap)

    sign_last, high_seed = pl.pallas_call(
        last_kernel,
        out_shape=[rows, seed],
        in_specs=[vmem] * 5,
        out_specs=[vmem] * 2,
        scratch_shapes=[pltpu.VMEM((2, GROUP * HALF, WIDE), F32)],
        compiler_params=params,
        cost_estimate=pl.CostEstimate(
            flops=3 * 2 * 4 * WIDE**3, bytes_accessed=4 * 2**20, transcendentals=0
        ),
    )(matrix, lines, full, mine, keep)

    return tuple(
        pl.pallas_call(
            functools.partial(border_kernel, half_axis=half_axis),
            out_shape=(band, band),
            in_specs=[vmem] * 16 + [hbm] * 2,
            out_specs=[hbm] * 2,
            scratch_shapes=[
                pltpu.VMEM((2, 2, WIDE, 2 * WIDE), BF),
                pltpu.VMEM((2, 2, REACH * BS, WIDE), F32),
                pltpu.VMEM((2, 2, REACH * HALF, WIDE), F32),
                pltpu.VMEM((2, 2, REACH, SPAN, HALF, BS), F32),
                pltpu.SemaphoreType.DMA((2, 2, REACH)),
                pltpu.SemaphoreType.DMA((GROUP,)),
            ],
            input_output_aliases={16: 0, 17: 1},
            compiler_params=params,
            cost_estimate=pl.CostEstimate(
                flops=3 * 2 * 4 * WIDE**3, bytes_accessed=2 * 2**20, transcendentals=0
            ),
        )(
            low_own, low_other, high_own, high_other, lines, sign_last, low_seed, *ends[:4], high_seed,
            *ends[4:], square, sign,
        )
    )


def solution(mesh):
    band = P(("group", "row", "col"), None, "rep", None)
    return jax.shard_map(
        functools.partial(shards, axes=("row", "col"), half_axis="rep"),
        mesh=mesh,
        in_specs=(band, P("group", None)),
        out_specs=(band, band),
        check_vma=False,
    )
```

```python
import functools

import jax
import jax.numpy as jnp
from jax import lax
from jax.experimental import pallas as pl
from jax.experimental.pallas import tpu as pltpu
from jax.sharding import PartitionSpec as P

REACH = 3
SPAN = 7
BS = 64
HALF = 32
GROUP = 4
WIDE = GROUP * BS
BF = jnp.bfloat16
F32 = jnp.float32
LIMIT = 32 * 1024 * 1024
EDGE_LIMIT = int(53 * 1024 * 1024)


def split(x):
    hi = x.astype(BF)
    return hi, (x - hi.astype(F32)).astype(BF)


def product(pairs, transposed=False):
    side = 1 if transposed else 0
    high, low = [jnp.concatenate([a[p] for a, _ in pairs], axis=1) for p in range(2)]
    right = [jnp.concatenate([b[p] for _, b in pairs], axis=side) for p in range(2)]
    dot = functools.partial(
        lax.dot_general,
        dimension_numbers=(((1,), (side,)), ((), ())),
        preferred_element_type=F32,
    )
    both = dot(jnp.concatenate([high, low], axis=0), right[0])
    count = high.shape[0]
    return both[:count] + (both[count:] + dot(high, right[1]))


def turn(x):
    return split((x[0].astype(F32) + x[1].astype(F32)).T)


def line_kernel(pat, lines, *, axes, count):
    first = lax.axis_index(axes) * count
    total = pat.shape[1]
    rows = lines.shape[0]
    iota = functools.partial(lax.broadcasted_iota, jnp.int32)
    dot = functools.partial(lax.dot_general, preferred_element_type=F32)
    wanted = lax.rem(first - GROUP + total + iota((rows, total), 0), total)
    chosen = (iota((rows, total), 1) == wanted).astype(BF)
    flags = dot(chosen, pat[...].astype(BF), (((1,), (1,)), ((), ())))
    place = iota((rows, 1), 0) % GROUP
    spread = jnp.concatenate(
        [jnp.where(place == s, flags, 0.0) for s in range(GROUP)], axis=1
    ).astype(BF)
    block = iota((SPAN, 3 * WIDE), 1) // BS - iota((SPAN, 3 * WIDE), 0) - 1
    spots = jnp.concatenate([(block == s).astype(BF) for s in range(GROUP)], axis=0)
    lines[...] = dot(spread, spots, (((1,), (0,)), ((), ())))


def line_of(lines, g, s, h):
    at = (g + 1) * GROUP + s
    lo = (h - g + 1) * WIDE
    return lines[at : at + 1, lo : lo + WIDE]


def span_of(a, count, is_square):
    if a < REACH:
        return (REACH - a if is_square else 2 * REACH - a), SPAN
    s = a - (count - REACH)
    if s >= 0:
        return 0, (2 * REACH - s if is_square else REACH - s)
    return 0, SPAN


def edge_kernel(matrix, to_left, to_right, blocks, sems):
    count = matrix.shape[0]
    loads = [
        pltpu.make_async_copy(source, blocks.at[i], sems.at[i])
        for i, source in enumerate(
            (
                matrix.at[pl.ds(0, REACH), pl.ds(REACH, REACH + 1)],
                matrix.at[pl.ds(count - REACH, REACH), pl.ds(0, REACH + 1)],
            )
        )
    ]
    for load in loads:
        load.start()
    for i, target in enumerate((to_left, to_right)):
        loads[i].wait()
        for s in range(REACH):
            for t in range(2):
                target[s * HALF : (s + 1) * HALF, t * 2 * BS : (t + 1) * 2 * BS] = jnp.concatenate(
                    [blocks[i, s, 2 * t], blocks[i, s, 2 * t + 1]], axis=1
                )


class Interior:
    def __init__(self, own, lines, full, mine, keep):
        self.own = own
        self.lines = lines
        self.full = full
        self.mine = mine
        self.keep = keep
        self.count = own.shape[0]
        self.groups = self.count // GROUP
        self.stores = []

    def part(self, g, h, rows=slice(None)):
        at = (h - g + 1) * WIDE
        return [self.full[p, g, rows, at : at + WIDE] for p in range(2)]

    def my_part(self, g, h):
        at = (h - g + 1) * WIDE
        return [self.mine[p, g, :, at : at + WIDE] for p in range(2)]

    def tile(self, g, h):
        return 3 * g + h - g + 1

    def kept(self, g, h):
        return [self.keep[p, self.tile(g, h)] for p in range(2)]

    def near(self, g):
        return [e for e in (g - 1, g, g + 1) if 0 <= e < self.groups]

    def second(self, g, h, sign, seed, result):
        span = range(1 if h > g else 0, GROUP - 1 if h < g else GROUP)
        rows = slice(span[0] * HALF, (span[-1] + 1) * HALF)

        def dot():
            return product(
                [
                    ([x[rows] for x in self.my_part(g, e)], self.kept(e, h))
                    for e in self.near(g)
                    if abs(e - h) <= 1
                ]
            )

        def store(value):
            result[rows] = value

        def post():
            for s in span:
                a = g * GROUP + s
                k0, k1 = span_of(a, self.count, False)
                part = result[s * HALF : (s + 1) * HALF] * (line_of(self.lines, g, s, h) * 0.5)
                for t in range(GROUP):
                    k = t + GROUP * (h - g) - s + REACH
                    if 0 <= k < SPAN:
                        block = 1.5 * self.own[a, k] - part[:, t * BS : (t + 1) * BS]
                        if k0 <= k < k1:
                            sign[s, k] = block
                        else:
                            seed[a if a < REACH else a - (self.count - REACH), k] = block

        return dot, store, post

    def far_seed(self, g, seed):
        for s in range(REACH):
            a = s if g == 0 else self.count - REACH + s
            for k in range(0, REACH - s) if g == 0 else range(2 * REACH - s, SPAN):
                seed[s, k] = 1.5 * self.own[a, k]

    def reaching(self, a_ref, b_ref, m_ref, p_ref, g, e, r0):
        rows = slice(r0, r0 + REACH * BS)
        mine_rows = slice(r0 // 2, r0 // 2 + REACH * HALF)
        outer = slice(BS - r0, BS - r0 + REACH * BS)

        def dot():
            out = self.part(g, e)
            return (
                product([([x[outer] for x in turn(out)], out)]),
                product([(self.part(g, g, rows), out)]),
            )

        def store(value):
            a_ref[...], b_ref[...] = value

        def post():
            for p in range(2):
                m_ref[p] = self.part(g, e)[p][rows]
                p_ref[p, 0] = self.my_part(g, e)[p][mine_rows]
                p_ref[p, 1] = self.my_part(g, g)[p][mine_rows]

        return dot, store, post

    def send(self, g, i, source, target, sems):
        for s in range(GROUP):
            a = g * GROUP + s
            k0, k1 = span_of(a, self.count, i == 0)
            store = pltpu.make_async_copy(
                source.at[s, pl.ds(k0, k1 - k0)], target.at[a, pl.ds(k0, k1 - k0)], sems.at[i, a]
            )
            store.start()
            self.stores.append(store)

    def finish(self):
        for store in self.stores:
            store.wait()


def count_dots(steps):
    return sum(isinstance(step, tuple) for step in steps)


def staggered(steps):
    pending = []
    for step in steps:
        if not isinstance(step, tuple):
            pending.append(step)
            continue
        dot, store, post = step
        value = dot()
        for work in pending:
            work()
        store(value)
        pending = [post]
    for work in pending:
        work()


def first_kernel(
    own, other, lines, square_out, sign_out, seed, full, mine, keep, low_a, low_b, low_m, low_p,
    high_a, high_b, high_m, high_p, square, sign, results, sems, *, half_axis
):
    it = Interior(own, lines, full, mine, keep)
    groups = it.groups
    upper_half = lax.axis_index(half_axis) == 1

    def build(g):
        for s in range(GROUP):
            a = g * GROUP + s
            for t in range(3 * GROUP // 2):
                ks = [2 * t + e - s - 1 for e in range(2)]
                lanes = slice(t * 2 * BS, (t + 1) * 2 * BS)
                rows = slice(s * BS, (s + 1) * BS)
                mine_rows = slice(s * HALF, (s + 1) * HALF)
                if all(k < 0 or k >= SPAN for k in ks):
                    for p in range(2):
                        full[p, g, rows, lanes] = jnp.zeros((BS, 2 * BS), BF)
                        mine[p, g, mine_rows, lanes] = jnp.zeros((HALF, 2 * BS), BF)
                    continue
                two = [
                    jnp.concatenate(
                        [src[a, k] if 0 <= k < SPAN else jnp.zeros((HALF, BS), F32) for k in ks],
                        axis=1,
                    )
                    for src in (own, other)
                ]
                for p, (x, y) in enumerate(zip(*[split(x) for x in two])):
                    mine[p, g, mine_rows, lanes] = x
                    full[p, g, rows, lanes] = jnp.concatenate(
                        [jnp.where(upper_half, y, x), jnp.where(upper_half, x, y)], axis=0
                    )

    def squares(g, h, result):
        pairs = []
        for e in (g - 1, g, g + 1):
            if abs(e - h) <= 1:
                inside = 0 <= e < groups
                pairs.append((e, (lambda e=e: it.part(e, h)) if inside else (lambda e=e: turn(it.part(h, e)))))
        span = range(1 if h > g else 0, GROUP)
        rows = slice(span[0] * BS, WIDE)

        def dot():
            return product([([x[rows] for x in it.part(g, e)], f()) for e, f in pairs])

        def store(value):
            result[rows] = value

        def post():
            masked = [jnp.zeros((BS, WIDE), F32)] * GROUP
            for s in span:
                masked[s] = result[s * BS : (s + 1) * BS] * line_of(lines, g, s, h)
            for s in range(GROUP):
                for p, x in enumerate(split(masked[s])):
                    keep[p, it.tile(g, h), s * BS : (s + 1) * BS] = x
            for s in span:
                part = jnp.where(upper_half, masked[s][HALF:], masked[s][:HALF])
                for t in range(GROUP):
                    k = t + GROUP * (h - g) - s + REACH
                    if 0 <= k < SPAN:
                        staged[g][s, k] = part[:, t * BS : (t + 1) * BS]
            if h == g:
                return
            for c in range(0, GROUP, 2):
                turned = jnp.concatenate(masked[c : c + 2], axis=0).T
                lanes = slice(c * BS, (c + 2) * BS)
                for p, x in enumerate(split(turned)):
                    keep[p, it.tile(h, g), :, lanes] = x
                for t in range(GROUP):
                    rows = turned[t * BS : (t + 1) * BS]
                    part = jnp.where(upper_half, rows[HALF:], rows[:HALF])
                    for s in range(c, c + 2):
                        k = s + GROUP * (g - h) - t + REACH
                        if 0 <= k < SPAN:
                            staged[h][t, k] = part[:, (s - c) * BS : (s - c + 1) * BS]

        return dot, store, post

    staged = [square.at[g] for g in range(groups)]

    def begin():
        it.far_seed(0, seed)

    build(0)
    build(1)
    steps = [begin]
    for g in range(groups):
        if g + 1 < groups:
            steps.append(squares(g, g + 1, results.at[count_dots(steps)]))
            if g + 2 < groups:
                steps.append(functools.partial(build, g + 2))
        steps.append(squares(g, g, results.at[count_dots(steps)]))
        steps.append(functools.partial(it.send, g, 0, staged[g], square_out, sems))
    for g in range(groups - 1):
        for h in it.near(g):
            steps.append(it.second(g, h, sign.at[g], seed, results.at[count_dots(steps)]))
        steps.append(functools.partial(it.send, g, 1, sign.at[g], sign_out, sems))
    steps.append(it.reaching(low_a, low_b, low_m, low_p, 0, -1, 0))
    steps.append(it.reaching(high_a, high_b, high_m, high_p, groups - 1, groups, BS))
    staggered(steps)
    it.finish()


def last_kernel(own, lines, full, mine, keep, sign, seed, results):
    it = Interior(own, lines, full, mine, keep)
    last = it.groups - 1
    steps = [it.second(last, h, sign, seed, results.at[i]) for i, h in enumerate(it.near(last))]
    steps.append(functools.partial(it.far_seed, last, seed))

    staggered(steps)


def border_kernel(
    low_own, low_other, high_own, high_other, lines, sign_last, low_seed, low_a, low_b, low_m, low_p, high_seed,
    high_a, high_b, high_m, high_p, square_in, sign_in, square_out, sign_out, halo, first, last, blocks, sems, last_sems,
    *, half_axis
):
    count = square_in.shape[0]
    groups = count // GROUP
    upper_half = lax.axis_index(half_axis) == 1
    ends = (0, count - REACH)
    given = (
        (low_own, low_other, low_seed, low_a, low_b, low_m, low_p),
        (high_own, high_other, high_seed, high_a, high_b, high_m, high_p),
    )
    shift = (1, 0)
    zero = jnp.zeros((BS, WIDE), F32)

    def build(side):
        mine, theirs = given[side][:2]
        below = REACH if side == 0 else 0
        whole_rows = []
        for p in range(REACH):
            rows = slice(p * HALF, (p + 1) * HALF)
            whole_rows.append(
                jnp.concatenate(
                    [
                        jnp.where(upper_half, theirs[rows, :], mine[rows, :]),
                        jnp.where(upper_half, mine[rows, :], theirs[rows, :]),
                    ],
                    axis=0,
                )
            )

        def block(p, c):
            k = c - p + below
            if 0 <= k <= REACH:
                return whole_rows[p][:, k * BS : (k + 1) * BS]
            k = p - c + below
            if 0 <= c < REACH and 0 <= k <= REACH:
                return whole_rows[c][:, k * BS : (k + 1) * BS].T
            return jnp.zeros((BS, BS), F32)

        base = -5 if side == 0 else 0
        for p in range(REACH):
            rows = slice((p + shift[side]) * BS, (p + shift[side] + 1) * BS)
            for t in range(4):
                value = jnp.concatenate([block(p, base + 2 * t), block(p, base + 2 * t + 1)], axis=1)
                for q, x in enumerate(split(value)):
                    halo[side, q, rows, t * 2 * BS : (t + 1) * 2 * BS] = x
        rows = slice(0, BS) if side == 0 else slice(REACH * BS, WIDE)
        for q in range(2):
            halo[side, q, rows, :] = jnp.zeros((BS, 2 * WIDE), BF)

    edge_groups, outer_groups = (0, groups - 1), (-1, groups)
    offsets = (0, 2 * REACH)
    corners = [None, None]
    across = [None, None]
    stores = []

    def dots(side):
        m_ref = given[side][5]
        whole = [halo[side, q] for q in range(2)]
        outer_rows = slice(shift[side] * BS, (shift[side] + REACH) * BS)
        inner = slice(WIDE, 2 * WIDE) if side == 0 else slice(0, WIDE)
        return (
            product([([x[outer_rows] for x in whole], whole)], True),
            product([([m_ref[q] for q in range(2)], [x[:, inner] for x in whole])], True),
        )

    def keep_first(side, value):
        _, _, _, a_ref, b_ref, _, _ = given[side]
        first[side, 0] = value[0] + a_ref[...]
        first[side, 1] = value[1] + b_ref[...]

    def masks(side):
        at = shift[side]
        edge_group, outer_group = edge_groups[side], outer_groups[side]
        pad = (lambda rows: [zero] + rows, lambda rows: rows + [zero])
        rows = [
            first[side, 0, p * BS : (p + 1) * BS] * line_of(lines, outer_group, p + at, outer_group)
            for p in range(REACH)
        ]
        corners[side] = split(jnp.concatenate(pad[side](rows), axis=0))
        rows = [
            first[side, 1, s * BS : (s + 1) * BS]
            * line_of(lines, edge_group, s + 1 - at, outer_group)
            for s in range(REACH)
        ]
        across[side] = split(jnp.concatenate(pad[1 - side](rows), axis=0))
        for s in range(REACH):
            part = jnp.where(upper_half, rows[s][HALF:], rows[s][:HALF])
            for t in range(REACH):
                k = t - s + offsets[side]
                if 0 <= k < SPAN:
                    blocks[0, side, s, k] = part[:, (t + at) * BS : (t + at + 1) * BS]
        send(side, 0, square_out)

    def send(side, i, ref):
        for s in range(REACH):
            a = ends[side] + s
            k0, k1 = span_of(a, count, i == 0)
            k0, k1 = (0, k0) if side == 0 else (k1, SPAN)
            store = pltpu.make_async_copy(
                blocks.at[i, side, s, pl.ds(k0, k1 - k0)],
                ref.at[a, pl.ds(k0, k1 - k0)],
                sems.at[i, side, s],
            )
            store.start()
            stores.append(store)

    def second_dots(side):
        p_ref = given[side][6]
        reach_out = [p_ref[q, 0] for q in range(2)]
        inside = [p_ref[q, 1] for q in range(2)]
        return (
            product([(reach_out, corners[side]), (inside, across[side])]),
            product([(reach_out, across[side])], True),
        )

    def keep_last(side, value):
        last[side, 0], last[side, 1] = value

    def emit(side):
        seed = given[side][2]
        at = shift[side]
        edge_group, outer_group = edge_groups[side], outer_groups[side]
        for s in range(REACH):
            rows = slice(s * HALF, (s + 1) * HALF)
            far = last[side, 0, rows] * (line_of(lines, edge_group, s + 1 - at, outer_group) * 0.5)
            close = last[side, 1, rows] * (line_of(lines, edge_group, s + 1 - at, edge_group) * 0.5)
            for t in range(REACH):
                k = t - s + offsets[side]
                if 0 <= k < SPAN:
                    lanes = slice((t + at) * BS, (t + at + 1) * BS)
                    blocks[1, side, s, k] = seed[s, k] - far[:, lanes]
                k = t - s + REACH
                lanes = slice((t + 1 - at) * BS, (t + 2 - at) * BS)
                blocks[1, side, s, k] = seed[s, k] - close[:, lanes]
        send(side, 1, sign_out)

    for s in range(GROUP):
        a = count - GROUP + s
        k0, k1 = span_of(a, count, False)
        store = pltpu.make_async_copy(
            sign_last.at[s, pl.ds(k0, k1 - k0)], sign_out.at[a, pl.ds(k0, k1 - k0)], last_sems.at[s]
        )
        store.start()
        stores.append(store)
    build(0)
    value = dots(0)
    build(1)
    keep_first(0, value)
    value = dots(1)
    masks(0)
    keep_first(1, value)
    value = second_dots(0)
    masks(1)
    keep_last(0, value)
    value = second_dots(1)
    emit(0)
    keep_last(1, value)
    emit(1)
    for store in stores:
        store.wait()


def shards(matrix, pattern, *, axes, half_axis):
    count = matrix.shape[0]
    groups = count // GROUP
    flags = pattern.T
    vmem = pl.BlockSpec(memory_space=pltpu.VMEM)
    hbm = pl.BlockSpec(memory_space=pl.ANY)
    params = pltpu.CompilerParams(vmem_limit_bytes=LIMIT)

    edge = jax.ShapeDtypeStruct((REACH * HALF, (REACH + 1) * BS), F32)
    to_left, to_right = pl.pallas_call(
        edge_kernel,
        out_shape=(edge, edge),
        in_specs=[hbm],
        out_specs=[vmem] * 2,
        scratch_shapes=[
            pltpu.VMEM((2, REACH, REACH + 1, HALF, BS), F32),
            pltpu.SemaphoreType.DMA((2,)),
        ],
        compiler_params=pltpu.CompilerParams(vmem_limit_bytes=EDGE_LIMIT),
        cost_estimate=pl.CostEstimate(flops=1, bytes_accessed=2**18, transcendentals=0),
    )(matrix)
    lines = pl.pallas_call(
        functools.partial(line_kernel, axes=axes, count=count),
        out_shape=jax.ShapeDtypeStruct(((groups + 2) * GROUP, 3 * WIDE), F32),
        in_specs=[vmem],
        out_specs=vmem,
        compiler_params=params,
        cost_estimate=pl.CostEstimate(flops=2*10**9, bytes_accessed=2**16, transcendentals=0),
    )(flags)

    to_left, to_right, lines = lax.optimization_barrier((to_left, to_right, lines))
    size = 1
    for axis in axes:
        size *= lax.axis_size(axis)
    swap = [(0, 1), (1, 0)]
    other = lax.ppermute(matrix, half_axis, swap)
    forward = [(i, (i + 1) % size) for i in range(size)]
    backward = [(target, source) for source, target in forward]
    high_own = lax.ppermute(to_left, axes, backward)
    low_own = lax.ppermute(to_right, axes, forward)

    band = jax.ShapeDtypeStruct(matrix.shape, F32)
    seed = jax.ShapeDtypeStruct((REACH, SPAN, HALF, BS), F32)
    full = jax.ShapeDtypeStruct((2, groups, WIDE, 3 * WIDE), BF)
    mine = jax.ShapeDtypeStruct((2, groups, GROUP * HALF, 3 * WIDE), BF)
    keep = jax.ShapeDtypeStruct((2, 3 * groups, WIDE, WIDE), BF)
    ends_out = [
        jax.ShapeDtypeStruct((REACH * BS, WIDE), F32),
        jax.ShapeDtypeStruct((REACH * BS, WIDE), F32),
        jax.ShapeDtypeStruct((2, REACH * BS, WIDE), BF),
        jax.ShapeDtypeStruct((2, 2, REACH * HALF, WIDE), BF),
    ]
    rows = jax.ShapeDtypeStruct((GROUP,) + matrix.shape[1:], F32)
    square, sign, low_seed, full, mine, keep, *ends = pl.pallas_call(
        functools.partial(first_kernel, half_axis=half_axis),
        out_shape=[band, band, seed, full, mine, keep] + ends_out * 2,
        in_specs=[vmem] * 3,
        out_specs=[hbm] * 2 + [vmem] * 12,
        scratch_shapes=[
            pltpu.VMEM((groups,) + rows.shape, F32),
            pltpu.VMEM((groups - 1,) + rows.shape, F32),
            pltpu.VMEM((2 * groups - 1 + 3 * groups - 4, WIDE, WIDE), F32),
            pltpu.SemaphoreType.DMA((2, count)),
        ],
        compiler_params=params,
        cost_estimate=pl.CostEstimate(
            flops=3 * 2 * 16 * WIDE**3, bytes_accessed=16 * 2**20, transcendentals=0
        ),
    )(matrix, other, lines)

    low_own, high_own, low_seed = lax.optimization_barrier((low_own, high_own, low_seed))
    low_other = lax.ppermute(low_own, half_axis, swap)
    high_other = lax.ppermute(high_own, half_axis, swap)

    sign_last, high_seed = pl.pallas_call(
        last_kernel,
        out_shape=[rows, seed],
        in_specs=[vmem] * 5,
        out_specs=[vmem] * 2,
        scratch_shapes=[pltpu.VMEM((2, GROUP * HALF, WIDE), F32)],
        compiler_params=params,
        cost_estimate=pl.CostEstimate(
            flops=3 * 2 * 4 * WIDE**3, bytes_accessed=4 * 2**20, transcendentals=0
        ),
    )(matrix, lines, full, mine, keep)

    return tuple(
        pl.pallas_call(
            functools.partial(border_kernel, half_axis=half_axis),
            out_shape=(band, band),
            in_specs=[vmem] * 16 + [hbm] * 2,
            out_specs=[hbm] * 2,
            scratch_shapes=[
                pltpu.VMEM((2, 2, WIDE, 2 * WIDE), BF),
                pltpu.VMEM((2, 2, REACH * BS, WIDE), F32),
                pltpu.VMEM((2, 2, REACH * HALF, WIDE), F32),
                pltpu.VMEM((2, 2, REACH, SPAN, HALF, BS), F32),
                pltpu.SemaphoreType.DMA((2, 2, REACH)),
                pltpu.SemaphoreType.DMA((GROUP,)),
            ],
            input_output_aliases={16: 0, 17: 1},
            compiler_params=params,
            cost_estimate=pl.CostEstimate(
                flops=3 * 2 * 4 * WIDE**3, bytes_accessed=2 * 2**20, transcendentals=0
            ),
        )(
            low_own, low_other, high_own, high_other, lines, sign_last, low_seed, *ends[:4], high_seed,
            *ends[4:], square, sign,
        )
    )


def solution(mesh):
    band = P(("group", "row", "col"), None, "rep", None)
    return jax.shard_map(
        functools.partial(shards, axes=("row", "col"), half_axis="rep"),
        mesh=mesh,
        in_specs=(band, P("group", None)),
        out_specs=(band, band),
        check_vma=False,
    )
```

```python
import functools

import jax
import jax.numpy as jnp
from jax import lax
from jax.experimental import pallas as pl
from jax.experimental.pallas import tpu as pltpu
from jax.sharding import PartitionSpec as P

REACH = 3
SPAN = 7
BS = 64
HALF = 32
GROUP = 4
WIDE = GROUP * BS
BF = jnp.bfloat16
F32 = jnp.float32
LIMIT = 32 * 1024 * 1024


def split(x):
    hi = x.astype(BF)
    return hi, (x - hi.astype(F32)).astype(BF)


def product(pairs, transposed=False):
    side = 1 if transposed else 0
    high, low = [jnp.concatenate([a[p] for a, _ in pairs], axis=1) for p in range(2)]
    right = [jnp.concatenate([b[p] for _, b in pairs], axis=side) for p in range(2)]
    dot = functools.partial(
        lax.dot_general,
        dimension_numbers=(((1,), (side,)), ((), ())),
        preferred_element_type=F32,
    )
    both = dot(jnp.concatenate([high, low], axis=0), right[0])
    count = high.shape[0]
    return both[:count] + (both[count:] + dot(high, right[1]))


def turn(x):
    return split((x[0].astype(F32) + x[1].astype(F32)).T)


def write_lines(pat, lines, first, groups):
    total = pat.shape[1]
    rows = lines.shape[0]
    iota = functools.partial(lax.broadcasted_iota, jnp.int32)
    dot = functools.partial(lax.dot_general, preferred_element_type=F32)
    wanted = lax.rem(first - GROUP + total + iota((rows, total), 0), total)
    chosen = (iota((rows, total), 1) == wanted).astype(BF)
    flags = dot(chosen, pat[...].astype(BF), (((1,), (1,)), ((), ())))
    place = iota((rows, 1), 0) % GROUP
    spread = jnp.concatenate(
        [jnp.where(place == s, flags, 0.0) for s in range(GROUP)], axis=1
    ).astype(BF)
    block = iota((SPAN, 3 * WIDE), 1) // BS - iota((SPAN, 3 * WIDE), 0) - 1
    spots = jnp.concatenate([(block == s).astype(BF) for s in range(GROUP)], axis=0)
    lines[...] = dot(spread, spots, (((1,), (0,)), ((), ())))


def line_of(lines, g, s, h):
    at = (g + 1) * GROUP + s
    lo = (h - g + 1) * WIDE
    return lines[at : at + 1, lo : lo + WIDE]


def span_of(a, count, is_square):
    if a < REACH:
        return (REACH - a if is_square else 2 * REACH - a), SPAN
    s = a - (count - REACH)
    if s >= 0:
        return 0, (2 * REACH - s if is_square else REACH - s)
    return 0, SPAN


def edge_kernel(top, bottom, to_left, to_right):
    for source, target in ((top, to_left), (bottom, to_right)):
        for s in range(REACH):
            for t in range(2):
                target[s * HALF : (s + 1) * HALF, t * 2 * BS : (t + 1) * 2 * BS] = jnp.concatenate(
                    [source[s, 2 * t], source[s, 2 * t + 1]], axis=1
                )


class Interior:
    def __init__(self, own, lines, full, mine, keep):
        self.own = own
        self.lines = lines
        self.full = full
        self.mine = mine
        self.keep = keep
        self.count = own.shape[0]
        self.groups = self.count // GROUP
        self.stores = []

    def part(self, g, h, rows=slice(None)):
        at = (h - g + 1) * WIDE
        return [self.full[p, g, rows, at : at + WIDE] for p in range(2)]

    def my_part(self, g, h):
        at = (h - g + 1) * WIDE
        return [self.mine[p, g, :, at : at + WIDE] for p in range(2)]

    def tile(self, g, h):
        return 3 * g + h - g + 1

    def kept(self, g, h):
        return [self.keep[p, self.tile(g, h)] for p in range(2)]

    def near(self, g):
        return [e for e in (g - 1, g, g + 1) if 0 <= e < self.groups]

    def second(self, g, h, sign, seed, result):
        span = range(1 if h > g else 0, GROUP - 1 if h < g else GROUP)
        rows = slice(span[0] * HALF, (span[-1] + 1) * HALF)

        def dot():
            return product(
                [
                    ([x[rows] for x in self.my_part(g, e)], self.kept(e, h))
                    for e in self.near(g)
                    if abs(e - h) <= 1
                ]
            )

        def store(value):
            result[rows] = value

        def post():
            for s in span:
                a = g * GROUP + s
                k0, k1 = span_of(a, self.count, False)
                part = result[s * HALF : (s + 1) * HALF] * (line_of(self.lines, g, s, h) * 0.5)
                for t in range(GROUP):
                    k = t + GROUP * (h - g) - s + REACH
                    if 0 <= k < SPAN:
                        block = 1.5 * self.own[a, k] - part[:, t * BS : (t + 1) * BS]
                        if k0 <= k < k1:
                            sign[s, k] = block
                        else:
                            seed[a if a < REACH else a - (self.count - REACH), k] = block

        return dot, store, post

    def far_seed(self, g, seed):
        for s in range(REACH):
            a = s if g == 0 else self.count - REACH + s
            for k in range(0, REACH - s) if g == 0 else range(2 * REACH - s, SPAN):
                seed[s, k] = 1.5 * self.own[a, k]

    def reaching(self, a_ref, b_ref, m_ref, p_ref, g, e, r0):
        rows = slice(r0, r0 + REACH * BS)
        mine_rows = slice(r0 // 2, r0 // 2 + REACH * HALF)
        outer = slice(BS - r0, BS - r0 + REACH * BS)

        def dot():
            out = self.part(g, e)
            return (
                product([([x[outer] for x in turn(out)], out)]),
                product([(self.part(g, g, rows), out)]),
            )

        def store(value):
            a_ref[...], b_ref[...] = value

        def post():
            for p in range(2):
                m_ref[p] = self.part(g, e)[p][rows]
                p_ref[p, 0] = self.my_part(g, e)[p][mine_rows]
                p_ref[p, 1] = self.my_part(g, g)[p][mine_rows]

        return dot, store, post

    def send(self, g, i, source, target, sems):
        for s in range(GROUP):
            a = g * GROUP + s
            k0, k1 = span_of(a, self.count, i == 0)
            store = pltpu.make_async_copy(
                source.at[s, pl.ds(k0, k1 - k0)], target.at[a, pl.ds(k0, k1 - k0)], sems.at[i, a]
            )
            store.start()
            self.stores.append(store)

    def finish(self):
        for store in self.stores:
            store.wait()


def count_dots(steps):
    return sum(isinstance(step, tuple) for step in steps)


def staggered(steps):
    pending = []
    for step in steps:
        if not isinstance(step, tuple):
            pending.append(step)
            continue
        dot, store, post = step
        value = dot()
        for work in pending:
            work()
        store(value)
        pending = [post]
    for work in pending:
        work()


def first_kernel(
    own, other, pat, square_out, sign_out, seed, full, mine, keep, lines, low_a, low_b, low_m, low_p,
    high_a, high_b, high_m, high_p, square, sign, results, sems, *, axes, half_axis
):
    it = Interior(own, lines, full, mine, keep)
    groups = it.groups
    upper_half = lax.axis_index(half_axis) == 1

    def build(g):
        for s in range(GROUP):
            a = g * GROUP + s
            for t in range(3 * GROUP // 2):
                ks = [2 * t + e - s - 1 for e in range(2)]
                lanes = slice(t * 2 * BS, (t + 1) * 2 * BS)
                rows = slice(s * BS, (s + 1) * BS)
                mine_rows = slice(s * HALF, (s + 1) * HALF)
                if all(k < 0 or k >= SPAN for k in ks):
                    for p in range(2):
                        full[p, g, rows, lanes] = jnp.zeros((BS, 2 * BS), BF)
                        mine[p, g, mine_rows, lanes] = jnp.zeros((HALF, 2 * BS), BF)
                    continue
                two = [
                    jnp.concatenate(
                        [src[a, k] if 0 <= k < SPAN else jnp.zeros((HALF, BS), F32) for k in ks],
                        axis=1,
                    )
                    for src in (own, other)
                ]
                for p, (x, y) in enumerate(zip(*[split(x) for x in two])):
                    mine[p, g, mine_rows, lanes] = x
                    full[p, g, rows, lanes] = jnp.concatenate(
                        [jnp.where(upper_half, y, x), jnp.where(upper_half, x, y)], axis=0
                    )

    def squares(g, h, result):
        pairs = []
        for e in (g - 1, g, g + 1):
            if abs(e - h) <= 1:
                inside = 0 <= e < groups
                pairs.append((e, (lambda e=e: it.part(e, h)) if inside else (lambda e=e: turn(it.part(h, e)))))
        span = range(1 if h > g else 0, GROUP)
        rows = slice(span[0] * BS, WIDE)

        def dot():
            return product([([x[rows] for x in it.part(g, e)], f()) for e, f in pairs])

        def store(value):
            result[rows] = value

        def post():
            masked = [jnp.zeros((BS, WIDE), F32)] * GROUP
            for s in span:
                masked[s] = result[s * BS : (s + 1) * BS] * line_of(lines, g, s, h)
            for s in range(GROUP):
                for p, x in enumerate(split(masked[s])):
                    keep[p, it.tile(g, h), s * BS : (s + 1) * BS] = x
            for s in span:
                part = jnp.where(upper_half, masked[s][HALF:], masked[s][:HALF])
                for t in range(GROUP):
                    k = t + GROUP * (h - g) - s + REACH
                    if 0 <= k < SPAN:
                        staged[g][s, k] = part[:, t * BS : (t + 1) * BS]
            if h == g:
                return
            for c in range(0, GROUP, 2):
                turned = jnp.concatenate(masked[c : c + 2], axis=0).T
                lanes = slice(c * BS, (c + 2) * BS)
                for p, x in enumerate(split(turned)):
                    keep[p, it.tile(h, g), :, lanes] = x
                for t in range(GROUP):
                    rows = turned[t * BS : (t + 1) * BS]
                    part = jnp.where(upper_half, rows[HALF:], rows[:HALF])
                    for s in range(c, c + 2):
                        k = s + GROUP * (g - h) - t + REACH
                        if 0 <= k < SPAN:
                            staged[h][t, k] = part[:, (s - c) * BS : (s - c + 1) * BS]

        return dot, store, post

    staged = [square.at[g] for g in range(groups)]

    def begin():
        write_lines(pat, lines, lax.axis_index(axes) * it.count, groups)
        it.far_seed(0, seed)

    build(0)
    build(1)
    steps = [begin]
    for g in range(groups):
        if g + 1 < groups:
            steps.append(squares(g, g + 1, results.at[count_dots(steps)]))
            if g + 2 < groups:
                steps.append(functools.partial(build, g + 2))
        steps.append(squares(g, g, results.at[count_dots(steps)]))
        steps.append(functools.partial(it.send, g, 0, staged[g], square_out, sems))
    for g in range(groups - 1):
        for h in it.near(g):
            steps.append(it.second(g, h, sign.at[g], seed, results.at[count_dots(steps)]))
        steps.append(functools.partial(it.send, g, 1, sign.at[g], sign_out, sems))
    steps.append(it.reaching(low_a, low_b, low_m, low_p, 0, -1, 0))
    steps.append(it.reaching(high_a, high_b, high_m, high_p, groups - 1, groups, BS))
    staggered(steps)
    it.finish()


def last_kernel(own, lines, full, mine, keep, sign, seed, results):
    it = Interior(own, lines, full, mine, keep)
    last = it.groups - 1
    steps = [it.second(last, h, sign, seed, results.at[i]) for i, h in enumerate(it.near(last))]
    steps.append(functools.partial(it.far_seed, last, seed))

    staggered(steps)


def border(
    side, groups, half_axis, mine, theirs, lines, seed, a_ref, b_ref, m_ref, p_ref, halo, first, last,
    square, sign, sent
):
    upper_half = lax.axis_index(half_axis) == 1
    at = 1 - side
    edge_group, outer_group = (0, -1) if side == 0 else (groups - 1, groups)
    offset = 0 if side == 0 else 2 * REACH
    below = REACH if side == 0 else 0
    zero = jnp.zeros((BS, WIDE), F32)

    def padded(rows, front):
        return split(jnp.concatenate([zero] + rows if front else rows + [zero], axis=0))

    whole_rows = []
    for p in range(REACH):
        rows = slice(p * HALF, (p + 1) * HALF)
        whole_rows.append(
            jnp.concatenate(
                [
                    jnp.where(upper_half, theirs[rows, :], mine[rows, :]),
                    jnp.where(upper_half, mine[rows, :], theirs[rows, :]),
                ],
                axis=0,
            )
        )

    def block(p, c):
        k = c - p + below
        if 0 <= k <= REACH:
            return whole_rows[p][:, k * BS : (k + 1) * BS]
        k = p - c + below
        if 0 <= c < REACH and 0 <= k <= REACH:
            return whole_rows[c][:, k * BS : (k + 1) * BS].T
        return jnp.zeros((BS, BS), F32)

    base = -5 if side == 0 else 0
    for p in range(REACH):
        rows = slice((p + at) * BS, (p + at + 1) * BS)
        for t in range(4):
            value = jnp.concatenate([block(p, base + 2 * t), block(p, base + 2 * t + 1)], axis=1)
            for q, x in enumerate(split(value)):
                halo[q, rows, t * 2 * BS : (t + 1) * 2 * BS] = x
    rows = slice(0, BS) if side == 0 else slice(REACH * BS, WIDE)
    for q in range(2):
        halo[q, rows, :] = jnp.zeros((BS, 2 * WIDE), BF)

    whole = [halo[q] for q in range(2)]
    outer_rows = slice(at * BS, (at + REACH) * BS)
    inner = slice(WIDE, 2 * WIDE) if side == 0 else slice(0, WIDE)
    to_edge = product([([m_ref[q] for q in range(2)], [x[:, inner] for x in whole])], True)
    among = product([([x[outer_rows] for x in whole], whole)], True)
    first[0] = to_edge + b_ref[...]
    rows = [
        first[0, s * BS : (s + 1) * BS] * line_of(lines, edge_group, s + 1 - at, outer_group)
        for s in range(REACH)
    ]
    across = padded(rows, side == 1)
    reach_out = [p_ref[q, 0] for q in range(2)]
    back = product([(reach_out, across)], True)
    for s in range(REACH):
        part = jnp.where(upper_half, rows[s][HALF:], rows[s][:HALF])
        for t in range(REACH):
            k = t - s + offset
            if 0 <= k < SPAN:
                square[s, k] = part[:, (t + at) * BS : (t + at + 1) * BS]
        sent(0, s)
    first[1] = among + a_ref[...]
    rows = [
        first[1, p * BS : (p + 1) * BS] * line_of(lines, outer_group, p + at, outer_group)
        for p in range(REACH)
    ]
    inside = [p_ref[q, 1] for q in range(2)]
    last[0] = product([(reach_out, padded(rows, side == 0)), (inside, across)])
    last[1] = back
    for s in range(REACH):
        rows = slice(s * HALF, (s + 1) * HALF)
        far = last[0, rows] * (line_of(lines, edge_group, s + 1 - at, outer_group) * 0.5)
        close = last[1, rows] * (line_of(lines, edge_group, s + 1 - at, edge_group) * 0.5)
        for t in range(REACH):
            k = t - s + offset
            if 0 <= k < SPAN:
                lanes = slice((t + at) * BS, (t + at + 1) * BS)
                sign[s, k] = seed[s, k] - far[:, lanes]
            k = t - s + REACH
            lanes = slice((t + 1 - at) * BS, (t + 2 - at) * BS)
            sign[s, k] = seed[s, k] - close[:, lanes]
        sent(1, s)


def low_kernel(
    mine, theirs, lines, seed, a_ref, b_ref, m_ref, p_ref, square, sign, halo, first, last, *,
    groups, half_axis
):
    border(
        0, groups, half_axis, mine, theirs, lines, seed, a_ref, b_ref, m_ref, p_ref, halo, first,
        last, square, sign, lambda i, s: None,
    )


def high_kernel(
    mine, theirs, lines, seed, a_ref, b_ref, m_ref, p_ref, low_square, low_sign, sign_last, square_in,
    sign_in, square_out, sign_out, halo, first, last, square, sign, sems, last_sems, *, groups,
    half_axis
):
    count = square_in.shape[0]
    stores = []

    def send(source, s, a, i, k0, k1, sem):
        target = (square_out, sign_out)[i]
        store = pltpu.make_async_copy(
            source.at[s, pl.ds(k0, k1 - k0)], target.at[a, pl.ds(k0, k1 - k0)], sem
        )
        store.start()
        stores.append(store)

    for i, source in enumerate((low_square, low_sign)):
        for s in range(REACH):
            send(source, s, s, i, 0, span_of(s, count, i == 0)[0], sems.at[0, i, s])
    for s in range(GROUP):
        a = count - GROUP + s
        send(sign_last, s, a, 1, *span_of(a, count, False), last_sems.at[s])

    def sent(i, s):
        a = count - REACH + s
        source = (square, sign)[i]
        send(source, s, a, i, span_of(a, count, i == 0)[1], SPAN, sems.at[1, i, s])

    border(
        1, groups, half_axis, mine, theirs, lines, seed, a_ref, b_ref, m_ref, p_ref, halo, first,
        last, square, sign, sent,
    )
    for store in stores:
        store.wait()


def shards(matrix, pattern, *, axes, half_axis):
    count = matrix.shape[0]
    groups = count // GROUP
    flags = pattern.T
    vmem = pl.BlockSpec(memory_space=pltpu.VMEM)
    hbm = pl.BlockSpec(memory_space=pl.ANY)
    params = pltpu.CompilerParams(vmem_limit_bytes=LIMIT)

    top, bottom = matrix[:REACH, REACH:], matrix[count - REACH :, : REACH + 1]
    matrix, top, bottom = lax.optimization_barrier((matrix, top, bottom))
    edge = jax.ShapeDtypeStruct((REACH * HALF, (REACH + 1) * BS), F32)
    to_left, to_right = pl.pallas_call(
        edge_kernel,
        out_shape=(edge, edge),
        in_specs=[vmem] * 2,
        out_specs=[vmem] * 2,
        compiler_params=params,
        cost_estimate=pl.CostEstimate(
            flops=1 * 10**9, bytes_accessed=2**20, transcendentals=0
        ),
    )(top, bottom)
    size = 1
    for axis in axes:
        size *= lax.axis_size(axis)
    swap = [(0, 1), (1, 0)]
    other = lax.ppermute(matrix, half_axis, swap)
    forward = [(i, (i + 1) % size) for i in range(size)]
    backward = [(target, source) for source, target in forward]
    high_own = lax.ppermute(to_left, axes, backward)
    low_own = lax.ppermute(to_right, axes, forward)

    band = jax.ShapeDtypeStruct(matrix.shape, F32)
    seed = jax.ShapeDtypeStruct((REACH, SPAN, HALF, BS), F32)
    full = jax.ShapeDtypeStruct((2, groups, WIDE, 3 * WIDE), BF)
    mine = jax.ShapeDtypeStruct((2, groups, GROUP * HALF, 3 * WIDE), BF)
    keep = jax.ShapeDtypeStruct((2, 3 * groups, WIDE, WIDE), BF)
    lines = jax.ShapeDtypeStruct(((groups + 2) * GROUP, 3 * WIDE), F32)
    ends_out = [
        jax.ShapeDtypeStruct((REACH * BS, WIDE), F32),
        jax.ShapeDtypeStruct((REACH * BS, WIDE), F32),
        jax.ShapeDtypeStruct((2, REACH * BS, WIDE), BF),
        jax.ShapeDtypeStruct((2, 2, REACH * HALF, WIDE), BF),
    ]
    rows = jax.ShapeDtypeStruct((GROUP,) + matrix.shape[1:], F32)
    square, sign, low_seed, full, mine, keep, lines, *ends = pl.pallas_call(
        functools.partial(first_kernel, axes=axes, half_axis=half_axis),
        out_shape=[band, band, seed, full, mine, keep, lines] + ends_out * 2,
        in_specs=[vmem] * 3,
        out_specs=[hbm] * 2 + [vmem] * 13,
        scratch_shapes=[
            pltpu.VMEM((groups,) + rows.shape, F32),
            pltpu.VMEM((groups - 1,) + rows.shape, F32),
            pltpu.VMEM((2 * groups - 1 + 3 * groups - 4, WIDE, WIDE), F32),
            pltpu.SemaphoreType.DMA((2, count)),
        ],
        compiler_params=params,
        cost_estimate=pl.CostEstimate(
            flops=3 * 2 * 16 * WIDE**3, bytes_accessed=16 * 2**20, transcendentals=0
        ),
    )(matrix, other, flags)

    low_own, high_own, low_seed = lax.optimization_barrier((low_own, high_own, low_seed))
    low_other = lax.ppermute(low_own, half_axis, swap)
    high_other = lax.ppermute(high_own, half_axis, swap)

    sign_last, high_seed = pl.pallas_call(
        last_kernel,
        out_shape=[rows, seed],
        in_specs=[vmem] * 5,
        out_specs=[vmem] * 2,
        scratch_shapes=[pltpu.VMEM((2, GROUP * HALF, WIDE), F32)],
        compiler_params=params,
        cost_estimate=pl.CostEstimate(
            flops=3 * 2 * 4 * WIDE**3, bytes_accessed=4 * 2**20, transcendentals=0
        ),
    )(matrix, lines, full, mine, keep)

    names = dict(groups=groups, half_axis=half_axis)
    scratch = [
        pltpu.VMEM((2, WIDE, 2 * WIDE), BF),
        pltpu.VMEM((2, REACH * BS, WIDE), F32),
        pltpu.VMEM((2, REACH * HALF, WIDE), F32),
    ]
    cost = pl.CostEstimate(
        flops=3 * 2 * 2 * WIDE**3, bytes_accessed=2 * 2**20, transcendentals=0
    )
    low_square, low_sign = pl.pallas_call(
        functools.partial(low_kernel, **names),
        out_shape=(seed, seed),
        in_specs=[vmem] * 8,
        out_specs=[vmem] * 2,
        scratch_shapes=scratch,
        compiler_params=params,
        cost_estimate=cost,
    )(low_own, low_other, lines, low_seed, *ends[:4])
    return tuple(
        pl.pallas_call(
            functools.partial(high_kernel, **names),
            out_shape=(band, band),
            in_specs=[vmem] * 11 + [hbm] * 2,
            out_specs=[hbm] * 2,
            scratch_shapes=scratch
            + [
                pltpu.VMEM(seed.shape, F32),
                pltpu.VMEM(seed.shape, F32),
                pltpu.SemaphoreType.DMA((2, 2, REACH)),
                pltpu.SemaphoreType.DMA((GROUP,)),
            ],
            input_output_aliases={11: 0, 12: 1},
            compiler_params=params,
            cost_estimate=cost,
        )(
            high_own, high_other, lines, high_seed, *ends[4:], low_square, low_sign, sign_last,
            square, sign,
        )
    )


def solution(mesh):
    band = P(("group", "row", "col"), None, "rep", None)
    return jax.shard_map(
        functools.partial(shards, axes=("row", "col"), half_axis="rep"),
        mesh=mesh,
        in_specs=(band, P("group", None)),
        out_specs=(band, band),
        check_vma=False,
    )
```

```python
import functools

import jax
import jax.numpy as jnp
from jax import lax
from jax.experimental import pallas as pl
from jax.experimental.pallas import tpu as pltpu
from jax.sharding import PartitionSpec as P

REACH = 3
SPAN = 7
BS = 64
HALF = 32
GROUP = 4
WIDE = GROUP * BS
BF = jnp.bfloat16
F32 = jnp.float32
LIMIT = 32 * 1024 * 1024


def split(x):
    hi = x.astype(BF)
    return hi, (x - hi.astype(F32)).astype(BF)


def product(pairs, transposed=False):
    side = 1 if transposed else 0
    high, low = [jnp.concatenate([a[p] for a, _ in pairs], axis=1) for p in range(2)]
    right = [jnp.concatenate([b[p] for _, b in pairs], axis=side) for p in range(2)]
    dot = functools.partial(
        lax.dot_general,
        dimension_numbers=(((1,), (side,)), ((), ())),
        preferred_element_type=F32,
    )
    both = dot(jnp.concatenate([high, low], axis=0), right[0])
    count = high.shape[0]
    return both[:count] + (both[count:] + dot(high, right[1]))


def turn(x):
    return split((x[0].astype(F32) + x[1].astype(F32)).T)


def write_lines(pat, lines, first, groups):
    total = pat.shape[1]
    rows = lines.shape[0]
    iota = functools.partial(lax.broadcasted_iota, jnp.int32)
    dot = functools.partial(lax.dot_general, preferred_element_type=F32)
    wanted = lax.rem(first - GROUP + total + iota((rows, total), 0), total)
    chosen = (iota((rows, total), 1) == wanted).astype(BF)
    flags = dot(chosen, pat[...].astype(BF), (((1,), (1,)), ((), ())))
    place = iota((rows, 1), 0) % GROUP
    spread = jnp.concatenate(
        [jnp.where(place == s, flags, 0.0) for s in range(GROUP)], axis=1
    ).astype(BF)
    block = iota((SPAN, 3 * WIDE), 1) // BS - iota((SPAN, 3 * WIDE), 0) - 1
    spots = jnp.concatenate([(block == s).astype(BF) for s in range(GROUP)], axis=0)
    lines[...] = dot(spread, spots, (((1,), (0,)), ((), ())))


def line_of(lines, g, s, h):
    at = (g + 1) * GROUP + s
    lo = (h - g + 1) * WIDE
    return lines[at : at + 1, lo : lo + WIDE]


def inner_rows(g, groups):
    return range(REACH if g == 0 else 0, GROUP - REACH if g == groups - 1 else GROUP)


def row_of(g, s, groups, rows, low, high):
    if s in inner_rows(g, groups):
        return rows.at[s]
    return low.at[s] if g == 0 else high.at[s - (GROUP - REACH)]


def edge_kernel(top, bottom, to_left, to_right):
    for source, target in ((top, to_left), (bottom, to_right)):
        for s in range(REACH):
            for t in range(2):
                target[s * HALF : (s + 1) * HALF, t * 2 * BS : (t + 1) * 2 * BS] = jnp.concatenate(
                    [source[s, 2 * t], source[s, 2 * t + 1]], axis=1
                )


class Interior:
    def __init__(self, own, lines, full, mine, keep):
        self.own = own
        self.lines = lines
        self.full = full
        self.mine = mine
        self.keep = keep
        self.count = own.shape[0]
        self.groups = self.count // GROUP
        self.stores = []

    def part(self, g, h, rows=slice(None)):
        at = (h - g + 1) * WIDE
        return [self.full[p, g, rows, at : at + WIDE] for p in range(2)]

    def my_part(self, g, h):
        at = (h - g + 1) * WIDE
        return [self.mine[p, g, :, at : at + WIDE] for p in range(2)]

    def tile(self, g, h):
        return 3 * g + h - g + 1

    def kept(self, g, h):
        return [self.keep[p, self.tile(g, h)] for p in range(2)]

    def near(self, g):
        return [e for e in (g - 1, g, g + 1) if 0 <= e < self.groups]

    def second(self, g, h, sign, low, high, result):
        span = range(1 if h > g else 0, GROUP - 1 if h < g else GROUP)
        rows = slice(span[0] * HALF, (span[-1] + 1) * HALF)

        def dot():
            return product(
                [
                    ([x[rows] for x in self.my_part(g, e)], self.kept(e, h))
                    for e in self.near(g)
                    if abs(e - h) <= 1
                ]
            )

        def store(value):
            result[rows] = value

        def post():
            for s in span:
                a = g * GROUP + s
                target = row_of(g, s, self.groups, sign, low, high)
                part = result[s * HALF : (s + 1) * HALF] * (line_of(self.lines, g, s, h) * 0.5)
                for t in range(GROUP):
                    k = t + GROUP * (h - g) - s + REACH
                    if 0 <= k < SPAN:
                        target[k] = 1.5 * self.own[a, k] - part[:, t * BS : (t + 1) * BS]

        return dot, store, post

    def far_seed(self, g, seed):
        for s in range(REACH):
            a = s if g == 0 else self.count - REACH + s
            for k in range(0, REACH - s) if g == 0 else range(2 * REACH - s, SPAN):
                seed[s, k] = 1.5 * self.own[a, k]

    def reaching(self, a_ref, b_ref, m_ref, p_ref, g, e, r0):
        rows = slice(r0, r0 + REACH * BS)
        mine_rows = slice(r0 // 2, r0 // 2 + REACH * HALF)
        outer = slice(BS - r0, BS - r0 + REACH * BS)

        def dot():
            out = self.part(g, e)
            return (
                product([([x[outer] for x in turn(out)], out)]),
                product([(self.part(g, g, rows), out)]),
            )

        def store(value):
            a_ref[...], b_ref[...] = value

        def post():
            for p in range(2):
                m_ref[p] = self.part(g, e)[p][rows]
                p_ref[p, 0] = self.my_part(g, e)[p][mine_rows]
                p_ref[p, 1] = self.my_part(g, g)[p][mine_rows]

        return dot, store, post

    def send(self, g, i, source, target, sems):
        rows = inner_rows(g, self.groups)
        store = pltpu.make_async_copy(
            source.at[pl.ds(rows[0], len(rows))],
            target.at[pl.ds(g * GROUP + rows[0], len(rows))],
            sems.at[i, g],
        )
        store.start()
        self.stores.append(store)

    def finish(self):
        for store in self.stores:
            store.wait()


def count_dots(steps):
    return sum(isinstance(step, tuple) for step in steps)


def staggered(steps):
    pending = []
    for step in steps:
        if not isinstance(step, tuple):
            pending.append(step)
            continue
        dot, store, post = step
        value = dot()
        for work in pending:
            work()
        store(value)
        pending = [post]
    for work in pending:
        work()


def first_kernel(
    own, other, pat, square_out, sign_out, low_square, high_square, low_sign, full, mine, keep, lines, low_a, low_b, low_m, low_p,
    high_a, high_b, high_m, high_p, square, sign, results, sems, *, axes, half_axis
):
    it = Interior(own, lines, full, mine, keep)
    groups = it.groups
    upper_half = lax.axis_index(half_axis) == 1

    def build(g):
        for s in range(GROUP):
            a = g * GROUP + s
            for t in range(3 * GROUP // 2):
                ks = [2 * t + e - s - 1 for e in range(2)]
                lanes = slice(t * 2 * BS, (t + 1) * 2 * BS)
                rows = slice(s * BS, (s + 1) * BS)
                mine_rows = slice(s * HALF, (s + 1) * HALF)
                if all(k < 0 or k >= SPAN for k in ks):
                    for p in range(2):
                        full[p, g, rows, lanes] = jnp.zeros((BS, 2 * BS), BF)
                        mine[p, g, mine_rows, lanes] = jnp.zeros((HALF, 2 * BS), BF)
                    continue
                two = [
                    jnp.concatenate(
                        [src[a, k] if 0 <= k < SPAN else jnp.zeros((HALF, BS), F32) for k in ks],
                        axis=1,
                    )
                    for src in (own, other)
                ]
                for p, (x, y) in enumerate(zip(*[split(x) for x in two])):
                    mine[p, g, mine_rows, lanes] = x
                    full[p, g, rows, lanes] = jnp.concatenate(
                        [jnp.where(upper_half, y, x), jnp.where(upper_half, x, y)], axis=0
                    )

    def squares(g, h, result):
        pairs = []
        for e in (g - 1, g, g + 1):
            if abs(e - h) <= 1:
                inside = 0 <= e < groups
                pairs.append((e, (lambda e=e: it.part(e, h)) if inside else (lambda e=e: turn(it.part(h, e)))))
        span = range(1 if h > g else 0, GROUP)
        rows = slice(span[0] * BS, WIDE)

        def dot():
            return product([([x[rows] for x in it.part(g, e)], f()) for e, f in pairs])

        def store(value):
            result[rows] = value

        def post():
            masked = [jnp.zeros((BS, WIDE), F32)] * GROUP
            for s in span:
                masked[s] = result[s * BS : (s + 1) * BS] * line_of(lines, g, s, h)
            for s in range(GROUP):
                for p, x in enumerate(split(masked[s])):
                    keep[p, it.tile(g, h), s * BS : (s + 1) * BS] = x
            for s in span:
                part = jnp.where(upper_half, masked[s][HALF:], masked[s][:HALF])
                for t in range(GROUP):
                    k = t + GROUP * (h - g) - s + REACH
                    if 0 <= k < SPAN:
                        row_of(g, s, groups, square.at[g], low_square, high_square)[k] = part[
                            :, t * BS : (t + 1) * BS
                        ]
            if h == g:
                return
            for c in range(0, GROUP, 2):
                turned = jnp.concatenate(masked[c : c + 2], axis=0).T
                lanes = slice(c * BS, (c + 2) * BS)
                for p, x in enumerate(split(turned)):
                    keep[p, it.tile(h, g), :, lanes] = x
                for t in range(GROUP):
                    rows = turned[t * BS : (t + 1) * BS]
                    part = jnp.where(upper_half, rows[HALF:], rows[:HALF])
                    for s in range(c, c + 2):
                        k = s + GROUP * (g - h) - t + REACH
                        if 0 <= k < SPAN:
                            row_of(h, t, groups, square.at[h], low_square, high_square)[k] = part[
                                :, (s - c) * BS : (s - c + 1) * BS
                            ]

        return dot, store, post


    def begin():
        write_lines(pat, lines, lax.axis_index(axes) * it.count, groups)
        it.far_seed(0, low_sign)

    build(0)
    build(1)
    steps = [begin]
    for g in range(groups):
        if g + 1 < groups:
            steps.append(squares(g, g + 1, results.at[count_dots(steps)]))
            if g + 2 < groups:
                steps.append(functools.partial(build, g + 2))
        steps.append(squares(g, g, results.at[count_dots(steps)]))
        steps.append(functools.partial(it.send, g, 0, square.at[g], square_out, sems))
    for g in range(groups - 1):
        for h in it.near(g):
            steps.append(it.second(g, h, sign.at[g], low_sign, None, results.at[count_dots(steps)]))
        steps.append(functools.partial(it.send, g, 1, sign.at[g], sign_out, sems))
    steps.append(it.reaching(low_a, low_b, low_m, low_p, 0, -1, 0))
    steps.append(it.reaching(high_a, high_b, high_m, high_p, groups - 1, groups, BS))
    staggered(steps)
    it.finish()


def last_kernel(own, lines, full, mine, keep, sign, high_sign, results):
    it = Interior(own, lines, full, mine, keep)
    last = it.groups - 1
    steps = [it.second(last, h, sign, None, high_sign, results.at[i]) for i, h in enumerate(it.near(last))]
    steps.append(functools.partial(it.far_seed, last, high_sign))

    staggered(steps)


def border(
    side, groups, upper_half, lines, mine, theirs, a_ref, b_ref, m_ref, p_ref, square, sign, halo,
    first, last, sent
):
    at = 1 - side
    edge_group, outer_group = (0, -1) if side == 0 else (groups - 1, groups)
    offset = 0 if side == 0 else 2 * REACH
    below = REACH if side == 0 else 0
    zero = jnp.zeros((BS, WIDE), F32)

    def padded(rows, front):
        return split(jnp.concatenate([zero] + rows if front else rows + [zero], axis=0))

    whole_rows = []
    for p in range(REACH):
        rows = slice(p * HALF, (p + 1) * HALF)
        whole_rows.append(
            jnp.concatenate(
                [
                    jnp.where(upper_half, theirs[rows, :], mine[rows, :]),
                    jnp.where(upper_half, mine[rows, :], theirs[rows, :]),
                ],
                axis=0,
            )
        )

    def block(p, c):
        k = c - p + below
        if 0 <= k <= REACH:
            return whole_rows[p][:, k * BS : (k + 1) * BS]
        k = p - c + below
        if 0 <= c < REACH and 0 <= k <= REACH:
            return whole_rows[c][:, k * BS : (k + 1) * BS].T
        return jnp.zeros((BS, BS), F32)

    base = -5 if side == 0 else 0
    for p in range(REACH):
        rows = slice((p + at) * BS, (p + at + 1) * BS)
        for t in range(4):
            value = jnp.concatenate([block(p, base + 2 * t), block(p, base + 2 * t + 1)], axis=1)
            for q, x in enumerate(split(value)):
                halo[q, rows, t * 2 * BS : (t + 1) * 2 * BS] = x
    rows = slice(0, BS) if side == 0 else slice(REACH * BS, WIDE)
    for q in range(2):
        halo[q, rows, :] = jnp.zeros((BS, 2 * WIDE), BF)

    whole = [halo[q] for q in range(2)]
    outer_rows = slice(at * BS, (at + REACH) * BS)
    inner = slice(WIDE, 2 * WIDE) if side == 0 else slice(0, WIDE)
    to_edge = product([([m_ref[q] for q in range(2)], [x[:, inner] for x in whole])], True)
    among = product([([x[outer_rows] for x in whole], whole)], True)
    yield
    first[0] = to_edge + b_ref[...]
    rows = [
        first[0, s * BS : (s + 1) * BS] * line_of(lines, edge_group, s + 1 - at, outer_group)
        for s in range(REACH)
    ]
    across = padded(rows, side == 1)
    reach_out = [p_ref[q, 0] for q in range(2)]
    back = product([(reach_out, across)], True)
    for s in range(REACH):
        part = jnp.where(upper_half, rows[s][HALF:], rows[s][:HALF])
        for t in range(REACH):
            k = t - s + offset
            if 0 <= k < SPAN:
                square[s, k] = part[:, (t + at) * BS : (t + at + 1) * BS]
    sent(0)
    yield
    first[1] = among + a_ref[...]
    rows = [
        first[1, p * BS : (p + 1) * BS] * line_of(lines, outer_group, p + at, outer_group)
        for p in range(REACH)
    ]
    inside = [p_ref[q, 1] for q in range(2)]
    out = product([(reach_out, padded(rows, side == 0)), (inside, across)])
    last[1] = back
    for s in range(REACH):
        close = last[1, s * HALF : (s + 1) * HALF] * (
            line_of(lines, edge_group, s + 1 - at, edge_group) * 0.5
        )
        for t in range(REACH):
            k = t - s + REACH
            sign[s, k] = sign[s, k] - close[:, (t + 1 - at) * BS : (t + 2 - at) * BS]
    yield
    last[0] = out
    for s in range(REACH):
        far = last[0, s * HALF : (s + 1) * HALF] * (
            line_of(lines, edge_group, s + 1 - at, outer_group) * 0.5
        )
        for t in range(REACH):
            k = t - s + offset
            if 0 <= k < SPAN:
                sign[s, k] = sign[s, k] - far[:, (t + at) * BS : (t + at + 1) * BS]
    sent(1)


def border_kernel(
    low_own, low_other, high_own, high_other, lines, sign_last, low_a, low_b, low_m, low_p, high_a,
    high_b, high_m, high_p, low_square_in, high_square_in, low_sign_in, high_sign_in, square_in,
    sign_in, low_square, high_square, low_sign, high_sign, square_out, sign_out, halo, first, last,
    sems, last_sem, *, groups, half_axis
):
    count = square_in.shape[0]
    upper_half = lax.axis_index(half_axis) == 1
    stores = []

    def send(source, target, a, sem):
        store = pltpu.make_async_copy(source, target.at[pl.ds(a, source.shape[0])], sem)
        store.start()
        stores.append(store)

    send(sign_last.at[pl.ds(0, GROUP - REACH)], sign_out, count - GROUP, last_sem)
    squares, signs = (low_square, high_square), (low_sign, high_sign)

    def side(n, *refs):
        def sent(i):
            source, target = ((squares[n], square_out), (signs[n], sign_out))[i]
            send(source, target, (0, count - REACH)[n], sems.at[n, i])

        return border(
            n, groups, upper_half, lines, *refs, squares[n], signs[n], halo.at[n], first.at[n],
            last.at[n], sent,
        )

    works = [
        side(0, low_own, low_other, low_a, low_b, low_m, low_p),
        side(1, high_own, high_other, high_a, high_b, high_m, high_p),
    ]
    for _ in range(4):
        for work in works:
            next(work, None)
    for store in stores:
        store.wait()


def shards(matrix, pattern, *, axes, half_axis):
    count = matrix.shape[0]
    groups = count // GROUP
    flags = pattern.T
    vmem = pl.BlockSpec(memory_space=pltpu.VMEM)
    hbm = pl.BlockSpec(memory_space=pl.ANY)
    params = pltpu.CompilerParams(vmem_limit_bytes=LIMIT)

    top, bottom = matrix[:REACH, REACH:], matrix[count - REACH :, : REACH + 1]
    matrix, top, bottom = lax.optimization_barrier((matrix, top, bottom))
    edge = jax.ShapeDtypeStruct((REACH * HALF, (REACH + 1) * BS), F32)
    to_left, to_right = pl.pallas_call(
        edge_kernel,
        out_shape=(edge, edge),
        in_specs=[vmem] * 2,
        out_specs=[vmem] * 2,
        compiler_params=params,
        cost_estimate=pl.CostEstimate(
            flops=1 * 10**9, bytes_accessed=2**20, transcendentals=0
        ),
    )(top, bottom)
    size = 1
    for axis in axes:
        size *= lax.axis_size(axis)
    swap = [(0, 1), (1, 0)]
    other = lax.ppermute(matrix, half_axis, swap)
    forward = [(i, (i + 1) % size) for i in range(size)]
    backward = [(target, source) for source, target in forward]
    high_own = lax.ppermute(to_left, axes, backward)
    low_own = lax.ppermute(to_right, axes, forward)

    band = jax.ShapeDtypeStruct(matrix.shape, F32)
    edges = jax.ShapeDtypeStruct((REACH, SPAN, HALF, BS), F32)
    full = jax.ShapeDtypeStruct((2, groups, WIDE, 3 * WIDE), BF)
    mine = jax.ShapeDtypeStruct((2, groups, GROUP * HALF, 3 * WIDE), BF)
    keep = jax.ShapeDtypeStruct((2, 3 * groups, WIDE, WIDE), BF)
    lines = jax.ShapeDtypeStruct(((groups + 2) * GROUP, 3 * WIDE), F32)
    ends_out = [
        jax.ShapeDtypeStruct((REACH * BS, WIDE), F32),
        jax.ShapeDtypeStruct((REACH * BS, WIDE), F32),
        jax.ShapeDtypeStruct((2, REACH * BS, WIDE), BF),
        jax.ShapeDtypeStruct((2, 2, REACH * HALF, WIDE), BF),
    ]
    rows = jax.ShapeDtypeStruct((GROUP,) + matrix.shape[1:], F32)
    square, sign, low_square, high_square, low_sign, full, mine, keep, lines, *ends = pl.pallas_call(
        functools.partial(first_kernel, axes=axes, half_axis=half_axis),
        out_shape=[band, band, edges, edges, edges, full, mine, keep, lines] + ends_out * 2,
        in_specs=[vmem] * 3,
        out_specs=[hbm] * 2 + [vmem] * 15,
        scratch_shapes=[
            pltpu.VMEM((groups,) + rows.shape, F32),
            pltpu.VMEM((groups - 1,) + rows.shape, F32),
            pltpu.VMEM((2 * groups - 1 + 3 * groups - 4, WIDE, WIDE), F32),
            pltpu.SemaphoreType.DMA((2, groups)),
        ],
        compiler_params=params,
        cost_estimate=pl.CostEstimate(
            flops=3 * 2 * 16 * WIDE**3, bytes_accessed=16 * 2**20, transcendentals=0
        ),
    )(matrix, other, flags)

    low_own, high_own, low_sign = lax.optimization_barrier((low_own, high_own, low_sign))
    low_other = lax.ppermute(low_own, half_axis, swap)
    high_other = lax.ppermute(high_own, half_axis, swap)

    sign_last, high_sign = pl.pallas_call(
        last_kernel,
        out_shape=[rows, edges],
        in_specs=[vmem] * 5,
        out_specs=[vmem] * 2,
        scratch_shapes=[pltpu.VMEM((2, GROUP * HALF, WIDE), F32)],
        compiler_params=params,
        cost_estimate=pl.CostEstimate(
            flops=3 * 2 * 4 * WIDE**3, bytes_accessed=4 * 2**20, transcendentals=0
        ),
    )(matrix, lines, full, mine, keep)

    outs = pl.pallas_call(
        functools.partial(border_kernel, groups=groups, half_axis=half_axis),
        out_shape=[edges] * 4 + [band] * 2,
        in_specs=[vmem] * 18 + [hbm] * 2,
        out_specs=[vmem] * 4 + [hbm] * 2,
        scratch_shapes=[
            pltpu.VMEM((2, 2, WIDE, 2 * WIDE), BF),
            pltpu.VMEM((2, 2, REACH * BS, WIDE), F32),
            pltpu.VMEM((2, 2, REACH * HALF, WIDE), F32),
            pltpu.SemaphoreType.DMA((2, 2)),
            pltpu.SemaphoreType.DMA,
        ],
        input_output_aliases={14 + i: i for i in range(6)},
        compiler_params=params,
        cost_estimate=pl.CostEstimate(
            flops=3 * 2 * 4 * WIDE**3, bytes_accessed=2 * 2**20, transcendentals=0
        ),
    )(
        low_own, low_other, high_own, high_other, lines, sign_last, *ends, low_square, high_square,
        low_sign, high_sign, square, sign,
    )
    return tuple(outs[4:])


def solution(mesh):
    band = P(("group", "row", "col"), None, "rep", None)
    return jax.shard_map(
        functools.partial(shards, axes=("row", "col"), half_axis="rep"),
        mesh=mesh,
        in_specs=(band, P("group", None)),
        out_specs=(band, band),
        check_vma=False,
    )
```

```python
import functools

import jax
import jax.numpy as jnp
from jax import lax
from jax.experimental import pallas as pl
from jax.experimental.pallas import tpu as pltpu
from jax.sharding import PartitionSpec as P

REACH = 3
SPAN = 7
BS = 64
HALF = 32
GROUP = 4
WIDE = GROUP * BS
BF = jnp.bfloat16
F32 = jnp.float32
LIMIT = 32 * 1024 * 1024


def split(x):
    hi = x.astype(BF)
    return hi, (x - hi.astype(F32)).astype(BF)


def product(pairs, transposed=False):
    side = 1 if transposed else 0
    high, low = [jnp.concatenate([a[p] for a, _ in pairs], axis=1) for p in range(2)]
    right = [jnp.concatenate([b[p] for _, b in pairs], axis=side) for p in range(2)]
    dot = functools.partial(
        lax.dot_general,
        dimension_numbers=(((1,), (side,)), ((), ())),
        preferred_element_type=F32,
    )
    both = dot(jnp.concatenate([high, low], axis=0), right[0])
    count = high.shape[0]
    return both[:count] + (both[count:] + dot(high, right[1]))


def turn(x):
    return split((x[0].astype(F32) + x[1].astype(F32)).T)


def write_lines(pat, lines, first, groups):
    total = pat.shape[1]
    rows = lines.shape[0]
    iota = functools.partial(lax.broadcasted_iota, jnp.int32)
    dot = functools.partial(lax.dot_general, preferred_element_type=F32)
    wanted = lax.rem(first - GROUP + total + iota((rows, total), 0), total)
    chosen = (iota((rows, total), 1) == wanted).astype(BF)
    flags = dot(chosen, pat[...].astype(BF), (((1,), (1,)), ((), ())))
    place = iota((rows, 1), 0) % GROUP
    spread = jnp.concatenate(
        [jnp.where(place == s, flags, 0.0) for s in range(GROUP)], axis=1
    ).astype(BF)
    block = iota((SPAN, 3 * WIDE), 1) // BS - iota((SPAN, 3 * WIDE), 0) - 1
    spots = jnp.concatenate([(block == s).astype(BF) for s in range(GROUP)], axis=0)
    lines[...] = dot(spread, spots, (((1,), (0,)), ((), ())))


def line_of(lines, g, s, h):
    at = (g + 1) * GROUP + s
    lo = (h - g + 1) * WIDE
    return lines[at : at + 1, lo : lo + WIDE]


def inner_rows(g, groups):
    return range(REACH if g == 0 else 0, GROUP - REACH if g == groups - 1 else GROUP)


def inner_blocks(side, is_square):
    first = REACH if is_square else 2 * REACH
    return (first, SPAN) if side == 0 else (0, SPAN - first)


def outer_blocks(side, is_square):
    k0, k1 = inner_blocks(side, is_square)
    return (0, k0) if side == 0 else (k1, SPAN)


def blocks_of(ref, rows, blocks):
    return ref.at[pl.ds(rows[0], rows[1] - rows[0]), pl.ds(blocks[0], blocks[1] - blocks[0])]


def row_of(g, s, groups, rows, low, high):
    if s in inner_rows(g, groups):
        return rows.at[s]
    return low.at[s] if g == 0 else high.at[s - (GROUP - REACH)]


def edge_kernel(top, bottom, to_left, to_right):
    for source, target in ((top, to_left), (bottom, to_right)):
        for s in range(REACH):
            for t in range(2):
                target[s * HALF : (s + 1) * HALF, t * 2 * BS : (t + 1) * 2 * BS] = jnp.concatenate(
                    [source[s, 2 * t], source[s, 2 * t + 1]], axis=1
                )


class Interior:
    def __init__(self, own, lines, full, mine, keep):
        self.own = own
        self.lines = lines
        self.full = full
        self.mine = mine
        self.keep = keep
        self.count = own.shape[0]
        self.groups = self.count // GROUP
        self.stores = []

    def part(self, g, h, rows=slice(None)):
        at = (h - g + 1) * WIDE
        return [self.full[p, g, rows, at : at + WIDE] for p in range(2)]

    def my_part(self, g, h):
        at = (h - g + 1) * WIDE
        return [self.mine[p, g, :, at : at + WIDE] for p in range(2)]

    def tile(self, g, h):
        return 3 * g + h - g + 1

    def kept(self, g, h):
        return [self.keep[p, self.tile(g, h)] for p in range(2)]

    def near(self, g):
        return [e for e in (g - 1, g, g + 1) if 0 <= e < self.groups]

    def second(self, g, h, sign, low, high, result):
        span = range(1 if h > g else 0, GROUP - 1 if h < g else GROUP)
        rows = slice(span[0] * HALF, (span[-1] + 1) * HALF)

        def dot():
            return product(
                [
                    ([x[rows] for x in self.my_part(g, e)], self.kept(e, h))
                    for e in self.near(g)
                    if abs(e - h) <= 1
                ]
            )

        def store(value):
            result[rows] = value

        def post():
            for s in span:
                a = g * GROUP + s
                target = row_of(g, s, self.groups, sign, low, high)
                part = result[s * HALF : (s + 1) * HALF] * (line_of(self.lines, g, s, h) * 0.5)
                for t in range(GROUP):
                    k = t + GROUP * (h - g) - s + REACH
                    if 0 <= k < SPAN:
                        target[k] = 1.5 * self.own[a, k] - part[:, t * BS : (t + 1) * BS]

        return dot, store, post

    def far_seed(self, g, seed):
        for s in range(REACH):
            a = s if g == 0 else self.count - REACH + s
            for k in range(0, REACH - s) if g == 0 else range(2 * REACH - s, SPAN):
                seed[s, k] = 1.5 * self.own[a, k]

    def reaching(self, a_ref, b_ref, m_ref, p_ref, g, e, r0):
        rows = slice(r0, r0 + REACH * BS)
        mine_rows = slice(r0 // 2, r0 // 2 + REACH * HALF)
        outer = slice(BS - r0, BS - r0 + REACH * BS)

        def dot():
            out = self.part(g, e)
            return (
                product([([x[outer] for x in turn(out)], out)]),
                product([(self.part(g, g, rows), out)]),
            )

        def store(value):
            a_ref[...], b_ref[...] = value

        def post():
            for p in range(2):
                m_ref[p] = self.part(g, e)[p][rows]
                p_ref[p, 0] = self.my_part(g, e)[p][mine_rows]
                p_ref[p, 1] = self.my_part(g, g)[p][mine_rows]

        return dot, store, post

    def send(self, g, i, source, target, sems):
        rows = inner_rows(g, self.groups)
        store = pltpu.make_async_copy(
            source.at[pl.ds(rows[0], len(rows))],
            target.at[pl.ds(g * GROUP + rows[0], len(rows))],
            sems.at[i, g],
        )
        store.start()
        self.stores.append(store)

    def send_edge(self, side, i, source, target, sem):
        first = 0 if side == 0 else self.count - REACH
        blocks = inner_blocks(side, i == 0)
        store = pltpu.make_async_copy(
            blocks_of(source, (0, REACH), blocks),
            blocks_of(target, (first, first + REACH), blocks),
            sem,
        )
        store.start()
        self.stores.append(store)

    def finish(self):
        for store in self.stores:
            store.wait()


def count_dots(steps):
    return sum(isinstance(step, tuple) for step in steps)


def staggered(steps):
    pending = []
    for step in steps:
        if not isinstance(step, tuple):
            pending.append(step)
            continue
        dot, store, post = step
        value = dot()
        for work in pending:
            work()
        store(value)
        pending = [post]
    for work in pending:
        work()


def first_kernel(
    own, other, pat, square_out, sign_out, low_square, high_square, low_sign, full, mine, keep, lines, low_a, low_b, low_m, low_p,
    high_a, high_b, high_m, high_p, square, sign, results, sems, edge_sems, *, axes, half_axis
):
    it = Interior(own, lines, full, mine, keep)
    groups = it.groups
    upper_half = lax.axis_index(half_axis) == 1

    def build(g):
        for s in range(GROUP):
            a = g * GROUP + s
            for t in range(3 * GROUP // 2):
                ks = [2 * t + e - s - 1 for e in range(2)]
                lanes = slice(t * 2 * BS, (t + 1) * 2 * BS)
                rows = slice(s * BS, (s + 1) * BS)
                mine_rows = slice(s * HALF, (s + 1) * HALF)
                if all(k < 0 or k >= SPAN for k in ks):
                    for p in range(2):
                        full[p, g, rows, lanes] = jnp.zeros((BS, 2 * BS), BF)
                        mine[p, g, mine_rows, lanes] = jnp.zeros((HALF, 2 * BS), BF)
                    continue
                two = [
                    jnp.concatenate(
                        [src[a, k] if 0 <= k < SPAN else jnp.zeros((HALF, BS), F32) for k in ks],
                        axis=1,
                    )
                    for src in (own, other)
                ]
                for p, (x, y) in enumerate(zip(*[split(x) for x in two])):
                    mine[p, g, mine_rows, lanes] = x
                    full[p, g, rows, lanes] = jnp.concatenate(
                        [jnp.where(upper_half, y, x), jnp.where(upper_half, x, y)], axis=0
                    )

    def squares(g, h, result):
        pairs = []
        for e in (g - 1, g, g + 1):
            if abs(e - h) <= 1:
                inside = 0 <= e < groups
                pairs.append((e, (lambda e=e: it.part(e, h)) if inside else (lambda e=e: turn(it.part(h, e)))))
        span = range(1 if h > g else 0, GROUP)
        rows = slice(span[0] * BS, WIDE)

        def dot():
            return product([([x[rows] for x in it.part(g, e)], f()) for e, f in pairs])

        def store(value):
            result[rows] = value

        def post():
            masked = [jnp.zeros((BS, WIDE), F32)] * GROUP
            for s in span:
                masked[s] = result[s * BS : (s + 1) * BS] * line_of(lines, g, s, h)
            for s in range(GROUP):
                for p, x in enumerate(split(masked[s])):
                    keep[p, it.tile(g, h), s * BS : (s + 1) * BS] = x
            for s in span:
                part = jnp.where(upper_half, masked[s][HALF:], masked[s][:HALF])
                for t in range(GROUP):
                    k = t + GROUP * (h - g) - s + REACH
                    if 0 <= k < SPAN:
                        row_of(g, s, groups, square.at[g], low_square, high_square)[k] = part[
                            :, t * BS : (t + 1) * BS
                        ]
            if h == g:
                return
            for c in range(0, GROUP, 2):
                turned = jnp.concatenate(masked[c : c + 2], axis=0).T
                lanes = slice(c * BS, (c + 2) * BS)
                for p, x in enumerate(split(turned)):
                    keep[p, it.tile(h, g), :, lanes] = x
                for t in range(GROUP):
                    rows = turned[t * BS : (t + 1) * BS]
                    part = jnp.where(upper_half, rows[HALF:], rows[:HALF])
                    for s in range(c, c + 2):
                        k = s + GROUP * (g - h) - t + REACH
                        if 0 <= k < SPAN:
                            row_of(h, t, groups, square.at[h], low_square, high_square)[k] = part[
                                :, (s - c) * BS : (s - c + 1) * BS
                            ]

        return dot, store, post


    def begin():
        write_lines(pat, lines, lax.axis_index(axes) * it.count, groups)
        it.far_seed(0, low_sign)

    build(0)
    build(1)
    steps = [begin]
    for g in range(groups):
        if g + 1 < groups:
            steps.append(squares(g, g + 1, results.at[count_dots(steps)]))
            if g + 2 < groups:
                steps.append(functools.partial(build, g + 2))
        steps.append(squares(g, g, results.at[count_dots(steps)]))
        steps.append(functools.partial(it.send, g, 0, square.at[g], square_out, sems))
        if g in (0, groups - 1):
            side, source = (0, low_square) if g == 0 else (1, high_square)
            steps.append(
                functools.partial(it.send_edge, side, 0, source, square_out, edge_sems.at[side])
            )
    for g in range(groups - 1):
        for h in it.near(g):
            steps.append(it.second(g, h, sign.at[g], low_sign, None, results.at[count_dots(steps)]))
        steps.append(functools.partial(it.send, g, 1, sign.at[g], sign_out, sems))
        if g == 0:
            steps.append(functools.partial(it.send_edge, 0, 1, low_sign, sign_out, edge_sems.at[2]))
    steps.append(it.reaching(low_a, low_b, low_m, low_p, 0, -1, 0))
    steps.append(it.reaching(high_a, high_b, high_m, high_p, groups - 1, groups, BS))
    staggered(steps)
    it.finish()


def last_kernel(own, lines, full, mine, keep, sign, high_sign, results):
    it = Interior(own, lines, full, mine, keep)
    last = it.groups - 1
    steps = [it.second(last, h, sign, None, high_sign, results.at[i]) for i, h in enumerate(it.near(last))]
    steps.append(functools.partial(it.far_seed, last, high_sign))

    staggered(steps)


def border(
    side, groups, upper_half, lines, mine, theirs, a_ref, b_ref, m_ref, p_ref, square, sign, halo,
    first, last, sent
):
    at = 1 - side
    edge_group, outer_group = (0, -1) if side == 0 else (groups - 1, groups)
    offset = 0 if side == 0 else 2 * REACH
    below = REACH if side == 0 else 0
    zero = jnp.zeros((BS, WIDE), F32)

    def padded(rows, front):
        return split(jnp.concatenate([zero] + rows if front else rows + [zero], axis=0))

    whole_rows = []
    for p in range(REACH):
        rows = slice(p * HALF, (p + 1) * HALF)
        whole_rows.append(
            jnp.concatenate(
                [
                    jnp.where(upper_half, theirs[rows, :], mine[rows, :]),
                    jnp.where(upper_half, mine[rows, :], theirs[rows, :]),
                ],
                axis=0,
            )
        )

    def block(p, c):
        k = c - p + below
        if 0 <= k <= REACH:
            return whole_rows[p][:, k * BS : (k + 1) * BS]
        k = p - c + below
        if 0 <= c < REACH and 0 <= k <= REACH:
            return whole_rows[c][:, k * BS : (k + 1) * BS].T
        return jnp.zeros((BS, BS), F32)

    base = -5 if side == 0 else 0
    for p in range(REACH):
        rows = slice((p + at) * BS, (p + at + 1) * BS)
        for t in range(4):
            value = jnp.concatenate([block(p, base + 2 * t), block(p, base + 2 * t + 1)], axis=1)
            for q, x in enumerate(split(value)):
                halo[q, rows, t * 2 * BS : (t + 1) * 2 * BS] = x
    rows = slice(0, BS) if side == 0 else slice(REACH * BS, WIDE)
    for q in range(2):
        halo[q, rows, :] = jnp.zeros((BS, 2 * WIDE), BF)

    whole = [halo[q] for q in range(2)]
    outer_rows = slice(at * BS, (at + REACH) * BS)
    inner = slice(WIDE, 2 * WIDE) if side == 0 else slice(0, WIDE)
    to_edge = product([([m_ref[q] for q in range(2)], [x[:, inner] for x in whole])], True)
    among = product([([x[outer_rows] for x in whole], whole)], True)
    yield
    first[0] = to_edge + b_ref[...]
    rows = [
        first[0, s * BS : (s + 1) * BS] * line_of(lines, edge_group, s + 1 - at, outer_group)
        for s in range(REACH)
    ]
    across = padded(rows, side == 1)
    reach_out = [p_ref[q, 0] for q in range(2)]
    back = product([(reach_out, across)], True)
    for s in range(REACH):
        part = jnp.where(upper_half, rows[s][HALF:], rows[s][:HALF])
        for t in range(REACH):
            k = t - s + offset
            if 0 <= k < SPAN:
                square[s, k] = part[:, (t + at) * BS : (t + at + 1) * BS]
    sent(0)
    yield
    first[1] = among + a_ref[...]
    rows = [
        first[1, p * BS : (p + 1) * BS] * line_of(lines, outer_group, p + at, outer_group)
        for p in range(REACH)
    ]
    inside = [p_ref[q, 1] for q in range(2)]
    out = product([(reach_out, padded(rows, side == 0)), (inside, across)])
    last[1] = back
    for s in range(REACH):
        close = last[1, s * HALF : (s + 1) * HALF] * (
            line_of(lines, edge_group, s + 1 - at, edge_group) * 0.5
        )
        for t in range(REACH):
            k = t - s + REACH
            sign[s, k] = sign[s, k] - close[:, (t + 1 - at) * BS : (t + 2 - at) * BS]
    yield
    last[0] = out
    for s in range(REACH):
        far = last[0, s * HALF : (s + 1) * HALF] * (
            line_of(lines, edge_group, s + 1 - at, outer_group) * 0.5
        )
        for t in range(REACH):
            k = t - s + offset
            if 0 <= k < SPAN:
                sign[s, k] = sign[s, k] - far[:, (t + at) * BS : (t + at + 1) * BS]
    sent(1)


def border_kernel(
    low_own, low_other, high_own, high_other, lines, sign_last, low_a, low_b, low_m, low_p, high_a,
    high_b, high_m, high_p, low_square_in, high_square_in, low_sign_in, high_sign_in, square_in,
    sign_in, low_square, high_square, low_sign, high_sign, square_out, sign_out, halo, first, last,
    sems, last_sems, *, groups, half_axis
):
    count = square_in.shape[0]
    upper_half = lax.axis_index(half_axis) == 1
    stores = []

    def send(source, target, rows, blocks, sem):
        from_rows = (0, rows[1] - rows[0])
        store = pltpu.make_async_copy(
            blocks_of(source, from_rows, blocks), blocks_of(target, rows, blocks), sem
        )
        store.start()
        stores.append(store)

    send(sign_last, sign_out, (count - GROUP, count - REACH), (0, SPAN), last_sems.at[0])
    send(high_sign, sign_out, (count - REACH, count), inner_blocks(1, False), last_sems.at[1])
    squares, signs = (low_square, high_square), (low_sign, high_sign)

    def side(n, *refs):
        def sent(i):
            source, target = ((squares[n], square_out), (signs[n], sign_out))[i]
            rows = (0, REACH) if n == 0 else (count - REACH, count)
            send(source, target, rows, outer_blocks(n, i == 0), sems.at[n, i])

        return border(
            n, groups, upper_half, lines, *refs, squares[n], signs[n], halo.at[n], first.at[n],
            last.at[n], sent,
        )

    works = [
        side(0, low_own, low_other, low_a, low_b, low_m, low_p),
        side(1, high_own, high_other, high_a, high_b, high_m, high_p),
    ]
    for _ in range(4):
        for work in works:
            next(work, None)
    for store in stores:
        store.wait()


def shards(matrix, pattern, *, axes, half_axis):
    count = matrix.shape[0]
    groups = count // GROUP
    flags = pattern.T
    vmem = pl.BlockSpec(memory_space=pltpu.VMEM)
    hbm = pl.BlockSpec(memory_space=pl.ANY)
    params = pltpu.CompilerParams(vmem_limit_bytes=LIMIT)

    top, bottom = matrix[:REACH, REACH:], matrix[count - REACH :, : REACH + 1]
    matrix, top, bottom = lax.optimization_barrier((matrix, top, bottom))
    edge = jax.ShapeDtypeStruct((REACH * HALF, (REACH + 1) * BS), F32)
    to_left, to_right = pl.pallas_call(
        edge_kernel,
        out_shape=(edge, edge),
        in_specs=[vmem] * 2,
        out_specs=[vmem] * 2,
        compiler_params=params,
        cost_estimate=pl.CostEstimate(
            flops=1 * 10**9, bytes_accessed=2**20, transcendentals=0
        ),
    )(top, bottom)
    size = 1
    for axis in axes:
        size *= lax.axis_size(axis)
    swap = [(0, 1), (1, 0)]
    other = lax.ppermute(matrix, half_axis, swap)
    forward = [(i, (i + 1) % size) for i in range(size)]
    backward = [(target, source) for source, target in forward]
    high_own = lax.ppermute(to_left, axes, backward)
    low_own = lax.ppermute(to_right, axes, forward)

    band = jax.ShapeDtypeStruct(matrix.shape, F32)
    edges = jax.ShapeDtypeStruct((REACH, SPAN, HALF, BS), F32)
    full = jax.ShapeDtypeStruct((2, groups, WIDE, 3 * WIDE), BF)
    mine = jax.ShapeDtypeStruct((2, groups, GROUP * HALF, 3 * WIDE), BF)
    keep = jax.ShapeDtypeStruct((2, 3 * groups, WIDE, WIDE), BF)
    lines = jax.ShapeDtypeStruct(((groups + 2) * GROUP, 3 * WIDE), F32)
    ends_out = [
        jax.ShapeDtypeStruct((REACH * BS, WIDE), F32),
        jax.ShapeDtypeStruct((REACH * BS, WIDE), F32),
        jax.ShapeDtypeStruct((2, REACH * BS, WIDE), BF),
        jax.ShapeDtypeStruct((2, 2, REACH * HALF, WIDE), BF),
    ]
    rows = jax.ShapeDtypeStruct((GROUP,) + matrix.shape[1:], F32)
    square, sign, low_square, high_square, low_sign, full, mine, keep, lines, *ends = pl.pallas_call(
        functools.partial(first_kernel, axes=axes, half_axis=half_axis),
        out_shape=[band, band, edges, edges, edges, full, mine, keep, lines] + ends_out * 2,
        in_specs=[vmem] * 3,
        out_specs=[hbm] * 2 + [vmem] * 15,
        scratch_shapes=[
            pltpu.VMEM((groups,) + rows.shape, F32),
            pltpu.VMEM((groups - 1,) + rows.shape, F32),
            pltpu.VMEM((2 * groups - 1 + 3 * groups - 4, WIDE, WIDE), F32),
            pltpu.SemaphoreType.DMA((2, groups)),
            pltpu.SemaphoreType.DMA((3,)),
        ],
        compiler_params=params,
        cost_estimate=pl.CostEstimate(
            flops=3 * 2 * 16 * WIDE**3, bytes_accessed=16 * 2**20, transcendentals=0
        ),
    )(matrix, other, flags)

    low_own, low_sign = lax.optimization_barrier((low_own, low_sign))
    high_own, low_sign = lax.optimization_barrier((high_own, low_sign))
    low_other = lax.ppermute(low_own, half_axis, swap)
    high_other = lax.ppermute(high_own, half_axis, swap)

    sign_last, high_sign = pl.pallas_call(
        last_kernel,
        out_shape=[rows, edges],
        in_specs=[vmem] * 5,
        out_specs=[vmem] * 2,
        scratch_shapes=[pltpu.VMEM((2, GROUP * HALF, WIDE), F32)],
        compiler_params=params,
        cost_estimate=pl.CostEstimate(
            flops=3 * 2 * 4 * WIDE**3, bytes_accessed=4 * 2**20, transcendentals=0
        ),
    )(matrix, lines, full, mine, keep)

    outs = pl.pallas_call(
        functools.partial(border_kernel, groups=groups, half_axis=half_axis),
        out_shape=[edges] * 4 + [band] * 2,
        in_specs=[vmem] * 18 + [hbm] * 2,
        out_specs=[vmem] * 4 + [hbm] * 2,
        scratch_shapes=[
            pltpu.VMEM((2, 2, WIDE, 2 * WIDE), BF),
            pltpu.VMEM((2, 2, REACH * BS, WIDE), F32),
            pltpu.VMEM((2, 2, REACH * HALF, WIDE), F32),
            pltpu.SemaphoreType.DMA((2, 2)),
            pltpu.SemaphoreType.DMA((2,)),
        ],
        input_output_aliases={14 + i: i for i in range(6)},
        compiler_params=params,
        cost_estimate=pl.CostEstimate(
            flops=3 * 2 * 4 * WIDE**3, bytes_accessed=2 * 2**20, transcendentals=0
        ),
    )(
        low_own, low_other, high_own, high_other, lines, sign_last, *ends, low_square, high_square,
        low_sign, high_sign, square, sign,
    )
    return tuple(outs[4:])


def solution(mesh):
    band = P(("group", "row", "col"), None, "rep", None)
    return jax.shard_map(
        functools.partial(shards, axes=("row", "col"), half_axis="rep"),
        mesh=mesh,
        in_specs=(band, P("group", None)),
        out_specs=(band, band),
        check_vma=False,
    )
```

```python
import functools

import jax
import jax.numpy as jnp
from jax import lax
from jax.experimental import pallas as pl
from jax.experimental.pallas import tpu as pltpu
from jax.sharding import PartitionSpec as P

REACH = 3
SPAN = 7
BS = 64
HALF = 32
GROUP = 4
WIDE = GROUP * BS
BF = jnp.bfloat16
F32 = jnp.float32
LIMIT = 32 * 1024 * 1024


def split(x):
    hi = x.astype(BF)
    return hi, (x - hi.astype(F32)).astype(BF)


def product(pairs, transposed=False):
    side = 1 if transposed else 0
    high, low = [jnp.concatenate([a[p] for a, _ in pairs], axis=1) for p in range(2)]
    right = [jnp.concatenate([b[p] for _, b in pairs], axis=side) for p in range(2)]
    dot = functools.partial(
        lax.dot_general,
        dimension_numbers=(((1,), (side,)), ((), ())),
        preferred_element_type=F32,
    )
    both = dot(jnp.concatenate([high, low], axis=0), right[0])
    count = high.shape[0]
    return both[:count] + (both[count:] + dot(high, right[1]))


def turn(x):
    return split((x[0].astype(F32) + x[1].astype(F32)).T)


def write_lines(pat, lines, first, groups):
    total = pat.shape[1]
    rows = lines.shape[0]
    iota = functools.partial(lax.broadcasted_iota, jnp.int32)
    dot = functools.partial(lax.dot_general, preferred_element_type=F32)
    wanted = lax.rem(first - GROUP + total + iota((rows, total), 0), total)
    chosen = (iota((rows, total), 1) == wanted).astype(BF)
    flags = dot(chosen, pat[...].astype(BF), (((1,), (1,)), ((), ())))
    place = iota((rows, 1), 0) % GROUP
    spread = jnp.concatenate(
        [jnp.where(place == s, flags, 0.0) for s in range(GROUP)], axis=1
    ).astype(BF)
    block = iota((SPAN, 3 * WIDE), 1) // BS - iota((SPAN, 3 * WIDE), 0) - 1
    spots = jnp.concatenate([(block == s).astype(BF) for s in range(GROUP)], axis=0)
    lines[...] = dot(spread, spots, (((1,), (0,)), ((), ())))


def line_of(lines, g, s, h):
    at = (g + 1) * GROUP + s
    lo = (h - g + 1) * WIDE
    return lines[at : at + 1, lo : lo + WIDE]


def inner_rows(g, groups):
    return range(REACH if g == 0 else 0, GROUP - REACH if g == groups - 1 else GROUP)


def inner_blocks(side, is_square):
    first = REACH if is_square else 2 * REACH
    return (first, SPAN) if side == 0 else (0, SPAN - first)


def outer_blocks(side, is_square):
    k0, k1 = inner_blocks(side, is_square)
    return (0, k0) if side == 0 else (k1, SPAN)


def blocks_of(ref, rows, blocks):
    return ref.at[pl.ds(rows[0], rows[1] - rows[0]), pl.ds(blocks[0], blocks[1] - blocks[0])]


def row_of(g, s, groups, rows, low, high):
    if s in inner_rows(g, groups):
        return rows.at[s]
    return low.at[s] if g == 0 else high.at[s - (GROUP - REACH)]


def is_odd(axes):
    return lax.rem(lax.axis_index(axes), 2) == 1


def edge_kernel(top, bottom, across, along, *, axes):
    odd = is_odd(axes)
    for s in range(REACH):
        rows = slice(s * HALF, (s + 1) * HALF)
        for t in range(2):
            lanes = slice(t * 2 * BS, (t + 1) * 2 * BS)
            low, high = [
                jnp.concatenate([source[s, 2 * t], source[s, 2 * t + 1]], axis=1)
                for source in (top, bottom)
            ]
            across[rows, lanes] = jnp.where(odd, high, low)
            along[rows, lanes] = jnp.where(odd, low, high)


class Interior:
    def __init__(self, own, lines, full, mine, keep):
        self.own = own
        self.lines = lines
        self.full = full
        self.mine = mine
        self.keep = keep
        self.count = own.shape[0]
        self.groups = self.count // GROUP
        self.stores = []

    def part(self, g, h, rows=slice(None)):
        at = (h - g + 1) * WIDE
        return [self.full[p, g, rows, at : at + WIDE] for p in range(2)]

    def my_part(self, g, h):
        at = (h - g + 1) * WIDE
        return [self.mine[p, g, :, at : at + WIDE] for p in range(2)]

    def tile(self, g, h):
        return 3 * g + h - g + 1

    def kept(self, g, h):
        return [self.keep[p, self.tile(g, h)] for p in range(2)]

    def near(self, g):
        return [e for e in (g - 1, g, g + 1) if 0 <= e < self.groups]

    def second(self, g, h, sign, low, high, result):
        span = range(1 if h > g else 0, GROUP - 1 if h < g else GROUP)
        rows = slice(span[0] * HALF, (span[-1] + 1) * HALF)

        def dot():
            return product(
                [
                    ([x[rows] for x in self.my_part(g, e)], self.kept(e, h))
                    for e in self.near(g)
                    if abs(e - h) <= 1
                ]
            )

        def store(value):
            result[rows] = value

        def post():
            for s in span:
                a = g * GROUP + s
                target = row_of(g, s, self.groups, sign, low, high)
                part = result[s * HALF : (s + 1) * HALF] * (line_of(self.lines, g, s, h) * 0.5)
                for t in range(GROUP):
                    k = t + GROUP * (h - g) - s + REACH
                    if 0 <= k < SPAN:
                        target[k] = 1.5 * self.own[a, k] - part[:, t * BS : (t + 1) * BS]

        return dot, store, post

    def far_seed(self, g, seed):
        for s in range(REACH):
            a = s if g == 0 else self.count - REACH + s
            for k in range(0, REACH - s) if g == 0 else range(2 * REACH - s, SPAN):
                seed[s, k] = 1.5 * self.own[a, k]

    def reaching(self, a_ref, b_ref, m_ref, p_ref, g, e, r0):
        rows = slice(r0, r0 + REACH * BS)
        mine_rows = slice(r0 // 2, r0 // 2 + REACH * HALF)
        outer = slice(BS - r0, BS - r0 + REACH * BS)

        def dot():
            out = self.part(g, e)
            return (
                product([([x[outer] for x in turn(out)], out)]),
                product([(self.part(g, g, rows), out)]),
            )

        def store(value):
            a_ref[...], b_ref[...] = value

        def post():
            for p in range(2):
                m_ref[p] = self.part(g, e)[p][rows]
                p_ref[p, 0] = self.my_part(g, e)[p][mine_rows]
                p_ref[p, 1] = self.my_part(g, g)[p][mine_rows]

        return dot, store, post

    def send(self, g, i, source, target, sems):
        rows = inner_rows(g, self.groups)
        store = pltpu.make_async_copy(
            source.at[pl.ds(rows[0], len(rows))],
            target.at[pl.ds(g * GROUP + rows[0], len(rows))],
            sems.at[i, g],
        )
        store.start()
        self.stores.append(store)

    def send_edge(self, side, i, source, target, sem):
        first = 0 if side == 0 else self.count - REACH
        blocks = inner_blocks(side, i == 0)
        store = pltpu.make_async_copy(
            blocks_of(source, (0, REACH), blocks),
            blocks_of(target, (first, first + REACH), blocks),
            sem,
        )
        store.start()
        self.stores.append(store)

    def finish(self):
        for store in self.stores:
            store.wait()


def count_dots(steps):
    return sum(isinstance(step, tuple) for step in steps)


def staggered(steps):
    pending = []
    for step in steps:
        if not isinstance(step, tuple):
            pending.append(step)
            continue
        dot, store, post = step
        value = dot()
        for work in pending:
            work()
        store(value)
        pending = [post]
    for work in pending:
        work()


def first_kernel(
    own, other, pat, square_out, sign_out, low_square, high_square, low_sign, full, mine, keep, lines, low_a, low_b, low_m, low_p,
    square, sign, results, sems, edge_sems, *, axes, half_axis
):
    it = Interior(own, lines, full, mine, keep)
    groups = it.groups
    upper_half = lax.axis_index(half_axis) == 1

    def build(g):
        for s in range(GROUP):
            a = g * GROUP + s
            for t in range(3 * GROUP // 2):
                ks = [2 * t + e - s - 1 for e in range(2)]
                lanes = slice(t * 2 * BS, (t + 1) * 2 * BS)
                rows = slice(s * BS, (s + 1) * BS)
                mine_rows = slice(s * HALF, (s + 1) * HALF)
                if all(k < 0 or k >= SPAN for k in ks):
                    for p in range(2):
                        full[p, g, rows, lanes] = jnp.zeros((BS, 2 * BS), BF)
                        mine[p, g, mine_rows, lanes] = jnp.zeros((HALF, 2 * BS), BF)
                    continue
                two = [
                    jnp.concatenate(
                        [src[a, k] if 0 <= k < SPAN else jnp.zeros((HALF, BS), F32) for k in ks],
                        axis=1,
                    )
                    for src in (own, other)
                ]
                for p, (x, y) in enumerate(zip(*[split(x) for x in two])):
                    mine[p, g, mine_rows, lanes] = x
                    full[p, g, rows, lanes] = jnp.concatenate(
                        [jnp.where(upper_half, y, x), jnp.where(upper_half, x, y)], axis=0
                    )

    def squares(g, h, result):
        pairs = []
        for e in (g - 1, g, g + 1):
            if abs(e - h) <= 1:
                inside = 0 <= e < groups
                pairs.append((e, (lambda e=e: it.part(e, h)) if inside else (lambda e=e: turn(it.part(h, e)))))
        span = range(1 if h > g else 0, GROUP)
        rows = slice(span[0] * BS, WIDE)

        def dot():
            return product([([x[rows] for x in it.part(g, e)], f()) for e, f in pairs])

        def store(value):
            result[rows] = value

        def post():
            masked = [jnp.zeros((BS, WIDE), F32)] * GROUP
            for s in span:
                masked[s] = result[s * BS : (s + 1) * BS] * line_of(lines, g, s, h)
            for s in range(GROUP):
                for p, x in enumerate(split(masked[s])):
                    keep[p, it.tile(g, h), s * BS : (s + 1) * BS] = x
            for s in span:
                part = jnp.where(upper_half, masked[s][HALF:], masked[s][:HALF])
                for t in range(GROUP):
                    k = t + GROUP * (h - g) - s + REACH
                    if 0 <= k < SPAN:
                        row_of(g, s, groups, square.at[g], low_square, high_square)[k] = part[
                            :, t * BS : (t + 1) * BS
                        ]
            if h == g:
                return
            for c in range(0, GROUP, 2):
                turned = jnp.concatenate(masked[c : c + 2], axis=0).T
                lanes = slice(c * BS, (c + 2) * BS)
                for p, x in enumerate(split(turned)):
                    keep[p, it.tile(h, g), :, lanes] = x
                for t in range(GROUP):
                    rows = turned[t * BS : (t + 1) * BS]
                    part = jnp.where(upper_half, rows[HALF:], rows[:HALF])
                    for s in range(c, c + 2):
                        k = s + GROUP * (g - h) - t + REACH
                        if 0 <= k < SPAN:
                            row_of(h, t, groups, square.at[h], low_square, high_square)[k] = part[
                                :, (s - c) * BS : (s - c + 1) * BS
                            ]

        return dot, store, post


    def begin():
        write_lines(pat, lines, lax.axis_index(axes) * it.count, groups)
        it.far_seed(0, low_sign)

    build(0)
    build(1)
    steps = [begin]
    for g in range(groups):
        if g + 1 < groups:
            steps.append(squares(g, g + 1, results.at[count_dots(steps)]))
            if g + 2 < groups:
                steps.append(functools.partial(build, g + 2))
        steps.append(squares(g, g, results.at[count_dots(steps)]))
        steps.append(functools.partial(it.send, g, 0, square.at[g], square_out, sems))
        if g in (0, groups - 1):
            side, source = (0, low_square) if g == 0 else (1, high_square)
            steps.append(
                functools.partial(it.send_edge, side, 0, source, square_out, edge_sems.at[side])
            )
    for g in range(groups - 1):
        for h in it.near(g):
            steps.append(it.second(g, h, sign.at[g], low_sign, None, results.at[count_dots(steps)]))
        steps.append(functools.partial(it.send, g, 1, sign.at[g], sign_out, sems))
        if g == 0:
            steps.append(functools.partial(it.send_edge, 0, 1, low_sign, sign_out, edge_sems.at[2]))
    steps.append(it.reaching(low_a, low_b, low_m, low_p, 0, -1, 0))
    staggered(steps)
    it.finish()


def last_kernel(
    own, lines, full, mine, keep, sign, high_sign, high_a, high_b, high_m, high_p, results
):
    it = Interior(own, lines, full, mine, keep)
    last = it.groups - 1
    steps = [it.second(last, h, sign, None, high_sign, results.at[i]) for i, h in enumerate(it.near(last))]
    steps.append(functools.partial(it.far_seed, last, high_sign))
    steps.append(it.reaching(high_a, high_b, high_m, high_p, last, it.groups, BS))

    staggered(steps)


def border(
    side, groups, upper_half, lines, mine, theirs, a_ref, b_ref, m_ref, p_ref, square, sign, halo,
    first, last, sent
):
    at = 1 - side
    edge_group, outer_group = (0, -1) if side == 0 else (groups - 1, groups)
    offset = 0 if side == 0 else 2 * REACH
    below = REACH if side == 0 else 0
    zero = jnp.zeros((BS, WIDE), F32)

    def padded(rows, front):
        return split(jnp.concatenate([zero] + rows if front else rows + [zero], axis=0))

    whole_rows = []
    for p in range(REACH):
        rows = slice(p * HALF, (p + 1) * HALF)
        whole_rows.append(
            jnp.concatenate(
                [
                    jnp.where(upper_half, theirs[rows, :], mine[rows, :]),
                    jnp.where(upper_half, mine[rows, :], theirs[rows, :]),
                ],
                axis=0,
            )
        )

    def block(p, c):
        k = c - p + below
        if 0 <= k <= REACH:
            return whole_rows[p][:, k * BS : (k + 1) * BS]
        k = p - c + below
        if 0 <= c < REACH and 0 <= k <= REACH:
            return whole_rows[c][:, k * BS : (k + 1) * BS].T
        return jnp.zeros((BS, BS), F32)

    base = -5 if side == 0 else 0
    for p in range(REACH):
        rows = slice((p + at) * BS, (p + at + 1) * BS)
        for t in range(4):
            value = jnp.concatenate([block(p, base + 2 * t), block(p, base + 2 * t + 1)], axis=1)
            for q, x in enumerate(split(value)):
                halo[q, rows, t * 2 * BS : (t + 1) * 2 * BS] = x
    rows = slice(0, BS) if side == 0 else slice(REACH * BS, WIDE)
    for q in range(2):
        halo[q, rows, :] = jnp.zeros((BS, 2 * WIDE), BF)

    whole = [halo[q] for q in range(2)]
    outer_rows = slice(at * BS, (at + REACH) * BS)
    inner = slice(WIDE, 2 * WIDE) if side == 0 else slice(0, WIDE)
    to_edge = product([([m_ref[q] for q in range(2)], [x[:, inner] for x in whole])])
    among = product([([x[outer_rows] for x in whole], whole)], True)
    yield
    first[0] = to_edge + b_ref[...]
    rows = [
        first[0, s * BS : (s + 1) * BS] * line_of(lines, edge_group, s + 1 - at, outer_group)
        for s in range(REACH)
    ]
    across = padded(rows, side == 1)
    reach_out = [p_ref[q, 0] for q in range(2)]
    back = product([(reach_out, across)], True)
    for s in range(REACH):
        part = jnp.where(upper_half, rows[s][HALF:], rows[s][:HALF])
        for t in range(REACH):
            k = t - s + offset
            if 0 <= k < SPAN:
                square[s, k] = part[:, (t + at) * BS : (t + at + 1) * BS]
    sent(0)
    yield
    first[1] = among + a_ref[...]
    rows = [
        first[1, p * BS : (p + 1) * BS] * line_of(lines, outer_group, p + at, outer_group)
        for p in range(REACH)
    ]
    inside = [p_ref[q, 1] for q in range(2)]
    out = product([(reach_out, padded(rows, side == 0)), (inside, across)])
    last[1] = back
    for s in range(REACH):
        close = last[1, s * HALF : (s + 1) * HALF] * (
            line_of(lines, edge_group, s + 1 - at, edge_group) * 0.5
        )
        for t in range(REACH):
            k = t - s + REACH
            sign[s, k] = sign[s, k] - close[:, (t + 1 - at) * BS : (t + 2 - at) * BS]
    yield
    last[0] = out
    for s in range(REACH):
        far = last[0, s * HALF : (s + 1) * HALF] * (
            line_of(lines, edge_group, s + 1 - at, outer_group) * 0.5
        )
        for t in range(REACH):
            k = t - s + offset
            if 0 <= k < SPAN:
                sign[s, k] = sign[s, k] - far[:, (t + at) * BS : (t + at + 1) * BS]
    sent(1)


def border_kernel(
    across_own, across_other, along_own, along_other, lines, sign_last, low_a, low_b, low_m, low_p, high_a,
    high_b, high_m, high_p, low_square_in, high_square_in, low_sign_in, high_sign_in, square_in,
    sign_in, low_square, high_square, low_sign, high_sign, square_out, sign_out, halo, first, last,
    sems, last_sems, *, groups, axes, half_axis
):
    count = square_in.shape[0]
    upper_half = lax.axis_index(half_axis) == 1
    odd = is_odd(axes)
    stores = []

    def send(source, target, rows, blocks, sem):
        from_rows = (0, rows[1] - rows[0])
        store = pltpu.make_async_copy(
            blocks_of(source, from_rows, blocks), blocks_of(target, rows, blocks), sem
        )
        store.start()
        stores.append(store)

    send(sign_last, sign_out, (count - GROUP, count - REACH), (0, SPAN), last_sems.at[0])
    send(high_sign, sign_out, (count - REACH, count), inner_blocks(1, False), last_sems.at[1])
    squares, signs = (low_square, high_square), (low_sign, high_sign)

    def side(n, *refs):
        def sent(i):
            source, target = ((squares[n], square_out), (signs[n], sign_out))[i]
            rows = (0, REACH) if n == 0 else (count - REACH, count)
            send(source, target, rows, outer_blocks(n, i == 0), sems.at[n, i])

        return border(
            n, groups, upper_half, lines, *refs, squares[n], signs[n], halo.at[n], first.at[n],
            last.at[n], sent,
        )

    low_own = jnp.where(odd, along_own[...], across_own[...])
    low_other = jnp.where(odd, along_other[...], across_other[...])
    high_own = jnp.where(odd, across_own[...], along_own[...])
    high_other = jnp.where(odd, across_other[...], along_other[...])
    works = [
        side(0, low_own, low_other, low_a, low_b, low_m, low_p),
        side(1, high_own, high_other, high_a, high_b, high_m, high_p),
    ]
    for _ in range(4):
        for work in works:
            next(work, None)
    for store in stores:
        store.wait()


def shards(matrix, pattern, *, axes, half_axis):
    count = matrix.shape[0]
    groups = count // GROUP
    flags = pattern.T
    vmem = pl.BlockSpec(memory_space=pltpu.VMEM)
    hbm = pl.BlockSpec(memory_space=pl.ANY)
    params = pltpu.CompilerParams(vmem_limit_bytes=LIMIT)

    top, bottom = matrix[:REACH, REACH:], matrix[count - REACH :, : REACH + 1]
    matrix, top, bottom = lax.optimization_barrier((matrix, top, bottom))
    edge = jax.ShapeDtypeStruct((REACH * HALF, (REACH + 1) * BS), F32)
    across, along = pl.pallas_call(
        functools.partial(edge_kernel, axes=axes),
        out_shape=(edge, edge),
        in_specs=[vmem] * 2,
        out_specs=[vmem] * 2,
        compiler_params=params,
        cost_estimate=pl.CostEstimate(
            flops=1 * 10**9, bytes_accessed=2**20, transcendentals=0
        ),
    )(top, bottom)
    size = 1
    for axis in axes:
        size *= lax.axis_size(axis)
    swap = [(0, 1), (1, 0)]
    other = lax.ppermute(matrix, half_axis, swap)
    pairs = [(i, (i + 1) % size) for i in range(1, size, 2)]
    across = lax.ppermute(across, axes, pairs + [(b, a) for a, b in pairs])
    pairs = [(i, i + 1) for i in range(0, size, 2)]
    along = lax.ppermute(along, axes, pairs + [(b, a) for a, b in pairs])

    band = jax.ShapeDtypeStruct(matrix.shape, F32)
    edges = jax.ShapeDtypeStruct((REACH, SPAN, HALF, BS), F32)
    full = jax.ShapeDtypeStruct((2, groups, WIDE, 3 * WIDE), BF)
    mine = jax.ShapeDtypeStruct((2, groups, GROUP * HALF, 3 * WIDE), BF)
    keep = jax.ShapeDtypeStruct((2, 3 * groups, WIDE, WIDE), BF)
    lines = jax.ShapeDtypeStruct(((groups + 2) * GROUP, 3 * WIDE), F32)
    ends_out = [
        jax.ShapeDtypeStruct((REACH * BS, WIDE), F32),
        jax.ShapeDtypeStruct((REACH * BS, WIDE), F32),
        jax.ShapeDtypeStruct((2, REACH * BS, WIDE), BF),
        jax.ShapeDtypeStruct((2, 2, REACH * HALF, WIDE), BF),
    ]
    rows = jax.ShapeDtypeStruct((GROUP,) + matrix.shape[1:], F32)
    square, sign, low_square, high_square, low_sign, full, mine, keep, lines, *low_ends = pl.pallas_call(
        functools.partial(first_kernel, axes=axes, half_axis=half_axis),
        out_shape=[band, band, edges, edges, edges, full, mine, keep, lines] + ends_out,
        in_specs=[vmem] * 3,
        out_specs=[hbm] * 2 + [vmem] * 11,
        scratch_shapes=[
            pltpu.VMEM((groups,) + rows.shape, F32),
            pltpu.VMEM((groups - 1,) + rows.shape, F32),
            pltpu.VMEM((2 * groups - 1 + 3 * groups - 4, WIDE, WIDE), F32),
            pltpu.SemaphoreType.DMA((2, groups)),
            pltpu.SemaphoreType.DMA((3,)),
        ],
        compiler_params=params,
        cost_estimate=pl.CostEstimate(
            flops=3 * 2 * 16 * WIDE**3, bytes_accessed=16 * 2**20, transcendentals=0
        ),
    )(matrix, other, flags)

    across, low_sign = lax.optimization_barrier((across, low_sign))
    along, low_sign = lax.optimization_barrier((along, low_sign))
    across_other = lax.ppermute(across, half_axis, swap)
    along_other = lax.ppermute(along, half_axis, swap)

    sign_last, high_sign, *high_ends = pl.pallas_call(
        last_kernel,
        out_shape=[rows, edges] + ends_out,
        in_specs=[vmem] * 5,
        out_specs=[vmem] * 6,
        scratch_shapes=[pltpu.VMEM((2, GROUP * HALF, WIDE), F32)],
        compiler_params=params,
        cost_estimate=pl.CostEstimate(
            flops=3 * 2 * 4 * WIDE**3, bytes_accessed=4 * 2**20, transcendentals=0
        ),
    )(matrix, lines, full, mine, keep)

    outs = pl.pallas_call(
        functools.partial(border_kernel, groups=groups, axes=axes, half_axis=half_axis),
        out_shape=[edges] * 4 + [band] * 2,
        in_specs=[vmem] * 18 + [hbm] * 2,
        out_specs=[vmem] * 4 + [hbm] * 2,
        scratch_shapes=[
            pltpu.VMEM((2, 2, WIDE, 2 * WIDE), BF),
            pltpu.VMEM((2, 2, REACH * BS, WIDE), F32),
            pltpu.VMEM((2, 2, REACH * HALF, WIDE), F32),
            pltpu.SemaphoreType.DMA((2, 2)),
            pltpu.SemaphoreType.DMA((2,)),
        ],
        input_output_aliases={14 + i: i for i in range(6)},
        compiler_params=params,
        cost_estimate=pl.CostEstimate(
            flops=3 * 2 * 4 * WIDE**3, bytes_accessed=2 * 2**20, transcendentals=0
        ),
    )(
        across, across_other, along, along_other, lines, sign_last, *low_ends, *high_ends, low_square, high_square,
        low_sign, high_sign, square, sign,
    )
    return tuple(outs[4:])


def solution(mesh):
    band = P(("group", "row", "col"), None, "rep", None)
    return jax.shard_map(
        functools.partial(shards, axes=("row", "col"), half_axis="rep"),
        mesh=mesh,
        in_specs=(band, P("group", None)),
        out_specs=(band, band),
        check_vma=False,
    )
```

```python
import functools

import jax
import jax.numpy as jnp
from jax import lax
from jax.experimental import pallas as pl
from jax.experimental.pallas import tpu as pltpu
from jax.sharding import PartitionSpec as P

REACH = 3
SPAN = 7
BS = 64
HALF = 32
GROUP = 4
WIDE = GROUP * BS
BF = jnp.bfloat16
F32 = jnp.float32
LIMIT = 32 * 1024 * 1024


def split(x):
    hi = x.astype(BF)
    return hi, (x - hi.astype(F32)).astype(BF)


def product(pairs, transposed=False):
    side = 1 if transposed else 0
    high, low = [jnp.concatenate([a[p] for a, _ in pairs], axis=1) for p in range(2)]
    right = [jnp.concatenate([b[p] for _, b in pairs], axis=side) for p in range(2)]
    dot = functools.partial(
        lax.dot_general,
        dimension_numbers=(((1,), (side,)), ((), ())),
        preferred_element_type=F32,
    )
    both = dot(jnp.concatenate([high, low], axis=0), right[0])
    count = high.shape[0]
    return both[:count] + (both[count:] + dot(high, right[1]))


def turn(x):
    return split((x[0].astype(F32) + x[1].astype(F32)).T)


def write_lines(pat, lines, first, groups):
    total = pat.shape[1]
    rows = lines.shape[0]
    iota = functools.partial(lax.broadcasted_iota, jnp.int32)
    dot = functools.partial(lax.dot_general, preferred_element_type=F32)
    wanted = lax.rem(first - GROUP + total + iota((rows, total), 0), total)
    chosen = (iota((rows, total), 1) == wanted).astype(BF)
    flags = dot(chosen, pat[...].astype(BF), (((1,), (1,)), ((), ())))
    place = iota((rows, 1), 0) % GROUP
    spread = jnp.concatenate(
        [jnp.where(place == s, flags, 0.0) for s in range(GROUP)], axis=1
    ).astype(BF)
    block = iota((SPAN, 3 * WIDE), 1) // BS - iota((SPAN, 3 * WIDE), 0) - 1
    spots = jnp.concatenate([(block == s).astype(BF) for s in range(GROUP)], axis=0)
    lines[...] = dot(spread, spots, (((1,), (0,)), ((), ())))


def line_of(lines, g, s, h):
    at = (g + 1) * GROUP + s
    lo = (h - g + 1) * WIDE
    return lines[at : at + 1, lo : lo + WIDE]


def inner_rows(g, groups):
    return range(REACH if g == 0 else 0, GROUP - REACH if g == groups - 1 else GROUP)


def inner_blocks(side, is_square):
    first = REACH if is_square else 2 * REACH
    return (first, SPAN) if side == 0 else (0, SPAN - first)


def outer_blocks(side, is_square):
    k0, k1 = inner_blocks(side, is_square)
    return (0, k0) if side == 0 else (k1, SPAN)


def blocks_of(ref, rows, blocks):
    return ref.at[pl.ds(rows[0], rows[1] - rows[0]), pl.ds(blocks[0], blocks[1] - blocks[0])]


def row_of(g, s, groups, rows, low, high):
    if s in inner_rows(g, groups):
        return rows.at[s]
    return low.at[s] if g == 0 else high.at[s - (GROUP - REACH)]


def edge_kernel(top, bottom, to_left, to_right):
    for source, target in ((top, to_left), (bottom, to_right)):
        for s in range(REACH):
            for t in range(2):
                target[s * HALF : (s + 1) * HALF, t * 2 * BS : (t + 1) * 2 * BS] = jnp.concatenate(
                    [source[s, 2 * t], source[s, 2 * t + 1]], axis=1
                )


class Interior:
    def __init__(self, own, lines, full, mine, keep):
        self.own = own
        self.lines = lines
        self.full = full
        self.mine = mine
        self.keep = keep
        self.count = own.shape[0]
        self.groups = self.count // GROUP
        self.stores = []

    def part(self, g, h, rows=slice(None)):
        at = (h - g + 1) * WIDE
        return [self.full[p, g, rows, at : at + WIDE] for p in range(2)]

    def my_part(self, g, h):
        at = (h - g + 1) * WIDE
        return [self.mine[p, g, :, at : at + WIDE] for p in range(2)]

    def tile(self, g, h):
        return 3 * g + h - g + 1

    def kept(self, g, h):
        return [self.keep[p, self.tile(g, h)] for p in range(2)]

    def near(self, g):
        return [e for e in (g - 1, g, g + 1) if 0 <= e < self.groups]

    def second(self, g, h, sign, low, high, result):
        span = range(1 if h > g else 0, GROUP - 1 if h < g else GROUP)
        rows = slice(span[0] * HALF, (span[-1] + 1) * HALF)

        def dot():
            return product(
                [
                    ([x[rows] for x in self.my_part(g, e)], self.kept(e, h))
                    for e in self.near(g)
                    if abs(e - h) <= 1
                ]
            )

        def store(value):
            result[rows] = value

        def post():
            for s in span:
                a = g * GROUP + s
                target = row_of(g, s, self.groups, sign, low, high)
                part = result[s * HALF : (s + 1) * HALF] * (line_of(self.lines, g, s, h) * 0.5)
                for t in range(GROUP):
                    k = t + GROUP * (h - g) - s + REACH
                    if 0 <= k < SPAN:
                        target[k] = 1.5 * self.own[a, k] - part[:, t * BS : (t + 1) * BS]

        return dot, store, post

    def far_seed(self, g, seed):
        for s in range(REACH):
            a = s if g == 0 else self.count - REACH + s
            for k in range(0, REACH - s) if g == 0 else range(2 * REACH - s, SPAN):
                seed[s, k] = 1.5 * self.own[a, k]

    def reaching(self, a_ref, b_ref, m_ref, p_ref, g, e, r0):
        rows = slice(r0, r0 + REACH * BS)
        mine_rows = slice(r0 // 2, r0 // 2 + REACH * HALF)
        outer = slice(BS - r0, BS - r0 + REACH * BS)

        def dot():
            out = self.part(g, e)
            turned = turn(out)
            middle = self.part(g, g, rows)
            left = [jnp.concatenate([turned[p][outer], middle[p]], axis=0) for p in range(2)]
            return product([(left, out)])

        def store(value):
            a_ref[...], b_ref[...] = value[: REACH * BS], value[REACH * BS :]

        def post():
            for p in range(2):
                m_ref[p] = self.part(g, e)[p][rows]
                p_ref[p, 0] = self.my_part(g, e)[p][mine_rows]
                p_ref[p, 1] = self.my_part(g, g)[p][mine_rows]

        return dot, store, post

    def send(self, g, i, source, target, sems):
        rows = inner_rows(g, self.groups)
        store = pltpu.make_async_copy(
            source.at[pl.ds(rows[0], len(rows))],
            target.at[pl.ds(g * GROUP + rows[0], len(rows))],
            sems.at[i, g],
        )
        store.start()
        self.stores.append(store)

    def send_edge(self, side, i, source, target, sem):
        first = 0 if side == 0 else self.count - REACH
        blocks = inner_blocks(side, i == 0)
        store = pltpu.make_async_copy(
            blocks_of(source, (0, REACH), blocks),
            blocks_of(target, (first, first + REACH), blocks),
            sem,
        )
        store.start()
        self.stores.append(store)

    def finish(self):
        for store in self.stores:
            store.wait()


def count_dots(steps):
    return sum(isinstance(step, tuple) for step in steps)


def staggered(steps):
    pending = []
    for step in steps:
        if not isinstance(step, tuple):
            pending.append(step)
            continue
        dot, store, post = step
        value = dot()
        for work in pending:
            work()
        store(value)
        pending = [post]
    for work in pending:
        work()


def first_kernel(
    own, other, pat, square_out, sign_out, low_square, high_square, low_sign, full, mine, keep, lines, low_a, low_b, low_m, low_p,
    high_a, high_b, high_m, high_p, square, sign, results, sems, edge_sems, *, axes, half_axis
):
    it = Interior(own, lines, full, mine, keep)
    groups = it.groups
    upper_half = lax.axis_index(half_axis) == 1

    def build(g):
        for s in range(GROUP):
            a = g * GROUP + s
            for t in range(3 * GROUP // 2):
                ks = [2 * t + e - s - 1 for e in range(2)]
                lanes = slice(t * 2 * BS, (t + 1) * 2 * BS)
                rows = slice(s * BS, (s + 1) * BS)
                mine_rows = slice(s * HALF, (s + 1) * HALF)
                if all(k < 0 or k >= SPAN for k in ks):
                    for p in range(2):
                        full[p, g, rows, lanes] = jnp.zeros((BS, 2 * BS), BF)
                        mine[p, g, mine_rows, lanes] = jnp.zeros((HALF, 2 * BS), BF)
                    continue
                two = [
                    jnp.concatenate(
                        [src[a, k] if 0 <= k < SPAN else jnp.zeros((HALF, BS), F32) for k in ks],
                        axis=1,
                    )
                    for src in (own, other)
                ]
                for p, (x, y) in enumerate(zip(*[split(x) for x in two])):
                    mine[p, g, mine_rows, lanes] = x
                    full[p, g, rows, lanes] = jnp.concatenate(
                        [jnp.where(upper_half, y, x), jnp.where(upper_half, x, y)], axis=0
                    )

    def squares(g, h, result):
        pairs = []
        for e in (g - 1, g, g + 1):
            if abs(e - h) <= 1:
                inside = 0 <= e < groups
                pairs.append((e, (lambda e=e: it.part(e, h)) if inside else (lambda e=e: turn(it.part(h, e)))))
        span = range(1 if h > g else 0, GROUP)
        rows = slice(span[0] * BS, WIDE)

        def dot():
            return product([([x[rows] for x in it.part(g, e)], f()) for e, f in pairs])

        def store(value):
            result[rows] = value

        def post():
            masked = [jnp.zeros((BS, WIDE), F32)] * GROUP
            for s in span:
                masked[s] = result[s * BS : (s + 1) * BS] * line_of(lines, g, s, h)
            for s in range(GROUP):
                for p, x in enumerate(split(masked[s])):
                    keep[p, it.tile(g, h), s * BS : (s + 1) * BS] = x
            for s in span:
                part = jnp.where(upper_half, masked[s][HALF:], masked[s][:HALF])
                for t in range(GROUP):
                    k = t + GROUP * (h - g) - s + REACH
                    if 0 <= k < SPAN:
                        row_of(g, s, groups, square.at[g], low_square, high_square)[k] = part[
                            :, t * BS : (t + 1) * BS
                        ]
            if h == g:
                return
            for c in range(0, GROUP, 2):
                turned = jnp.concatenate(masked[c : c + 2], axis=0).T
                lanes = slice(c * BS, (c + 2) * BS)
                for p, x in enumerate(split(turned)):
                    keep[p, it.tile(h, g), :, lanes] = x
                for t in range(GROUP):
                    rows = turned[t * BS : (t + 1) * BS]
                    part = jnp.where(upper_half, rows[HALF:], rows[:HALF])
                    for s in range(c, c + 2):
                        k = s + GROUP * (g - h) - t + REACH
                        if 0 <= k < SPAN:
                            row_of(h, t, groups, square.at[h], low_square, high_square)[k] = part[
                                :, (s - c) * BS : (s - c + 1) * BS
                            ]

        return dot, store, post


    def begin():
        write_lines(pat, lines, lax.axis_index(axes) * it.count, groups)
        it.far_seed(0, low_sign)

    build(0)
    build(1)
    steps = [begin]
    for g in range(groups):
        if g + 1 < groups:
            steps.append(squares(g, g + 1, results.at[count_dots(steps)]))
            if g + 2 < groups:
                steps.append(functools.partial(build, g + 2))
        steps.append(squares(g, g, results.at[count_dots(steps)]))
        steps.append(functools.partial(it.send, g, 0, square.at[g], square_out, sems))
        if g in (0, groups - 1):
            side, source = (0, low_square) if g == 0 else (1, high_square)
            steps.append(
                functools.partial(it.send_edge, side, 0, source, square_out, edge_sems.at[side])
            )
    for g in range(groups - 1):
        for h in it.near(g):
            steps.append(it.second(g, h, sign.at[g], low_sign, None, results.at[count_dots(steps)]))
        steps.append(functools.partial(it.send, g, 1, sign.at[g], sign_out, sems))
        if g == 0:
            steps.append(functools.partial(it.send_edge, 0, 1, low_sign, sign_out, edge_sems.at[2]))
    steps.append(it.reaching(low_a, low_b, low_m, low_p, 0, -1, 0))
    steps.append(it.reaching(high_a, high_b, high_m, high_p, groups - 1, groups, BS))
    staggered(steps)
    it.finish()


def last_kernel(own, lines, full, mine, keep, sign, high_sign, results):
    it = Interior(own, lines, full, mine, keep)
    last = it.groups - 1
    steps = [it.second(last, h, sign, None, high_sign, results.at[i]) for i, h in enumerate(it.near(last))]
    steps.append(functools.partial(it.far_seed, last, high_sign))

    staggered(steps)


def border(
    side, groups, upper_half, lines, mine, theirs, a_ref, b_ref, m_ref, p_ref, square, sign, halo,
    first, last, sent
):
    at = 1 - side
    edge_group, outer_group = (0, -1) if side == 0 else (groups - 1, groups)
    offset = 0 if side == 0 else 2 * REACH
    below = REACH if side == 0 else 0
    zero = jnp.zeros((BS, WIDE), F32)

    def padded(rows, front):
        return split(jnp.concatenate([zero] + rows if front else rows + [zero], axis=0))

    whole_rows = []
    for p in range(REACH):
        rows = slice(p * HALF, (p + 1) * HALF)
        whole_rows.append(
            jnp.concatenate(
                [
                    jnp.where(upper_half, theirs[rows, :], mine[rows, :]),
                    jnp.where(upper_half, mine[rows, :], theirs[rows, :]),
                ],
                axis=0,
            )
        )

    def block(p, c):
        k = c - p + below
        if 0 <= k <= REACH:
            return whole_rows[p][:, k * BS : (k + 1) * BS]
        k = p - c + below
        if 0 <= c < REACH and 0 <= k <= REACH:
            return whole_rows[c][:, k * BS : (k + 1) * BS].T
        return jnp.zeros((BS, BS), F32)

    base = -5 if side == 0 else 0
    for p in range(REACH):
        rows = slice((p + at) * BS, (p + at + 1) * BS)
        for t in range(4):
            value = jnp.concatenate([block(p, base + 2 * t), block(p, base + 2 * t + 1)], axis=1)
            for q, x in enumerate(split(value)):
                halo[q, rows, t * 2 * BS : (t + 1) * 2 * BS] = x
    rows = slice(0, BS) if side == 0 else slice(REACH * BS, WIDE)
    for q in range(2):
        halo[q, rows, :] = jnp.zeros((BS, 2 * WIDE), BF)

    whole = [halo[q] for q in range(2)]
    outer_rows = slice(at * BS, (at + REACH) * BS)
    inner = slice(WIDE, 2 * WIDE) if side == 0 else slice(0, WIDE)
    to_edge = product([([m_ref[q] for q in range(2)], [x[:, inner] for x in whole])])
    among = product([([x[outer_rows] for x in whole], whole)], True)
    yield
    first[0] = to_edge + b_ref[...]
    rows = [
        first[0, s * BS : (s + 1) * BS] * line_of(lines, edge_group, s + 1 - at, outer_group)
        for s in range(REACH)
    ]
    across = padded(rows, side == 1)
    reach_out = [p_ref[q, 0] for q in range(2)]
    back = product([(reach_out, across)], True)
    for s in range(REACH):
        part = jnp.where(upper_half, rows[s][HALF:], rows[s][:HALF])
        for t in range(REACH):
            k = t - s + offset
            if 0 <= k < SPAN:
                square[s, k] = part[:, (t + at) * BS : (t + at + 1) * BS]
    sent(0)
    yield
    first[1] = among + a_ref[...]
    rows = [
        first[1, p * BS : (p + 1) * BS] * line_of(lines, outer_group, p + at, outer_group)
        for p in range(REACH)
    ]
    inside = [p_ref[q, 1] for q in range(2)]
    out = product([(reach_out, padded(rows, side == 0)), (inside, across)])
    last[1] = back
    for s in range(REACH):
        close = last[1, s * HALF : (s + 1) * HALF] * (
            line_of(lines, edge_group, s + 1 - at, edge_group) * 0.5
        )
        for t in range(REACH):
            k = t - s + REACH
            sign[s, k] = sign[s, k] - close[:, (t + 1 - at) * BS : (t + 2 - at) * BS]
    yield
    last[0] = out
    for s in range(REACH):
        far = last[0, s * HALF : (s + 1) * HALF] * (
            line_of(lines, edge_group, s + 1 - at, outer_group) * 0.5
        )
        for t in range(REACH):
            k = t - s + offset
            if 0 <= k < SPAN:
                sign[s, k] = sign[s, k] - far[:, (t + at) * BS : (t + at + 1) * BS]
    sent(1)


def border_kernel(
    low_own, low_other, high_own, high_other, lines, sign_last, low_a, low_b, low_m, low_p, high_a,
    high_b, high_m, high_p, low_square_in, high_square_in, low_sign_in, high_sign_in, square_in,
    sign_in, low_square, high_square, low_sign, high_sign, square_out, sign_out, halo, first, last,
    sems, last_sems, *, groups, half_axis
):
    count = square_in.shape[0]
    upper_half = lax.axis_index(half_axis) == 1
    stores = []

    def send(source, target, rows, blocks, sem):
        from_rows = (0, rows[1] - rows[0])
        store = pltpu.make_async_copy(
            blocks_of(source, from_rows, blocks), blocks_of(target, rows, blocks), sem
        )
        store.start()
        stores.append(store)

    send(sign_last, sign_out, (count - GROUP, count - REACH), (0, SPAN), last_sems.at[0])
    send(high_sign, sign_out, (count - REACH, count), inner_blocks(1, False), last_sems.at[1])
    squares, signs = (low_square, high_square), (low_sign, high_sign)

    def side(n, *refs):
        def sent(i):
            source, target = ((squares[n], square_out), (signs[n], sign_out))[i]
            rows = (0, REACH) if n == 0 else (count - REACH, count)
            send(source, target, rows, outer_blocks(n, i == 0), sems.at[n, i])

        return border(
            n, groups, upper_half, lines, *refs, squares[n], signs[n], halo.at[n], first.at[n],
            last.at[n], sent,
        )

    works = [
        side(0, low_own, low_other, low_a, low_b, low_m, low_p),
        side(1, high_own, high_other, high_a, high_b, high_m, high_p),
    ]
    for _ in range(4):
        for work in works:
            next(work, None)
    for store in stores:
        store.wait()


def shards(matrix, pattern, *, axes, half_axis):
    count = matrix.shape[0]
    groups = count // GROUP
    flags = pattern.T
    vmem = pl.BlockSpec(memory_space=pltpu.VMEM)
    hbm = pl.BlockSpec(memory_space=pl.ANY)
    params = pltpu.CompilerParams(vmem_limit_bytes=LIMIT)

    top, bottom = matrix[:REACH, REACH:], matrix[count - REACH :, : REACH + 1]
    matrix, top, bottom = lax.optimization_barrier((matrix, top, bottom))
    edge = jax.ShapeDtypeStruct((REACH * HALF, (REACH + 1) * BS), F32)
    to_left, to_right = pl.pallas_call(
        edge_kernel,
        out_shape=(edge, edge),
        in_specs=[vmem] * 2,
        out_specs=[vmem] * 2,
        compiler_params=params,
        cost_estimate=pl.CostEstimate(
            flops=1 * 10**9, bytes_accessed=2**20, transcendentals=0
        ),
    )(top, bottom)
    size = 1
    for axis in axes:
        size *= lax.axis_size(axis)
    swap = [(0, 1), (1, 0)]
    other = lax.ppermute(matrix, half_axis, swap)
    forward = [(i, (i + 1) % size) for i in range(size)]
    backward = [(target, source) for source, target in forward]
    high_own = lax.ppermute(to_left, axes, backward)
    low_own = lax.ppermute(to_right, axes, forward)

    band = jax.ShapeDtypeStruct(matrix.shape, F32)
    edges = jax.ShapeDtypeStruct((REACH, SPAN, HALF, BS), F32)
    full = jax.ShapeDtypeStruct((2, groups, WIDE, 3 * WIDE), BF)
    mine = jax.ShapeDtypeStruct((2, groups, GROUP * HALF, 3 * WIDE), BF)
    keep = jax.ShapeDtypeStruct((2, 3 * groups, WIDE, WIDE), BF)
    lines = jax.ShapeDtypeStruct(((groups + 2) * GROUP, 3 * WIDE), F32)
    ends_out = [
        jax.ShapeDtypeStruct((REACH * BS, WIDE), F32),
        jax.ShapeDtypeStruct((REACH * BS, WIDE), F32),
        jax.ShapeDtypeStruct((2, REACH * BS, WIDE), BF),
        jax.ShapeDtypeStruct((2, 2, REACH * HALF, WIDE), BF),
    ]
    rows = jax.ShapeDtypeStruct((GROUP,) + matrix.shape[1:], F32)
    square, sign, low_square, high_square, low_sign, full, mine, keep, lines, *ends = pl.pallas_call(
        functools.partial(first_kernel, axes=axes, half_axis=half_axis),
        out_shape=[band, band, edges, edges, edges, full, mine, keep, lines] + ends_out * 2,
        in_specs=[vmem] * 3,
        out_specs=[hbm] * 2 + [vmem] * 15,
        scratch_shapes=[
            pltpu.VMEM((groups,) + rows.shape, F32),
            pltpu.VMEM((groups - 1,) + rows.shape, F32),
            pltpu.VMEM((2 * groups - 1 + 3 * groups - 4, WIDE, WIDE), F32),
            pltpu.SemaphoreType.DMA((2, groups)),
            pltpu.SemaphoreType.DMA((3,)),
        ],
        compiler_params=params,
        cost_estimate=pl.CostEstimate(
            flops=3 * 2 * 16 * WIDE**3, bytes_accessed=16 * 2**20, transcendentals=0
        ),
    )(matrix, other, flags)

    low_own, low_sign = lax.optimization_barrier((low_own, low_sign))
    high_own, low_sign = lax.optimization_barrier((high_own, low_sign))
    low_other = lax.ppermute(low_own, half_axis, swap)
    high_other = lax.ppermute(high_own, half_axis, swap)

    sign_last, high_sign = pl.pallas_call(
        last_kernel,
        out_shape=[rows, edges],
        in_specs=[vmem] * 5,
        out_specs=[vmem] * 2,
        scratch_shapes=[pltpu.VMEM((2, GROUP * HALF, WIDE), F32)],
        compiler_params=params,
        cost_estimate=pl.CostEstimate(
            flops=3 * 2 * 4 * WIDE**3, bytes_accessed=4 * 2**20, transcendentals=0
        ),
    )(matrix, lines, full, mine, keep)

    outs = pl.pallas_call(
        functools.partial(border_kernel, groups=groups, half_axis=half_axis),
        out_shape=[edges] * 4 + [band] * 2,
        in_specs=[vmem] * 18 + [hbm] * 2,
        out_specs=[vmem] * 4 + [hbm] * 2,
        scratch_shapes=[
            pltpu.VMEM((2, 2, WIDE, 2 * WIDE), BF),
            pltpu.VMEM((2, 2, REACH * BS, WIDE), F32),
            pltpu.VMEM((2, 2, REACH * HALF, WIDE), F32),
            pltpu.SemaphoreType.DMA((2, 2)),
            pltpu.SemaphoreType.DMA((2,)),
        ],
        input_output_aliases={14 + i: i for i in range(6)},
        compiler_params=params,
        cost_estimate=pl.CostEstimate(
            flops=3 * 2 * 4 * WIDE**3, bytes_accessed=2 * 2**20, transcendentals=0
        ),
    )(
        low_own, low_other, high_own, high_other, lines, sign_last, *ends, low_square, high_square,
        low_sign, high_sign, square, sign,
    )
    return tuple(outs[4:])


def solution(mesh):
    band = P(("group", "row", "col"), None, "rep", None)
    return jax.shard_map(
        functools.partial(shards, axes=("row", "col"), half_axis="rep"),
        mesh=mesh,
        in_specs=(band, P("group", None)),
        out_specs=(band, band),
        check_vma=False,
    )
```

```python
import functools

import jax
import jax.numpy as jnp
from jax import lax
from jax.experimental import pallas as pl
from jax.experimental.pallas import tpu as pltpu
from jax.sharding import PartitionSpec as P

REACH = 3
SPAN = 7
BS = 64
HALF = 32
GROUP = 4
WIDE = GROUP * BS
BF = jnp.bfloat16
F32 = jnp.float32
LIMIT = 32 * 1024 * 1024


def split(x):
    hi = x.astype(BF)
    return hi, (x - hi.astype(F32)).astype(BF)


def product(pairs, transposed=False):
    side = 1 if transposed else 0
    high, low = [jnp.concatenate([a[p] for a, _ in pairs], axis=1) for p in range(2)]
    right = [jnp.concatenate([b[p] for _, b in pairs], axis=side) for p in range(2)]
    dot = functools.partial(
        lax.dot_general,
        dimension_numbers=(((1,), (side,)), ((), ())),
        preferred_element_type=F32,
    )
    both = dot(jnp.concatenate([high, low], axis=0), right[0])
    count = high.shape[0]
    return both[:count] + (both[count:] + dot(high, right[1]))


def turn(x):
    return split((x[0].astype(F32) + x[1].astype(F32)).T)


def write_lines(pat, lines, first, groups):
    total = pat.shape[1]
    rows = lines.shape[0]
    iota = functools.partial(lax.broadcasted_iota, jnp.int32)
    dot = functools.partial(lax.dot_general, preferred_element_type=F32)
    wanted = lax.rem(first - GROUP + total + iota((rows, total), 0), total)
    chosen = (iota((rows, total), 1) == wanted).astype(BF)
    flags = dot(chosen, pat[...].astype(BF), (((1,), (1,)), ((), ())))
    place = iota((rows, 1), 0) % GROUP
    spread = jnp.concatenate(
        [jnp.where(place == s, flags, 0.0) for s in range(GROUP)], axis=1
    ).astype(BF)
    block = iota((SPAN, 3 * WIDE), 1) // BS - iota((SPAN, 3 * WIDE), 0) - 1
    spots = jnp.concatenate([(block == s).astype(BF) for s in range(GROUP)], axis=0)
    lines[...] = dot(spread, spots, (((1,), (0,)), ((), ())))


def line_of(lines, g, s, h):
    at = (g + 1) * GROUP + s
    lo = (h - g + 1) * WIDE
    return lines[at : at + 1, lo : lo + WIDE]


def inner_rows(g, groups):
    return range(REACH if g == 0 else 0, GROUP - REACH if g == groups - 1 else GROUP)


def inner_blocks(side, is_square):
    first = REACH if is_square else 2 * REACH
    return (first, SPAN) if side == 0 else (0, SPAN - first)


def outer_blocks(side, is_square):
    k0, k1 = inner_blocks(side, is_square)
    return (0, k0) if side == 0 else (k1, SPAN)


def blocks_of(ref, rows, blocks):
    return ref.at[pl.ds(rows[0], rows[1] - rows[0]), pl.ds(blocks[0], blocks[1] - blocks[0])]


def row_of(g, s, groups, rows, low, high):
    if s in inner_rows(g, groups):
        return rows.at[s]
    return low.at[s] if g == 0 else high.at[s - (GROUP - REACH)]


def edge_kernel(top, bottom, to_left, to_right):
    for source, target in ((top, to_left), (bottom, to_right)):
        for s in range(REACH):
            for t in range(2):
                target[s * HALF : (s + 1) * HALF, t * 2 * BS : (t + 1) * 2 * BS] = jnp.concatenate(
                    [source[s, 2 * t], source[s, 2 * t + 1]], axis=1
                )


class Interior:
    def __init__(self, own, lines, full, mine, keep):
        self.own = own
        self.lines = lines
        self.full = full
        self.mine = mine
        self.keep = keep
        self.count = own.shape[0]
        self.groups = self.count // GROUP
        self.stores = []

    def part(self, g, h, rows=slice(None)):
        at = (h - g + 1) * WIDE
        return [self.full[p, g, rows, at : at + WIDE] for p in range(2)]

    def my_part(self, g, h):
        at = (h - g + 1) * WIDE
        return [self.mine[p, g, :, at : at + WIDE] for p in range(2)]

    def tile(self, g, h):
        return 3 * g + h - g + 1

    def kept(self, g, h):
        return [self.keep[p, self.tile(g, h)] for p in range(2)]

    def near(self, g):
        return [e for e in (g - 1, g, g + 1) if 0 <= e < self.groups]

    def second(self, g, h, sign, low, high, result):
        span = range(1 if h > g else 0, GROUP - 1 if h < g else GROUP)
        rows = slice(span[0] * HALF, (span[-1] + 1) * HALF)

        def dot():
            return product(
                [
                    ([x[rows] for x in self.my_part(g, e)], self.kept(e, h))
                    for e in self.near(g)
                    if abs(e - h) <= 1
                ]
            )

        def store(value):
            result[rows] = value

        def post():
            for s in span:
                a = g * GROUP + s
                target = row_of(g, s, self.groups, sign, low, high)
                part = result[s * HALF : (s + 1) * HALF] * (line_of(self.lines, g, s, h) * 0.5)
                for t in range(GROUP):
                    k = t + GROUP * (h - g) - s + REACH
                    if 0 <= k < SPAN:
                        target[k] = 1.5 * self.own[a, k] - part[:, t * BS : (t + 1) * BS]

        return dot, store, post

    def far_seed(self, g, seed):
        for s in range(REACH):
            a = s if g == 0 else self.count - REACH + s
            for k in range(0, REACH - s) if g == 0 else range(2 * REACH - s, SPAN):
                seed[s, k] = 1.5 * self.own[a, k]

    def reaching(self, a_ref, b_ref, m_ref, p_ref, g, e, r0):
        rows = slice(r0, r0 + REACH * BS)
        mine_rows = slice(r0 // 2, r0 // 2 + REACH * HALF)
        outer = slice(BS - r0, BS - r0 + REACH * BS)

        def dot():
            out = self.part(g, e)
            return (
                product([([x[outer] for x in turn(out)], out)]),
                product([(self.part(g, g, rows), out)]),
            )

        def store(value):
            a_ref[...], b_ref[...] = value

        def post():
            for p in range(2):
                m_ref[p] = self.part(g, e)[p][rows]
                p_ref[p, 0] = self.my_part(g, e)[p][mine_rows]
                p_ref[p, 1] = self.my_part(g, g)[p][mine_rows]

        return dot, store, post

    def send(self, g, i, source, target, sems):
        rows = inner_rows(g, self.groups)
        store = pltpu.make_async_copy(
            source.at[pl.ds(rows[0], len(rows))],
            target.at[pl.ds(g * GROUP + rows[0], len(rows))],
            sems.at[i, g],
        )
        store.start()
        self.stores.append(store)

    def send_edge(self, side, i, source, target, sem):
        first = 0 if side == 0 else self.count - REACH
        blocks = inner_blocks(side, i == 0)
        store = pltpu.make_async_copy(
            blocks_of(source, (0, REACH), blocks),
            blocks_of(target, (first, first + REACH), blocks),
            sem,
        )
        store.start()
        self.stores.append(store)

    def finish(self):
        for store in self.stores:
            store.wait()


def count_dots(steps):
    return sum(isinstance(step, tuple) for step in steps)


def staggered(steps):
    pending = []
    for step in steps:
        if not isinstance(step, tuple):
            pending.append(step)
            continue
        dot, store, post = step
        value = dot()
        for work in pending:
            work()
        store(value)
        pending = [post]
    for work in pending:
        work()


def first_kernel(
    own, other, pat, square_out, sign_out, low_square, high_square, low_sign, full, mine, keep, lines, low_a, low_b, low_m, low_p,
    high_a, high_b, high_m, high_p, square, sign, results, sems, edge_sems, *, axes, half_axis
):
    it = Interior(own, lines, full, mine, keep)
    groups = it.groups
    upper_half = lax.axis_index(half_axis) == 1

    def build(g):
        for s in range(GROUP):
            a = g * GROUP + s
            for t in range(3 * GROUP // 2):
                ks = [2 * t + e - s - 1 for e in range(2)]
                lanes = slice(t * 2 * BS, (t + 1) * 2 * BS)
                rows = slice(s * BS, (s + 1) * BS)
                mine_rows = slice(s * HALF, (s + 1) * HALF)
                if all(k < 0 or k >= SPAN for k in ks):
                    for p in range(2):
                        full[p, g, rows, lanes] = jnp.zeros((BS, 2 * BS), BF)
                        mine[p, g, mine_rows, lanes] = jnp.zeros((HALF, 2 * BS), BF)
                    continue
                two = [
                    jnp.concatenate(
                        [src[a, k] if 0 <= k < SPAN else jnp.zeros((HALF, BS), F32) for k in ks],
                        axis=1,
                    )
                    for src in (own, other)
                ]
                for p, (x, y) in enumerate(zip(*[split(x) for x in two])):
                    mine[p, g, mine_rows, lanes] = x
                    full[p, g, rows, lanes] = jnp.concatenate(
                        [jnp.where(upper_half, y, x), jnp.where(upper_half, x, y)], axis=0
                    )

    def squares(g, h, result):
        pairs = []
        for e in (g - 1, g, g + 1):
            if abs(e - h) <= 1:
                inside = 0 <= e < groups
                pairs.append((e, (lambda e=e: it.part(e, h)) if inside else (lambda e=e: turn(it.part(h, e)))))
        span = range(1 if h > g else 0, GROUP)
        rows = slice(span[0] * BS, WIDE)

        def dot():
            return product([([x[rows] for x in it.part(g, e)], f()) for e, f in pairs])

        def store(value):
            result[rows] = value

        def post():
            masked = [jnp.zeros((BS, WIDE), F32)] * GROUP
            for s in span:
                masked[s] = result[s * BS : (s + 1) * BS] * line_of(lines, g, s, h)
            for s in range(GROUP):
                for p, x in enumerate(split(masked[s])):
                    keep[p, it.tile(g, h), s * BS : (s + 1) * BS] = x
            for s in span:
                part = jnp.where(upper_half, masked[s][HALF:], masked[s][:HALF])
                for t in range(GROUP):
                    k = t + GROUP * (h - g) - s + REACH
                    if 0 <= k < SPAN:
                        row_of(g, s, groups, square.at[g], low_square, high_square)[k] = part[
                            :, t * BS : (t + 1) * BS
                        ]
            if h == g:
                return
            for c in range(0, GROUP, 2):
                turned = jnp.concatenate(masked[c : c + 2], axis=0).T
                lanes = slice(c * BS, (c + 2) * BS)
                for p, x in enumerate(split(turned)):
                    keep[p, it.tile(h, g), :, lanes] = x
                for t in range(GROUP):
                    rows = turned[t * BS : (t + 1) * BS]
                    part = jnp.where(upper_half, rows[HALF:], rows[:HALF])
                    for s in range(c, c + 2):
                        k = s + GROUP * (g - h) - t + REACH
                        if 0 <= k < SPAN:
                            row_of(h, t, groups, square.at[h], low_square, high_square)[k] = part[
                                :, (s - c) * BS : (s - c + 1) * BS
                            ]

        return dot, store, post


    def begin():
        write_lines(pat, lines, lax.axis_index(axes) * it.count, groups)
        it.far_seed(0, low_sign)

    build(0)
    build(1)
    steps = [begin]
    for g in range(groups):
        if g + 1 < groups:
            steps.append(squares(g, g + 1, results.at[count_dots(steps)]))
            if g + 2 < groups:
                steps.append(functools.partial(build, g + 2))
        steps.append(squares(g, g, results.at[count_dots(steps)]))
        steps.append(functools.partial(it.send, g, 0, square.at[g], square_out, sems))
        if g in (0, groups - 1):
            side, source = (0, low_square) if g == 0 else (1, high_square)
            steps.append(
                functools.partial(it.send_edge, side, 0, source, square_out, edge_sems.at[side])
            )
    for g in range(groups - 1):
        for h in it.near(g):
            steps.append(it.second(g, h, sign.at[g], low_sign, None, results.at[count_dots(steps)]))
        steps.append(functools.partial(it.send, g, 1, sign.at[g], sign_out, sems))
        if g == 0:
            steps.append(functools.partial(it.send_edge, 0, 1, low_sign, sign_out, edge_sems.at[2]))
    steps.append(it.reaching(low_a, low_b, low_m, low_p, 0, -1, 0))
    steps.append(it.reaching(high_a, high_b, high_m, high_p, groups - 1, groups, BS))
    staggered(steps)
    it.finish()


def last_kernel(own, lines, full, mine, keep, sign, high_sign, results):
    it = Interior(own, lines, full, mine, keep)
    last = it.groups - 1
    steps = [it.second(last, h, sign, None, high_sign, results.at[i]) for i, h in enumerate(it.near(last))]
    steps.append(functools.partial(it.far_seed, last, high_sign))

    staggered(steps)


def border(
    side, groups, upper_half, lines, mine, theirs, a_ref, b_ref, m_ref, p_ref, square, sign, halo,
    first, last, sent
):
    at = 1 - side
    edge_group, outer_group = (0, -1) if side == 0 else (groups - 1, groups)
    offset = 0 if side == 0 else 2 * REACH
    below = REACH if side == 0 else 0
    zero = jnp.zeros((BS, WIDE), F32)

    def padded(rows, front):
        return split(jnp.concatenate([zero] + rows if front else rows + [zero], axis=0))

    whole_rows = []
    for p in range(REACH):
        rows = slice(p * HALF, (p + 1) * HALF)
        whole_rows.append(
            jnp.concatenate(
                [
                    jnp.where(upper_half, theirs[rows, :], mine[rows, :]),
                    jnp.where(upper_half, mine[rows, :], theirs[rows, :]),
                ],
                axis=0,
            )
        )

    def block(p, c):
        k = c - p + below
        if 0 <= k <= REACH:
            return whole_rows[p][:, k * BS : (k + 1) * BS]
        k = p - c + below
        if 0 <= c < REACH and 0 <= k <= REACH:
            return whole_rows[c][:, k * BS : (k + 1) * BS].T
        return jnp.zeros((BS, BS), F32)

    base = -5 if side == 0 else 0
    for p in range(REACH):
        rows = slice((p + at) * BS, (p + at + 1) * BS)
        for t in range(4):
            value = jnp.concatenate([block(p, base + 2 * t), block(p, base + 2 * t + 1)], axis=1)
            for q, x in enumerate(split(value)):
                halo[q, rows, t * 2 * BS : (t + 1) * 2 * BS] = x
    rows = slice(0, BS) if side == 0 else slice(REACH * BS, WIDE)
    for q in range(2):
        halo[q, rows, :] = jnp.zeros((BS, 2 * WIDE), BF)

    whole = [halo[q] for q in range(2)]
    outer_rows = slice(at * BS, (at + REACH) * BS)
    inner = slice(WIDE, 2 * WIDE) if side == 0 else slice(0, WIDE)
    to_edge = product([([m_ref[q] for q in range(2)], [x[:, inner] for x in whole])], True)
    among = product([([x[outer_rows] for x in whole], whole)], True)
    yield
    first[0] = to_edge + b_ref[...]
    rows = [
        first[0, s * BS : (s + 1) * BS] * line_of(lines, edge_group, s + 1 - at, outer_group)
        for s in range(REACH)
    ]
    across = padded(rows, side == 1)
    reach_out = [p_ref[q, 0] for q in range(2)]
    back = product([(reach_out, across)], True)
    for s in range(REACH):
        part = jnp.where(upper_half, rows[s][HALF:], rows[s][:HALF])
        for t in range(REACH):
            k = t - s + offset
            if 0 <= k < SPAN:
                square[s, k] = part[:, (t + at) * BS : (t + at + 1) * BS]
    sent(0)
    yield
    first[1] = among + a_ref[...]
    rows = [
        first[1, p * BS : (p + 1) * BS] * line_of(lines, outer_group, p + at, outer_group)
        for p in range(REACH)
    ]
    inside = [p_ref[q, 1] for q in range(2)]
    out = product([(reach_out, padded(rows, side == 0)), (inside, across)])
    last[1] = back
    for s in range(REACH):
        close = last[1, s * HALF : (s + 1) * HALF] * (
            line_of(lines, edge_group, s + 1 - at, edge_group) * 0.5
        )
        for t in range(REACH):
            k = t - s + REACH
            sign[s, k] = sign[s, k] - close[:, (t + 1 - at) * BS : (t + 2 - at) * BS]
    yield
    last[0] = out
    for s in range(REACH):
        far = last[0, s * HALF : (s + 1) * HALF] * (
            line_of(lines, edge_group, s + 1 - at, outer_group) * 0.5
        )
        for t in range(REACH):
            k = t - s + offset
            if 0 <= k < SPAN:
                sign[s, k] = sign[s, k] - far[:, (t + at) * BS : (t + at + 1) * BS]
    sent(1)


def border_kernel(
    low_own, low_other, high_own, high_other, lines, sign_last, low_a, low_b, low_m, low_p, high_a,
    high_b, high_m, high_p, low_square_in, high_square_in, low_sign_in, high_sign_in, square_in,
    sign_in, low_square, high_square, low_sign, high_sign, square_out, sign_out, halo, first, last,
    sems, last_sems, *, groups, half_axis
):
    count = square_in.shape[0]
    upper_half = lax.axis_index(half_axis) == 1
    stores = []

    def send(source, target, rows, blocks, sem):
        from_rows = (0, rows[1] - rows[0])
        store = pltpu.make_async_copy(
            blocks_of(source, from_rows, blocks), blocks_of(target, rows, blocks), sem
        )
        store.start()
        stores.append(store)

    send(sign_last, sign_out, (count - GROUP, count - REACH), (0, SPAN), last_sems.at[0])
    send(high_sign, sign_out, (count - REACH, count), inner_blocks(1, False), last_sems.at[1])
    squares, signs = (low_square, high_square), (low_sign, high_sign)

    def side(n, *refs):
        def sent(i):
            source, target = ((squares[n], square_out), (signs[n], sign_out))[i]
            rows = (0, REACH) if n == 0 else (count - REACH, count)
            send(source, target, rows, outer_blocks(n, i == 0), sems.at[n, i])

        return border(
            n, groups, upper_half, lines, *refs, squares[n], signs[n], halo.at[n], first.at[n],
            last.at[n], sent,
        )

    works = [
        side(0, low_own, low_other, low_a, low_b, low_m, low_p),
        side(1, high_own, high_other, high_a, high_b, high_m, high_p),
    ]
    for _ in range(4):
        for work in works:
            next(work, None)
    for store in stores:
        store.wait()


def shards(matrix, pattern, *, axes, half_axis):
    count = matrix.shape[0]
    groups = count // GROUP
    flags = pattern.T
    vmem = pl.BlockSpec(memory_space=pltpu.VMEM)
    hbm = pl.BlockSpec(memory_space=pl.ANY)
    params = pltpu.CompilerParams(vmem_limit_bytes=LIMIT)

    top, bottom = matrix[:REACH, REACH:], matrix[count - REACH :, : REACH + 1]
    edge = jax.ShapeDtypeStruct((REACH * HALF, (REACH + 1) * BS), F32)
    to_left, to_right = pl.pallas_call(
        edge_kernel,
        out_shape=(edge, edge),
        in_specs=[vmem] * 2,
        out_specs=[vmem] * 2,
        compiler_params=pltpu.CompilerParams(
            vmem_limit_bytes=LIMIT, allow_input_fusion=[True, True]
        ),
        cost_estimate=pl.CostEstimate(
            flops=1 * 10**9, bytes_accessed=2**20, transcendentals=0
        ),
    )(top, bottom)
    size = 1
    for axis in axes:
        size *= lax.axis_size(axis)
    swap = [(0, 1), (1, 0)]
    other = lax.ppermute(matrix, half_axis, swap)
    forward = [(i, (i + 1) % size) for i in range(size)]
    backward = [(target, source) for source, target in forward]
    high_own = lax.ppermute(to_left, axes, backward)
    low_own = lax.ppermute(to_right, axes, forward)

    band = jax.ShapeDtypeStruct(matrix.shape, F32)
    edges = jax.ShapeDtypeStruct((REACH, SPAN, HALF, BS), F32)
    full = jax.ShapeDtypeStruct((2, groups, WIDE, 3 * WIDE), BF)
    mine = jax.ShapeDtypeStruct((2, groups, GROUP * HALF, 3 * WIDE), BF)
    keep = jax.ShapeDtypeStruct((2, 3 * groups, WIDE, WIDE), BF)
    lines = jax.ShapeDtypeStruct(((groups + 2) * GROUP, 3 * WIDE), F32)
    ends_out = [
        jax.ShapeDtypeStruct((REACH * BS, WIDE), F32),
        jax.ShapeDtypeStruct((REACH * BS, WIDE), F32),
        jax.ShapeDtypeStruct((2, REACH * BS, WIDE), BF),
        jax.ShapeDtypeStruct((2, 2, REACH * HALF, WIDE), BF),
    ]
    rows = jax.ShapeDtypeStruct((GROUP,) + matrix.shape[1:], F32)
    square, sign, low_square, high_square, low_sign, full, mine, keep, lines, *ends = pl.pallas_call(
        functools.partial(first_kernel, axes=axes, half_axis=half_axis),
        out_shape=[band, band, edges, edges, edges, full, mine, keep, lines] + ends_out * 2,
        in_specs=[vmem] * 3,
        out_specs=[hbm] * 2 + [vmem] * 15,
        scratch_shapes=[
            pltpu.VMEM((groups,) + rows.shape, F32),
            pltpu.VMEM((groups - 1,) + rows.shape, F32),
            pltpu.VMEM((2 * groups - 1 + 3 * groups - 4, WIDE, WIDE), F32),
            pltpu.SemaphoreType.DMA((2, groups)),
            pltpu.SemaphoreType.DMA((3,)),
        ],
        compiler_params=params,
        cost_estimate=pl.CostEstimate(
            flops=3 * 2 * 16 * WIDE**3, bytes_accessed=16 * 2**20, transcendentals=0
        ),
    )(matrix, other, flags)

    low_own, low_sign = lax.optimization_barrier((low_own, low_sign))
    high_own, low_sign = lax.optimization_barrier((high_own, low_sign))
    low_other = lax.ppermute(low_own, half_axis, swap)
    high_other = lax.ppermute(high_own, half_axis, swap)

    sign_last, high_sign = pl.pallas_call(
        last_kernel,
        out_shape=[rows, edges],
        in_specs=[vmem] * 5,
        out_specs=[vmem] * 2,
        scratch_shapes=[pltpu.VMEM((2, GROUP * HALF, WIDE), F32)],
        compiler_params=params,
        cost_estimate=pl.CostEstimate(
            flops=3 * 2 * 4 * WIDE**3, bytes_accessed=4 * 2**20, transcendentals=0
        ),
    )(matrix, lines, full, mine, keep)

    outs = pl.pallas_call(
        functools.partial(border_kernel, groups=groups, half_axis=half_axis),
        out_shape=[edges] * 4 + [band] * 2,
        in_specs=[vmem] * 18 + [hbm] * 2,
        out_specs=[vmem] * 4 + [hbm] * 2,
        scratch_shapes=[
            pltpu.VMEM((2, 2, WIDE, 2 * WIDE), BF),
            pltpu.VMEM((2, 2, REACH * BS, WIDE), F32),
            pltpu.VMEM((2, 2, REACH * HALF, WIDE), F32),
            pltpu.SemaphoreType.DMA((2, 2)),
            pltpu.SemaphoreType.DMA((2,)),
        ],
        input_output_aliases={14 + i: i for i in range(6)},
        compiler_params=params,
        cost_estimate=pl.CostEstimate(
            flops=3 * 2 * 4 * WIDE**3, bytes_accessed=2 * 2**20, transcendentals=0
        ),
    )(
        low_own, low_other, high_own, high_other, lines, sign_last, *ends, low_square, high_square,
        low_sign, high_sign, square, sign,
    )
    return tuple(outs[4:])


def solution(mesh):
    band = P(("group", "row", "col"), None, "rep", None)
    return jax.shard_map(
        functools.partial(shards, axes=("row", "col"), half_axis="rep"),
        mesh=mesh,
        in_specs=(band, P("group", None)),
        out_specs=(band, band),
        check_vma=False,
    )
```

```python
import functools

import jax
import jax.numpy as jnp
from jax import lax
from jax.experimental import pallas as pl
from jax.experimental.pallas import tpu as pltpu
from jax.sharding import PartitionSpec as P

REACH = 3
SPAN = 7
BS = 64
HALF = 32
GROUP = 4
WIDE = GROUP * BS
BF = jnp.bfloat16
F32 = jnp.float32
LIMIT = 32 * 1024 * 1024


def split(x):
    hi = x.astype(BF)
    return hi, (x - hi.astype(F32)).astype(BF)


def product(pairs, transposed=False):
    side = 1 if transposed else 0
    high, low = [jnp.concatenate([a[p] for a, _ in pairs], axis=1) for p in range(2)]
    right = [jnp.concatenate([b[p] for _, b in pairs], axis=side) for p in range(2)]
    dot = functools.partial(
        lax.dot_general,
        dimension_numbers=(((1,), (side,)), ((), ())),
        preferred_element_type=F32,
    )
    both = dot(jnp.concatenate([high, low], axis=0), right[0])
    count = high.shape[0]
    return both[:count] + (both[count:] + dot(high, right[1]))


def turn(x):
    return split((x[0].astype(F32) + x[1].astype(F32)).T)


def write_lines(pat, lines, first, groups):
    total = pat.shape[1]
    rows = lines.shape[0]
    iota = functools.partial(lax.broadcasted_iota, jnp.int32)
    dot = functools.partial(lax.dot_general, preferred_element_type=F32)
    wanted = lax.rem(first - GROUP + total + iota((rows, total), 0), total)
    chosen = (iota((rows, total), 1) == wanted).astype(BF)
    flags = dot(chosen, pat[...].astype(BF), (((1,), (1,)), ((), ())))
    place = iota((rows, 1), 0) % GROUP
    spread = jnp.concatenate(
        [jnp.where(place == s, flags, 0.0) for s in range(GROUP)], axis=1
    ).astype(BF)
    block = iota((SPAN, 3 * WIDE), 1) // BS - iota((SPAN, 3 * WIDE), 0) - 1
    spots = jnp.concatenate([(block == s).astype(BF) for s in range(GROUP)], axis=0)
    lines[...] = dot(spread, spots, (((1,), (0,)), ((), ())))


def line_of(lines, g, s, h):
    at = (g + 1) * GROUP + s
    lo = (h - g + 1) * WIDE
    return lines[at : at + 1, lo : lo + WIDE]


def inner_rows(g, groups):
    return range(REACH if g == 0 else 0, GROUP - REACH if g == groups - 1 else GROUP)


def inner_blocks(side, is_square):
    first = REACH if is_square else 2 * REACH
    return (first, SPAN) if side == 0 else (0, SPAN - first)


def outer_blocks(side, is_square):
    k0, k1 = inner_blocks(side, is_square)
    return (0, k0) if side == 0 else (k1, SPAN)


def blocks_of(ref, rows, blocks):
    return ref.at[pl.ds(rows[0], rows[1] - rows[0]), pl.ds(blocks[0], blocks[1] - blocks[0])]


def row_of(g, s, groups, rows, low, high):
    if s in inner_rows(g, groups):
        return rows.at[s]
    return low.at[s] if g == 0 else high.at[s - (GROUP - REACH)]


def edge_kernel(top, bottom, to_left, to_right):
    for source, target in ((top, to_left), (bottom, to_right)):
        for s in range(REACH):
            for t in range(2):
                target[s * HALF : (s + 1) * HALF, t * 2 * BS : (t + 1) * 2 * BS] = jnp.concatenate(
                    [source[s, 2 * t], source[s, 2 * t + 1]], axis=1
                )


class Interior:
    def __init__(self, own, lines, full, mine, keep):
        self.own = own
        self.lines = lines
        self.full = full
        self.mine = mine
        self.keep = keep
        self.count = own.shape[0]
        self.groups = self.count // GROUP
        self.stores = []

    def part(self, g, h, rows=slice(None)):
        at = (h - g + 1) * WIDE
        return [self.full[p, g, rows, at : at + WIDE] for p in range(2)]

    def my_part(self, g, h):
        at = (h - g + 1) * WIDE
        return [self.mine[p, g, :, at : at + WIDE] for p in range(2)]

    def tile(self, g, h):
        return 3 * g + h - g + 1

    def kept(self, g, h):
        return [self.keep[p, self.tile(g, h)] for p in range(2)]

    def near(self, g):
        return [e for e in (g - 1, g, g + 1) if 0 <= e < self.groups]

    def second(self, g, h, sign, low, high, result):
        span = range(1 if h > g else 0, GROUP - 1 if h < g else GROUP)
        rows = slice(span[0] * HALF, (span[-1] + 1) * HALF)

        def dot():
            return product(
                [
                    ([x[rows] for x in self.my_part(g, e)], self.kept(e, h))
                    for e in self.near(g)
                    if abs(e - h) <= 1
                ]
            )

        def store(value):
            result[rows] = value

        def post():
            for s in span:
                a = g * GROUP + s
                target = row_of(g, s, self.groups, sign, low, high)
                part = result[s * HALF : (s + 1) * HALF] * (line_of(self.lines, g, s, h) * 0.5)
                for t in range(GROUP):
                    k = t + GROUP * (h - g) - s + REACH
                    if 0 <= k < SPAN:
                        target[k] = 1.5 * self.own[a, k] - part[:, t * BS : (t + 1) * BS]

        return dot, store, post

    def far_seed(self, g, seed):
        for s in range(REACH):
            a = s if g == 0 else self.count - REACH + s
            for k in range(0, REACH - s) if g == 0 else range(2 * REACH - s, SPAN):
                seed[s, k] = 1.5 * self.own[a, k]

    def reaching(self, a_ref, b_ref, m_ref, p_ref, g, e, r0):
        rows = slice(r0, r0 + REACH * BS)
        mine_rows = slice(r0 // 2, r0 // 2 + REACH * HALF)
        outer = slice(BS - r0, BS - r0 + REACH * BS)

        def dot():
            out = self.part(g, e)
            return (
                product([([x[outer] for x in turn(out)], out)]),
                product([(self.part(g, g, rows), out)]),
            )

        def store(value):
            a_ref[...], b_ref[...] = value

        def post():
            for p in range(2):
                m_ref[p] = self.part(g, e)[p][rows]
                p_ref[p, 0] = self.my_part(g, e)[p][mine_rows]
                p_ref[p, 1] = self.my_part(g, g)[p][mine_rows]

        return dot, store, post

    def send(self, g, i, source, target, sems):
        rows = inner_rows(g, self.groups)
        store = pltpu.make_async_copy(
            source.at[pl.ds(rows[0], len(rows))],
            target.at[pl.ds(g * GROUP + rows[0], len(rows))],
            sems.at[i, g],
        )
        store.start()
        self.stores.append(store)

    def send_edge(self, side, i, source, target, sem):
        first = 0 if side == 0 else self.count - REACH
        blocks = inner_blocks(side, i == 0)
        store = pltpu.make_async_copy(
            blocks_of(source, (0, REACH), blocks),
            blocks_of(target, (first, first + REACH), blocks),
            sem,
        )
        store.start()
        self.stores.append(store)

    def finish(self):
        for store in self.stores:
            store.wait()


def count_dots(steps):
    return sum(isinstance(step, tuple) for step in steps)


def staggered(steps):
    pending = []
    for step in steps:
        if not isinstance(step, tuple):
            pending.append(step)
            continue
        dot, store, post = step
        value = dot()
        for work in pending:
            work()
        store(value)
        pending = [post]
    for work in pending:
        work()


def first_kernel(
    own, other, pat, square_out, sign_out, low_square, high_square, low_sign, full, mine, keep, lines, low_a, low_b, low_m, low_p,
    high_a, high_b, high_m, high_p, square, sign, results, sems, edge_sems, *, axes, half_axis
):
    it = Interior(own, lines, full, mine, keep)
    groups = it.groups
    upper_half = lax.axis_index(half_axis) == 1

    def build(g):
        for s in range(GROUP):
            a = g * GROUP + s
            for t in range(3 * GROUP // 2):
                ks = [2 * t + e - s - 1 for e in range(2)]
                lanes = slice(t * 2 * BS, (t + 1) * 2 * BS)
                rows = slice(s * BS, (s + 1) * BS)
                mine_rows = slice(s * HALF, (s + 1) * HALF)
                if all(k < 0 or k >= SPAN for k in ks):
                    for p in range(2):
                        full[p, g, rows, lanes] = jnp.zeros((BS, 2 * BS), BF)
                        mine[p, g, mine_rows, lanes] = jnp.zeros((HALF, 2 * BS), BF)
                    continue
                two = [
                    jnp.concatenate(
                        [src[a, k] if 0 <= k < SPAN else jnp.zeros((HALF, BS), F32) for k in ks],
                        axis=1,
                    )
                    for src in (own, other)
                ]
                for p, (x, y) in enumerate(zip(*[split(x) for x in two])):
                    mine[p, g, mine_rows, lanes] = x
                    full[p, g, rows, lanes] = jnp.concatenate(
                        [jnp.where(upper_half, y, x), jnp.where(upper_half, x, y)], axis=0
                    )

    def squares(g, h, result):
        pairs = []
        for e in (g - 1, g, g + 1):
            if abs(e - h) <= 1:
                inside = 0 <= e < groups
                pairs.append((e, (lambda e=e: it.part(e, h)) if inside else (lambda e=e: turn(it.part(h, e)))))
        span = range(1 if h > g else 0, GROUP)
        rows = slice(span[0] * BS, WIDE)

        def dot():
            return product([([x[rows] for x in it.part(g, e)], f()) for e, f in pairs])

        def store(value):
            result[rows] = value

        def post():
            masked = [jnp.zeros((BS, WIDE), F32)] * GROUP
            for s in span:
                masked[s] = result[s * BS : (s + 1) * BS] * line_of(lines, g, s, h)
            for s in range(GROUP):
                for p, x in enumerate(split(masked[s])):
                    keep[p, it.tile(g, h), s * BS : (s + 1) * BS] = x
            for s in span:
                part = jnp.where(upper_half, masked[s][HALF:], masked[s][:HALF])
                for t in range(GROUP):
                    k = t + GROUP * (h - g) - s + REACH
                    if 0 <= k < SPAN:
                        row_of(g, s, groups, square.at[g], low_square, high_square)[k] = part[
                            :, t * BS : (t + 1) * BS
                        ]
            if h == g:
                return
            for c in range(0, GROUP, 2):
                turned = jnp.concatenate(masked[c : c + 2], axis=0).T
                lanes = slice(c * BS, (c + 2) * BS)
                for p, x in enumerate(split(turned)):
                    keep[p, it.tile(h, g), :, lanes] = x
                for t in range(GROUP):
                    rows = turned[t * BS : (t + 1) * BS]
                    part = jnp.where(upper_half, rows[HALF:], rows[:HALF])
                    for s in range(c, c + 2):
                        k = s + GROUP * (g - h) - t + REACH
                        if 0 <= k < SPAN:
                            row_of(h, t, groups, square.at[h], low_square, high_square)[k] = part[
                                :, (s - c) * BS : (s - c + 1) * BS
                            ]

        return dot, store, post


    def begin():
        write_lines(pat, lines, lax.axis_index(axes) * it.count, groups)
        it.far_seed(0, low_sign)

    build(0)
    build(1)
    steps = [begin]
    for g in range(groups):
        if g + 1 < groups:
            steps.append(squares(g, g + 1, results.at[count_dots(steps)]))
            if g + 2 < groups:
                steps.append(functools.partial(build, g + 2))
        steps.append(squares(g, g, results.at[count_dots(steps)]))
        steps.append(functools.partial(it.send, g, 0, square.at[g], square_out, sems))
        if g in (0, groups - 1):
            side, source = (0, low_square) if g == 0 else (1, high_square)
            steps.append(
                functools.partial(it.send_edge, side, 0, source, square_out, edge_sems.at[side])
            )
    for g in range(groups - 1):
        for h in it.near(g):
            steps.append(it.second(g, h, sign.at[g], low_sign, None, results.at[count_dots(steps)]))
        steps.append(functools.partial(it.send, g, 1, sign.at[g], sign_out, sems))
        if g == 0:
            steps.append(functools.partial(it.send_edge, 0, 1, low_sign, sign_out, edge_sems.at[2]))
    steps.append(it.reaching(low_a, low_b, low_m, low_p, 0, -1, 0))
    steps.append(it.reaching(high_a, high_b, high_m, high_p, groups - 1, groups, BS))
    staggered(steps)
    it.finish()


def last_kernel(own, lines, full, mine, keep, sign, high_sign, results):
    it = Interior(own, lines, full, mine, keep)
    last = it.groups - 1
    steps = [it.second(last, h, sign, None, high_sign, results.at[i]) for i, h in enumerate(it.near(last))]
    steps.append(functools.partial(it.far_seed, last, high_sign))

    staggered(steps)


def border(
    side, groups, upper_half, lines, mine, theirs, a_ref, b_ref, m_ref, p_ref, square, sign, halo,
    first, last, sent
):
    at = 1 - side
    edge_group, outer_group = (0, -1) if side == 0 else (groups - 1, groups)
    offset = 0 if side == 0 else 2 * REACH
    below = REACH if side == 0 else 0
    zero = jnp.zeros((BS, WIDE), F32)

    def padded(rows, front):
        return split(jnp.concatenate([zero] + rows if front else rows + [zero], axis=0))

    whole_rows = []
    for p in range(REACH):
        rows = slice(p * HALF, (p + 1) * HALF)
        whole_rows.append(
            jnp.concatenate(
                [
                    jnp.where(upper_half, theirs[rows, :], mine[rows, :]),
                    jnp.where(upper_half, mine[rows, :], theirs[rows, :]),
                ],
                axis=0,
            )
        )

    def block(p, c):
        k = c - p + below
        if 0 <= k <= REACH:
            return whole_rows[p][:, k * BS : (k + 1) * BS]
        k = p - c + below
        if 0 <= c < REACH and 0 <= k <= REACH:
            return whole_rows[c][:, k * BS : (k + 1) * BS].T
        return jnp.zeros((BS, BS), F32)

    base = -5 if side == 0 else 0
    for p in range(REACH):
        rows = slice((p + at) * BS, (p + at + 1) * BS)
        for t in range(4):
            value = jnp.concatenate([block(p, base + 2 * t), block(p, base + 2 * t + 1)], axis=1)
            for q, x in enumerate(split(value)):
                halo[q, rows, t * 2 * BS : (t + 1) * 2 * BS] = x
    rows = slice(0, BS) if side == 0 else slice(REACH * BS, WIDE)
    for q in range(2):
        halo[q, rows, :] = jnp.zeros((BS, 2 * WIDE), BF)

    whole = [halo[q] for q in range(2)]
    outer_rows = slice(at * BS, (at + REACH) * BS)
    inner = slice(WIDE, 2 * WIDE) if side == 0 else slice(0, WIDE)
    to_edge = product([([m_ref[q] for q in range(2)], [x[:, inner] for x in whole])], True)
    among = product([([x[outer_rows] for x in whole], whole)], True)
    yield
    first[0] = to_edge + b_ref[...]
    rows = [
        first[0, s * BS : (s + 1) * BS] * line_of(lines, edge_group, s + 1 - at, outer_group)
        for s in range(REACH)
    ]
    across = padded(rows, side == 1)
    reach_out = [p_ref[q, 0] for q in range(2)]
    back = product([(reach_out, across)], True)
    for s in range(REACH):
        part = jnp.where(upper_half, rows[s][HALF:], rows[s][:HALF])
        for t in range(REACH):
            k = t - s + offset
            if 0 <= k < SPAN:
                square[s, k] = part[:, (t + at) * BS : (t + at + 1) * BS]
    sent(0, None, outer_blocks(side, True))
    yield
    first[1] = among + a_ref[...]
    rows = [
        first[1, p * BS : (p + 1) * BS] * line_of(lines, outer_group, p + at, outer_group)
        for p in range(REACH)
    ]
    inside = [p_ref[q, 1] for q in range(2)]
    out = product([(reach_out, padded(rows, side == 0)), (inside, across)])
    last[1] = back
    for s in range(REACH):
        close = last[1, s * HALF : (s + 1) * HALF] * (
            line_of(lines, edge_group, s + 1 - at, edge_group) * 0.5
        )
        for t in range(REACH):
            k = t - s + REACH
            sign[s, k] = sign[s, k] - close[:, (t + 1 - at) * BS : (t + 2 - at) * BS]
        k0, k1 = outer_blocks(side, False)
        sent(1, s, (REACH - s, k1) if side == 0 else (k0, 2 * REACH - s))
    yield
    last[0] = out
    for s in range(REACH):
        far = last[0, s * HALF : (s + 1) * HALF] * (
            line_of(lines, edge_group, s + 1 - at, outer_group) * 0.5
        )
        for t in range(REACH):
            k = t - s + offset
            if 0 <= k < SPAN:
                sign[s, k] = sign[s, k] - far[:, (t + at) * BS : (t + at + 1) * BS]
        sent(2, s, (0, REACH - s) if side == 0 else (2 * REACH - s, SPAN))


def border_kernel(
    low_own, low_other, high_own, high_other, lines, sign_last, low_a, low_b, low_m, low_p, high_a,
    high_b, high_m, high_p, low_square_in, high_square_in, low_sign_in, high_sign_in, square_in,
    sign_in, low_square, high_square, low_sign, high_sign, square_out, sign_out, halo, first, last,
    sems, last_sems, *, groups, half_axis
):
    count = square_in.shape[0]
    upper_half = lax.axis_index(half_axis) == 1
    stores = []

    def send(source, target, rows, blocks, sem):
        from_rows = (0, rows[1] - rows[0])
        store = pltpu.make_async_copy(
            blocks_of(source, from_rows, blocks), blocks_of(target, rows, blocks), sem
        )
        store.start()
        stores.append(store)

    send(sign_last, sign_out, (count - GROUP, count - REACH), (0, SPAN), last_sems.at[0])
    send(high_sign, sign_out, (count - REACH, count), inner_blocks(1, False), last_sems.at[1])
    squares, signs = (low_square, high_square), (low_sign, high_sign)

    def side(n, *refs):
        def sent(i, s, blocks):
            source, target = (squares[n], square_out) if i == 0 else (signs[n], sign_out)
            first_row = 0 if n == 0 else count - REACH
            rows = (0, REACH) if s is None else (s, s + 1)
            store = pltpu.make_async_copy(
                blocks_of(source, rows, blocks),
                blocks_of(target, (first_row + rows[0], first_row + rows[1]), blocks),
                sems.at[n, i, 0 if s is None else s],
            )
            store.start()
            stores.append(store)

        return border(
            n, groups, upper_half, lines, *refs, squares[n], signs[n], halo.at[n], first.at[n],
            last.at[n], sent,
        )

    works = [
        side(0, low_own, low_other, low_a, low_b, low_m, low_p),
        side(1, high_own, high_other, high_a, high_b, high_m, high_p),
    ]
    for _ in range(4):
        for work in works:
            next(work, None)
    for store in stores:
        store.wait()


def shards(matrix, pattern, *, axes, half_axis):
    count = matrix.shape[0]
    groups = count // GROUP
    flags = pattern.T
    vmem = pl.BlockSpec(memory_space=pltpu.VMEM)
    hbm = pl.BlockSpec(memory_space=pl.ANY)
    params = pltpu.CompilerParams(vmem_limit_bytes=LIMIT)

    top, bottom = matrix[:REACH, REACH:], matrix[count - REACH :, : REACH + 1]
    edge = jax.ShapeDtypeStruct((REACH * HALF, (REACH + 1) * BS), F32)
    to_left, to_right = pl.pallas_call(
        edge_kernel,
        out_shape=(edge, edge),
        in_specs=[vmem] * 2,
        out_specs=[vmem] * 2,
        compiler_params=pltpu.CompilerParams(
            vmem_limit_bytes=LIMIT, allow_input_fusion=[True, True]
        ),
        cost_estimate=pl.CostEstimate(
            flops=1 * 10**9, bytes_accessed=2**20, transcendentals=0
        ),
    )(top, bottom)
    size = 1
    for axis in axes:
        size *= lax.axis_size(axis)
    swap = [(0, 1), (1, 0)]
    other = lax.ppermute(matrix, half_axis, swap)
    forward = [(i, (i + 1) % size) for i in range(size)]
    backward = [(target, source) for source, target in forward]
    high_own = lax.ppermute(to_left, axes, backward)
    low_own = lax.ppermute(to_right, axes, forward)

    band = jax.ShapeDtypeStruct(matrix.shape, F32)
    edges = jax.ShapeDtypeStruct((REACH, SPAN, HALF, BS), F32)
    full = jax.ShapeDtypeStruct((2, groups, WIDE, 3 * WIDE), BF)
    mine = jax.ShapeDtypeStruct((2, groups, GROUP * HALF, 3 * WIDE), BF)
    keep = jax.ShapeDtypeStruct((2, 3 * groups, WIDE, WIDE), BF)
    lines = jax.ShapeDtypeStruct(((groups + 2) * GROUP, 3 * WIDE), F32)
    ends_out = [
        jax.ShapeDtypeStruct((REACH * BS, WIDE), F32),
        jax.ShapeDtypeStruct((REACH * BS, WIDE), F32),
        jax.ShapeDtypeStruct((2, REACH * BS, WIDE), BF),
        jax.ShapeDtypeStruct((2, 2, REACH * HALF, WIDE), BF),
    ]
    rows = jax.ShapeDtypeStruct((GROUP,) + matrix.shape[1:], F32)
    square, sign, low_square, high_square, low_sign, full, mine, keep, lines, *ends = pl.pallas_call(
        functools.partial(first_kernel, axes=axes, half_axis=half_axis),
        out_shape=[band, band, edges, edges, edges, full, mine, keep, lines] + ends_out * 2,
        in_specs=[vmem] * 3,
        out_specs=[hbm] * 2 + [vmem] * 15,
        scratch_shapes=[
            pltpu.VMEM((groups,) + rows.shape, F32),
            pltpu.VMEM((groups - 1,) + rows.shape, F32),
            pltpu.VMEM((2 * groups - 1 + 3 * groups - 4, WIDE, WIDE), F32),
            pltpu.SemaphoreType.DMA((2, groups)),
            pltpu.SemaphoreType.DMA((3,)),
        ],
        compiler_params=params,
        cost_estimate=pl.CostEstimate(
            flops=3 * 2 * 16 * WIDE**3, bytes_accessed=16 * 2**20, transcendentals=0
        ),
    )(matrix, other, flags)

    low_own, low_sign = lax.optimization_barrier((low_own, low_sign))
    high_own, low_sign = lax.optimization_barrier((high_own, low_sign))
    low_other = lax.ppermute(low_own, half_axis, swap)
    high_other = lax.ppermute(high_own, half_axis, swap)

    sign_last, high_sign = pl.pallas_call(
        last_kernel,
        out_shape=[rows, edges],
        in_specs=[vmem] * 5,
        out_specs=[vmem] * 2,
        scratch_shapes=[pltpu.VMEM((2, GROUP * HALF, WIDE), F32)],
        compiler_params=params,
        cost_estimate=pl.CostEstimate(
            flops=3 * 2 * 4 * WIDE**3, bytes_accessed=4 * 2**20, transcendentals=0
        ),
    )(matrix, lines, full, mine, keep)

    outs = pl.pallas_call(
        functools.partial(border_kernel, groups=groups, half_axis=half_axis),
        out_shape=[edges] * 4 + [band] * 2,
        in_specs=[vmem] * 18 + [hbm] * 2,
        out_specs=[vmem] * 4 + [hbm] * 2,
        scratch_shapes=[
            pltpu.VMEM((2, 2, WIDE, 2 * WIDE), BF),
            pltpu.VMEM((2, 2, REACH * BS, WIDE), F32),
            pltpu.VMEM((2, 2, REACH * HALF, WIDE), F32),
            pltpu.SemaphoreType.DMA((2, 3, REACH)),
            pltpu.SemaphoreType.DMA((2,)),
        ],
        input_output_aliases={14 + i: i for i in range(6)},
        compiler_params=params,
        cost_estimate=pl.CostEstimate(
            flops=3 * 2 * 4 * WIDE**3, bytes_accessed=2 * 2**20, transcendentals=0
        ),
    )(
        low_own, low_other, high_own, high_other, lines, sign_last, *ends, low_square, high_square,
        low_sign, high_sign, square, sign,
    )
    return tuple(outs[4:])


def solution(mesh):
    band = P(("group", "row", "col"), None, "rep", None)
    return jax.shard_map(
        functools.partial(shards, axes=("row", "col"), half_axis="rep"),
        mesh=mesh,
        in_specs=(band, P("group", None)),
        out_specs=(band, band),
        check_vma=False,
    )
```

```python
import functools

import jax
import jax.numpy as jnp
from jax import lax
from jax.experimental import pallas as pl
from jax.experimental.pallas import tpu as pltpu
from jax.sharding import PartitionSpec as P

REACH = 3
SPAN = 7
BS = 64
HALF = 32
GROUP = 4
WIDE = GROUP * BS
BF = jnp.bfloat16
F32 = jnp.float32
LIMIT = 32 * 1024 * 1024


def split(x):
    hi = x.astype(BF)
    return hi, (x - hi.astype(F32)).astype(BF)


def product(pairs, transposed=False):
    side = 1 if transposed else 0
    high, low = [jnp.concatenate([a[p] for a, _ in pairs], axis=1) for p in range(2)]
    right = [jnp.concatenate([b[p] for _, b in pairs], axis=side) for p in range(2)]
    dot = functools.partial(
        lax.dot_general,
        dimension_numbers=(((1,), (side,)), ((), ())),
        preferred_element_type=F32,
    )
    both = dot(jnp.concatenate([high, low], axis=0), right[0])
    count = high.shape[0]
    return both[:count] + (both[count:] + dot(high, right[1]))


def turn(x):
    return split((x[0].astype(F32) + x[1].astype(F32)).T)


def write_lines(pat, lines, first, groups):
    total = pat.shape[1]
    rows = lines.shape[0]
    iota = functools.partial(lax.broadcasted_iota, jnp.int32)
    dot = functools.partial(lax.dot_general, preferred_element_type=F32)
    wanted = lax.rem(first - GROUP + total + iota((rows, total), 0), total)
    chosen = (iota((rows, total), 1) == wanted).astype(BF)
    flags = dot(chosen, pat[...].astype(BF), (((1,), (1,)), ((), ())))
    place = iota((rows, 1), 0) % GROUP
    spread = jnp.concatenate(
        [jnp.where(place == s, flags, 0.0) for s in range(GROUP)], axis=1
    ).astype(BF)
    block = iota((SPAN, 3 * WIDE), 1) // BS - iota((SPAN, 3 * WIDE), 0) - 1
    spots = jnp.concatenate([(block == s).astype(BF) for s in range(GROUP)], axis=0)
    lines[...] = dot(spread, spots, (((1,), (0,)), ((), ())))


def line_of(lines, g, s, h):
    at = (g + 1) * GROUP + s
    lo = (h - g + 1) * WIDE
    return lines[at : at + 1, lo : lo + WIDE]


def inner_rows(g, groups):
    return range(REACH if g == 0 else 0, GROUP - REACH if g == groups - 1 else GROUP)


def inner_blocks(side, is_square):
    first = REACH if is_square else 2 * REACH
    return (first, SPAN) if side == 0 else (0, SPAN - first)


def outer_blocks(side, is_square):
    k0, k1 = inner_blocks(side, is_square)
    return (0, k0) if side == 0 else (k1, SPAN)


def blocks_of(ref, rows, blocks):
    return ref.at[pl.ds(rows[0], rows[1] - rows[0]), pl.ds(blocks[0], blocks[1] - blocks[0])]


def row_of(g, s, groups, rows, low, high):
    if s in inner_rows(g, groups):
        return rows.at[s]
    return low.at[s] if g == 0 else high.at[s - (GROUP - REACH)]


def edge_kernel(top, bottom, to_left, to_right):
    for source, target in ((top, to_left), (bottom, to_right)):
        for s in range(REACH):
            for t in range(2):
                target[s * HALF : (s + 1) * HALF, t * 2 * BS : (t + 1) * 2 * BS] = jnp.concatenate(
                    [source[s, 2 * t], source[s, 2 * t + 1]], axis=1
                )


class Interior:
    def __init__(self, own, lines, full, mine, keep):
        self.own = own
        self.lines = lines
        self.full = full
        self.mine = mine
        self.keep = keep
        self.count = own.shape[0]
        self.groups = self.count // GROUP
        self.stores = []

    def part(self, g, h, rows=slice(None)):
        at = (h - g + 1) * WIDE
        return [self.full[p, g, rows, at : at + WIDE] for p in range(2)]

    def my_part(self, g, h):
        at = (h - g + 1) * WIDE
        return [self.mine[p, g, :, at : at + WIDE] for p in range(2)]

    def tile(self, g, h):
        return 3 * g + h - g + 1

    def kept(self, g, h):
        return [self.keep[p, self.tile(g, h)] for p in range(2)]

    def near(self, g):
        return [e for e in (g - 1, g, g + 1) if 0 <= e < self.groups]

    def second(self, g, h, sign, low, high, result):
        span = range(1 if h > g else 0, GROUP - 1 if h < g else GROUP)
        rows = slice(span[0] * HALF, (span[-1] + 1) * HALF)

        def dot():
            return product(
                [
                    ([x[rows] for x in self.my_part(g, e)], self.kept(e, h))
                    for e in self.near(g)
                    if abs(e - h) <= 1
                ]
            )

        def store(value):
            result[rows] = value

        def post():
            for s in span:
                a = g * GROUP + s
                target = row_of(g, s, self.groups, sign, low, high)
                part = result[s * HALF : (s + 1) * HALF] * (line_of(self.lines, g, s, h) * 0.5)
                for t in range(GROUP):
                    k = t + GROUP * (h - g) - s + REACH
                    if 0 <= k < SPAN:
                        target[k] = 1.5 * self.own[a, k] - part[:, t * BS : (t + 1) * BS]

        return dot, store, post

    def far_seed(self, g, seed):
        for s in range(REACH):
            a = s if g == 0 else self.count - REACH + s
            for k in range(0, REACH - s) if g == 0 else range(2 * REACH - s, SPAN):
                seed[s, k] = 1.5 * self.own[a, k]

    def reaching(self, a_ref, b_ref, m_ref, p_ref, g, e, r0):
        rows = slice(r0, r0 + REACH * BS)
        mine_rows = slice(r0 // 2, r0 // 2 + REACH * HALF)
        outer = slice(BS - r0, BS - r0 + REACH * BS)

        def dot():
            out = self.part(g, e)
            return (
                product([([x[outer] for x in turn(out)], out)]),
                product([(self.part(g, g, rows), out)]),
            )

        def store(value):
            a_ref[...], b_ref[...] = value

        def post():
            for p in range(2):
                m_ref[p] = self.part(g, e)[p][rows]
                p_ref[p, 0] = self.my_part(g, e)[p][mine_rows]
                p_ref[p, 1] = self.my_part(g, g)[p][mine_rows]

        return dot, store, post

    def send(self, g, i, source, target, sems):
        rows = inner_rows(g, self.groups)
        store = pltpu.make_async_copy(
            source.at[pl.ds(rows[0], len(rows))],
            target.at[pl.ds(g * GROUP + rows[0], len(rows))],
            sems.at[i, g],
        )
        store.start()
        self.stores.append(store)

    def send_edge(self, side, i, source, target, sem):
        first = 0 if side == 0 else self.count - REACH
        blocks = inner_blocks(side, i == 0)
        store = pltpu.make_async_copy(
            blocks_of(source, (0, REACH), blocks),
            blocks_of(target, (first, first + REACH), blocks),
            sem,
        )
        store.start()
        self.stores.append(store)

    def finish(self):
        for store in self.stores:
            store.wait()


def count_dots(steps):
    return sum(isinstance(step, tuple) for step in steps)


def staggered(steps):
    pending = []
    for step in steps:
        if not isinstance(step, tuple):
            pending.append(step)
            continue
        dot, store, post = step
        value = dot()
        for work in pending:
            work()
        store(value)
        pending = [post]
    for work in pending:
        work()


def first_kernel(
    own, other, pat, square_out, sign_out, low_square, high_square, low_sign, full, mine, keep, lines, low_a, low_b, low_m, low_p,
    high_a, high_b, high_m, high_p, square, sign, results, sems, edge_sems, *, axes, half_axis
):
    it = Interior(own, lines, full, mine, keep)
    groups = it.groups
    upper_half = lax.axis_index(half_axis) == 1

    def build(g):
        for s in range(GROUP):
            a = g * GROUP + s
            for t in range(3 * GROUP // 2):
                ks = [2 * t + e - s - 1 for e in range(2)]
                lanes = slice(t * 2 * BS, (t + 1) * 2 * BS)
                rows = slice(s * BS, (s + 1) * BS)
                mine_rows = slice(s * HALF, (s + 1) * HALF)
                if all(k < 0 or k >= SPAN for k in ks):
                    for p in range(2):
                        full[p, g, rows, lanes] = jnp.zeros((BS, 2 * BS), BF)
                        mine[p, g, mine_rows, lanes] = jnp.zeros((HALF, 2 * BS), BF)
                    continue
                two = [
                    jnp.concatenate(
                        [src[a, k] if 0 <= k < SPAN else jnp.zeros((HALF, BS), F32) for k in ks],
                        axis=1,
                    )
                    for src in (own, other)
                ]
                for p, (x, y) in enumerate(zip(*[split(x) for x in two])):
                    mine[p, g, mine_rows, lanes] = x
                    full[p, g, rows, lanes] = jnp.concatenate(
                        [jnp.where(upper_half, y, x), jnp.where(upper_half, x, y)], axis=0
                    )

    def squares(g, h, result):
        pairs = []
        for e in (g - 1, g, g + 1):
            if abs(e - h) <= 1:
                inside = 0 <= e < groups
                pairs.append((e, (lambda e=e: it.part(e, h)) if inside else (lambda e=e: turn(it.part(h, e)))))
        span = range(1 if h > g else 0, GROUP)
        rows = slice(span[0] * BS, WIDE)

        def dot():
            return product([([x[rows] for x in it.part(g, e)], f()) for e, f in pairs])

        def store(value):
            result[rows] = value

        def post():
            masked = [jnp.zeros((BS, WIDE), F32)] * GROUP
            for s in span:
                masked[s] = result[s * BS : (s + 1) * BS] * line_of(lines, g, s, h)
            for s in range(GROUP):
                for p, x in enumerate(split(masked[s])):
                    keep[p, it.tile(g, h), s * BS : (s + 1) * BS] = x
            for s in span:
                part = jnp.where(upper_half, masked[s][HALF:], masked[s][:HALF])
                for t in range(GROUP):
                    k = t + GROUP * (h - g) - s + REACH
                    if 0 <= k < SPAN:
                        row_of(g, s, groups, square.at[g], low_square, high_square)[k] = part[
                            :, t * BS : (t + 1) * BS
                        ]
            if h == g:
                return
            for c in range(0, GROUP, 2):
                turned = jnp.concatenate(masked[c : c + 2], axis=0).T
                lanes = slice(c * BS, (c + 2) * BS)
                for p, x in enumerate(split(turned)):
                    keep[p, it.tile(h, g), :, lanes] = x
                for t in range(GROUP):
                    rows = turned[t * BS : (t + 1) * BS]
                    part = jnp.where(upper_half, rows[HALF:], rows[:HALF])
                    for s in range(c, c + 2):
                        k = s + GROUP * (g - h) - t + REACH
                        if 0 <= k < SPAN:
                            row_of(h, t, groups, square.at[h], low_square, high_square)[k] = part[
                                :, (s - c) * BS : (s - c + 1) * BS
                            ]

        return dot, store, post


    def begin():
        write_lines(pat, lines, lax.axis_index(axes) * it.count, groups)
        it.far_seed(0, low_sign)

    build(0)
    build(1)
    steps = [begin]
    for g in range(groups):
        if g + 1 < groups:
            steps.append(squares(g, g + 1, results.at[count_dots(steps)]))
            if g + 2 < groups:
                steps.append(functools.partial(build, g + 2))
        steps.append(squares(g, g, results.at[count_dots(steps)]))
        steps.append(functools.partial(it.send, g, 0, square.at[g], square_out, sems))
        if g in (0, groups - 1):
            side, source = (0, low_square) if g == 0 else (1, high_square)
            steps.append(
                functools.partial(it.send_edge, side, 0, source, square_out, edge_sems.at[side])
            )
    for g in range(groups - 1):
        for h in it.near(g):
            steps.append(it.second(g, h, sign.at[g], low_sign, None, results.at[count_dots(steps)]))
        steps.append(functools.partial(it.send, g, 1, sign.at[g], sign_out, sems))
        if g == 0:
            steps.append(functools.partial(it.send_edge, 0, 1, low_sign, sign_out, edge_sems.at[2]))
    steps.append(it.reaching(low_a, low_b, low_m, low_p, 0, -1, 0))
    steps.append(it.reaching(high_a, high_b, high_m, high_p, groups - 1, groups, BS))
    staggered(steps)
    it.finish()


def last_kernel(own, lines, full, mine, keep, sign, high_sign, results):
    it = Interior(own, lines, full, mine, keep)
    last = it.groups - 1
    steps = [it.second(last, h, sign, None, high_sign, results.at[i]) for i, h in enumerate(it.near(last))]
    steps.append(functools.partial(it.far_seed, last, high_sign))

    staggered(steps)


def border(
    side, groups, upper_half, lines, mine, theirs, a_ref, b_ref, m_ref, p_ref, square, sign, halo,
    first, last, sent
):
    at = 1 - side
    edge_group, outer_group = (0, -1) if side == 0 else (groups - 1, groups)
    offset = 0 if side == 0 else 2 * REACH
    below = REACH if side == 0 else 0
    zero = jnp.zeros((BS, WIDE), F32)

    def padded(rows, front):
        return split(jnp.concatenate([zero] + rows if front else rows + [zero], axis=0))

    whole_rows = []
    for p in range(REACH):
        rows = slice(p * HALF, (p + 1) * HALF)
        whole_rows.append(
            jnp.concatenate(
                [
                    jnp.where(upper_half, theirs[rows, :], mine[rows, :]),
                    jnp.where(upper_half, mine[rows, :], theirs[rows, :]),
                ],
                axis=0,
            )
        )

    def block(p, c):
        k = c - p + below
        if 0 <= k <= REACH:
            return whole_rows[p][:, k * BS : (k + 1) * BS]
        k = p - c + below
        if 0 <= c < REACH and 0 <= k <= REACH:
            return whole_rows[c][:, k * BS : (k + 1) * BS].T
        return jnp.zeros((BS, BS), F32)

    base = -5 if side == 0 else 0
    empty = slice(0, BS) if side == 0 else slice(REACH * BS, WIDE)

    def build(part):
        for p in range(REACH):
            rows = slice((p + at) * BS, (p + at + 1) * BS)
            for t in (2 * part, 2 * part + 1):
                value = jnp.concatenate(
                    [block(p, base + 2 * t), block(p, base + 2 * t + 1)], axis=1
                )
                for q, x in enumerate(split(value)):
                    halo[q, rows, t * 2 * BS : (t + 1) * 2 * BS] = x
        for q in range(2):
            halo[q, empty, part * WIDE : (part + 1) * WIDE] = jnp.zeros((BS, WIDE), BF)
        return [halo[q, :, part * WIDE : (part + 1) * WIDE] for q in range(2)]

    outer_rows = slice(at * BS, (at + REACH) * BS)
    beyond = build(0 if side == 0 else 1)
    further = product([([x[outer_rows] for x in beyond], beyond)], True)
    yield
    tile = build(1 if side == 0 else 0)
    to_edge = product([([m_ref[q] for q in range(2)], tile)])
    among = product([([x[outer_rows] for x in tile], tile)], True)
    yield
    first[0] = to_edge + b_ref[...]
    rows = [
        first[0, s * BS : (s + 1) * BS] * line_of(lines, edge_group, s + 1 - at, outer_group)
        for s in range(REACH)
    ]
    across = padded(rows, side == 1)
    reach_out = [p_ref[q, 0] for q in range(2)]
    back = product([(reach_out, across)], True)
    for s in range(REACH):
        part = jnp.where(upper_half, rows[s][HALF:], rows[s][:HALF])
        for t in range(REACH):
            k = t - s + offset
            if 0 <= k < SPAN:
                square[s, k] = part[:, (t + at) * BS : (t + at + 1) * BS]
    sent(0)
    yield
    first[1] = among + (further + a_ref[...])
    rows = [
        first[1, p * BS : (p + 1) * BS] * line_of(lines, outer_group, p + at, outer_group)
        for p in range(REACH)
    ]
    inside = [p_ref[q, 1] for q in range(2)]
    out = product([(reach_out, padded(rows, side == 0)), (inside, across)])
    last[1] = back
    for s in range(REACH):
        close = last[1, s * HALF : (s + 1) * HALF] * (
            line_of(lines, edge_group, s + 1 - at, edge_group) * 0.5
        )
        for t in range(REACH):
            k = t - s + REACH
            sign[s, k] = sign[s, k] - close[:, (t + 1 - at) * BS : (t + 2 - at) * BS]
    yield
    last[0] = out
    for s in range(REACH):
        far = last[0, s * HALF : (s + 1) * HALF] * (
            line_of(lines, edge_group, s + 1 - at, outer_group) * 0.5
        )
        for t in range(REACH):
            k = t - s + offset
            if 0 <= k < SPAN:
                sign[s, k] = sign[s, k] - far[:, (t + at) * BS : (t + at + 1) * BS]
    sent(1)


def border_kernel(
    low_own, low_other, high_own, high_other, lines, sign_last, low_a, low_b, low_m, low_p, high_a,
    high_b, high_m, high_p, low_square_in, high_square_in, low_sign_in, high_sign_in, square_in,
    sign_in, low_square, high_square, low_sign, high_sign, square_out, sign_out, halo, first, last,
    sems, last_sems, *, groups, half_axis
):
    count = square_in.shape[0]
    upper_half = lax.axis_index(half_axis) == 1
    stores = []

    def send(source, target, rows, blocks, sem):
        from_rows = (0, rows[1] - rows[0])
        store = pltpu.make_async_copy(
            blocks_of(source, from_rows, blocks), blocks_of(target, rows, blocks), sem
        )
        store.start()
        stores.append(store)

    send(sign_last, sign_out, (count - GROUP, count - REACH), (0, SPAN), last_sems.at[0])
    send(high_sign, sign_out, (count - REACH, count), inner_blocks(1, False), last_sems.at[1])
    squares, signs = (low_square, high_square), (low_sign, high_sign)

    def side(n, *refs):
        def sent(i):
            source, target = ((squares[n], square_out), (signs[n], sign_out))[i]
            rows = (0, REACH) if n == 0 else (count - REACH, count)
            send(source, target, rows, outer_blocks(n, i == 0), sems.at[n, i])

        return border(
            n, groups, upper_half, lines, *refs, squares[n], signs[n], halo.at[n], first.at[n],
            last.at[n], sent,
        )

    works = [
        side(0, low_own, low_other, low_a, low_b, low_m, low_p),
        side(1, high_own, high_other, high_a, high_b, high_m, high_p),
    ]
    for _ in range(5):
        for work in works:
            next(work, None)
    for store in stores:
        store.wait()


def shards(matrix, pattern, *, axes, half_axis):
    count = matrix.shape[0]
    groups = count // GROUP
    flags = pattern.T
    vmem = pl.BlockSpec(memory_space=pltpu.VMEM)
    hbm = pl.BlockSpec(memory_space=pl.ANY)
    params = pltpu.CompilerParams(vmem_limit_bytes=LIMIT)

    top, bottom = matrix[:REACH, REACH:], matrix[count - REACH :, : REACH + 1]
    matrix, top, bottom = lax.optimization_barrier((matrix, top, bottom))
    edge = jax.ShapeDtypeStruct((REACH * HALF, (REACH + 1) * BS), F32)
    to_left, to_right = pl.pallas_call(
        edge_kernel,
        out_shape=(edge, edge),
        in_specs=[vmem] * 2,
        out_specs=[vmem] * 2,
        compiler_params=params,
        cost_estimate=pl.CostEstimate(
            flops=1 * 10**9, bytes_accessed=2**20, transcendentals=0
        ),
    )(top, bottom)
    size = 1
    for axis in axes:
        size *= lax.axis_size(axis)
    swap = [(0, 1), (1, 0)]
    other = lax.ppermute(matrix, half_axis, swap)
    forward = [(i, (i + 1) % size) for i in range(size)]
    backward = [(target, source) for source, target in forward]
    high_own = lax.ppermute(to_left, axes, backward)
    low_own = lax.ppermute(to_right, axes, forward)

    band = jax.ShapeDtypeStruct(matrix.shape, F32)
    edges = jax.ShapeDtypeStruct((REACH, SPAN, HALF, BS), F32)
    full = jax.ShapeDtypeStruct((2, groups, WIDE, 3 * WIDE), BF)
    mine = jax.ShapeDtypeStruct((2, groups, GROUP * HALF, 3 * WIDE), BF)
    keep = jax.ShapeDtypeStruct((2, 3 * groups, WIDE, WIDE), BF)
    lines = jax.ShapeDtypeStruct(((groups + 2) * GROUP, 3 * WIDE), F32)
    ends_out = [
        jax.ShapeDtypeStruct((REACH * BS, WIDE), F32),
        jax.ShapeDtypeStruct((REACH * BS, WIDE), F32),
        jax.ShapeDtypeStruct((2, REACH * BS, WIDE), BF),
        jax.ShapeDtypeStruct((2, 2, REACH * HALF, WIDE), BF),
    ]
    rows = jax.ShapeDtypeStruct((GROUP,) + matrix.shape[1:], F32)
    square, sign, low_square, high_square, low_sign, full, mine, keep, lines, *ends = pl.pallas_call(
        functools.partial(first_kernel, axes=axes, half_axis=half_axis),
        out_shape=[band, band, edges, edges, edges, full, mine, keep, lines] + ends_out * 2,
        in_specs=[vmem] * 3,
        out_specs=[hbm] * 2 + [vmem] * 15,
        scratch_shapes=[
            pltpu.VMEM((groups,) + rows.shape, F32),
            pltpu.VMEM((groups - 1,) + rows.shape, F32),
            pltpu.VMEM((2 * groups - 1 + 3 * groups - 4, WIDE, WIDE), F32),
            pltpu.SemaphoreType.DMA((2, groups)),
            pltpu.SemaphoreType.DMA((3,)),
        ],
        compiler_params=params,
        cost_estimate=pl.CostEstimate(
            flops=3 * 2 * 16 * WIDE**3, bytes_accessed=16 * 2**20, transcendentals=0
        ),
    )(matrix, other, flags)

    low_own, low_sign = lax.optimization_barrier((low_own, low_sign))
    high_own, low_sign = lax.optimization_barrier((high_own, low_sign))
    low_other = lax.ppermute(low_own, half_axis, swap)
    high_other = lax.ppermute(high_own, half_axis, swap)

    sign_last, high_sign = pl.pallas_call(
        last_kernel,
        out_shape=[rows, edges],
        in_specs=[vmem] * 5,
        out_specs=[vmem] * 2,
        scratch_shapes=[pltpu.VMEM((2, GROUP * HALF, WIDE), F32)],
        compiler_params=params,
        cost_estimate=pl.CostEstimate(
            flops=3 * 2 * 4 * WIDE**3, bytes_accessed=4 * 2**20, transcendentals=0
        ),
    )(matrix, lines, full, mine, keep)

    outs = pl.pallas_call(
        functools.partial(border_kernel, groups=groups, half_axis=half_axis),
        out_shape=[edges] * 4 + [band] * 2,
        in_specs=[vmem] * 18 + [hbm] * 2,
        out_specs=[vmem] * 4 + [hbm] * 2,
        scratch_shapes=[
            pltpu.VMEM((2, 2, WIDE, 2 * WIDE), BF),
            pltpu.VMEM((2, 2, REACH * BS, WIDE), F32),
            pltpu.VMEM((2, 2, REACH * HALF, WIDE), F32),
            pltpu.SemaphoreType.DMA((2, 2)),
            pltpu.SemaphoreType.DMA((2,)),
        ],
        input_output_aliases={14 + i: i for i in range(6)},
        compiler_params=params,
        cost_estimate=pl.CostEstimate(
            flops=3 * 2 * 4 * WIDE**3, bytes_accessed=2 * 2**20, transcendentals=0
        ),
    )(
        low_own, low_other, high_own, high_other, lines, sign_last, *ends, low_square, high_square,
        low_sign, high_sign, square, sign,
    )
    return tuple(outs[4:])


def solution(mesh):
    band = P(("group", "row", "col"), None, "rep", None)
    return jax.shard_map(
        functools.partial(shards, axes=("row", "col"), half_axis="rep"),
        mesh=mesh,
        in_specs=(band, P("group", None)),
        out_specs=(band, band),
        check_vma=False,
    )
```

```python
import functools

import jax
import jax.numpy as jnp
from jax import lax
from jax.experimental import pallas as pl
from jax.experimental.pallas import tpu as pltpu
from jax.sharding import PartitionSpec as P

REACH = 3
SPAN = 7
BS = 64
HALF = 32
GROUP = 4
WIDE = GROUP * BS
BF = jnp.bfloat16
F32 = jnp.float32
LIMIT = 32 * 1024 * 1024


def split(x):
    hi = x.astype(BF)
    return hi, (x - hi.astype(F32)).astype(BF)


def product(pairs, transposed=False):
    side = 1 if transposed else 0
    high, low = [jnp.concatenate([a[p] for a, _ in pairs], axis=1) for p in range(2)]
    right = [jnp.concatenate([b[p] for _, b in pairs], axis=side) for p in range(2)]
    dot = functools.partial(
        lax.dot_general,
        dimension_numbers=(((1,), (side,)), ((), ())),
        preferred_element_type=F32,
    )
    both = dot(jnp.concatenate([high, low], axis=0), right[0])
    count = high.shape[0]
    return both[:count] + (both[count:] + dot(high, right[1]))


def turn(x):
    return split((x[0].astype(F32) + x[1].astype(F32)).T)


def write_lines(pat, lines, first, groups):
    total = pat.shape[1]
    rows = lines.shape[0]
    iota = functools.partial(lax.broadcasted_iota, jnp.int32)
    dot = functools.partial(lax.dot_general, preferred_element_type=F32)
    wanted = lax.rem(first - GROUP + total + iota((rows, total), 0), total)
    chosen = (iota((rows, total), 1) == wanted).astype(BF)
    flags = dot(chosen, pat[...].astype(BF), (((1,), (1,)), ((), ())))
    place = iota((rows, 1), 0) % GROUP
    spread = jnp.concatenate(
        [jnp.where(place == s, flags, 0.0) for s in range(GROUP)], axis=1
    ).astype(BF)
    block = iota((SPAN, 3 * WIDE), 1) // BS - iota((SPAN, 3 * WIDE), 0) - 1
    spots = jnp.concatenate([(block == s).astype(BF) for s in range(GROUP)], axis=0)
    lines[...] = dot(spread, spots, (((1,), (0,)), ((), ())))


def line_of(lines, g, s, h):
    at = (g + 1) * GROUP + s
    lo = (h - g + 1) * WIDE
    return lines[at : at + 1, lo : lo + WIDE]


def inner_rows(g, groups):
    return range(REACH if g == 0 else 0, GROUP - REACH if g == groups - 1 else GROUP)


def inner_blocks(side, is_square):
    first = REACH if is_square else 2 * REACH
    return (first, SPAN) if side == 0 else (0, SPAN - first)


def outer_blocks(side, is_square):
    k0, k1 = inner_blocks(side, is_square)
    return (0, k0) if side == 0 else (k1, SPAN)


def blocks_of(ref, rows, blocks):
    return ref.at[pl.ds(rows[0], rows[1] - rows[0]), pl.ds(blocks[0], blocks[1] - blocks[0])]


def row_of(g, s, groups, rows, low, high):
    if s in inner_rows(g, groups):
        return rows.at[s]
    return low.at[s] if g == 0 else high.at[s - (GROUP - REACH)]


def edge_kernel(top, bottom, to_left, to_right):
    for source, target in ((top, to_left), (bottom, to_right)):
        for s in range(REACH):
            for t in range(2):
                target[s * HALF : (s + 1) * HALF, t * 2 * BS : (t + 1) * 2 * BS] = jnp.concatenate(
                    [source[s, 2 * t], source[s, 2 * t + 1]], axis=1
                )


class Interior:
    def __init__(self, own, lines, full, mine, keep):
        self.own = own
        self.lines = lines
        self.full = full
        self.mine = mine
        self.keep = keep
        self.count = own.shape[0]
        self.groups = self.count // GROUP
        self.stores = []

    def part(self, g, h, rows=slice(None)):
        at = (h - g + 1) * WIDE
        return [self.full[p, g, rows, at : at + WIDE] for p in range(2)]

    def my_part(self, g, h):
        at = (h - g + 1) * WIDE
        return [self.mine[p, g, :, at : at + WIDE] for p in range(2)]

    def tile(self, g, h):
        return 3 * g + h - g + 1

    def kept(self, g, h):
        return [self.keep[p, self.tile(g, h)] for p in range(2)]

    def near(self, g):
        return [e for e in (g - 1, g, g + 1) if 0 <= e < self.groups]

    def second(self, g, h, sign, low, high, result):
        span = range(1 if h > g else 0, GROUP - 1 if h < g else GROUP)
        rows = slice(span[0] * HALF, (span[-1] + 1) * HALF)

        def dot():
            return product(
                [
                    ([x[rows] for x in self.my_part(g, e)], self.kept(e, h))
                    for e in self.near(g)
                    if abs(e - h) <= 1
                ]
            )

        def store(value):
            result[rows] = value

        def post():
            for s in span:
                a = g * GROUP + s
                target = row_of(g, s, self.groups, sign, low, high)
                part = result[s * HALF : (s + 1) * HALF] * (line_of(self.lines, g, s, h) * 0.5)
                for t in range(GROUP):
                    k = t + GROUP * (h - g) - s + REACH
                    if 0 <= k < SPAN:
                        target[k] = 1.5 * self.own[a, k] - part[:, t * BS : (t + 1) * BS]

        return dot, store, post

    def far_seed(self, g, seed):
        for s in range(REACH):
            a = s if g == 0 else self.count - REACH + s
            for k in range(0, REACH - s) if g == 0 else range(2 * REACH - s, SPAN):
                seed[s, k] = 1.5 * self.own[a, k]

    def reaching(self, a_ref, b_ref, m_ref, p_ref, g, e, r0):
        rows = slice(r0, r0 + REACH * BS)
        mine_rows = slice(r0 // 2, r0 // 2 + REACH * HALF)
        outer = slice(BS - r0, BS - r0 + REACH * BS)

        def dot():
            out = self.part(g, e)
            return (
                product([([x[outer] for x in turn(out)], out)]),
                product([(self.part(g, g, rows), out)]),
            )

        def store(value):
            a_ref[...], b_ref[...] = value

        def post():
            for p in range(2):
                m_ref[p] = self.part(g, e)[p][rows]
                p_ref[p, 0] = self.my_part(g, e)[p][mine_rows]
                p_ref[p, 1] = self.my_part(g, g)[p][mine_rows]

        return dot, store, post

    def send(self, g, i, source, target, sems):
        rows = inner_rows(g, self.groups)
        store = pltpu.make_async_copy(
            source.at[pl.ds(rows[0], len(rows))],
            target.at[pl.ds(g * GROUP + rows[0], len(rows))],
            sems.at[i, g],
        )
        store.start()
        self.stores.append(store)

    def send_edge(self, side, i, source, target, sem):
        first = 0 if side == 0 else self.count - REACH
        blocks = inner_blocks(side, i == 0)
        store = pltpu.make_async_copy(
            blocks_of(source, (0, REACH), blocks),
            blocks_of(target, (first, first + REACH), blocks),
            sem,
        )
        store.start()
        self.stores.append(store)

    def finish(self):
        for store in self.stores:
            store.wait()


def count_dots(steps):
    return sum(isinstance(step, tuple) for step in steps)


def staggered(steps):
    pending = []
    for step in steps:
        if not isinstance(step, tuple):
            pending.append(step)
            continue
        dot, store, post = step
        value = dot()
        for work in pending:
            work()
        store(value)
        pending = [post]
    for work in pending:
        work()


def first_kernel(
    own, other, pat, square_out, sign_out, low_square, high_square, low_sign, full, mine, keep, lines, low_a, low_b, low_m, low_p,
    high_a, high_b, high_m, high_p, square, sign, results, sems, edge_sems, *, axes, half_axis
):
    it = Interior(own, lines, full, mine, keep)
    groups = it.groups
    upper_half = lax.axis_index(half_axis) == 1

    def build(g):
        for s in range(GROUP):
            a = g * GROUP + s
            for t in range(3 * GROUP // 2):
                ks = [2 * t + e - s - 1 for e in range(2)]
                lanes = slice(t * 2 * BS, (t + 1) * 2 * BS)
                rows = slice(s * BS, (s + 1) * BS)
                mine_rows = slice(s * HALF, (s + 1) * HALF)
                if all(k < 0 or k >= SPAN for k in ks):
                    for p in range(2):
                        full[p, g, rows, lanes] = jnp.zeros((BS, 2 * BS), BF)
                        mine[p, g, mine_rows, lanes] = jnp.zeros((HALF, 2 * BS), BF)
                    continue
                two = [
                    jnp.concatenate(
                        [src[a, k] if 0 <= k < SPAN else jnp.zeros((HALF, BS), F32) for k in ks],
                        axis=1,
                    )
                    for src in (own, other)
                ]
                for p, (x, y) in enumerate(zip(*[split(x) for x in two])):
                    mine[p, g, mine_rows, lanes] = x
                    full[p, g, rows, lanes] = jnp.concatenate(
                        [jnp.where(upper_half, y, x), jnp.where(upper_half, x, y)], axis=0
                    )

    def squares(g, h, result):
        pairs = []
        for e in (g - 1, g, g + 1):
            if abs(e - h) <= 1:
                inside = 0 <= e < groups
                pairs.append((e, (lambda e=e: it.part(e, h)) if inside else (lambda e=e: turn(it.part(h, e)))))
        span = range(1 if h > g else 0, GROUP)
        rows = slice(span[0] * BS, WIDE)

        def dot():
            return product([([x[rows] for x in it.part(g, e)], f()) for e, f in pairs])

        def store(value):
            result[rows] = value

        def post():
            masked = [jnp.zeros((BS, WIDE), F32)] * GROUP
            for s in span:
                masked[s] = result[s * BS : (s + 1) * BS] * line_of(lines, g, s, h)
            for s in range(GROUP):
                for p, x in enumerate(split(masked[s])):
                    keep[p, it.tile(g, h), s * BS : (s + 1) * BS] = x
            for s in span:
                part = jnp.where(upper_half, masked[s][HALF:], masked[s][:HALF])
                for t in range(GROUP):
                    k = t + GROUP * (h - g) - s + REACH
                    if 0 <= k < SPAN:
                        row_of(g, s, groups, square.at[g], low_square, high_square)[k] = part[
                            :, t * BS : (t + 1) * BS
                        ]
            if h == g:
                return
            for c in range(0, GROUP, 2):
                turned = jnp.concatenate(masked[c : c + 2], axis=0).T
                lanes = slice(c * BS, (c + 2) * BS)
                for p, x in enumerate(split(turned)):
                    keep[p, it.tile(h, g), :, lanes] = x
                for t in range(GROUP):
                    rows = turned[t * BS : (t + 1) * BS]
                    part = jnp.where(upper_half, rows[HALF:], rows[:HALF])
                    for s in range(c, c + 2):
                        k = s + GROUP * (g - h) - t + REACH
                        if 0 <= k < SPAN:
                            row_of(h, t, groups, square.at[h], low_square, high_square)[k] = part[
                                :, (s - c) * BS : (s - c + 1) * BS
                            ]

        return dot, store, post


    def begin():
        write_lines(pat, lines, lax.axis_index(axes) * it.count, groups)
        it.far_seed(0, low_sign)

    build(0)
    build(1)
    steps = [begin]
    for g in range(groups):
        if g + 1 < groups:
            steps.append(squares(g, g + 1, results.at[count_dots(steps)]))
            if g + 2 < groups:
                steps.append(functools.partial(build, g + 2))
        steps.append(squares(g, g, results.at[count_dots(steps)]))
        steps.append(functools.partial(it.send, g, 0, square.at[g], square_out, sems))
        if g in (0, groups - 1):
            side, source = (0, low_square) if g == 0 else (1, high_square)
            steps.append(
                functools.partial(it.send_edge, side, 0, source, square_out, edge_sems.at[side])
            )
    for g in range(groups - 1):
        for h in it.near(g):
            steps.append(it.second(g, h, sign.at[g], low_sign, None, results.at[count_dots(steps)]))
        steps.append(functools.partial(it.send, g, 1, sign.at[g], sign_out, sems))
        if g == 0:
            steps.append(functools.partial(it.send_edge, 0, 1, low_sign, sign_out, edge_sems.at[2]))
    steps.append(it.reaching(low_a, low_b, low_m, low_p, 0, -1, 0))
    steps.append(it.reaching(high_a, high_b, high_m, high_p, groups - 1, groups, BS))
    staggered(steps)
    it.finish()


def last_kernel(own, lines, full, mine, keep, sign, high_sign, results):
    it = Interior(own, lines, full, mine, keep)
    last = it.groups - 1
    steps = [it.second(last, h, sign, None, high_sign, results.at[i]) for i, h in enumerate(it.near(last))]
    steps.append(functools.partial(it.far_seed, last, high_sign))

    staggered(steps)


def border(
    side, groups, upper_half, lines, mine, theirs, a_ref, b_ref, m_ref, p_ref, square, sign, halo,
    first, last, sent
):
    at = 1 - side
    edge_group, outer_group = (0, -1) if side == 0 else (groups - 1, groups)
    offset = 0 if side == 0 else 2 * REACH
    below = REACH if side == 0 else 0
    zero = jnp.zeros((BS, WIDE), F32)

    def padded(rows, front):
        return split(jnp.concatenate([zero] + rows if front else rows + [zero], axis=0))

    whole_rows = []
    for p in range(REACH):
        rows = slice(p * HALF, (p + 1) * HALF)
        whole_rows.append(
            jnp.concatenate(
                [
                    jnp.where(upper_half, theirs[rows, :], mine[rows, :]),
                    jnp.where(upper_half, mine[rows, :], theirs[rows, :]),
                ],
                axis=0,
            )
        )

    def block(p, c):
        k = c - p + below
        if 0 <= k <= REACH:
            return whole_rows[p][:, k * BS : (k + 1) * BS]
        k = p - c + below
        if 0 <= c < REACH and 0 <= k <= REACH:
            return whole_rows[c][:, k * BS : (k + 1) * BS].T
        return jnp.zeros((BS, BS), F32)

    base = -5 if side == 0 else 0
    for p in range(REACH):
        rows = slice((p + at) * BS, (p + at + 1) * BS)
        for t in range(4):
            value = jnp.concatenate([block(p, base + 2 * t), block(p, base + 2 * t + 1)], axis=1)
            for q, x in enumerate(split(value)):
                halo[q, rows, t * 2 * BS : (t + 1) * 2 * BS] = x
    rows = slice(0, BS) if side == 0 else slice(REACH * BS, WIDE)
    for q in range(2):
        halo[q, rows, :] = jnp.zeros((BS, 2 * WIDE), BF)

    whole = [halo[q] for q in range(2)]
    outer_rows = slice(at * BS, (at + REACH) * BS)
    inner = slice(WIDE, 2 * WIDE) if side == 0 else slice(0, WIDE)
    to_edge = product([([m_ref[q] for q in range(2)], [x[:, inner] for x in whole])], True)
    among = product([([x[outer_rows] for x in whole], whole)], True)
    yield
    first[0] = to_edge + b_ref[...]
    rows = [
        first[0, s * BS : (s + 1) * BS] * line_of(lines, edge_group, s + 1 - at, outer_group)
        for s in range(REACH)
    ]
    across = padded(rows, side == 1)
    reach_out = [p_ref[q, 0] for q in range(2)]
    back = product([(reach_out, across)], True)
    partly = product([([p_ref[q, 1] for q in range(2)], across)])
    for s in range(REACH):
        part = jnp.where(upper_half, rows[s][HALF:], rows[s][:HALF])
        for t in range(REACH):
            k = t - s + offset
            if 0 <= k < SPAN:
                square[s, k] = part[:, (t + at) * BS : (t + at + 1) * BS]
    sent(0)
    yield
    first[1] = among + a_ref[...]
    rows = [
        first[1, p * BS : (p + 1) * BS] * line_of(lines, outer_group, p + at, outer_group)
        for p in range(REACH)
    ]
    out = product([(reach_out, padded(rows, side == 0))])
    last[1] = back
    for s in range(REACH):
        close = last[1, s * HALF : (s + 1) * HALF] * (
            line_of(lines, edge_group, s + 1 - at, edge_group) * 0.5
        )
        for t in range(REACH):
            k = t - s + REACH
            sign[s, k] = sign[s, k] - close[:, (t + 1 - at) * BS : (t + 2 - at) * BS]
    yield
    last[0] = out + partly
    for s in range(REACH):
        far = last[0, s * HALF : (s + 1) * HALF] * (
            line_of(lines, edge_group, s + 1 - at, outer_group) * 0.5
        )
        for t in range(REACH):
            k = t - s + offset
            if 0 <= k < SPAN:
                sign[s, k] = sign[s, k] - far[:, (t + at) * BS : (t + at + 1) * BS]
    sent(1)


def border_kernel(
    low_own, low_other, high_own, high_other, lines, sign_last, low_a, low_b, low_m, low_p, high_a,
    high_b, high_m, high_p, low_square_in, high_square_in, low_sign_in, high_sign_in, square_in,
    sign_in, low_square, high_square, low_sign, high_sign, square_out, sign_out, halo, first, last,
    sems, last_sems, *, groups, half_axis
):
    count = square_in.shape[0]
    upper_half = lax.axis_index(half_axis) == 1
    stores = []

    def send(source, target, rows, blocks, sem):
        from_rows = (0, rows[1] - rows[0])
        store = pltpu.make_async_copy(
            blocks_of(source, from_rows, blocks), blocks_of(target, rows, blocks), sem
        )
        store.start()
        stores.append(store)

    send(sign_last, sign_out, (count - GROUP, count - REACH), (0, SPAN), last_sems.at[0])
    send(high_sign, sign_out, (count - REACH, count), inner_blocks(1, False), last_sems.at[1])
    squares, signs = (low_square, high_square), (low_sign, high_sign)

    def side(n, *refs):
        def sent(i):
            source, target = ((squares[n], square_out), (signs[n], sign_out))[i]
            rows = (0, REACH) if n == 0 else (count - REACH, count)
            send(source, target, rows, outer_blocks(n, i == 0), sems.at[n, i])

        return border(
            n, groups, upper_half, lines, *refs, squares[n], signs[n], halo.at[n], first.at[n],
            last.at[n], sent,
        )

    works = [
        side(0, low_own, low_other, low_a, low_b, low_m, low_p),
        side(1, high_own, high_other, high_a, high_b, high_m, high_p),
    ]
    for _ in range(4):
        for work in works:
            next(work, None)
    for store in stores:
        store.wait()


def shards(matrix, pattern, *, axes, half_axis):
    count = matrix.shape[0]
    groups = count // GROUP
    flags = pattern.T
    vmem = pl.BlockSpec(memory_space=pltpu.VMEM)
    hbm = pl.BlockSpec(memory_space=pl.ANY)
    params = pltpu.CompilerParams(vmem_limit_bytes=LIMIT)

    top, bottom = matrix[:REACH, REACH:], matrix[count - REACH :, : REACH + 1]
    matrix, top, bottom = lax.optimization_barrier((matrix, top, bottom))
    edge = jax.ShapeDtypeStruct((REACH * HALF, (REACH + 1) * BS), F32)
    to_left, to_right = pl.pallas_call(
        edge_kernel,
        out_shape=(edge, edge),
        in_specs=[vmem] * 2,
        out_specs=[vmem] * 2,
        compiler_params=params,
        cost_estimate=pl.CostEstimate(
            flops=1 * 10**9, bytes_accessed=2**20, transcendentals=0
        ),
    )(top, bottom)
    size = 1
    for axis in axes:
        size *= lax.axis_size(axis)
    swap = [(0, 1), (1, 0)]
    other = lax.ppermute(matrix, half_axis, swap)
    forward = [(i, (i + 1) % size) for i in range(size)]
    backward = [(target, source) for source, target in forward]
    high_own = lax.ppermute(to_left, axes, backward)
    low_own = lax.ppermute(to_right, axes, forward)

    band = jax.ShapeDtypeStruct(matrix.shape, F32)
    edges = jax.ShapeDtypeStruct((REACH, SPAN, HALF, BS), F32)
    full = jax.ShapeDtypeStruct((2, groups, WIDE, 3 * WIDE), BF)
    mine = jax.ShapeDtypeStruct((2, groups, GROUP * HALF, 3 * WIDE), BF)
    keep = jax.ShapeDtypeStruct((2, 3 * groups, WIDE, WIDE), BF)
    lines = jax.ShapeDtypeStruct(((groups + 2) * GROUP, 3 * WIDE), F32)
    ends_out = [
        jax.ShapeDtypeStruct((REACH * BS, WIDE), F32),
        jax.ShapeDtypeStruct((REACH * BS, WIDE), F32),
        jax.ShapeDtypeStruct((2, REACH * BS, WIDE), BF),
        jax.ShapeDtypeStruct((2, 2, REACH * HALF, WIDE), BF),
    ]
    rows = jax.ShapeDtypeStruct((GROUP,) + matrix.shape[1:], F32)
    square, sign, low_square, high_square, low_sign, full, mine, keep, lines, *ends = pl.pallas_call(
        functools.partial(first_kernel, axes=axes, half_axis=half_axis),
        out_shape=[band, band, edges, edges, edges, full, mine, keep, lines] + ends_out * 2,
        in_specs=[vmem] * 3,
        out_specs=[hbm] * 2 + [vmem] * 15,
        scratch_shapes=[
            pltpu.VMEM((groups,) + rows.shape, F32),
            pltpu.VMEM((groups - 1,) + rows.shape, F32),
            pltpu.VMEM((2 * groups - 1 + 3 * groups - 4, WIDE, WIDE), F32),
            pltpu.SemaphoreType.DMA((2, groups)),
            pltpu.SemaphoreType.DMA((3,)),
        ],
        compiler_params=params,
        cost_estimate=pl.CostEstimate(
            flops=3 * 2 * 16 * WIDE**3, bytes_accessed=16 * 2**20, transcendentals=0
        ),
    )(matrix, other, flags)

    low_own, low_sign = lax.optimization_barrier((low_own, low_sign))
    high_own, low_sign = lax.optimization_barrier((high_own, low_sign))
    low_other = lax.ppermute(low_own, half_axis, swap)
    high_other = lax.ppermute(high_own, half_axis, swap)

    sign_last, high_sign = pl.pallas_call(
        last_kernel,
        out_shape=[rows, edges],
        in_specs=[vmem] * 5,
        out_specs=[vmem] * 2,
        scratch_shapes=[pltpu.VMEM((2, GROUP * HALF, WIDE), F32)],
        compiler_params=params,
        cost_estimate=pl.CostEstimate(
            flops=3 * 2 * 4 * WIDE**3, bytes_accessed=4 * 2**20, transcendentals=0
        ),
    )(matrix, lines, full, mine, keep)

    outs = pl.pallas_call(
        functools.partial(border_kernel, groups=groups, half_axis=half_axis),
        out_shape=[edges] * 4 + [band] * 2,
        in_specs=[vmem] * 18 + [hbm] * 2,
        out_specs=[vmem] * 4 + [hbm] * 2,
        scratch_shapes=[
            pltpu.VMEM((2, 2, WIDE, 2 * WIDE), BF),
            pltpu.VMEM((2, 2, REACH * BS, WIDE), F32),
            pltpu.VMEM((2, 2, REACH * HALF, WIDE), F32),
            pltpu.SemaphoreType.DMA((2, 2)),
            pltpu.SemaphoreType.DMA((2,)),
        ],
        input_output_aliases={14 + i: i for i in range(6)},
        compiler_params=params,
        cost_estimate=pl.CostEstimate(
            flops=3 * 2 * 4 * WIDE**3, bytes_accessed=2 * 2**20, transcendentals=0
        ),
    )(
        low_own, low_other, high_own, high_other, lines, sign_last, *ends, low_square, high_square,
        low_sign, high_sign, square, sign,
    )
    return tuple(outs[4:])


def solution(mesh):
    band = P(("group", "row", "col"), None, "rep", None)
    return jax.shard_map(
        functools.partial(shards, axes=("row", "col"), half_axis="rep"),
        mesh=mesh,
        in_specs=(band, P("group", None)),
        out_specs=(band, band),
        check_vma=False,
    )
```

```python
import functools

import jax
import jax.numpy as jnp
from jax import lax
from jax.experimental import pallas as pl
from jax.experimental.pallas import tpu as pltpu
from jax.sharding import PartitionSpec as P

REACH = 3
SPAN = 7
BS = 64
HALF = 32
GROUP = 4
WIDE = GROUP * BS
BF = jnp.bfloat16
F32 = jnp.float32
LIMIT = 32 * 1024 * 1024


def split(x):
    hi = x.astype(BF)
    return hi, (x - hi.astype(F32)).astype(BF)


def product(pairs, transposed=False):
    side = 1 if transposed else 0
    high, low = [jnp.concatenate([a[p] for a, _ in pairs], axis=1) for p in range(2)]
    right = [jnp.concatenate([b[p] for _, b in pairs], axis=side) for p in range(2)]
    dot = functools.partial(
        lax.dot_general,
        dimension_numbers=(((1,), (side,)), ((), ())),
        preferred_element_type=F32,
    )
    both = dot(jnp.concatenate([high, low], axis=0), right[0])
    count = high.shape[0]
    return both[:count] + (both[count:] + dot(high, right[1]))


def turn(x):
    return split((x[0].astype(F32) + x[1].astype(F32)).T)


def write_lines(pat, lines, first, groups):
    total = pat.shape[1]
    rows = lines.shape[0]
    iota = functools.partial(lax.broadcasted_iota, jnp.int32)
    dot = functools.partial(lax.dot_general, preferred_element_type=F32)
    wanted = lax.rem(first - GROUP + total + iota((rows, total), 0), total)
    chosen = (iota((rows, total), 1) == wanted).astype(BF)
    flags = dot(chosen, pat[...].astype(BF), (((1,), (1,)), ((), ())))
    place = iota((rows, 1), 0) % GROUP
    spread = jnp.concatenate(
        [jnp.where(place == s, flags, 0.0) for s in range(GROUP)], axis=1
    ).astype(BF)
    block = iota((SPAN, 3 * WIDE), 1) // BS - iota((SPAN, 3 * WIDE), 0) - 1
    spots = jnp.concatenate([(block == s).astype(BF) for s in range(GROUP)], axis=0)
    lines[...] = dot(spread, spots, (((1,), (0,)), ((), ())))


def line_of(lines, g, s, h):
    at = (g + 1) * GROUP + s
    lo = (h - g + 1) * WIDE
    return lines[at : at + 1, lo : lo + WIDE]


def inner_rows(g, groups):
    return range(REACH if g == 0 else 0, GROUP - REACH if g == groups - 1 else GROUP)


def inner_blocks(side, is_square):
    first = REACH if is_square else 2 * REACH
    return (first, SPAN) if side == 0 else (0, SPAN - first)


def outer_blocks(side, is_square):
    k0, k1 = inner_blocks(side, is_square)
    return (0, k0) if side == 0 else (k1, SPAN)


def blocks_of(ref, rows, blocks):
    return ref.at[pl.ds(rows[0], rows[1] - rows[0]), pl.ds(blocks[0], blocks[1] - blocks[0])]


def row_of(g, s, groups, rows, low, high):
    if s in inner_rows(g, groups):
        return rows.at[s]
    return low.at[s] if g == 0 else high.at[s - (GROUP - REACH)]


def edge_kernel(top, bottom, to_left, to_right):
    for source, target in ((top, to_left), (bottom, to_right)):
        for s in range(REACH):
            for t in range(2):
                target[s * HALF : (s + 1) * HALF, t * 2 * BS : (t + 1) * 2 * BS] = jnp.concatenate(
                    [source[s, 2 * t], source[s, 2 * t + 1]], axis=1
                )


class Interior:
    def __init__(self, own, lines, full, mine, keep):
        self.own = own
        self.lines = lines
        self.full = full
        self.mine = mine
        self.keep = keep
        self.count = own.shape[0]
        self.groups = self.count // GROUP
        self.stores = []

    def part(self, g, h, rows=slice(None)):
        at = (h - g + 1) * WIDE
        return [self.full[p, g, rows, at : at + WIDE] for p in range(2)]

    def my_part(self, g, h):
        at = (h - g + 1) * WIDE
        return [self.mine[p, g, :, at : at + WIDE] for p in range(2)]

    def tile(self, g, h):
        return 3 * g + h - g + 1

    def kept(self, g, h):
        return [self.keep[p, self.tile(g, h)] for p in range(2)]

    def near(self, g):
        return [e for e in (g - 1, g, g + 1) if 0 <= e < self.groups]

    def second(self, g, h, sign, low, high, result):
        span = range(1 if h > g else 0, GROUP - 1 if h < g else GROUP)
        rows = slice(span[0] * HALF, (span[-1] + 1) * HALF)

        def dot():
            return product(
                [
                    ([x[rows] for x in self.my_part(g, e)], self.kept(e, h))
                    for e in self.near(g)
                    if abs(e - h) <= 1
                ]
            )

        def store(value):
            result[rows] = value

        def post():
            for s in span:
                a = g * GROUP + s
                target = row_of(g, s, self.groups, sign, low, high)
                part = result[s * HALF : (s + 1) * HALF] * (line_of(self.lines, g, s, h) * 0.5)
                for t in range(GROUP):
                    k = t + GROUP * (h - g) - s + REACH
                    if 0 <= k < SPAN:
                        target[k] = 1.5 * self.own[a, k] - part[:, t * BS : (t + 1) * BS]

        return dot, store, post

    def far_seed(self, g, seed):
        for s in range(REACH):
            a = s if g == 0 else self.count - REACH + s
            for k in range(0, REACH - s) if g == 0 else range(2 * REACH - s, SPAN):
                seed[s, k] = 1.5 * self.own[a, k]

    def reaching(self, a_ref, b_ref, m_ref, p_ref, g, e, r0):
        rows = slice(r0, r0 + REACH * BS)
        mine_rows = slice(r0 // 2, r0 // 2 + REACH * HALF)
        outer = slice(BS - r0, BS - r0 + REACH * BS)

        def dot():
            out = self.part(g, e)
            return (
                product([([x[outer] for x in turn(out)], out)]),
                product([(self.part(g, g, rows), out)]),
            )

        def store(value):
            a_ref[...], b_ref[...] = value

        def post():
            for p in range(2):
                m_ref[p] = self.part(g, e)[p][rows]
                p_ref[p, 0] = self.my_part(g, e)[p][mine_rows]
                p_ref[p, 1] = self.my_part(g, g)[p][mine_rows]

        return dot, store, post

    def send(self, g, i, source, target, sems):
        rows = inner_rows(g, self.groups)
        store = pltpu.make_async_copy(
            source.at[pl.ds(rows[0], len(rows))],
            target.at[pl.ds(g * GROUP + rows[0], len(rows))],
            sems.at[i, g],
        )
        store.start()
        self.stores.append(store)

    def send_edge(self, side, i, source, target, sem):
        first = 0 if side == 0 else self.count - REACH
        blocks = inner_blocks(side, i == 0)
        store = pltpu.make_async_copy(
            blocks_of(source, (0, REACH), blocks),
            blocks_of(target, (first, first + REACH), blocks),
            sem,
        )
        store.start()
        self.stores.append(store)

    def finish(self):
        for store in self.stores:
            store.wait()


def count_dots(steps):
    return sum(isinstance(step, tuple) for step in steps)


def staggered(steps):
    pending = []
    for step in steps:
        if not isinstance(step, tuple):
            pending.append(step)
            continue
        dot, store, post = step
        value = dot()
        for work in pending:
            work()
        store(value)
        pending = [post]
    for work in pending:
        work()


def first_kernel(
    own, other, pat, square_out, sign_out, low_square, high_square, low_sign, full, mine, keep, lines, low_a, low_b, low_m, low_p,
    high_a, high_b, high_m, high_p, square, sign, results, sems, edge_sems, *, axes, half_axis
):
    it = Interior(own, lines, full, mine, keep)
    groups = it.groups
    upper_half = lax.axis_index(half_axis) == 1

    def build(g):
        for s in range(GROUP):
            a = g * GROUP + s
            for t in range(3 * GROUP // 2):
                ks = [2 * t + e - s - 1 for e in range(2)]
                lanes = slice(t * 2 * BS, (t + 1) * 2 * BS)
                rows = slice(s * BS, (s + 1) * BS)
                mine_rows = slice(s * HALF, (s + 1) * HALF)
                if all(k < 0 or k >= SPAN for k in ks):
                    for p in range(2):
                        full[p, g, rows, lanes] = jnp.zeros((BS, 2 * BS), BF)
                        mine[p, g, mine_rows, lanes] = jnp.zeros((HALF, 2 * BS), BF)
                    continue
                two = [
                    jnp.concatenate(
                        [src[a, k] if 0 <= k < SPAN else jnp.zeros((HALF, BS), F32) for k in ks],
                        axis=1,
                    )
                    for src in (own, other)
                ]
                for p, (x, y) in enumerate(zip(*[split(x) for x in two])):
                    mine[p, g, mine_rows, lanes] = x
                    full[p, g, rows, lanes] = jnp.concatenate(
                        [jnp.where(upper_half, y, x), jnp.where(upper_half, x, y)], axis=0
                    )

    def squares(g, h, result):
        pairs = []
        for e in (g - 1, g, g + 1):
            if abs(e - h) <= 1:
                inside = 0 <= e < groups
                pairs.append((e, (lambda e=e: it.part(e, h)) if inside else (lambda e=e: turn(it.part(h, e)))))
        span = range(1 if h > g else 0, GROUP)
        rows = slice(span[0] * BS, WIDE)

        def dot():
            return product([([x[rows] for x in it.part(g, e)], f()) for e, f in pairs])

        def store(value):
            result[rows] = value

        def post():
            masked = [jnp.zeros((BS, WIDE), F32)] * GROUP
            for s in span:
                masked[s] = result[s * BS : (s + 1) * BS] * line_of(lines, g, s, h)
            for s in range(GROUP):
                for p, x in enumerate(split(masked[s])):
                    keep[p, it.tile(g, h), s * BS : (s + 1) * BS] = x
            for s in span:
                part = jnp.where(upper_half, masked[s][HALF:], masked[s][:HALF])
                for t in range(GROUP):
                    k = t + GROUP * (h - g) - s + REACH
                    if 0 <= k < SPAN:
                        row_of(g, s, groups, square.at[g], low_square, high_square)[k] = part[
                            :, t * BS : (t + 1) * BS
                        ]
            if h == g:
                return
            for c in range(0, GROUP, 2):
                turned = jnp.concatenate(masked[c : c + 2], axis=0).T
                lanes = slice(c * BS, (c + 2) * BS)
                for p, x in enumerate(split(turned)):
                    keep[p, it.tile(h, g), :, lanes] = x
                for t in range(GROUP):
                    rows = turned[t * BS : (t + 1) * BS]
                    part = jnp.where(upper_half, rows[HALF:], rows[:HALF])
                    for s in range(c, c + 2):
                        k = s + GROUP * (g - h) - t + REACH
                        if 0 <= k < SPAN:
                            row_of(h, t, groups, square.at[h], low_square, high_square)[k] = part[
                                :, (s - c) * BS : (s - c + 1) * BS
                            ]

        return dot, store, post


    def begin():
        write_lines(pat, lines, lax.axis_index(axes) * it.count, groups)
        it.far_seed(0, low_sign)

    build(0)
    build(1)
    steps = [begin]
    for g in range(groups):
        if g + 1 < groups:
            steps.append(squares(g, g + 1, results.at[count_dots(steps)]))
            if g + 2 < groups:
                steps.append(functools.partial(build, g + 2))
        steps.append(squares(g, g, results.at[count_dots(steps)]))
        steps.append(functools.partial(it.send, g, 0, square.at[g], square_out, sems))
        if g in (0, groups - 1):
            side, source = (0, low_square) if g == 0 else (1, high_square)
            steps.append(
                functools.partial(it.send_edge, side, 0, source, square_out, edge_sems.at[side])
            )
    for g in range(groups - 1):
        for h in it.near(g):
            steps.append(it.second(g, h, sign.at[g], low_sign, None, results.at[count_dots(steps)]))
        steps.append(functools.partial(it.send, g, 1, sign.at[g], sign_out, sems))
        if g == 0:
            steps.append(functools.partial(it.send_edge, 0, 1, low_sign, sign_out, edge_sems.at[2]))
    steps.append(it.reaching(low_a, low_b, low_m, low_p, 0, -1, 0))
    steps.append(it.reaching(high_a, high_b, high_m, high_p, groups - 1, groups, BS))
    staggered(steps)
    it.finish()


def last_kernel(own, lines, full, mine, keep, sign, high_sign, results):
    it = Interior(own, lines, full, mine, keep)
    last = it.groups - 1
    steps = [it.second(last, h, sign, None, high_sign, results.at[i]) for i, h in enumerate(it.near(last))]
    steps.append(functools.partial(it.far_seed, last, high_sign))

    staggered(steps)


def border(
    side, groups, upper_half, lines, mine, theirs, a_ref, b_ref, m_ref, p_ref, square, sign, halo,
    first, last, sent
):
    at = 1 - side
    edge_group, outer_group = (0, -1) if side == 0 else (groups - 1, groups)
    offset = 0 if side == 0 else 2 * REACH
    below = REACH if side == 0 else 0
    zero = jnp.zeros((BS, WIDE), F32)

    def padded(rows, front):
        return split(jnp.concatenate([zero] + rows if front else rows + [zero], axis=0))

    whole_rows = []
    for p in range(REACH):
        rows = slice(p * HALF, (p + 1) * HALF)
        whole_rows.append(
            jnp.concatenate(
                [
                    jnp.where(upper_half, theirs[rows, :], mine[rows, :]),
                    jnp.where(upper_half, mine[rows, :], theirs[rows, :]),
                ],
                axis=0,
            )
        )

    def block(p, c):
        k = c - p + below
        if 0 <= k <= REACH:
            return whole_rows[p][:, k * BS : (k + 1) * BS]
        k = p - c + below
        if 0 <= c < REACH and 0 <= k <= REACH:
            return whole_rows[c][:, k * BS : (k + 1) * BS].T
        return jnp.zeros((BS, BS), F32)

    bases = (-1, -4) if side == 0 else (0, REACH)
    empty = slice(0, BS) if side == 0 else slice(REACH * BS, WIDE)

    def place(p, part, e):
        c = bases[part] + e
        return block(p, c) if part == 1 or 0 <= c < REACH else jnp.zeros((BS, BS), F32)

    def build(part):
        for p in range(REACH):
            rows = slice((p + at) * BS, (p + at + 1) * BS)
            for t in (2 * part, 2 * part + 1):
                value = jnp.concatenate(
                    [place(p, part, 2 * (t - 2 * part) + e) for e in range(2)], axis=1
                )
                for q, x in enumerate(split(value)):
                    halo[q, rows, t * 2 * BS : (t + 1) * 2 * BS] = x
        for q in range(2):
            halo[q, empty, part * WIDE : (part + 1) * WIDE] = jnp.zeros((BS, WIDE), BF)
        return [halo[q, :, part * WIDE : (part + 1) * WIDE] for q in range(2)]

    outer_rows = slice(at * BS, (at + REACH) * BS)
    beyond = build(1)
    further = product([([x[outer_rows] for x in beyond], beyond)], True)
    yield
    tile = build(0)
    both = product(
        [([jnp.concatenate([m_ref[q], tile[q][outer_rows]], axis=0) for q in range(2)], tile)]
    )
    yield
    first[0] = both[: REACH * BS] + b_ref[...]
    rows = [
        first[0, s * BS : (s + 1) * BS] * line_of(lines, edge_group, s + 1 - at, outer_group)
        for s in range(REACH)
    ]
    across = padded(rows, side == 1)
    reach_out = [p_ref[q, 0] for q in range(2)]
    back = product([(reach_out, across)], True)
    for s in range(REACH):
        part = jnp.where(upper_half, rows[s][HALF:], rows[s][:HALF])
        for t in range(REACH):
            k = t - s + offset
            if 0 <= k < SPAN:
                square[s, k] = part[:, (t + at) * BS : (t + at + 1) * BS]
    sent(0)
    yield
    first[1] = both[REACH * BS :] + (further + a_ref[...])
    rows = [
        first[1, p * BS : (p + 1) * BS] * line_of(lines, outer_group, p + at, outer_group)
        for p in range(REACH)
    ]
    inside = [p_ref[q, 1] for q in range(2)]
    out = product([(reach_out, padded(rows, side == 0)), (inside, across)])
    last[1] = back
    for s in range(REACH):
        close = last[1, s * HALF : (s + 1) * HALF] * (
            line_of(lines, edge_group, s + 1 - at, edge_group) * 0.5
        )
        for t in range(REACH):
            k = t - s + REACH
            sign[s, k] = sign[s, k] - close[:, (t + 1 - at) * BS : (t + 2 - at) * BS]
    yield
    last[0] = out
    for s in range(REACH):
        far = last[0, s * HALF : (s + 1) * HALF] * (
            line_of(lines, edge_group, s + 1 - at, outer_group) * 0.5
        )
        for t in range(REACH):
            k = t - s + offset
            if 0 <= k < SPAN:
                sign[s, k] = sign[s, k] - far[:, (t + at) * BS : (t + at + 1) * BS]
    sent(1)


def border_kernel(
    low_own, low_other, high_own, high_other, lines, sign_last, low_a, low_b, low_m, low_p, high_a,
    high_b, high_m, high_p, low_square_in, high_square_in, low_sign_in, high_sign_in, square_in,
    sign_in, low_square, high_square, low_sign, high_sign, square_out, sign_out, halo, first, last,
    sems, last_sems, *, groups, half_axis
):
    count = square_in.shape[0]
    upper_half = lax.axis_index(half_axis) == 1
    stores = []

    def send(source, target, rows, blocks, sem):
        from_rows = (0, rows[1] - rows[0])
        store = pltpu.make_async_copy(
            blocks_of(source, from_rows, blocks), blocks_of(target, rows, blocks), sem
        )
        store.start()
        stores.append(store)

    send(sign_last, sign_out, (count - GROUP, count - REACH), (0, SPAN), last_sems.at[0])
    send(high_sign, sign_out, (count - REACH, count), inner_blocks(1, False), last_sems.at[1])
    squares, signs = (low_square, high_square), (low_sign, high_sign)

    def side(n, *refs):
        def sent(i):
            source, target = ((squares[n], square_out), (signs[n], sign_out))[i]
            rows = (0, REACH) if n == 0 else (count - REACH, count)
            send(source, target, rows, outer_blocks(n, i == 0), sems.at[n, i])

        return border(
            n, groups, upper_half, lines, *refs, squares[n], signs[n], halo.at[n], first.at[n],
            last.at[n], sent,
        )

    works = [
        side(0, low_own, low_other, low_a, low_b, low_m, low_p),
        side(1, high_own, high_other, high_a, high_b, high_m, high_p),
    ]
    for _ in range(5):
        for work in works:
            next(work, None)
    for store in stores:
        store.wait()


def shards(matrix, pattern, *, axes, half_axis):
    count = matrix.shape[0]
    groups = count // GROUP
    flags = pattern.T
    vmem = pl.BlockSpec(memory_space=pltpu.VMEM)
    hbm = pl.BlockSpec(memory_space=pl.ANY)
    params = pltpu.CompilerParams(vmem_limit_bytes=LIMIT)

    top, bottom = matrix[:REACH, REACH:], matrix[count - REACH :, : REACH + 1]
    matrix, top, bottom = lax.optimization_barrier((matrix, top, bottom))
    edge = jax.ShapeDtypeStruct((REACH * HALF, (REACH + 1) * BS), F32)
    to_left, to_right = pl.pallas_call(
        edge_kernel,
        out_shape=(edge, edge),
        in_specs=[vmem] * 2,
        out_specs=[vmem] * 2,
        compiler_params=params,
        cost_estimate=pl.CostEstimate(
            flops=1 * 10**9, bytes_accessed=2**20, transcendentals=0
        ),
    )(top, bottom)
    size = 1
    for axis in axes:
        size *= lax.axis_size(axis)
    swap = [(0, 1), (1, 0)]
    other = lax.ppermute(matrix, half_axis, swap)
    forward = [(i, (i + 1) % size) for i in range(size)]
    backward = [(target, source) for source, target in forward]
    high_own = lax.ppermute(to_left, axes, backward)
    low_own = lax.ppermute(to_right, axes, forward)

    band = jax.ShapeDtypeStruct(matrix.shape, F32)
    edges = jax.ShapeDtypeStruct((REACH, SPAN, HALF, BS), F32)
    full = jax.ShapeDtypeStruct((2, groups, WIDE, 3 * WIDE), BF)
    mine = jax.ShapeDtypeStruct((2, groups, GROUP * HALF, 3 * WIDE), BF)
    keep = jax.ShapeDtypeStruct((2, 3 * groups, WIDE, WIDE), BF)
    lines = jax.ShapeDtypeStruct(((groups + 2) * GROUP, 3 * WIDE), F32)
    ends_out = [
        jax.ShapeDtypeStruct((REACH * BS, WIDE), F32),
        jax.ShapeDtypeStruct((REACH * BS, WIDE), F32),
        jax.ShapeDtypeStruct((2, REACH * BS, WIDE), BF),
        jax.ShapeDtypeStruct((2, 2, REACH * HALF, WIDE), BF),
    ]
    rows = jax.ShapeDtypeStruct((GROUP,) + matrix.shape[1:], F32)
    square, sign, low_square, high_square, low_sign, full, mine, keep, lines, *ends = pl.pallas_call(
        functools.partial(first_kernel, axes=axes, half_axis=half_axis),
        out_shape=[band, band, edges, edges, edges, full, mine, keep, lines] + ends_out * 2,
        in_specs=[vmem] * 3,
        out_specs=[hbm] * 2 + [vmem] * 15,
        scratch_shapes=[
            pltpu.VMEM((groups,) + rows.shape, F32),
            pltpu.VMEM((groups - 1,) + rows.shape, F32),
            pltpu.VMEM((2 * groups - 1 + 3 * groups - 4, WIDE, WIDE), F32),
            pltpu.SemaphoreType.DMA((2, groups)),
            pltpu.SemaphoreType.DMA((3,)),
        ],
        compiler_params=params,
        cost_estimate=pl.CostEstimate(
            flops=3 * 2 * 16 * WIDE**3, bytes_accessed=16 * 2**20, transcendentals=0
        ),
    )(matrix, other, flags)

    low_own, low_sign = lax.optimization_barrier((low_own, low_sign))
    high_own, low_sign = lax.optimization_barrier((high_own, low_sign))
    low_other = lax.ppermute(low_own, half_axis, swap)
    high_other = lax.ppermute(high_own, half_axis, swap)

    sign_last, high_sign = pl.pallas_call(
        last_kernel,
        out_shape=[rows, edges],
        in_specs=[vmem] * 5,
        out_specs=[vmem] * 2,
        scratch_shapes=[pltpu.VMEM((2, GROUP * HALF, WIDE), F32)],
        compiler_params=params,
        cost_estimate=pl.CostEstimate(
            flops=3 * 2 * 4 * WIDE**3, bytes_accessed=4 * 2**20, transcendentals=0
        ),
    )(matrix, lines, full, mine, keep)

    outs = pl.pallas_call(
        functools.partial(border_kernel, groups=groups, half_axis=half_axis),
        out_shape=[edges] * 4 + [band] * 2,
        in_specs=[vmem] * 18 + [hbm] * 2,
        out_specs=[vmem] * 4 + [hbm] * 2,
        scratch_shapes=[
            pltpu.VMEM((2, 2, WIDE, 2 * WIDE), BF),
            pltpu.VMEM((2, 2, REACH * BS, WIDE), F32),
            pltpu.VMEM((2, 2, REACH * HALF, WIDE), F32),
            pltpu.SemaphoreType.DMA((2, 2)),
            pltpu.SemaphoreType.DMA((2,)),
        ],
        input_output_aliases={14 + i: i for i in range(6)},
        compiler_params=params,
        cost_estimate=pl.CostEstimate(
            flops=3 * 2 * 4 * WIDE**3, bytes_accessed=2 * 2**20, transcendentals=0
        ),
    )(
        low_own, low_other, high_own, high_other, lines, sign_last, *ends, low_square, high_square,
        low_sign, high_sign, square, sign,
    )
    return tuple(outs[4:])


def solution(mesh):
    band = P(("group", "row", "col"), None, "rep", None)
    return jax.shard_map(
        functools.partial(shards, axes=("row", "col"), half_axis="rep"),
        mesh=mesh,
        in_specs=(band, P("group", None)),
        out_specs=(band, band),
        check_vma=False,
    )
```

```python
import functools

import jax
import jax.numpy as jnp
from jax import lax
from jax.experimental import pallas as pl
from jax.experimental.pallas import tpu as pltpu
from jax.sharding import PartitionSpec as P

REACH = 3
SPAN = 7
BS = 64
HALF = 32
GROUP = 4
WIDE = GROUP * BS
BF = jnp.bfloat16
F32 = jnp.float32
LIMIT = 32 * 1024 * 1024


def split(x):
    hi = x.astype(BF)
    return hi, (x - hi.astype(F32)).astype(BF)


def product(pairs, transposed=False):
    side = 1 if transposed else 0
    high, low = [jnp.concatenate([a[p] for a, _ in pairs], axis=1) for p in range(2)]
    right = [jnp.concatenate([b[p] for _, b in pairs], axis=side) for p in range(2)]
    dot = functools.partial(
        lax.dot_general,
        dimension_numbers=(((1,), (side,)), ((), ())),
        preferred_element_type=F32,
    )
    both = dot(jnp.concatenate([high, low], axis=0), right[0])
    count = high.shape[0]
    return both[:count] + (both[count:] + dot(high, right[1]))


def turn(x):
    return split((x[0].astype(F32) + x[1].astype(F32)).T)


def write_lines(pat, lines, first, groups):
    total = pat.shape[1]
    rows = lines.shape[0]
    iota = functools.partial(lax.broadcasted_iota, jnp.int32)
    dot = functools.partial(lax.dot_general, preferred_element_type=F32)
    wanted = lax.rem(first - GROUP + total + iota((rows, total), 0), total)
    chosen = (iota((rows, total), 1) == wanted).astype(BF)
    flags = dot(chosen, pat[...].astype(BF), (((1,), (1,)), ((), ())))
    place = iota((rows, 1), 0) % GROUP
    spread = jnp.concatenate(
        [jnp.where(place == s, flags, 0.0) for s in range(GROUP)], axis=1
    ).astype(BF)
    block = iota((SPAN, 3 * WIDE), 1) // BS - iota((SPAN, 3 * WIDE), 0) - 1
    spots = jnp.concatenate([(block == s).astype(BF) for s in range(GROUP)], axis=0)
    lines[...] = dot(spread, spots, (((1,), (0,)), ((), ())))


def line_of(lines, g, s, h):
    at = (g + 1) * GROUP + s
    lo = (h - g + 1) * WIDE
    return lines[at : at + 1, lo : lo + WIDE]


def inner_rows(g, groups):
    return range(REACH if g == 0 else 0, GROUP - REACH if g == groups - 1 else GROUP)


def inner_blocks(side, is_square):
    first = REACH if is_square else 2 * REACH
    return (first, SPAN) if side == 0 else (0, SPAN - first)


def outer_blocks(side, is_square):
    k0, k1 = inner_blocks(side, is_square)
    return (0, k0) if side == 0 else (k1, SPAN)


def blocks_of(ref, rows, blocks):
    return ref.at[pl.ds(rows[0], rows[1] - rows[0]), pl.ds(blocks[0], blocks[1] - blocks[0])]


def row_of(g, s, groups, rows, low, high):
    if s in inner_rows(g, groups):
        return rows.at[s]
    return low.at[s] if g == 0 else high.at[s - (GROUP - REACH)]


def edge_kernel(top, bottom, to_left, to_right):
    for source, target in ((top, to_left), (bottom, to_right)):
        for s in range(REACH):
            for t in range(2):
                target[s * HALF : (s + 1) * HALF, t * 2 * BS : (t + 1) * 2 * BS] = jnp.concatenate(
                    [source[s, 2 * t], source[s, 2 * t + 1]], axis=1
                )


class Interior:
    def __init__(self, own, lines, full, mine, keep):
        self.own = own
        self.lines = lines
        self.full = full
        self.mine = mine
        self.keep = keep
        self.count = own.shape[0]
        self.groups = self.count // GROUP
        self.stores = []

    def part(self, g, h, rows=slice(None)):
        at = (h - g + 1) * WIDE
        return [self.full[p, g, rows, at : at + WIDE] for p in range(2)]

    def my_part(self, g, h):
        at = (h - g + 1) * WIDE
        return [self.mine[p, g, :, at : at + WIDE] for p in range(2)]

    def tile(self, g, h):
        return 3 * g + h - g + 1

    def kept(self, g, h):
        return [self.keep[p, self.tile(g, h)] for p in range(2)]

    def near(self, g):
        return [e for e in (g - 1, g, g + 1) if 0 <= e < self.groups]

    def second(self, g, h, sign, low, high, result):
        span = range(1 if h > g else 0, GROUP - 1 if h < g else GROUP)
        rows = slice(span[0] * HALF, (span[-1] + 1) * HALF)

        def dot():
            return product(
                [
                    ([x[rows] for x in self.my_part(g, e)], self.kept(e, h))
                    for e in self.near(g)
                    if abs(e - h) <= 1
                ]
            )

        def store(value):
            result[rows] = value

        def post():
            for s in span:
                a = g * GROUP + s
                target = row_of(g, s, self.groups, sign, low, high)
                part = result[s * HALF : (s + 1) * HALF] * (line_of(self.lines, g, s, h) * 0.5)
                for t in range(GROUP):
                    k = t + GROUP * (h - g) - s + REACH
                    if 0 <= k < SPAN:
                        target[k] = 1.5 * self.own[a, k] - part[:, t * BS : (t + 1) * BS]

        return dot, store, post

    def far_seed(self, g, seed):
        for s in range(REACH):
            a = s if g == 0 else self.count - REACH + s
            for k in range(0, REACH - s) if g == 0 else range(2 * REACH - s, SPAN):
                seed[s, k] = 1.5 * self.own[a, k]

    def reaching(self, a_ref, b_ref, m_ref, p_ref, g, e, r0):
        rows = slice(r0, r0 + REACH * BS)
        mine_rows = slice(r0 // 2, r0 // 2 + REACH * HALF)
        outer = slice(BS - r0, BS - r0 + REACH * BS)

        def dot():
            out = self.part(g, e)
            return (
                product([([x[outer] for x in turn(out)], out)]),
                product([(self.part(g, g, rows), out)]),
            )

        def store(value):
            a_ref[...], b_ref[...] = value

        def post():
            for p in range(2):
                m_ref[p] = self.part(g, e)[p][rows]
                p_ref[p, 0] = self.my_part(g, e)[p][mine_rows]
                p_ref[p, 1] = self.my_part(g, g)[p][mine_rows]

        return dot, store, post

    def send(self, g, i, source, target, sems):
        rows = inner_rows(g, self.groups)
        store = pltpu.make_async_copy(
            source.at[pl.ds(rows[0], len(rows))],
            target.at[pl.ds(g * GROUP + rows[0], len(rows))],
            sems.at[i, g],
        )
        store.start()
        self.stores.append(store)

    def send_edge(self, side, i, source, target, sem):
        first = 0 if side == 0 else self.count - REACH
        blocks = inner_blocks(side, i == 0)
        store = pltpu.make_async_copy(
            blocks_of(source, (0, REACH), blocks),
            blocks_of(target, (first, first + REACH), blocks),
            sem,
        )
        store.start()
        self.stores.append(store)

    def finish(self):
        for store in self.stores:
            store.wait()


def count_dots(steps):
    return sum(isinstance(step, tuple) for step in steps)


def staggered(steps):
    pending = []
    for step in steps:
        if not isinstance(step, tuple):
            pending.append(step)
            continue
        dot, store, post = step
        value = dot()
        for work in pending:
            work()
        store(value)
        pending = [post]
    for work in pending:
        work()


def first_kernel(
    own, other, pat, square_out, sign_out, low_square, high_square, low_sign, full, mine, keep, lines,
    square, sign, results, sems, edge_sems, *, axes, half_axis
):
    it = Interior(own, lines, full, mine, keep)
    groups = it.groups
    upper_half = lax.axis_index(half_axis) == 1

    def build(g):
        for s in range(GROUP):
            a = g * GROUP + s
            for t in range(3 * GROUP // 2):
                ks = [2 * t + e - s - 1 for e in range(2)]
                lanes = slice(t * 2 * BS, (t + 1) * 2 * BS)
                rows = slice(s * BS, (s + 1) * BS)
                mine_rows = slice(s * HALF, (s + 1) * HALF)
                if all(k < 0 or k >= SPAN for k in ks):
                    for p in range(2):
                        full[p, g, rows, lanes] = jnp.zeros((BS, 2 * BS), BF)
                        mine[p, g, mine_rows, lanes] = jnp.zeros((HALF, 2 * BS), BF)
                    continue
                two = [
                    jnp.concatenate(
                        [src[a, k] if 0 <= k < SPAN else jnp.zeros((HALF, BS), F32) for k in ks],
                        axis=1,
                    )
                    for src in (own, other)
                ]
                for p, (x, y) in enumerate(zip(*[split(x) for x in two])):
                    mine[p, g, mine_rows, lanes] = x
                    full[p, g, rows, lanes] = jnp.concatenate(
                        [jnp.where(upper_half, y, x), jnp.where(upper_half, x, y)], axis=0
                    )

    def squares(g, h, result):
        pairs = []
        for e in (g - 1, g, g + 1):
            if abs(e - h) <= 1:
                inside = 0 <= e < groups
                pairs.append((e, (lambda e=e: it.part(e, h)) if inside else (lambda e=e: turn(it.part(h, e)))))
        span = range(1 if h > g else 0, GROUP)
        rows = slice(span[0] * BS, WIDE)

        def dot():
            return product([([x[rows] for x in it.part(g, e)], f()) for e, f in pairs])

        def store(value):
            result[rows] = value

        def post():
            masked = [jnp.zeros((BS, WIDE), F32)] * GROUP
            for s in span:
                masked[s] = result[s * BS : (s + 1) * BS] * line_of(lines, g, s, h)
            for s in range(GROUP):
                for p, x in enumerate(split(masked[s])):
                    keep[p, it.tile(g, h), s * BS : (s + 1) * BS] = x
            for s in span:
                part = jnp.where(upper_half, masked[s][HALF:], masked[s][:HALF])
                for t in range(GROUP):
                    k = t + GROUP * (h - g) - s + REACH
                    if 0 <= k < SPAN:
                        row_of(g, s, groups, square.at[g], low_square, high_square)[k] = part[
                            :, t * BS : (t + 1) * BS
                        ]
            if h == g:
                return
            for c in range(0, GROUP, 2):
                turned = jnp.concatenate(masked[c : c + 2], axis=0).T
                lanes = slice(c * BS, (c + 2) * BS)
                for p, x in enumerate(split(turned)):
                    keep[p, it.tile(h, g), :, lanes] = x
                for t in range(GROUP):
                    rows = turned[t * BS : (t + 1) * BS]
                    part = jnp.where(upper_half, rows[HALF:], rows[:HALF])
                    for s in range(c, c + 2):
                        k = s + GROUP * (g - h) - t + REACH
                        if 0 <= k < SPAN:
                            row_of(h, t, groups, square.at[h], low_square, high_square)[k] = part[
                                :, (s - c) * BS : (s - c + 1) * BS
                            ]

        return dot, store, post


    def begin():
        write_lines(pat, lines, lax.axis_index(axes) * it.count, groups)
        it.far_seed(0, low_sign)

    build(0)
    build(1)
    steps = [begin]
    for g in range(groups):
        if g + 1 < groups:
            steps.append(squares(g, g + 1, results.at[count_dots(steps)]))
            if g + 2 < groups:
                steps.append(functools.partial(build, g + 2))
        steps.append(squares(g, g, results.at[count_dots(steps)]))
        steps.append(functools.partial(it.send, g, 0, square.at[g], square_out, sems))
        if g in (0, groups - 1):
            side, source = (0, low_square) if g == 0 else (1, high_square)
            steps.append(
                functools.partial(it.send_edge, side, 0, source, square_out, edge_sems.at[side])
            )
    for g in range(groups - 1):
        for h in it.near(g):
            steps.append(it.second(g, h, sign.at[g], low_sign, None, results.at[count_dots(steps)]))
        steps.append(functools.partial(it.send, g, 1, sign.at[g], sign_out, sems))
        if g == 0:
            steps.append(functools.partial(it.send_edge, 0, 1, low_sign, sign_out, edge_sems.at[2]))
    staggered(steps)
    it.finish()


def last_kernel(
    own, lines, full, mine, keep, sign, high_sign, low_a, low_b, low_m, low_p, high_a, high_b, high_m,
    high_p, results
):
    it = Interior(own, lines, full, mine, keep)
    last = it.groups - 1
    steps = [it.second(last, h, sign, None, high_sign, results.at[i]) for i, h in enumerate(it.near(last))]
    steps.append(functools.partial(it.far_seed, last, high_sign))
    steps.append(it.reaching(low_a, low_b, low_m, low_p, 0, -1, 0))
    steps.append(it.reaching(high_a, high_b, high_m, high_p, last, it.groups, BS))

    staggered(steps)


def border(
    side, groups, upper_half, lines, mine, theirs, a_ref, b_ref, m_ref, p_ref, square, sign, halo,
    first, last, sent
):
    at = 1 - side
    edge_group, outer_group = (0, -1) if side == 0 else (groups - 1, groups)
    offset = 0 if side == 0 else 2 * REACH
    below = REACH if side == 0 else 0
    zero = jnp.zeros((BS, WIDE), F32)

    def padded(rows, front):
        return split(jnp.concatenate([zero] + rows if front else rows + [zero], axis=0))

    whole_rows = []
    for p in range(REACH):
        rows = slice(p * HALF, (p + 1) * HALF)
        whole_rows.append(
            jnp.concatenate(
                [
                    jnp.where(upper_half, theirs[rows, :], mine[rows, :]),
                    jnp.where(upper_half, mine[rows, :], theirs[rows, :]),
                ],
                axis=0,
            )
        )

    def block(p, c):
        k = c - p + below
        if 0 <= k <= REACH:
            return whole_rows[p][:, k * BS : (k + 1) * BS]
        k = p - c + below
        if 0 <= c < REACH and 0 <= k <= REACH:
            return whole_rows[c][:, k * BS : (k + 1) * BS].T
        return jnp.zeros((BS, BS), F32)

    base = -5 if side == 0 else 0
    for p in range(REACH):
        rows = slice((p + at) * BS, (p + at + 1) * BS)
        for t in range(4):
            value = jnp.concatenate([block(p, base + 2 * t), block(p, base + 2 * t + 1)], axis=1)
            for q, x in enumerate(split(value)):
                halo[q, rows, t * 2 * BS : (t + 1) * 2 * BS] = x
    rows = slice(0, BS) if side == 0 else slice(REACH * BS, WIDE)
    for q in range(2):
        halo[q, rows, :] = jnp.zeros((BS, 2 * WIDE), BF)

    whole = [halo[q] for q in range(2)]
    outer_rows = slice(at * BS, (at + REACH) * BS)
    inner = slice(WIDE, 2 * WIDE) if side == 0 else slice(0, WIDE)
    to_edge = product([([m_ref[q] for q in range(2)], [x[:, inner] for x in whole])], True)
    among = product([([x[outer_rows] for x in whole], whole)], True)
    yield
    first[0] = to_edge + b_ref[...]
    rows = [
        first[0, s * BS : (s + 1) * BS] * line_of(lines, edge_group, s + 1 - at, outer_group)
        for s in range(REACH)
    ]
    across = padded(rows, side == 1)
    reach_out = [p_ref[q, 0] for q in range(2)]
    back = product([(reach_out, across)], True)
    for s in range(REACH):
        part = jnp.where(upper_half, rows[s][HALF:], rows[s][:HALF])
        for t in range(REACH):
            k = t - s + offset
            if 0 <= k < SPAN:
                square[s, k] = part[:, (t + at) * BS : (t + at + 1) * BS]
    sent(0)
    yield
    first[1] = among + a_ref[...]
    rows = [
        first[1, p * BS : (p + 1) * BS] * line_of(lines, outer_group, p + at, outer_group)
        for p in range(REACH)
    ]
    inside = [p_ref[q, 1] for q in range(2)]
    out = product([(reach_out, padded(rows, side == 0)), (inside, across)])
    last[1] = back
    for s in range(REACH):
        close = last[1, s * HALF : (s + 1) * HALF] * (
            line_of(lines, edge_group, s + 1 - at, edge_group) * 0.5
        )
        for t in range(REACH):
            k = t - s + REACH
            sign[s, k] = sign[s, k] - close[:, (t + 1 - at) * BS : (t + 2 - at) * BS]
    yield
    last[0] = out
    for s in range(REACH):
        far = last[0, s * HALF : (s + 1) * HALF] * (
            line_of(lines, edge_group, s + 1 - at, outer_group) * 0.5
        )
        for t in range(REACH):
            k = t - s + offset
            if 0 <= k < SPAN:
                sign[s, k] = sign[s, k] - far[:, (t + at) * BS : (t + at + 1) * BS]
    sent(1)


def border_kernel(
    low_own, low_other, high_own, high_other, lines, sign_last, low_a, low_b, low_m, low_p, high_a,
    high_b, high_m, high_p, low_square_in, high_square_in, low_sign_in, high_sign_in, square_in,
    sign_in, low_square, high_square, low_sign, high_sign, square_out, sign_out, halo, first, last,
    sems, last_sems, *, groups, half_axis
):
    count = square_in.shape[0]
    upper_half = lax.axis_index(half_axis) == 1
    stores = []

    def send(source, target, rows, blocks, sem):
        from_rows = (0, rows[1] - rows[0])
        store = pltpu.make_async_copy(
            blocks_of(source, from_rows, blocks), blocks_of(target, rows, blocks), sem
        )
        store.start()
        stores.append(store)

    send(sign_last, sign_out, (count - GROUP, count - REACH), (0, SPAN), last_sems.at[0])
    send(high_sign, sign_out, (count - REACH, count), inner_blocks(1, False), last_sems.at[1])
    squares, signs = (low_square, high_square), (low_sign, high_sign)

    def side(n, *refs):
        def sent(i):
            source, target = ((squares[n], square_out), (signs[n], sign_out))[i]
            rows = (0, REACH) if n == 0 else (count - REACH, count)
            send(source, target, rows, outer_blocks(n, i == 0), sems.at[n, i])

        return border(
            n, groups, upper_half, lines, *refs, squares[n], signs[n], halo.at[n], first.at[n],
            last.at[n], sent,
        )

    works = [
        side(0, low_own, low_other, low_a, low_b, low_m, low_p),
        side(1, high_own, high_other, high_a, high_b, high_m, high_p),
    ]
    for _ in range(4):
        for work in works:
            next(work, None)
    for store in stores:
        store.wait()


def shards(matrix, pattern, *, axes, half_axis):
    count = matrix.shape[0]
    groups = count // GROUP
    flags = pattern.T
    vmem = pl.BlockSpec(memory_space=pltpu.VMEM)
    hbm = pl.BlockSpec(memory_space=pl.ANY)
    params = pltpu.CompilerParams(vmem_limit_bytes=LIMIT)

    top, bottom = matrix[:REACH, REACH:], matrix[count - REACH :, : REACH + 1]
    edge = jax.ShapeDtypeStruct((REACH * HALF, (REACH + 1) * BS), F32)
    to_left, to_right = pl.pallas_call(
        edge_kernel,
        out_shape=(edge, edge),
        in_specs=[vmem] * 2,
        out_specs=[vmem] * 2,
        compiler_params=pltpu.CompilerParams(
            vmem_limit_bytes=LIMIT, allow_input_fusion=[True, True]
        ),
        cost_estimate=pl.CostEstimate(
            flops=1 * 10**9, bytes_accessed=2**20, transcendentals=0
        ),
    )(top, bottom)
    size = 1
    for axis in axes:
        size *= lax.axis_size(axis)
    swap = [(0, 1), (1, 0)]
    other = lax.ppermute(matrix, half_axis, swap)
    forward = [(i, (i + 1) % size) for i in range(size)]
    backward = [(target, source) for source, target in forward]
    high_own = lax.ppermute(to_left, axes, backward)
    low_own = lax.ppermute(to_right, axes, forward)

    band = jax.ShapeDtypeStruct(matrix.shape, F32)
    edges = jax.ShapeDtypeStruct((REACH, SPAN, HALF, BS), F32)
    full = jax.ShapeDtypeStruct((2, groups, WIDE, 3 * WIDE), BF)
    mine = jax.ShapeDtypeStruct((2, groups, GROUP * HALF, 3 * WIDE), BF)
    keep = jax.ShapeDtypeStruct((2, 3 * groups, WIDE, WIDE), BF)
    lines = jax.ShapeDtypeStruct(((groups + 2) * GROUP, 3 * WIDE), F32)
    ends_out = [
        jax.ShapeDtypeStruct((REACH * BS, WIDE), F32),
        jax.ShapeDtypeStruct((REACH * BS, WIDE), F32),
        jax.ShapeDtypeStruct((2, REACH * BS, WIDE), BF),
        jax.ShapeDtypeStruct((2, 2, REACH * HALF, WIDE), BF),
    ]
    rows = jax.ShapeDtypeStruct((GROUP,) + matrix.shape[1:], F32)
    square, sign, low_square, high_square, low_sign, full, mine, keep, lines = pl.pallas_call(
        functools.partial(first_kernel, axes=axes, half_axis=half_axis),
        out_shape=[band, band, edges, edges, edges, full, mine, keep, lines],
        in_specs=[vmem] * 3,
        out_specs=[hbm] * 2 + [vmem] * 7,
        scratch_shapes=[
            pltpu.VMEM((groups,) + rows.shape, F32),
            pltpu.VMEM((groups - 1,) + rows.shape, F32),
            pltpu.VMEM((2 * groups - 1 + 3 * groups - 4, WIDE, WIDE), F32),
            pltpu.SemaphoreType.DMA((2, groups)),
            pltpu.SemaphoreType.DMA((3,)),
        ],
        compiler_params=params,
        cost_estimate=pl.CostEstimate(
            flops=3 * 2 * 16 * WIDE**3, bytes_accessed=16 * 2**20, transcendentals=0
        ),
    )(matrix, other, flags)

    high_own, low_sign = lax.optimization_barrier((high_own, low_sign))
    high_other = lax.ppermute(high_own, half_axis, swap)
    low_own, low_sign = lax.optimization_barrier((low_own, low_sign))
    low_other = lax.ppermute(low_own, half_axis, swap)

    sign_last, high_sign, *ends = pl.pallas_call(
        last_kernel,
        out_shape=[rows, edges] + ends_out * 2,
        in_specs=[vmem] * 5,
        out_specs=[vmem] * 10,
        scratch_shapes=[pltpu.VMEM((2, GROUP * HALF, WIDE), F32)],
        compiler_params=params,
        cost_estimate=pl.CostEstimate(
            flops=3 * 2 * 4 * WIDE**3, bytes_accessed=4 * 2**20, transcendentals=0
        ),
    )(matrix, lines, full, mine, keep)

    outs = pl.pallas_call(
        functools.partial(border_kernel, groups=groups, half_axis=half_axis),
        out_shape=[edges] * 4 + [band] * 2,
        in_specs=[vmem] * 18 + [hbm] * 2,
        out_specs=[vmem] * 4 + [hbm] * 2,
        scratch_shapes=[
            pltpu.VMEM((2, 2, WIDE, 2 * WIDE), BF),
            pltpu.VMEM((2, 2, REACH * BS, WIDE), F32),
            pltpu.VMEM((2, 2, REACH * HALF, WIDE), F32),
            pltpu.SemaphoreType.DMA((2, 2)),
            pltpu.SemaphoreType.DMA((2,)),
        ],
        input_output_aliases={14 + i: i for i in range(6)},
        compiler_params=params,
        cost_estimate=pl.CostEstimate(
            flops=3 * 2 * 4 * WIDE**3, bytes_accessed=2 * 2**20, transcendentals=0
        ),
    )(
        low_own, low_other, high_own, high_other, lines, sign_last, *ends, low_square, high_square,
        low_sign, high_sign, square, sign,
    )
    return tuple(outs[4:])


def solution(mesh):
    band = P(("group", "row", "col"), None, "rep", None)
    return jax.shard_map(
        functools.partial(shards, axes=("row", "col"), half_axis="rep"),
        mesh=mesh,
        in_specs=(band, P("group", None)),
        out_specs=(band, band),
        check_vma=False,
    )
```

```python
import functools

import jax
import jax.numpy as jnp
from jax import lax
from jax.experimental import pallas as pl
from jax.experimental.pallas import tpu as pltpu
from jax.sharding import PartitionSpec as P

REACH = 3
SPAN = 7
BS = 64
HALF = 32
GROUP = 4
WIDE = GROUP * BS
BF = jnp.bfloat16
F32 = jnp.float32
LIMIT = 32 * 1024 * 1024


def split(x):
    hi = x.astype(BF)
    return hi, (x - hi.astype(F32)).astype(BF)


def product(pairs, transposed=False):
    side = 1 if transposed else 0
    high, low = [jnp.concatenate([a[p] for a, _ in pairs], axis=1) for p in range(2)]
    right = [jnp.concatenate([b[p] for _, b in pairs], axis=side) for p in range(2)]
    dot = functools.partial(
        lax.dot_general,
        dimension_numbers=(((1,), (side,)), ((), ())),
        preferred_element_type=F32,
    )
    both = dot(jnp.concatenate([high, low], axis=0), right[0])
    count = high.shape[0]
    return both[:count] + (both[count:] + dot(high, right[1]))


def turn(x):
    return split((x[0].astype(F32) + x[1].astype(F32)).T)


def write_lines(pat, lines, first, groups):
    total = pat.shape[1]
    rows = lines.shape[0]
    iota = functools.partial(lax.broadcasted_iota, jnp.int32)
    dot = functools.partial(lax.dot_general, preferred_element_type=F32)
    wanted = lax.rem(first - GROUP + total + iota((rows, total), 0), total)
    chosen = (iota((rows, total), 1) == wanted).astype(BF)
    flags = dot(chosen, pat[...].astype(BF), (((1,), (1,)), ((), ())))
    place = iota((rows, 1), 0) % GROUP
    spread = jnp.concatenate(
        [jnp.where(place == s, flags, 0.0) for s in range(GROUP)], axis=1
    ).astype(BF)
    block = iota((SPAN, 3 * WIDE), 1) // BS - iota((SPAN, 3 * WIDE), 0) - 1
    spots = jnp.concatenate([(block == s).astype(BF) for s in range(GROUP)], axis=0)
    lines[...] = dot(spread, spots, (((1,), (0,)), ((), ())))


def line_of(lines, g, s, h):
    at = (g + 1) * GROUP + s
    lo = (h - g + 1) * WIDE
    return lines[at : at + 1, lo : lo + WIDE]


def inner_rows(g, groups):
    return range(REACH if g == 0 else 0, GROUP - REACH if g == groups - 1 else GROUP)


def inner_blocks(side, is_square):
    first = REACH if is_square else 2 * REACH
    return (first, SPAN) if side == 0 else (0, SPAN - first)


def outer_blocks(side, is_square):
    k0, k1 = inner_blocks(side, is_square)
    return (0, k0) if side == 0 else (k1, SPAN)


def blocks_of(ref, rows, blocks):
    return ref.at[pl.ds(rows[0], rows[1] - rows[0]), pl.ds(blocks[0], blocks[1] - blocks[0])]


def row_of(g, s, groups, rows, low, high):
    if s in inner_rows(g, groups):
        return rows.at[s]
    return low.at[s] if g == 0 else high.at[s - (GROUP - REACH)]


def edge_kernel(top, bottom, to_left, to_right):
    for source, target in ((top, to_left), (bottom, to_right)):
        for s in range(REACH):
            for t in range(2):
                target[s * HALF : (s + 1) * HALF, t * 2 * BS : (t + 1) * 2 * BS] = jnp.concatenate(
                    [source[s, 2 * t], source[s, 2 * t + 1]], axis=1
                )


class Interior:
    def __init__(self, own, lines, full, mine, keep):
        self.own = own
        self.lines = lines
        self.full = full
        self.mine = mine
        self.keep = keep
        self.count = own.shape[0]
        self.groups = self.count // GROUP
        self.stores = []

    def part(self, g, h, rows=slice(None)):
        at = (h - g + 1) * WIDE
        return [self.full[p, g, rows, at : at + WIDE] for p in range(2)]

    def my_part(self, g, h):
        at = (h - g + 1) * WIDE
        return [self.mine[p, g, :, at : at + WIDE] for p in range(2)]

    def tile(self, g, h):
        return 3 * g + h - g + 1

    def kept(self, g, h):
        return [self.keep[p, self.tile(g, h)] for p in range(2)]

    def near(self, g):
        return [e for e in (g - 1, g, g + 1) if 0 <= e < self.groups]

    def second(self, g, h, sign, low, high, result):
        span = range(1 if h > g else 0, GROUP - 1 if h < g else GROUP)
        rows = slice(span[0] * HALF, (span[-1] + 1) * HALF)

        def dot():
            return product(
                [
                    ([x[rows] for x in self.my_part(g, e)], self.kept(e, h))
                    for e in self.near(g)
                    if abs(e - h) <= 1
                ]
            )

        def store(value):
            result[rows] = value

        def post():
            for s in span:
                a = g * GROUP + s
                target = row_of(g, s, self.groups, sign, low, high)
                part = result[s * HALF : (s + 1) * HALF] * (line_of(self.lines, g, s, h) * 0.5)
                for t in range(GROUP):
                    k = t + GROUP * (h - g) - s + REACH
                    if 0 <= k < SPAN:
                        target[k] = 1.5 * self.own[a, k] - part[:, t * BS : (t + 1) * BS]

        return dot, store, post

    def far_seed(self, g, seed):
        for s in range(REACH):
            a = s if g == 0 else self.count - REACH + s
            for k in range(0, REACH - s) if g == 0 else range(2 * REACH - s, SPAN):
                seed[s, k] = 1.5 * self.own[a, k]

    def reaching(self, a_ref, b_ref, m_ref, p_ref, g, e, r0):
        rows = slice(r0, r0 + REACH * BS)
        mine_rows = slice(r0 // 2, r0 // 2 + REACH * HALF)
        outer = slice(BS - r0, BS - r0 + REACH * BS)

        def dot():
            out = self.part(g, e)
            return (
                product([([x[outer] for x in turn(out)], out)]),
                product([(self.part(g, g, rows), out)]),
            )

        def store(value):
            a_ref[...], b_ref[...] = value

        def post():
            for p in range(2):
                m_ref[p] = self.part(g, e)[p][rows]
                p_ref[p, 0] = self.my_part(g, e)[p][mine_rows]
                p_ref[p, 1] = self.my_part(g, g)[p][mine_rows]

        return dot, store, post

    def send(self, g, i, source, target, sems):
        rows = inner_rows(g, self.groups)
        store = pltpu.make_async_copy(
            source.at[pl.ds(rows[0], len(rows))],
            target.at[pl.ds(g * GROUP + rows[0], len(rows))],
            sems.at[i, g],
        )
        store.start()
        self.stores.append(store)

    def send_edge(self, side, i, source, target, sem):
        first = 0 if side == 0 else self.count - REACH
        blocks = inner_blocks(side, i == 0)
        store = pltpu.make_async_copy(
            blocks_of(source, (0, REACH), blocks),
            blocks_of(target, (first, first + REACH), blocks),
            sem,
        )
        store.start()
        self.stores.append(store)

    def finish(self):
        for store in self.stores:
            store.wait()


def count_dots(steps):
    return sum(isinstance(step, tuple) for step in steps)


def staggered(steps):
    pending = []
    for step in steps:
        if not isinstance(step, tuple):
            pending.append(step)
            continue
        dot, store, post = step
        value = dot()
        for work in pending:
            work()
        store(value)
        pending = [post]
    for work in pending:
        work()


def first_kernel(
    own, other, pat, square_out, sign_out, low_square, high_square, low_sign, full, mine, keep, lines,
    square, sign, results, sems, edge_sems, *, axes, half_axis
):
    it = Interior(own, lines, full, mine, keep)
    groups = it.groups
    upper_half = lax.axis_index(half_axis) == 1

    def build(g):
        for s in range(GROUP):
            a = g * GROUP + s
            for t in range(3 * GROUP // 2):
                ks = [2 * t + e - s - 1 for e in range(2)]
                lanes = slice(t * 2 * BS, (t + 1) * 2 * BS)
                rows = slice(s * BS, (s + 1) * BS)
                mine_rows = slice(s * HALF, (s + 1) * HALF)
                if all(k < 0 or k >= SPAN for k in ks):
                    for p in range(2):
                        full[p, g, rows, lanes] = jnp.zeros((BS, 2 * BS), BF)
                        mine[p, g, mine_rows, lanes] = jnp.zeros((HALF, 2 * BS), BF)
                    continue
                two = [
                    jnp.concatenate(
                        [src[a, k] if 0 <= k < SPAN else jnp.zeros((HALF, BS), F32) for k in ks],
                        axis=1,
                    )
                    for src in (own, other)
                ]
                for p, (x, y) in enumerate(zip(*[split(x) for x in two])):
                    mine[p, g, mine_rows, lanes] = x
                    full[p, g, rows, lanes] = jnp.concatenate(
                        [jnp.where(upper_half, y, x), jnp.where(upper_half, x, y)], axis=0
                    )

    def squares(g, h, result):
        pairs = []
        for e in (g - 1, g, g + 1):
            if abs(e - h) <= 1:
                inside = 0 <= e < groups
                pairs.append((e, (lambda e=e: it.part(e, h)) if inside else (lambda e=e: turn(it.part(h, e)))))
        span = range(1 if h > g else 0, GROUP)
        rows = slice(span[0] * BS, WIDE)

        def dot():
            return product([([x[rows] for x in it.part(g, e)], f()) for e, f in pairs])

        def store(value):
            result[rows] = value

        def post():
            masked = [jnp.zeros((BS, WIDE), F32)] * GROUP
            for s in span:
                masked[s] = result[s * BS : (s + 1) * BS] * line_of(lines, g, s, h)
            for s in range(GROUP):
                for p, x in enumerate(split(masked[s])):
                    keep[p, it.tile(g, h), s * BS : (s + 1) * BS] = x
            for s in span:
                part = jnp.where(upper_half, masked[s][HALF:], masked[s][:HALF])
                for t in range(GROUP):
                    k = t + GROUP * (h - g) - s + REACH
                    if 0 <= k < SPAN:
                        row_of(g, s, groups, square.at[g], low_square, high_square)[k] = part[
                            :, t * BS : (t + 1) * BS
                        ]
            if h == g:
                return
            for c in range(0, GROUP, 2):
                turned = jnp.concatenate(masked[c : c + 2], axis=0).T
                lanes = slice(c * BS, (c + 2) * BS)
                for p, x in enumerate(split(turned)):
                    keep[p, it.tile(h, g), :, lanes] = x
                for t in range(GROUP):
                    rows = turned[t * BS : (t + 1) * BS]
                    part = jnp.where(upper_half, rows[HALF:], rows[:HALF])
                    for s in range(c, c + 2):
                        k = s + GROUP * (g - h) - t + REACH
                        if 0 <= k < SPAN:
                            row_of(h, t, groups, square.at[h], low_square, high_square)[k] = part[
                                :, (s - c) * BS : (s - c + 1) * BS
                            ]

        return dot, store, post


    def begin():
        write_lines(pat, lines, lax.axis_index(axes) * it.count, groups)
        it.far_seed(0, low_sign)

    build(0)
    build(1)
    steps = [begin]
    for g in range(groups):
        if g + 1 < groups:
            steps.append(squares(g, g + 1, results.at[count_dots(steps)]))
            if g + 2 < groups:
                steps.append(functools.partial(build, g + 2))
        steps.append(squares(g, g, results.at[count_dots(steps)]))
        steps.append(functools.partial(it.send, g, 0, square.at[g], square_out, sems))
        if g in (0, groups - 1):
            side, source = (0, low_square) if g == 0 else (1, high_square)
            steps.append(
                functools.partial(it.send_edge, side, 0, source, square_out, edge_sems.at[side])
            )
    for g in range(groups - 1):
        for h in it.near(g):
            steps.append(it.second(g, h, sign.at[g], low_sign, None, results.at[count_dots(steps)]))
        steps.append(functools.partial(it.send, g, 1, sign.at[g], sign_out, sems))
        if g == 0:
            steps.append(functools.partial(it.send_edge, 0, 1, low_sign, sign_out, edge_sems.at[2]))
    staggered(steps)
    it.finish()


def last_kernel(
    own, lines, full, mine, keep, sign, high_sign, low_a, low_b, low_m, low_p, high_a, high_b, high_m,
    high_p, results
):
    it = Interior(own, lines, full, mine, keep)
    last = it.groups - 1
    steps = [it.second(last, h, sign, None, high_sign, results.at[i]) for i, h in enumerate(it.near(last))]
    steps.append(functools.partial(it.far_seed, last, high_sign))
    steps.append(it.reaching(low_a, low_b, low_m, low_p, 0, -1, 0))
    steps.append(it.reaching(high_a, high_b, high_m, high_p, last, it.groups, BS))

    staggered(steps)


def border(
    side, groups, upper_half, lines, mine, theirs, a_ref, b_ref, m_ref, p_ref, square, sign, halo,
    first, last, sent
):
    at = 1 - side
    edge_group, outer_group = (0, -1) if side == 0 else (groups - 1, groups)
    offset = 0 if side == 0 else 2 * REACH
    below = REACH if side == 0 else 0
    zero = jnp.zeros((BS, WIDE), F32)

    def padded(rows, front):
        return split(jnp.concatenate([zero] + rows if front else rows + [zero], axis=0))

    whole_rows = []
    for p in range(REACH):
        rows = slice(p * HALF, (p + 1) * HALF)
        whole_rows.append(
            jnp.concatenate(
                [
                    jnp.where(upper_half, theirs[rows, :], mine[rows, :]),
                    jnp.where(upper_half, mine[rows, :], theirs[rows, :]),
                ],
                axis=0,
            )
        )

    def block(p, c):
        k = c - p + below
        if 0 <= k <= REACH:
            return whole_rows[p][:, k * BS : (k + 1) * BS]
        k = p - c + below
        if 0 <= c < REACH and 0 <= k <= REACH:
            return whole_rows[c][:, k * BS : (k + 1) * BS].T
        return jnp.zeros((BS, BS), F32)

    base = -5 if side == 0 else 0
    for p in range(REACH):
        rows = slice((p + at) * BS, (p + at + 1) * BS)
        for t in range(4):
            value = jnp.concatenate([block(p, base + 2 * t), block(p, base + 2 * t + 1)], axis=1)
            for q, x in enumerate(split(value)):
                halo[q, rows, t * 2 * BS : (t + 1) * 2 * BS] = x
    rows = slice(0, BS) if side == 0 else slice(REACH * BS, WIDE)
    for q in range(2):
        halo[q, rows, :] = jnp.zeros((BS, 2 * WIDE), BF)

    whole = [halo[q] for q in range(2)]
    outer_rows = slice(at * BS, (at + REACH) * BS)
    inner = slice(WIDE, 2 * WIDE) if side == 0 else slice(0, WIDE)
    to_edge = product([([m_ref[q] for q in range(2)], [x[:, inner] for x in whole])], True)
    among = product([([x[outer_rows] for x in whole], whole)], True)
    yield
    first[0] = to_edge + b_ref[...]
    rows = [
        first[0, s * BS : (s + 1) * BS] * line_of(lines, edge_group, s + 1 - at, outer_group)
        for s in range(REACH)
    ]
    across = padded(rows, side == 1)
    reach_out = [p_ref[q, 0] for q in range(2)]
    back = product([(reach_out, across)], True)
    for s in range(REACH):
        part = jnp.where(upper_half, rows[s][HALF:], rows[s][:HALF])
        for t in range(REACH):
            k = t - s + offset
            if 0 <= k < SPAN:
                square[s, k] = part[:, (t + at) * BS : (t + at + 1) * BS]
    sent(0)
    yield
    first[1] = among + a_ref[...]
    rows = [
        first[1, p * BS : (p + 1) * BS] * line_of(lines, outer_group, p + at, outer_group)
        for p in range(REACH)
    ]
    inside = [p_ref[q, 1] for q in range(2)]
    out = product([(reach_out, padded(rows, side == 0)), (inside, across)])
    last[1] = back
    for s in range(REACH):
        close = last[1, s * HALF : (s + 1) * HALF] * (
            line_of(lines, edge_group, s + 1 - at, edge_group) * 0.5
        )
        for t in range(REACH):
            k = t - s + REACH
            sign[s, k] = sign[s, k] - close[:, (t + 1 - at) * BS : (t + 2 - at) * BS]
    yield
    last[0] = out
    for s in range(REACH):
        far = last[0, s * HALF : (s + 1) * HALF] * (
            line_of(lines, edge_group, s + 1 - at, outer_group) * 0.5
        )
        for t in range(REACH):
            k = t - s + offset
            if 0 <= k < SPAN:
                sign[s, k] = sign[s, k] - far[:, (t + at) * BS : (t + at + 1) * BS]
    sent(1)


def border_kernel(
    low_own, low_other, high_own, high_other, lines, sign_last, low_a, low_b, low_m, low_p, high_a,
    high_b, high_m, high_p, low_square_in, high_square_in, low_sign_in, high_sign_in, square_in,
    sign_in, low_square, high_square, low_sign, high_sign, square_out, sign_out, halo, first, last,
    sems, last_sems, *, groups, half_axis
):
    count = square_in.shape[0]
    upper_half = lax.axis_index(half_axis) == 1
    stores = []

    def send(source, target, rows, blocks, sem):
        from_rows = (0, rows[1] - rows[0])
        store = pltpu.make_async_copy(
            blocks_of(source, from_rows, blocks), blocks_of(target, rows, blocks), sem
        )
        store.start()
        stores.append(store)

    send(sign_last, sign_out, (count - GROUP, count - REACH), (0, SPAN), last_sems.at[0])
    send(high_sign, sign_out, (count - REACH, count), inner_blocks(1, False), last_sems.at[1])
    squares, signs = (low_square, high_square), (low_sign, high_sign)

    def side(n, *refs):
        def sent(i):
            source, target = ((squares[n], square_out), (signs[n], sign_out))[i]
            rows = (0, REACH) if n == 0 else (count - REACH, count)
            send(source, target, rows, outer_blocks(n, i == 0), sems.at[n, i])

        return border(
            n, groups, upper_half, lines, *refs, squares[n], signs[n], halo.at[n], first.at[n],
            last.at[n], sent,
        )

    works = [
        side(0, low_own, low_other, low_a, low_b, low_m, low_p),
        side(1, high_own, high_other, high_a, high_b, high_m, high_p),
    ]
    for _ in range(4):
        for work in works:
            next(work, None)
    for store in stores:
        store.wait()


def shards(matrix, pattern, *, axes, half_axis):
    count = matrix.shape[0]
    groups = count // GROUP
    flags = pattern.T
    vmem = pl.BlockSpec(memory_space=pltpu.VMEM)
    hbm = pl.BlockSpec(memory_space=pl.ANY)
    params = pltpu.CompilerParams(vmem_limit_bytes=LIMIT)

    top, bottom = matrix[:REACH, REACH:], matrix[count - REACH :, : REACH + 1]
    edge = jax.ShapeDtypeStruct((REACH * HALF, (REACH + 1) * BS), F32)
    to_left, to_right = pl.pallas_call(
        edge_kernel,
        out_shape=(edge, edge),
        in_specs=[vmem] * 2,
        out_specs=[vmem] * 2,
        compiler_params=pltpu.CompilerParams(
            vmem_limit_bytes=LIMIT, allow_input_fusion=[True, True]
        ),
        cost_estimate=pl.CostEstimate(
            flops=1 * 10**9, bytes_accessed=2**20, transcendentals=0
        ),
    )(top, bottom)
    size = 1
    for axis in axes:
        size *= lax.axis_size(axis)
    swap = [(0, 1), (1, 0)]
    other = lax.ppermute(matrix, half_axis, swap)
    forward = [(i, (i + 1) % size) for i in range(size)]
    backward = [(target, source) for source, target in forward]
    high_own = lax.ppermute(to_left, axes, backward)
    low_own = lax.ppermute(to_right, axes, forward)

    band = jax.ShapeDtypeStruct(matrix.shape, F32)
    edges = jax.ShapeDtypeStruct((REACH, SPAN, HALF, BS), F32)
    full = jax.ShapeDtypeStruct((2, groups, WIDE, 3 * WIDE), BF)
    mine = jax.ShapeDtypeStruct((2, groups, GROUP * HALF, 3 * WIDE), BF)
    keep = jax.ShapeDtypeStruct((2, 3 * groups, WIDE, WIDE), BF)
    lines = jax.ShapeDtypeStruct(((groups + 2) * GROUP, 3 * WIDE), F32)
    ends_out = [
        jax.ShapeDtypeStruct((REACH * BS, WIDE), F32),
        jax.ShapeDtypeStruct((REACH * BS, WIDE), F32),
        jax.ShapeDtypeStruct((2, REACH * BS, WIDE), BF),
        jax.ShapeDtypeStruct((2, 2, REACH * HALF, WIDE), BF),
    ]
    rows = jax.ShapeDtypeStruct((GROUP,) + matrix.shape[1:], F32)
    square, sign, low_square, high_square, low_sign, full, mine, keep, lines = pl.pallas_call(
        functools.partial(first_kernel, axes=axes, half_axis=half_axis),
        out_shape=[band, band, edges, edges, edges, full, mine, keep, lines],
        in_specs=[vmem] * 3,
        out_specs=[hbm] * 2 + [vmem] * 7,
        scratch_shapes=[
            pltpu.VMEM((groups,) + rows.shape, F32),
            pltpu.VMEM((groups - 1,) + rows.shape, F32),
            pltpu.VMEM((2 * groups - 1 + 3 * groups - 4, WIDE, WIDE), F32),
            pltpu.SemaphoreType.DMA((2, groups)),
            pltpu.SemaphoreType.DMA((3,)),
        ],
        compiler_params=params,
        cost_estimate=pl.CostEstimate(
            flops=3 * 2 * 16 * WIDE**3, bytes_accessed=16 * 2**20, transcendentals=0
        ),
    )(matrix, other, flags)

    low_own, low_sign = lax.optimization_barrier((low_own, low_sign))
    high_own, low_sign = lax.optimization_barrier((high_own, low_sign))
    low_other = lax.ppermute(low_own, half_axis, swap)
    high_other = lax.ppermute(high_own, half_axis, swap)

    sign_last, high_sign, *ends = pl.pallas_call(
        last_kernel,
        out_shape=[rows, edges] + ends_out * 2,
        in_specs=[vmem] * 5,
        out_specs=[vmem] * 10,
        scratch_shapes=[pltpu.VMEM((2, GROUP * HALF, WIDE), F32)],
        compiler_params=params,
        cost_estimate=pl.CostEstimate(
            flops=3 * 2 * 4 * WIDE**3, bytes_accessed=4 * 2**20, transcendentals=0
        ),
    )(matrix, lines, full, mine, keep)

    outs = pl.pallas_call(
        functools.partial(border_kernel, groups=groups, half_axis=half_axis),
        out_shape=[edges] * 4 + [band] * 2,
        in_specs=[vmem] * 18 + [hbm] * 2,
        out_specs=[vmem] * 4 + [hbm] * 2,
        scratch_shapes=[
            pltpu.VMEM((2, 2, WIDE, 2 * WIDE), BF),
            pltpu.VMEM((2, 2, REACH * BS, WIDE), F32),
            pltpu.VMEM((2, 2, REACH * HALF, WIDE), F32),
            pltpu.SemaphoreType.DMA((2, 2)),
            pltpu.SemaphoreType.DMA((2,)),
        ],
        input_output_aliases={14 + i: i for i in range(6)},
        compiler_params=params,
        cost_estimate=pl.CostEstimate(
            flops=3 * 2 * 4 * WIDE**3, bytes_accessed=2 * 2**20, transcendentals=0
        ),
    )(
        low_own, low_other, high_own, high_other, lines, sign_last, *ends, low_square, high_square,
        low_sign, high_sign, square, sign,
    )
    return tuple(outs[4:])


def solution(mesh):
    band = P(("group", "row", "col"), None, "rep", None)
    return jax.shard_map(
        functools.partial(shards, axes=("row", "col"), half_axis="rep"),
        mesh=mesh,
        in_specs=(band, P("group", None)),
        out_specs=(band, band),
        check_vma=False,
    )
```
